32 devices in a mesh: prop: 4 (over x, core), dom: 8 (over z, y).
Axes of the slice: x: 2, y: 2, z: 4, core: 2. Of those that a mesh axis runs over, the one named last changes fastest.
Arguments:
- states: float32 [4, 32, 64, 128], P('prop', 'dom'), may hold values from -4 to 4
- accepted: int32 [1], replicated, may hold values from 0 to 3
- noise: float32 [4, 32, 64, 128], P('prop', 'dom'), may hold values from -5 to 5
- source: float32 [32, 64, 128], P('dom'), may hold values from -6 to 6
Outputs:
- pressure: float32 [4, 32, 64, 128], P('prop', 'dom')
The draws below stay inside these ranges and needn't reach their ends.
All inputs are finite; a program needn't handle non-finite values.
Results may differ from the reference program's by a relative error of at most 0.0003.
Values sent between devices are 32-bit elements; how exact they have to be, the bound alone decides.
No kernel may reach another device: no remote copies, remote signals or barrier semaphores. Data moves between devices by JAX's collectives and lax.ppermute only.
A program may use at most 128 MiB of HBM per device.

```python
import math
import jax
import jax.numpy as jnp
from jax import lax

NX = 64
NY = 128
LEVELS = 4
SWEEPS = 2
COARSE_SWEEPS = 64
PROPS = 4
NZ = 32


def steps_of(own_key, shape, pieces, least, top_value):
    def one(position, blocks):
        steps = jax.random.uniform(jax.random.fold_in(jax.random.fold_in(own_key, 6), position), (blocks,), jnp.float32, least / len(pieces), top_value / len(pieces))
        return jnp.repeat(jnp.exp(steps), shape[position] // blocks).reshape((-1,) + (1,) * (len(shape) - position - 1))

    gain = one(*pieces[0])
    for cut in pieces[1:]:
        gain = gain * one(*cut)
    return gain


def bell_draw(own_key, extent, spread, limit, shards=(), held_as=jnp.bfloat16):
    array = spread * jax.random.normal(own_key, extent, jnp.float32)
    if shards:
        array = array * steps_of(own_key, extent, shards, -0.22, 0.18)
    return jnp.clip(array, -limit, limit).astype(held_as)


def setup_inputs(seed: int = 0) -> dict:
    key_list = jax.random.split(jax.random.key(seed), 5)
    states = bell_draw(key_list[0], (PROPS, NZ, NX, NY), 0.7, 4.0, ((0, 4), (1, 8)), jnp.float32)
    accepted = jax.random.randint(key_list[1], (1,), 0, PROPS).astype(jnp.int32)
    noise = bell_draw(key_list[2], (PROPS, NZ, NX, NY), 1.0, 5.0, ((0, 4), (1, 8)), jnp.float32)
    source = bell_draw(key_list[3], (NZ, NX, NY), 1.0, 6.0, ((0, 8),), jnp.float32)
    return dict(states=states, accepted=accepted, noise=noise, source=source)


OMEGA = 0.7
BETA = 0.4
SHRINK = math.sqrt(1.0 - BETA * BETA)
ZSCALE = 16.0

def shift_lower(values, axis):
    axis = values.ndim + axis
    count = values.shape[axis]
    kept = lax.slice_in_dim(values, 0, count - 1, axis=axis)
    return jnp.concatenate([jnp.zeros_like(lax.slice_in_dim(values, 0, 1, axis=axis)), kept], axis=axis)

def shift_upper(values, axis):
    axis = values.ndim + axis
    count = values.shape[axis]
    kept = lax.slice_in_dim(values, 1, count, axis=axis)
    return jnp.concatenate([kept, jnp.zeros_like(lax.slice_in_dim(values, 0, 1, axis=axis))], axis=axis)

def harmonic(first, second):
    return 2.0 * first * second / (first + second)

def coefficients(perm, padded, scale):
    inner_x = harmonic(perm[..., 1:, :], perm[..., :-1, :])
    west = jnp.concatenate([perm[..., :1, :], inner_x], axis=-2)
    east = jnp.concatenate([inner_x, perm[..., -1:, :]], axis=-2)
    inner_y = harmonic(perm[..., 1:], perm[..., :-1])
    south = jnp.concatenate([perm[..., :1], inner_y], axis=-1)
    north = jnp.concatenate([inner_y, perm[..., -1:]], axis=-1)
    below = harmonic(padded[..., :-2, :, :], perm)
    above = harmonic(padded[..., 2:, :, :], perm)
    zfactor = ZSCALE * scale
    parts = [west * scale, east * scale, south * scale, north * scale, below * zfactor, above * zfactor]
    diagonal = parts[0] + parts[1] + parts[2] + parts[3] + parts[4] + parts[5]
    return parts + [diagonal, OMEGA / diagonal]

def apply_op(values, padded, coefs):
    result = coefs[6] * values - coefs[0] * shift_lower(values, -2) - coefs[1] * shift_upper(values, -2)
    result = result - coefs[2] * shift_lower(values, -1) - coefs[3] * shift_upper(values, -1)
    return result - coefs[4] * padded[..., :-2, :, :] - coefs[5] * padded[..., 2:, :, :]

def sweep(values, right, coefs, pad_z):
    return values + coefs[7] * (right - apply_op(values, pad_z(values), coefs))

def sum_children(values):
    shape = values.shape
    split = values.reshape(shape[:-3] + (shape[-3] // 2, 2, shape[-2] // 2, 2, shape[-1] // 2, 2))
    return split.sum(axis=(-5, -3, -1))

def prolong(values):
    return jnp.repeat(jnp.repeat(jnp.repeat(values, 2, axis=-3), 2, axis=-2), 2, axis=-1)

def zero_pad(values):
    widths = [(0, 0)] * (values.ndim - 3) + [(1, 1), (0, 0), (0, 0)]
    return jnp.pad(values, widths)

def coarse_solve(right, perm, level, pad_z, pad_perm):
    coefs = coefficients(perm, pad_perm(perm), 4.0 ** level)
    start = coefs[7] * right
    return lax.fori_loop(0, COARSE_SWEEPS - 1, lambda step, values: sweep(values, right, coefs, pad_z), start)

def level_cycle(right, perm, level, pad_z, pad_perm, deeper):
    coefs = coefficients(perm, pad_perm(perm), 4.0 ** level)
    values = coefs[7] * right
    for step in range(SWEEPS - 1):
        values = sweep(values, right, coefs, pad_z)
    residue = right - apply_op(values, pad_z(values), coefs)
    update = deeper(sum_children(residue), sum_children(perm) * 0.125, level + 1)
    values = values + prolong(update)
    for step in range(SWEEPS):
        values = sweep(values, right, coefs, pad_z)
    return values

def local_cycle(right, perm, level):
    if level == LEVELS - 1:
        return coarse_solve(right, perm, level, zero_pad, zero_pad)
    return level_cycle(right, perm, level, zero_pad, zero_pad, local_cycle)

def reference(states, accepted, noise, source):
    current = lax.dynamic_index_in_dim(states, accepted[0], 0, keepdims=False)
    theta = SHRINK * current[None] + BETA * noise
    return lax.map(lambda field: local_cycle(source, jnp.exp(field), 0), theta)
```

```python
import functools
import math

import jax
import jax.numpy as jnp
from jax import lax
from jax.experimental import pallas as pl
from jax.experimental.pallas import tpu as pltpu
from jax.sharding import PartitionSpec as P

COARSE_SWEEPS = 64
OMEGA = 0.7
KEEP = 1.0 - OMEGA
BETA = 0.4
SHRINK = math.sqrt(1.0 - BETA * BETA)
ZSCALE = 16.0
LANES = 128
VMEM_LIMIT = 40 * 1024 * 1024
F32 = jnp.float32
WEST, EAST, SOUTH, NORTH, BELOW, ABOVE, CONST = range(7)


def iota(shape, dim):
    return lax.broadcasted_iota(jnp.int32, shape, dim)


def roll(x, amount, axis):
    axis = axis % x.ndim
    return pltpu.roll(x, amount % x.shape[axis], axis)


def harmonic(a, b):
    return 2.0 * a * b / (a + b)


def exact_dot(x, selector):
    high = x.astype(jnp.bfloat16)
    rest = x - high.astype(F32)
    middle = rest.astype(jnp.bfloat16)
    low = (rest - middle.astype(F32)).astype(jnp.bfloat16)
    dot = functools.partial(jnp.dot, preferred_element_type=F32)
    return dot(high, selector) + dot(middle, selector) + dot(low, selector)


def face_terms(perm, lower, upper, below_scale, above_scale, ny):
    shape = perm.shape
    rows = iota(shape, 0)
    columns = lax.rem(iota(shape, 1), ny)
    west = jnp.where(rows == 0, 0.0, harmonic(perm, roll(perm, 1, 0)))
    east = roll(west, -1, 0)
    south = jnp.where(columns == 0, 0.0, harmonic(perm, roll(perm, 1, 1)))
    north = roll(south, -1, 1)
    below = below_scale * harmonic(perm, lower)
    above = above_scale * harmonic(perm, upper)
    ends = jnp.where(rows == 0, perm, 0.0) + jnp.where(rows == shape[0] - 1, perm, 0.0)
    ends = ends + jnp.where(columns == 0, perm, 0.0) + jnp.where(columns == ny - 1, perm, 0.0)
    diagonal = west + east + south + north + below + above + ends
    return (west, east, south, north, below, above), diagonal


def neighbours(values, lower, upper, coefs):
    total = coefs[0] * roll(values, 1, 0) + coefs[1] * roll(values, -1, 0)
    total = total + (coefs[2] * roll(values, 1, 1) + coefs[3] * roll(values, -1, 1))
    return total + (coefs[4] * lower + coefs[5] * upper)


def lane_pairs(count, ny, step, offset):
    shape = (LANES, LANES)
    source, target = iota(shape, 0), iota(shape, 1)
    lane = (source // ny * step + offset) * (ny // 2) + lax.rem(source, ny) // 2
    return jnp.where((target == lane) & (source < count * ny), 1.0, 0.0).astype(jnp.bfloat16)


def lane_spread(count, ny, step, offset):
    shape = (LANES, LANES)
    source, target = iota(shape, 1), iota(shape, 0)
    lane = (source // ny * step + offset) * (ny // 2) + lax.rem(source, ny) // 2
    return jnp.where((target == lane) & (source < count * ny), 1.0, 0.0).astype(jnp.bfloat16)


def fine_kernel(
    layers,
    dom_ref,
    cur_lo, cur, cur_up,
    nos_lo, nos, nos_up,
    src_lo, src, src_up,
    coef_out, level_out, coarse_out,
    perm, coef, const, values, diag, pair_right, pair_perm, sems,
):
    height = cur.shape[0]
    ext = height + 6
    dom = dom_ref[0]

    for i in range(height):
        for at, c, n in ((0, cur_lo, nos_lo), (height, cur, nos), (2 * height, cur_up, nos_up)):
            perm[at + i] = jnp.exp(SHRINK * c[i] + BETA * n[i])

    shape = perm.shape[1:]

    def build(i, right):
        centre = perm[height - 3 + i]
        z = dom * height + i - 3
        below = jnp.where((z > 0) & (z < layers), ZSCALE, 0.0)
        above = jnp.where((z + 1 > 0) & (z + 1 < layers), ZSCALE, 0.0)
        faces, diagonal = face_terms(
            centre, perm[height - 4 + i], perm[height - 2 + i], below, above, LANES
        )
        inverse = OMEGA / diagonal
        for k in range(6):
            coef[k, i] = inverse * faces[k]
        const[i] = inverse * right
        return diagonal

    for i in range(3):
        build(i, src_lo[height - 3 + i])

    def own(i, carry):
        diag[i] = build(i + 3, src[i])
        return carry

    lax.fori_loop(0, height, own, 0)
    for i in range(3):
        build(height + 3 + i, src_up[i])

    copies = [
        pltpu.make_async_copy(coef.at[k, pl.ds(2, height + 2)], coef_out.at[k], sems.at[k])
        for k in range(6)
    ]
    copies.append(pltpu.make_async_copy(const.at[pl.ds(2, height + 2)], coef_out.at[6], sems.at[6]))
    for copy in copies:
        copy.start()

    def first(i, carry):
        start = const[i + 1]
        near = neighbours(start, const[i], const[i + 2], [coef[k, i + 1] for k in range(6)])
        values[i] = KEEP * start + start + near
        return carry

    lax.fori_loop(0, height + 4, first, 0)
    copies.append(pltpu.make_async_copy(values, level_out, sems.at[7]))
    copies[-1].start()

    def residue(i):
        centre = values[i + 2]
        near = neighbours(
            centre, values[i + 1], values[i + 3], [coef[k, i + 3] for k in range(6)]
        )
        return (const[i + 3] - OMEGA * centre + near) * (diag[i] * (1.0 / OMEGA))

    for m in range(height // 2):
        pair_right[m] = residue(2 * m) + residue(2 * m + 1)
        pair_perm[m] = (perm[height + 2 * m] + perm[height + 2 * m + 1]) * 0.125
    half = shape[0] // 2
    to_right = lane_pairs(1, LANES, 1, 0)
    to_perm = lane_pairs(1, LANES, 1, 1)
    for m in range(height // 2):
        right = pair_right[m, pl.ds(0, half, 2), :] + pair_right[m, pl.ds(1, half, 2), :]
        field = pair_perm[m, pl.ds(0, half, 2), :] + pair_perm[m, pl.ds(1, half, 2), :]
        coarse_out[m] = exact_dot(right, to_right) + exact_dot(field, to_perm)
    for copy in copies:
        copy.wait()


class Packed:
    def __init__(self, nz, nx, ny):
        self.nz, self.nx, self.ny = nz, nx, ny
        self.groups = min(LANES // ny, nz)
        self.planes = nz // self.groups

    def lower(self, planes, p):
        return planes[p - 1] if p else roll(planes[self.planes - 1], self.ny, 1)

    def upper(self, planes, p):
        return planes[p + 1] if p + 1 < self.planes else roll(planes[0], -self.ny, 1)

    def system(self, right, perm, level):
        lane = iota((self.nx, LANES), 1)
        used = lane < self.groups * self.ny
        if self.groups * self.ny < LANES:
            perm = [jnp.where(used, x, 1.0) for x in perm]
        coefs, const, diagonals = [], [], []
        for p in range(self.planes):
            below, above = ZSCALE, ZSCALE
            if p == 0:
                below = jnp.where(lane < self.ny, 0.0, ZSCALE)
            if p + 1 == self.planes:
                above = jnp.where(lane < (self.groups - 1) * self.ny, ZSCALE, 0.0)
            faces, diagonal = face_terms(
                perm[p], self.lower(perm, p), self.upper(perm, p), below, above, self.ny
            )
            inverse = OMEGA / diagonal
            coefs.append([inverse * face for face in faces])
            const.append(inverse * right[p] * (4.0**-level))
            diagonals.append(diagonal * (4.0**level / OMEGA))
        return coefs, const, diagonals

    def near(self, values, coefs):
        return [
            neighbours(values[p], self.lower(values, p), self.upper(values, p), coefs[p])
            for p in range(self.planes)
        ]

    def sweep(self, values, coefs, const):
        near = self.near(values, coefs)
        return [KEEP * v + (c + n) for v, c, n in zip(values, const, near)]

    def coarser(self):
        return Packed(self.nz // 2, self.nx // 2, self.ny // 2)

    def restrict(self, values, pad):
        coarse = self.coarser()
        step = coarse.groups // self.groups
        half = coarse.nx
        out = []
        for p in range(coarse.planes):
            total = None
            for j in range(step):
                m = j * coarse.planes + p
                pad[m] = values[2 * m] + values[2 * m + 1]
                rows = pad[m, pl.ds(0, half, 2), :] + pad[m, pl.ds(1, half, 2), :]
                part = exact_dot(rows, lane_pairs(self.groups, self.ny, step, j))
                total = part if total is None else total + part
            out.append(total)
        return out

    def prolong(self, values, pad):
        coarse = self.coarser()
        step = coarse.groups // self.groups
        half = coarse.nx
        out = []
        for m in range(self.planes // 2):
            j, p = divmod(m, coarse.planes)
            wide = exact_dot(values[p], lane_spread(self.groups, self.ny, step, j))
            pad[m, pl.ds(0, half, 2), :] = wide
            pad[m, pl.ds(1, half, 2), :] = wide
            spread = pad[m]
            out += [spread, spread]
        return out


def coarsest(grid, right, perm, level):
    coefs, const, _ = grid.system(right, perm, level)
    return lax.fori_loop(
        0,
        COARSE_SWEEPS - 1,
        lambda step, values: tuple(grid.sweep(values, coefs, const)),
        tuple(const),
        unroll=7,
    )


def packed_cycle(grid, right, perm, level, pads):
    if not pads:
        return coarsest(grid, right, perm, level)
    pad_right, pad_perm = pads[0]
    coefs, const, diagonals = grid.system(right, perm, level)
    values = grid.sweep(const, coefs, const)
    near = grid.near(values, coefs)
    residue = [
        (c - OMEGA * v + n) * d for c, v, n, d in zip(const, values, near, diagonals)
    ]
    coarse_right = grid.restrict(residue, pad_right)
    coarse_perm = [x * 0.125 for x in grid.restrict(perm, pad_perm)]
    update = packed_cycle(grid.coarser(), coarse_right, coarse_perm, level + 1, pads[1:])
    values = [v + e for v, e in zip(values, grid.prolong(update, pad_right))]
    for _ in range(2):
        values = grid.sweep(values, coefs, const)
    return values


def coarse_kernel(
    dom_ref, gathered, coef_in, level_in, out,
    coef, level, first, pad_right1, pad_perm1, pad_right2, pad_perm2, update, sems,
):
    height = out.shape[0]
    dom = dom_ref[0]
    copies = [
        pltpu.make_async_copy(coef_in, coef, sems.at[0]),
        pltpu.make_async_copy(level_in, level, sems.at[1]),
    ]
    for copy in copies:
        copy.start()
    domains, own, nx, _ = gathered.shape
    ny = LANES // 2
    grid = Packed(domains * own, nx, ny)
    left = iota((nx, LANES), 1) < ny
    right, perm = [], []
    for p in range(grid.planes):
        a = gathered[p // own, p % own]
        q = grid.planes + p
        b = gathered[q // own, q % own]
        right.append(jnp.where(left, a, roll(b, ny, 1)))
        perm.append(jnp.where(left, roll(a, ny, 1), b))
    pads = [(pad_right1, pad_perm1), (pad_right2, pad_perm2)]
    solved = packed_cycle(grid, right, perm, 1, pads)
    for p in range(grid.planes):
        update[p] = solved[p]
    for copy in copies:
        copy.wait()
    spread = lane_spread(1, LANES, 1, 0)
    for j in range(own + 2):
        layer = jnp.clip(dom * own + j - 1, 0, grid.nz - 1)
        group = layer // grid.planes
        plane = update[lax.rem(layer, grid.planes)]
        plane = jnp.where(group == 0, plane, roll(plane, ny, 1))
        wide = exact_dot(plane, spread)
        pad_perm0 = first.at[0]
        pad_perm0[pl.ds(0, nx, 2), :] = wide
        pad_perm0[pl.ds(1, nx, 2), :] = wide
        whole = first[0]
        level[2 * j] = level[2 * j] + whole
        level[2 * j + 1] = level[2 * j + 1] + whole

    def sweep(source, at, i):
        centre = source[i + 1]
        near = neighbours(
            centre, source[i], source[i + 2], [coef[k, at + i] for k in range(6)]
        )
        return KEEP * centre + (coef[6, at + i] + near)

    def one(i, carry):
        first[i] = sweep(level, 0, i)
        return carry

    lax.fori_loop(0, height + 2, one, 0)

    def two(i, carry):
        out[i] = sweep(first, 1, i)
        return carry

    lax.fori_loop(0, height, two, 0)


def fine_part(dom, current, noise, source, layers):
    height, nx, ny = current[1].shape
    field = lambda *lead: pltpu.VMEM(lead + (nx, ny), F32)
    vmem = pl.BlockSpec(memory_space=pltpu.VMEM)
    smem = pl.BlockSpec(memory_space=pltpu.SMEM)
    anywhere = pl.BlockSpec(memory_space=pl.ANY)
    return pl.pallas_call(
        functools.partial(fine_kernel, layers),
        out_shape=(
            jax.ShapeDtypeStruct((7, height + 2, nx, ny), F32),
            jax.ShapeDtypeStruct((height + 4, nx, ny), F32),
            jax.ShapeDtypeStruct((height // 2, nx // 2, ny), F32),
        ),
        in_specs=[smem] + [vmem] * 9,
        out_specs=(anywhere, anywhere, vmem),
        scratch_shapes=[
            field(3 * height),
            field(6, height + 6),
            field(height + 6),
            field(height + 4),
            field(height),
            field(height // 2),
            field(height // 2),
            pltpu.SemaphoreType.DMA((8,)),
        ],
        compiler_params=pltpu.CompilerParams(vmem_limit_bytes=VMEM_LIMIT),
        name="fine",
    )(dom, *current, *noise, *source)


def coarse_part(dom, gathered, coefs, values, height):
    _, _, nx, ny = coefs.shape
    field = lambda *shape: pltpu.VMEM(shape, F32)
    grid1 = Packed(gathered.shape[0] * gathered.shape[1], nx // 2, ny // 2)
    grid2 = grid1.coarser()
    pads1 = field(grid1.planes // 2, grid1.nx, LANES)
    pads2 = field(grid2.planes // 2, grid2.nx, LANES)
    vmem = pl.BlockSpec(memory_space=pltpu.VMEM)
    smem = pl.BlockSpec(memory_space=pltpu.SMEM)
    anywhere = pl.BlockSpec(memory_space=pl.ANY)
    return pl.pallas_call(
        coarse_kernel,
        out_shape=jax.ShapeDtypeStruct((height, nx, ny), F32),
        in_specs=[smem, vmem, anywhere, anywhere],
        out_specs=vmem,
        scratch_shapes=[
            field(*coefs.shape),
            field(*values.shape),
            field(height + 2, nx, ny),
            pads1, pads1, pads2, pads2,
            field(grid1.planes, grid1.nx, LANES),
            pltpu.SemaphoreType.DMA((2,)),
        ],
        compiler_params=pltpu.CompilerParams(vmem_limit_bytes=VMEM_LIMIT),
        name="coarse",
    )(dom, gathered, coefs, values)


def both_sides(x):
    count = lax.axis_size("dom")
    up = [(i, i + 1) for i in range(count - 1)]
    down = [(i + 1, i) for i in range(count - 1)]
    return lax.ppermute(x, "dom", up), lax.ppermute(x, "dom", down)


def body(states, accepted, noise, source):
    props, domains = lax.axis_size("prop"), lax.axis_size("dom")
    height = source.shape[0]
    dom = lax.axis_index("dom").astype(jnp.int32).reshape(1)
    mine = states[0]
    offers = [mine]
    for step in range(1, props):
        offers.append(lax.ppermute(mine, "prop", [(i, i ^ step) for i in range(props)]))
    forcing = jnp.concatenate([noise[0], source], axis=0)
    forcing_lo, forcing_up = both_sides(forcing)
    wanted = lax.axis_index("prop") ^ accepted[0]
    current = offers[0]
    for step in range(1, props):
        current = jnp.where(wanted == step, offers[step], current)
    current_lo, current_up = both_sides(current)
    coefs, values, coarse = fine_part(
        dom,
        (current_lo, current, current_up),
        (forcing_lo[:height], noise[0], forcing_up[:height]),
        (forcing_lo[height:], source, forcing_up[height:]),
        domains * height,
    )
    copies = jnp.broadcast_to(coarse[None], (domains,) + coarse.shape)
    gathered = lax.all_to_all(copies, "dom", 0, 0)
    return coarse_part(dom, gathered, coefs, values, height)[None]


def solution(mesh):
    in_specs = (
        P("prop", "dom", None, None),
        P(),
        P("prop", "dom", None, None),
        P("dom", None, None),
    )
    out_specs = P("prop", "dom", None, None)
    return jax.shard_map(body, mesh=mesh, in_specs=in_specs, out_specs=out_specs, check_vma=False)
```

```python
import functools
import math

import jax
import jax.numpy as jnp
from jax import lax
from jax.experimental import pallas as pl
from jax.experimental.pallas import tpu as pltpu
from jax.sharding import PartitionSpec as P

COARSE_SWEEPS = 64
OMEGA = 0.7
KEEP = 1.0 - OMEGA
BETA = 0.4
SHRINK = math.sqrt(1.0 - BETA * BETA)
ZSCALE = 16.0
LANES = 128
VMEM_LIMIT = 40 * 1024 * 1024
F32 = jnp.float32
WEST, EAST, SOUTH, NORTH, BELOW, ABOVE, CONST = range(7)


def iota(shape, dim):
    return lax.broadcasted_iota(jnp.int32, shape, dim)


def roll(x, amount, axis):
    axis = axis % x.ndim
    return pltpu.roll(x, amount % x.shape[axis], axis)


def harmonic(a, b):
    return 2.0 * a * b / (a + b)


def exact_dot(x, selector):
    high = x.astype(jnp.bfloat16)
    rest = x - high.astype(F32)
    middle = rest.astype(jnp.bfloat16)
    low = (rest - middle.astype(F32)).astype(jnp.bfloat16)
    dot = functools.partial(jnp.dot, preferred_element_type=F32)
    return dot(high, selector) + dot(middle, selector) + dot(low, selector)


def face_terms(perm, lower, upper, below_scale, above_scale, ny):
    shape = perm.shape
    rows = iota(shape, 0)
    columns = lax.rem(iota(shape, 1), ny)
    west = jnp.where(rows == 0, 0.0, harmonic(perm, roll(perm, 1, 0)))
    east = roll(west, -1, 0)
    south = jnp.where(columns == 0, 0.0, harmonic(perm, roll(perm, 1, 1)))
    north = roll(south, -1, 1)
    below = below_scale * harmonic(perm, lower)
    above = above_scale * harmonic(perm, upper)
    ends = jnp.where(rows == 0, perm, 0.0) + jnp.where(rows == shape[0] - 1, perm, 0.0)
    ends = ends + jnp.where(columns == 0, perm, 0.0) + jnp.where(columns == ny - 1, perm, 0.0)
    diagonal = west + east + south + north + below + above + ends
    return (west, east, south, north, below, above), diagonal


def neighbours(values, lower, upper, coefs):
    total = coefs[0] * roll(values, 1, 0) + coefs[1] * roll(values, -1, 0)
    total = total + (coefs[2] * roll(values, 1, 1) + coefs[3] * roll(values, -1, 1))
    return total + (coefs[4] * lower + coefs[5] * upper)


def lane_pairs(count, ny, step, offset):
    shape = (LANES, LANES)
    source, target = iota(shape, 0), iota(shape, 1)
    lane = (source // ny * step + offset) * (ny // 2) + lax.rem(source, ny) // 2
    return jnp.where((target == lane) & (source < count * ny), 1.0, 0.0).astype(jnp.bfloat16)


def lane_spread(count, ny, step, offset):
    shape = (LANES, LANES)
    source, target = iota(shape, 1), iota(shape, 0)
    lane = (source // ny * step + offset) * (ny // 2) + lax.rem(source, ny) // 2
    return jnp.where((target == lane) & (source < count * ny), 1.0, 0.0).astype(jnp.bfloat16)


def fine_kernel(
    layers,
    dom_ref,
    cur, cur_pair, cur_other,
    nos, nos_pair, nos_other,
    src, src_pair, src_other,
    coef_out, level_out, coarse_out,
    perm, right, coef, const, values, diag, pair_right, pair_perm, sems,
):
    height = cur.shape[0]
    dom = dom_ref[0]
    pair_at = jnp.where(lax.rem(dom, 2) == 0, 2 * height, 0)
    other_at = 2 * height - pair_at

    for i in range(height):
        for at, c, n, s in (
            (height, cur, nos, src),
            (pair_at, cur_pair, nos_pair, src_pair),
            (other_at, cur_other, nos_other, src_other),
        ):
            perm[at + i] = jnp.exp(SHRINK * c[i] + BETA * n[i])
            right[at + i] = s[i]

    def build(i, carry):
        z = dom * height + i - 3
        below = jnp.where((z > 0) & (z < layers), ZSCALE, 0.0)
        above = jnp.where((z + 1 > 0) & (z + 1 < layers), ZSCALE, 0.0)
        at = height - 3 + i
        faces, diagonal = face_terms(perm[at], perm[at - 1], perm[at + 1], below, above, LANES)
        inverse = OMEGA / diagonal
        for k in range(6):
            coef[k, i] = inverse * faces[k]
        const[i] = inverse * right[at]
        diag[i] = diagonal
        return carry

    lax.fori_loop(0, height + 6, build, 0)

    copies = [
        pltpu.make_async_copy(coef.at[k, pl.ds(2, height + 2)], coef_out.at[k], sems.at[k])
        for k in range(6)
    ]
    copies.append(pltpu.make_async_copy(const.at[pl.ds(2, height + 2)], coef_out.at[6], sems.at[6]))
    for copy in copies:
        copy.start()

    def first(i, carry):
        start = const[i + 1]
        near = neighbours(start, const[i], const[i + 2], [coef[k, i + 1] for k in range(6)])
        values[i] = KEEP * start + start + near
        return carry

    lax.fori_loop(0, height + 4, first, 0)
    copies.append(pltpu.make_async_copy(values, level_out, sems.at[7]))
    copies[-1].start()

    def residue(i):
        centre = values[i + 2]
        near = neighbours(
            centre, values[i + 1], values[i + 3], [coef[k, i + 3] for k in range(6)]
        )
        return (const[i + 3] - OMEGA * centre + near) * (diag[i + 3] * (1.0 / OMEGA))

    for m in range(height // 2):
        pair_right[m] = residue(2 * m) + residue(2 * m + 1)
        pair_perm[m] = (perm[height + 2 * m] + perm[height + 2 * m + 1]) * 0.125
    half = pair_right.shape[1] // 2
    to_right = lane_pairs(1, LANES, 1, 0)
    to_perm = lane_pairs(1, LANES, 1, 1)
    for m in range(height // 2):
        rows = pair_right[m, pl.ds(0, half, 2), :] + pair_right[m, pl.ds(1, half, 2), :]
        field = pair_perm[m, pl.ds(0, half, 2), :] + pair_perm[m, pl.ds(1, half, 2), :]
        coarse_out[m] = exact_dot(rows, to_right) + exact_dot(field, to_perm)
    for copy in copies:
        copy.wait()


class Packed:
    def __init__(self, nz, nx, ny):
        self.nz, self.nx, self.ny = nz, nx, ny
        self.groups = min(LANES // ny, nz)
        self.planes = nz // self.groups

    def lower(self, planes, p):
        return planes[p - 1] if p else roll(planes[self.planes - 1], self.ny, 1)

    def upper(self, planes, p):
        return planes[p + 1] if p + 1 < self.planes else roll(planes[0], -self.ny, 1)

    def system(self, right, perm, level):
        lane = iota((self.nx, LANES), 1)
        used = lane < self.groups * self.ny
        if self.groups * self.ny < LANES:
            perm = [jnp.where(used, x, 1.0) for x in perm]
        coefs, const, diagonals = [], [], []
        for p in range(self.planes):
            below, above = ZSCALE, ZSCALE
            if p == 0:
                below = jnp.where(lane < self.ny, 0.0, ZSCALE)
            if p + 1 == self.planes:
                above = jnp.where(lane < (self.groups - 1) * self.ny, ZSCALE, 0.0)
            faces, diagonal = face_terms(
                perm[p], self.lower(perm, p), self.upper(perm, p), below, above, self.ny
            )
            inverse = OMEGA / diagonal
            coefs.append([inverse * face for face in faces])
            const.append(inverse * right[p] * (4.0**-level))
            diagonals.append(diagonal * (4.0**level / OMEGA))
        return coefs, const, diagonals

    def near(self, values, coefs):
        return [
            neighbours(values[p], self.lower(values, p), self.upper(values, p), coefs[p])
            for p in range(self.planes)
        ]

    def sweep(self, values, coefs, const):
        near = self.near(values, coefs)
        return [KEEP * v + (c + n) for v, c, n in zip(values, const, near)]

    def coarser(self):
        return Packed(self.nz // 2, self.nx // 2, self.ny // 2)

    def restrict(self, values, pad):
        coarse = self.coarser()
        step = coarse.groups // self.groups
        half = coarse.nx
        out = []
        for p in range(coarse.planes):
            total = None
            for j in range(step):
                m = j * coarse.planes + p
                pad[m] = values[2 * m] + values[2 * m + 1]
                rows = pad[m, pl.ds(0, half, 2), :] + pad[m, pl.ds(1, half, 2), :]
                part = exact_dot(rows, lane_pairs(self.groups, self.ny, step, j))
                total = part if total is None else total + part
            out.append(total)
        return out

    def prolong(self, values, pad):
        coarse = self.coarser()
        step = coarse.groups // self.groups
        half = coarse.nx
        out = []
        for m in range(self.planes // 2):
            j, p = divmod(m, coarse.planes)
            wide = exact_dot(values[p], lane_spread(self.groups, self.ny, step, j))
            pad[m, pl.ds(0, half, 2), :] = wide
            pad[m, pl.ds(1, half, 2), :] = wide
            spread = pad[m]
            out += [spread, spread]
        return out


def coarsest(grid, right, perm, level):
    coefs, const, _ = grid.system(right, perm, level)
    return lax.fori_loop(
        0,
        COARSE_SWEEPS - 1,
        lambda step, values: tuple(grid.sweep(values, coefs, const)),
        tuple(const),
        unroll=7,
    )


def packed_cycle(grid, right, perm, level, pads):
    if not pads:
        return coarsest(grid, right, perm, level)
    pad_right, pad_perm = pads[0]
    coefs, const, diagonals = grid.system(right, perm, level)
    values = grid.sweep(const, coefs, const)
    near = grid.near(values, coefs)
    residue = [
        (c - OMEGA * v + n) * d for c, v, n, d in zip(const, values, near, diagonals)
    ]
    coarse_right = grid.restrict(residue, pad_right)
    coarse_perm = [x * 0.125 for x in grid.restrict(perm, pad_perm)]
    update = packed_cycle(grid.coarser(), coarse_right, coarse_perm, level + 1, pads[1:])
    values = [v + e for v, e in zip(values, grid.prolong(update, pad_right))]
    for _ in range(2):
        values = grid.sweep(values, coefs, const)
    return values


def coarse_kernel(
    domains, dom_ref, *refs,
):
    parts, refs = refs[:domains], refs[domains:]
    coef_in, level_in, out, gathered, coef, level, first, *refs = refs
    pad_right1, pad_perm1, pad_right2, pad_perm2, update, sems = refs
    height = out.shape[0]
    dom = dom_ref[0]
    copies = [
        pltpu.make_async_copy(coef_in, coef, sems.at[0]),
        pltpu.make_async_copy(level_in, level, sems.at[1]),
    ]
    for copy in copies:
        copy.start()
    for step, part in enumerate(parts):
        gathered[dom ^ step] = part[...]
    _, own, nx, _ = gathered.shape
    ny = LANES // 2
    grid = Packed(domains * own, nx, ny)
    left = iota((nx, LANES), 1) < ny
    right, perm = [], []
    for p in range(grid.planes):
        a = gathered[p // own, p % own]
        q = grid.planes + p
        b = gathered[q // own, q % own]
        right.append(jnp.where(left, a, roll(b, ny, 1)))
        perm.append(jnp.where(left, roll(a, ny, 1), b))
    pads = [(pad_right1, pad_perm1), (pad_right2, pad_perm2)]
    solved = packed_cycle(grid, right, perm, 1, pads)
    for p in range(grid.planes):
        update[p] = solved[p]
    for copy in copies:
        copy.wait()
    spread = lane_spread(1, LANES, 1, 0)
    for j in range(own + 2):
        layer = jnp.clip(dom * own + j - 1, 0, grid.nz - 1)
        group = layer // grid.planes
        plane = update[lax.rem(layer, grid.planes)]
        plane = jnp.where(group == 0, plane, roll(plane, ny, 1))
        wide = exact_dot(plane, spread)
        pad_perm0 = first.at[0]
        pad_perm0[pl.ds(0, nx, 2), :] = wide
        pad_perm0[pl.ds(1, nx, 2), :] = wide
        whole = first[0]
        level[2 * j] = level[2 * j] + whole
        level[2 * j + 1] = level[2 * j + 1] + whole

    def sweep(source, at, i):
        centre = source[i + 1]
        near = neighbours(
            centre, source[i], source[i + 2], [coef[k, at + i] for k in range(6)]
        )
        return KEEP * centre + (coef[6, at + i] + near)

    def one(i, carry):
        first[i] = sweep(level, 0, i)
        return carry

    lax.fori_loop(0, height + 2, one, 0)

    def two(i, carry):
        out[i] = sweep(first, 1, i)
        return carry

    lax.fori_loop(0, height, two, 0)


def fine_part(dom, current, noise, source, layers):
    height, nx, ny = current[0].shape
    field = lambda *lead: pltpu.VMEM(lead + (nx, ny), F32)
    vmem = pl.BlockSpec(memory_space=pltpu.VMEM)
    smem = pl.BlockSpec(memory_space=pltpu.SMEM)
    anywhere = pl.BlockSpec(memory_space=pl.ANY)
    return pl.pallas_call(
        functools.partial(fine_kernel, layers),
        out_shape=(
            jax.ShapeDtypeStruct((7, height + 2, nx, ny), F32),
            jax.ShapeDtypeStruct((height + 4, nx, ny), F32),
            jax.ShapeDtypeStruct((height // 2, nx // 2, ny), F32),
        ),
        in_specs=[smem] + [vmem] * 9,
        out_specs=(anywhere, anywhere, vmem),
        scratch_shapes=[
            field(3 * height),
            field(3 * height),
            field(6, height + 6),
            field(height + 6),
            field(height + 4),
            field(height + 6),
            field(height // 2),
            field(height // 2),
            pltpu.SemaphoreType.DMA((8,)),
        ],
        compiler_params=pltpu.CompilerParams(vmem_limit_bytes=VMEM_LIMIT),
        name="fine",
    )(dom, *current, *noise, *source)


def coarse_part(dom, parts, coefs, values, height):
    _, _, nx, ny = coefs.shape
    field = lambda *shape: pltpu.VMEM(shape, F32)
    domains = len(parts)
    grid1 = Packed(domains * parts[0].shape[0], nx // 2, ny // 2)
    grid2 = grid1.coarser()
    pads1 = field(grid1.planes // 2, grid1.nx, LANES)
    pads2 = field(grid2.planes // 2, grid2.nx, LANES)
    vmem = pl.BlockSpec(memory_space=pltpu.VMEM)
    smem = pl.BlockSpec(memory_space=pltpu.SMEM)
    anywhere = pl.BlockSpec(memory_space=pl.ANY)
    return pl.pallas_call(
        functools.partial(coarse_kernel, domains),
        out_shape=jax.ShapeDtypeStruct((height, nx, ny), F32),
        in_specs=[smem] + [vmem] * domains + [anywhere, anywhere],
        out_specs=vmem,
        scratch_shapes=[
            field(domains, *parts[0].shape),
            field(*coefs.shape),
            field(*values.shape),
            field(height + 2, nx, ny),
            pads1, pads1, pads2, pads2,
            field(grid1.planes, grid1.nx, LANES),
            pltpu.SemaphoreType.DMA((2,)),
        ],
        compiler_params=pltpu.CompilerParams(vmem_limit_bytes=VMEM_LIMIT),
        name="coarse",
    )(dom, *parts, coefs, values)


def swaps(x, axis, step):
    return lax.ppermute(x, axis, [(i, i ^ step) for i in range(lax.axis_size(axis))])


def both_sides(x):
    count = lax.axis_size("dom")
    pairs = [(0, 0), (count - 1, count - 1)]
    for i in range(1, count - 1, 2):
        pairs += [(i, i + 1), (i + 1, i)]
    return swaps(x, "dom", 1), lax.ppermute(x, "dom", pairs)


def body(states, accepted, noise, source):
    props, domains = lax.axis_size("prop"), lax.axis_size("dom")
    height = source.shape[0]
    dom = lax.axis_index("dom").astype(jnp.int32).reshape(1)
    mine = states[0]
    offers = [mine] + [swaps(mine, "prop", step) for step in range(1, props)]
    noises = (noise[0],) + both_sides(noise[0])
    sources = (source,) + both_sides(source)
    wanted = lax.axis_index("prop") ^ accepted[0]
    current = offers[0]
    for step in range(1, props):
        current = jnp.where(wanted == step, offers[step], current)
    currents = (current,) + both_sides(current)
    coefs, values, coarse = fine_part(dom, currents, noises, sources, domains * height)
    parts = [coarse] + [swaps(coarse, "dom", step) for step in range(1, domains)]
    return coarse_part(dom, parts, coefs, values, height)[None]


def solution(mesh):
    in_specs = (
        P("prop", "dom", None, None),
        P(),
        P("prop", "dom", None, None),
        P("dom", None, None),
    )
    out_specs = P("prop", "dom", None, None)
    return jax.shard_map(body, mesh=mesh, in_specs=in_specs, out_specs=out_specs, check_vma=False)
```

```python
import functools
import math

import jax
import jax.numpy as jnp
from jax import lax
from jax.experimental import pallas as pl
from jax.experimental.pallas import tpu as pltpu
from jax.sharding import PartitionSpec as P

COARSE_SWEEPS = 64
OMEGA = 0.7
KEEP = 1.0 - OMEGA
BETA = 0.4
SHRINK = math.sqrt(1.0 - BETA * BETA)
ZSCALE = 16.0
LANES = 128
VMEM_LIMIT = 40 * 1024 * 1024
F32 = jnp.float32
WEST, EAST, SOUTH, NORTH, BELOW, ABOVE, CONST = range(7)


def iota(shape, dim):
    return lax.broadcasted_iota(jnp.int32, shape, dim)


def roll(x, amount, axis):
    axis = axis % x.ndim
    return pltpu.roll(x, amount % x.shape[axis], axis)


def harmonic(a, b):
    return 2.0 * a * b / (a + b)


def exact_dot(x, selector):
    high = x.astype(jnp.bfloat16)
    rest = x - high.astype(F32)
    middle = rest.astype(jnp.bfloat16)
    low = (rest - middle.astype(F32)).astype(jnp.bfloat16)
    dot = functools.partial(jnp.dot, preferred_element_type=F32)
    return dot(high, selector) + dot(middle, selector) + dot(low, selector)


def face_terms(perm, lower, upper, below_scale, above_scale, ny):
    shape = perm.shape
    rows = iota(shape, 0)
    columns = lax.rem(iota(shape, 1), ny)
    west = jnp.where(rows == 0, 0.0, harmonic(perm, roll(perm, 1, 0)))
    east = roll(west, -1, 0)
    south = jnp.where(columns == 0, 0.0, harmonic(perm, roll(perm, 1, 1)))
    north = roll(south, -1, 1)
    below = below_scale * harmonic(perm, lower)
    above = above_scale * harmonic(perm, upper)
    ends = jnp.where(rows == 0, perm, 0.0) + jnp.where(rows == shape[0] - 1, perm, 0.0)
    ends = ends + jnp.where(columns == 0, perm, 0.0) + jnp.where(columns == ny - 1, perm, 0.0)
    diagonal = west + east + south + north + below + above + ends
    return (west, east, south, north, below, above), diagonal


def neighbours(values, lower, upper, coefs):
    total = coefs[0] * roll(values, 1, 0) + coefs[1] * roll(values, -1, 0)
    total = total + (coefs[2] * roll(values, 1, 1) + coefs[3] * roll(values, -1, 1))
    return total + (coefs[4] * lower + coefs[5] * upper)


def lane_pairs(count, ny, step, offset):
    shape = (LANES, LANES)
    source, target = iota(shape, 0), iota(shape, 1)
    lane = (source // ny * step + offset) * (ny // 2) + lax.rem(source, ny) // 2
    return jnp.where((target == lane) & (source < count * ny), 1.0, 0.0).astype(jnp.bfloat16)


def lane_spread(count, ny, step, offset):
    shape = (LANES, LANES)
    source, target = iota(shape, 1), iota(shape, 0)
    lane = (source // ny * step + offset) * (ny // 2) + lax.rem(source, ny) // 2
    return jnp.where((target == lane) & (source < count * ny), 1.0, 0.0).astype(jnp.bfloat16)


def fine_kernel(
    layers,
    dom_ref,
    per, per_pair, per_other,
    src, src_pair, src_other,
    coef_out, level_out, coarse_out,
    perm, right, coef, const, values, diag, pair_right, pair_perm, sems,
):
    height = per.shape[0]
    dom = dom_ref[0]
    pair_at = jnp.where(lax.rem(dom, 2) == 0, 2 * height, 0)
    other_at = 2 * height - pair_at

    for i in range(height):
        for at, p, s in (
            (height, per, src), (pair_at, per_pair, src_pair), (other_at, per_other, src_other)
        ):
            perm[at + i] = p[i]
            right[at + i] = s[i]

    def build(i, carry):
        z = dom * height + i - 3
        below = jnp.where((z > 0) & (z < layers), ZSCALE, 0.0)
        above = jnp.where((z + 1 > 0) & (z + 1 < layers), ZSCALE, 0.0)
        at = height - 3 + i
        faces, diagonal = face_terms(perm[at], perm[at - 1], perm[at + 1], below, above, LANES)
        inverse = OMEGA / diagonal
        for k in range(6):
            coef[k, i] = inverse * faces[k]
        const[i] = inverse * right[at]
        diag[i] = diagonal
        return carry

    lax.fori_loop(0, height + 6, build, 0)

    copies = [
        pltpu.make_async_copy(coef.at[k, pl.ds(2, height + 2)], coef_out.at[k], sems.at[k])
        for k in range(6)
    ]
    copies.append(pltpu.make_async_copy(const.at[pl.ds(2, height + 2)], coef_out.at[6], sems.at[6]))
    for copy in copies:
        copy.start()

    def first(i, carry):
        start = const[i + 1]
        near = neighbours(start, const[i], const[i + 2], [coef[k, i + 1] for k in range(6)])
        values[i] = KEEP * start + start + near
        return carry

    lax.fori_loop(0, height + 4, first, 0)
    copies.append(pltpu.make_async_copy(values, level_out, sems.at[7]))
    copies[-1].start()

    def residue(i):
        centre = values[i + 2]
        near = neighbours(
            centre, values[i + 1], values[i + 3], [coef[k, i + 3] for k in range(6)]
        )
        return (const[i + 3] - OMEGA * centre + near) * (diag[i + 3] * (1.0 / OMEGA))

    for m in range(height // 2):
        pair_right[m] = residue(2 * m) + residue(2 * m + 1)
        pair_perm[m] = (perm[height + 2 * m] + perm[height + 2 * m + 1]) * 0.125
    half = pair_right.shape[1] // 2
    to_right = lane_pairs(1, LANES, 1, 0)
    to_perm = lane_pairs(1, LANES, 1, 1)
    for m in range(height // 2):
        rows = pair_right[m, pl.ds(0, half, 2), :] + pair_right[m, pl.ds(1, half, 2), :]
        field = pair_perm[m, pl.ds(0, half, 2), :] + pair_perm[m, pl.ds(1, half, 2), :]
        coarse_out[m] = exact_dot(rows, to_right) + exact_dot(field, to_perm)
    for copy in copies:
        copy.wait()


class Packed:
    def __init__(self, nz, nx, ny):
        self.nz, self.nx, self.ny = nz, nx, ny
        self.groups = min(LANES // ny, nz)
        self.planes = nz // self.groups

    def lower(self, planes, p):
        return planes[p - 1] if p else roll(planes[self.planes - 1], self.ny, 1)

    def upper(self, planes, p):
        return planes[p + 1] if p + 1 < self.planes else roll(planes[0], -self.ny, 1)

    def system(self, right, perm, level):
        lane = iota((self.nx, LANES), 1)
        used = lane < self.groups * self.ny
        if self.groups * self.ny < LANES:
            perm = [jnp.where(used, x, 1.0) for x in perm]
        coefs, const, diagonals = [], [], []
        for p in range(self.planes):
            below, above = ZSCALE, ZSCALE
            if p == 0:
                below = jnp.where(lane < self.ny, 0.0, ZSCALE)
            if p + 1 == self.planes:
                above = jnp.where(lane < (self.groups - 1) * self.ny, ZSCALE, 0.0)
            faces, diagonal = face_terms(
                perm[p], self.lower(perm, p), self.upper(perm, p), below, above, self.ny
            )
            inverse = OMEGA / diagonal
            coefs.append([inverse * face for face in faces])
            const.append(inverse * right[p] * (4.0**-level))
            diagonals.append(diagonal * (4.0**level / OMEGA))
        return coefs, const, diagonals

    def near(self, values, coefs):
        return [
            neighbours(values[p], self.lower(values, p), self.upper(values, p), coefs[p])
            for p in range(self.planes)
        ]

    def sweep(self, values, coefs, const):
        near = self.near(values, coefs)
        return [KEEP * v + (c + n) for v, c, n in zip(values, const, near)]

    def coarser(self):
        return Packed(self.nz // 2, self.nx // 2, self.ny // 2)

    def restrict(self, values, pad):
        coarse = self.coarser()
        step = coarse.groups // self.groups
        half = coarse.nx
        out = []
        for p in range(coarse.planes):
            total = None
            for j in range(step):
                m = j * coarse.planes + p
                pad[m] = values[2 * m] + values[2 * m + 1]
                rows = pad[m, pl.ds(0, half, 2), :] + pad[m, pl.ds(1, half, 2), :]
                part = exact_dot(rows, lane_pairs(self.groups, self.ny, step, j))
                total = part if total is None else total + part
            out.append(total)
        return out

    def prolong(self, values, pad):
        coarse = self.coarser()
        step = coarse.groups // self.groups
        half = coarse.nx
        out = []
        for m in range(self.planes // 2):
            j, p = divmod(m, coarse.planes)
            wide = exact_dot(values[p], lane_spread(self.groups, self.ny, step, j))
            pad[m, pl.ds(0, half, 2), :] = wide
            pad[m, pl.ds(1, half, 2), :] = wide
            spread = pad[m]
            out += [spread, spread]
        return out


def coarsest(grid, right, perm, level):
    coefs, const, _ = grid.system(right, perm, level)
    return lax.fori_loop(
        0,
        COARSE_SWEEPS - 1,
        lambda step, values: tuple(grid.sweep(values, coefs, const)),
        tuple(const),
        unroll=7,
    )


def packed_cycle(grid, right, perm, level, pads):
    if not pads:
        return coarsest(grid, right, perm, level)
    pad_right, pad_perm = pads[0]
    coefs, const, diagonals = grid.system(right, perm, level)
    values = grid.sweep(const, coefs, const)
    near = grid.near(values, coefs)
    residue = [
        (c - OMEGA * v + n) * d for c, v, n, d in zip(const, values, near, diagonals)
    ]
    coarse_right = grid.restrict(residue, pad_right)
    coarse_perm = [x * 0.125 for x in grid.restrict(perm, pad_perm)]
    update = packed_cycle(grid.coarser(), coarse_right, coarse_perm, level + 1, pads[1:])
    values = [v + e for v, e in zip(values, grid.prolong(update, pad_right))]
    for _ in range(2):
        values = grid.sweep(values, coefs, const)
    return values


def coarse_kernel(
    domains, dom_ref, *refs,
):
    parts, refs = refs[:domains], refs[domains:]
    coef_in, level_in, out, gathered, coef, level, first, *refs = refs
    pad_right1, pad_perm1, pad_right2, pad_perm2, update, sems = refs
    height = out.shape[0]
    dom = dom_ref[0]
    copies = [
        pltpu.make_async_copy(coef_in, coef, sems.at[0]),
        pltpu.make_async_copy(level_in, level, sems.at[1]),
    ]
    for copy in copies:
        copy.start()
    for step, part in enumerate(parts):
        gathered[dom ^ step] = part[...]
    _, own, nx, _ = gathered.shape
    ny = LANES // 2
    grid = Packed(domains * own, nx, ny)
    left = iota((nx, LANES), 1) < ny
    right, perm = [], []
    for p in range(grid.planes):
        a = gathered[p // own, p % own]
        q = grid.planes + p
        b = gathered[q // own, q % own]
        right.append(jnp.where(left, a, roll(b, ny, 1)))
        perm.append(jnp.where(left, roll(a, ny, 1), b))
    pads = [(pad_right1, pad_perm1), (pad_right2, pad_perm2)]
    solved = packed_cycle(grid, right, perm, 1, pads)
    for p in range(grid.planes):
        update[p] = solved[p]
    for copy in copies:
        copy.wait()
    spread = lane_spread(1, LANES, 1, 0)
    for j in range(own + 2):
        layer = jnp.clip(dom * own + j - 1, 0, grid.nz - 1)
        group = layer // grid.planes
        plane = update[lax.rem(layer, grid.planes)]
        plane = jnp.where(group == 0, plane, roll(plane, ny, 1))
        wide = exact_dot(plane, spread)
        pad_perm0 = first.at[0]
        pad_perm0[pl.ds(0, nx, 2), :] = wide
        pad_perm0[pl.ds(1, nx, 2), :] = wide
        whole = first[0]
        level[2 * j] = level[2 * j] + whole
        level[2 * j + 1] = level[2 * j + 1] + whole

    def sweep(source, at, i):
        centre = source[i + 1]
        near = neighbours(
            centre, source[i], source[i + 2], [coef[k, at + i] for k in range(6)]
        )
        return KEEP * centre + (coef[6, at + i] + near)

    def one(i, carry):
        first[i] = sweep(level, 0, i)
        return carry

    lax.fori_loop(0, height + 2, one, 0)

    def two(i, carry):
        out[i] = sweep(first, 1, i)
        return carry

    lax.fori_loop(0, height, two, 0)


def fine_part(dom, perm, source, layers):
    height, nx, ny = perm[0].shape
    field = lambda *lead: pltpu.VMEM(lead + (nx, ny), F32)
    vmem = pl.BlockSpec(memory_space=pltpu.VMEM)
    smem = pl.BlockSpec(memory_space=pltpu.SMEM)
    anywhere = pl.BlockSpec(memory_space=pl.ANY)
    return pl.pallas_call(
        functools.partial(fine_kernel, layers),
        out_shape=(
            jax.ShapeDtypeStruct((7, height + 2, nx, ny), F32),
            jax.ShapeDtypeStruct((height + 4, nx, ny), F32),
            jax.ShapeDtypeStruct((height // 2, nx // 2, ny), F32),
        ),
        in_specs=[smem] + [vmem] * 6,
        out_specs=(anywhere, anywhere, vmem),
        scratch_shapes=[
            field(3 * height),
            field(3 * height),
            field(6, height + 6),
            field(height + 6),
            field(height + 4),
            field(height + 6),
            field(height // 2),
            field(height // 2),
            pltpu.SemaphoreType.DMA((8,)),
        ],
        compiler_params=pltpu.CompilerParams(vmem_limit_bytes=VMEM_LIMIT),
        name="fine",
    )(dom, *perm, *source)


def coarse_part(dom, parts, coefs, values, height):
    _, _, nx, ny = coefs.shape
    field = lambda *shape: pltpu.VMEM(shape, F32)
    domains = len(parts)
    grid1 = Packed(domains * parts[0].shape[0], nx // 2, ny // 2)
    grid2 = grid1.coarser()
    pads1 = field(grid1.planes // 2, grid1.nx, LANES)
    pads2 = field(grid2.planes // 2, grid2.nx, LANES)
    vmem = pl.BlockSpec(memory_space=pltpu.VMEM)
    smem = pl.BlockSpec(memory_space=pltpu.SMEM)
    anywhere = pl.BlockSpec(memory_space=pl.ANY)
    return pl.pallas_call(
        functools.partial(coarse_kernel, domains),
        out_shape=jax.ShapeDtypeStruct((height, nx, ny), F32),
        in_specs=[smem] + [vmem] * domains + [anywhere, anywhere],
        out_specs=vmem,
        scratch_shapes=[
            field(domains, *parts[0].shape),
            field(*coefs.shape),
            field(*values.shape),
            field(height + 2, nx, ny),
            pads1, pads1, pads2, pads2,
            field(grid1.planes, grid1.nx, LANES),
            pltpu.SemaphoreType.DMA((2,)),
        ],
        compiler_params=pltpu.CompilerParams(vmem_limit_bytes=VMEM_LIMIT),
        name="coarse",
    )(dom, *parts, coefs, values)


def swaps(x, axis, step):
    return lax.ppermute(x, axis, [(i, i ^ step) for i in range(lax.axis_size(axis))])


def both_sides(x):
    count = lax.axis_size("dom")
    pairs = [(0, count - 1), (count - 1, 0)]
    for i in range(1, count - 1, 2):
        pairs += [(i, i + 1), (i + 1, i)]
    return swaps(x, "dom", 1), lax.ppermute(x, "dom", pairs)


def from_accepted(mine, accepted):
    props = lax.axis_size("prop")
    offers = [mine]
    step = props // 2
    while step:
        offers += [swaps(x, "prop", step) for x in offers]
        step //= 2
    order = [0]
    step = props // 2
    while step:
        order += [x ^ step for x in order]
        step //= 2
    wanted = lax.axis_index("prop") ^ accepted
    current = offers[0]
    for at, offer in zip(order[1:], offers[1:]):
        current = jnp.where(wanted == at, offer, current)
    return current


def gather_parts(mine):
    domains = lax.axis_size("dom")
    parts = {0: mine}
    for step in reversed(range(2, domains, 2)):
        parts[step] = swaps(mine, "dom", step)
    for step in range(0, domains, 2):
        parts[step + 1] = swaps(parts[step], "dom", 1)
    return [parts[k] for k in range(domains)]


def body(states, accepted, noise, source):
    domains = lax.axis_size("dom")
    height = source.shape[0]
    dom = lax.axis_index("dom").astype(jnp.int32).reshape(1)
    current = from_accepted(states[0], accepted[0])
    sources = (source,) + both_sides(source)
    perm = jnp.exp(SHRINK * current + BETA * noise[0])
    perms = (perm,) + both_sides(perm)
    coefs, values, coarse = fine_part(dom, perms, sources, domains * height)
    return coarse_part(dom, gather_parts(coarse), coefs, values, height)[None]


def solution(mesh):
    in_specs = (
        P("prop", "dom", None, None),
        P(),
        P("prop", "dom", None, None),
        P("dom", None, None),
    )
    out_specs = P("prop", "dom", None, None)
    return jax.shard_map(body, mesh=mesh, in_specs=in_specs, out_specs=out_specs, check_vma=False)
```

```python
import functools
import math

import jax
import jax.numpy as jnp
from jax import lax
from jax.experimental import pallas as pl
from jax.experimental.pallas import tpu as pltpu
from jax.sharding import PartitionSpec as P

COARSE_SWEEPS = 64
OMEGA = 0.7
KEEP = 1.0 - OMEGA
BETA = 0.4
SHRINK = math.sqrt(1.0 - BETA * BETA)
ZSCALE = 16.0
LANES = 128
VMEM_LIMIT = 40 * 1024 * 1024
F32 = jnp.float32
WEST, EAST, SOUTH, NORTH, BELOW, ABOVE, CONST = range(7)


def iota(shape, dim):
    return lax.broadcasted_iota(jnp.int32, shape, dim)


def roll(x, amount, axis):
    axis = axis % x.ndim
    return pltpu.roll(x, amount % x.shape[axis], axis)


def harmonic(a, b):
    return 2.0 * a * b / (a + b)


def exact_dot(x, selector):
    high = x.astype(jnp.bfloat16)
    rest = x - high.astype(F32)
    middle = rest.astype(jnp.bfloat16)
    low = (rest - middle.astype(F32)).astype(jnp.bfloat16)
    dot = functools.partial(jnp.dot, preferred_element_type=F32)
    return dot(high, selector) + dot(middle, selector) + dot(low, selector)


def face_terms(perm, lower, upper, below_scale, above_scale, ny):
    shape = perm.shape
    rows = iota(shape, 0)
    columns = lax.rem(iota(shape, 1), ny)
    west = jnp.where(rows == 0, 0.0, harmonic(perm, roll(perm, 1, 0)))
    east = roll(west, -1, 0)
    south = jnp.where(columns == 0, 0.0, harmonic(perm, roll(perm, 1, 1)))
    north = roll(south, -1, 1)
    below = below_scale * harmonic(perm, lower)
    above = above_scale * harmonic(perm, upper)
    ends = jnp.where(rows == 0, perm, 0.0) + jnp.where(rows == shape[0] - 1, perm, 0.0)
    ends = ends + jnp.where(columns == 0, perm, 0.0) + jnp.where(columns == ny - 1, perm, 0.0)
    diagonal = west + east + south + north + below + above + ends
    return (west, east, south, north, below, above), diagonal


def neighbours(values, lower, upper, coefs):
    total = coefs[0] * roll(values, 1, 0) + coefs[1] * roll(values, -1, 0)
    total = total + (coefs[2] * roll(values, 1, 1) + coefs[3] * roll(values, -1, 1))
    return total + (coefs[4] * lower + coefs[5] * upper)


def lane_pairs(count, ny, step, offset):
    shape = (LANES, LANES)
    source, target = iota(shape, 0), iota(shape, 1)
    lane = (source // ny * step + offset) * (ny // 2) + lax.rem(source, ny) // 2
    return jnp.where((target == lane) & (source < count * ny), 1.0, 0.0).astype(jnp.bfloat16)


def lane_spread(count, ny, step, offset):
    shape = (LANES, LANES)
    source, target = iota(shape, 1), iota(shape, 0)
    lane = (source // ny * step + offset) * (ny // 2) + lax.rem(source, ny) // 2
    return jnp.where((target == lane) & (source < count * ny), 1.0, 0.0).astype(jnp.bfloat16)


def fine_kernel(
    layers,
    dom_ref,
    per, per_pair, per_other,
    src, src_pair, src_other,
    coef, const, values, coarse_out,
    perm, right, diag, pair_right, pair_perm,
):
    height = per.shape[0]
    dom = dom_ref[0]
    pair_at = jnp.where(lax.rem(dom, 2) == 0, 2 * height, 0)
    other_at = 2 * height - pair_at

    for i in range(height):
        for at, p, s in (
            (height, per, src), (pair_at, per_pair, src_pair), (other_at, per_other, src_other)
        ):
            perm[at + i] = p[i]
            right[at + i] = s[i]

    def build(i, carry):
        z = dom * height + i - 3
        below = jnp.where((z > 0) & (z < layers), ZSCALE, 0.0)
        above = jnp.where((z + 1 > 0) & (z + 1 < layers), ZSCALE, 0.0)
        at = height - 3 + i
        faces, diagonal = face_terms(perm[at], perm[at - 1], perm[at + 1], below, above, LANES)
        inverse = OMEGA / diagonal
        for k in range(6):
            coef[k, i] = inverse * faces[k]
        const[i] = (1.0 / diagonal) * right[at]
        diag[i] = diagonal
        return carry

    lax.fori_loop(0, height + 6, build, 0)

    def first(i, carry):
        start = const[i + 1]
        near = neighbours(start, const[i], const[i + 2], [coef[k, i + 1] for k in range(6)])
        values[i] = KEEP * start + start + near
        return carry

    lax.fori_loop(0, height + 4, first, 0)

    def residue(i):
        centre = values[i + 2]
        near = neighbours(
            centre, values[i + 1], values[i + 3], [coef[k, i + 3] for k in range(6)]
        )
        return (const[i + 3] - OMEGA * centre + near) * (diag[i + 3] * (1.0 / OMEGA))

    for m in range(height // 2):
        pair_right[m] = residue(2 * m) + residue(2 * m + 1)
        pair_perm[m] = (perm[height + 2 * m] + perm[height + 2 * m + 1]) * 0.125
    half = pair_right.shape[1] // 2
    to_right = lane_pairs(1, LANES, 1, 0)
    to_perm = lane_pairs(1, LANES, 1, 1)
    for m in range(height // 2):
        rows = pair_right[m, pl.ds(0, half, 2), :] + pair_right[m, pl.ds(1, half, 2), :]
        field = pair_perm[m, pl.ds(0, half, 2), :] + pair_perm[m, pl.ds(1, half, 2), :]
        coarse_out[m] = exact_dot(rows, to_right) + exact_dot(field, to_perm)


class Packed:
    def __init__(self, nz, nx, ny):
        self.nz, self.nx, self.ny = nz, nx, ny
        self.groups = min(LANES // ny, nz)
        self.planes = nz // self.groups

    def lower(self, planes, p):
        return planes[p - 1] if p else roll(planes[self.planes - 1], self.ny, 1)

    def upper(self, planes, p):
        return planes[p + 1] if p + 1 < self.planes else roll(planes[0], -self.ny, 1)

    def system(self, right, perm, level):
        lane = iota((self.nx, LANES), 1)
        used = lane < self.groups * self.ny
        if self.groups * self.ny < LANES:
            perm = [jnp.where(used, x, 1.0) for x in perm]
        coefs, const, diagonals = [], [], []
        for p in range(self.planes):
            below, above = ZSCALE, ZSCALE
            if p == 0:
                below = jnp.where(lane < self.ny, 0.0, ZSCALE)
            if p + 1 == self.planes:
                above = jnp.where(lane < (self.groups - 1) * self.ny, ZSCALE, 0.0)
            faces, diagonal = face_terms(
                perm[p], self.lower(perm, p), self.upper(perm, p), below, above, self.ny
            )
            inverse = OMEGA / diagonal
            coefs.append([inverse * face for face in faces])
            const.append(inverse * right[p] * (4.0**-level))
            diagonals.append(diagonal * (4.0**level / OMEGA))
        return coefs, const, diagonals

    def near(self, values, coefs):
        return [
            neighbours(values[p], self.lower(values, p), self.upper(values, p), coefs[p])
            for p in range(self.planes)
        ]

    def sweep(self, values, coefs, const):
        near = self.near(values, coefs)
        return [KEEP * v + (c + n) for v, c, n in zip(values, const, near)]

    def coarser(self):
        return Packed(self.nz // 2, self.nx // 2, self.ny // 2)

    def restrict(self, values, pad):
        coarse = self.coarser()
        step = coarse.groups // self.groups
        half = coarse.nx
        out = []
        for p in range(coarse.planes):
            total = None
            for j in range(step):
                m = j * coarse.planes + p
                pad[m] = values[2 * m] + values[2 * m + 1]
                rows = pad[m, pl.ds(0, half, 2), :] + pad[m, pl.ds(1, half, 2), :]
                part = exact_dot(rows, lane_pairs(self.groups, self.ny, step, j))
                total = part if total is None else total + part
            out.append(total)
        return out

    def prolong(self, values, pad):
        coarse = self.coarser()
        step = coarse.groups // self.groups
        half = coarse.nx
        out = []
        for m in range(self.planes // 2):
            j, p = divmod(m, coarse.planes)
            wide = exact_dot(values[p], lane_spread(self.groups, self.ny, step, j))
            pad[m, pl.ds(0, half, 2), :] = wide
            pad[m, pl.ds(1, half, 2), :] = wide
            spread = pad[m]
            out += [spread, spread]
        return out


def coarsest(grid, right, perm, level):
    coefs, const, _ = grid.system(right, perm, level)
    return lax.fori_loop(
        0,
        COARSE_SWEEPS - 1,
        lambda step, values: tuple(grid.sweep(values, coefs, const)),
        tuple(const),
        unroll=7,
    )


def packed_cycle(grid, right, perm, level, pads):
    if not pads:
        return coarsest(grid, right, perm, level)
    pad_right, pad_perm = pads[0]
    coefs, const, diagonals = grid.system(right, perm, level)
    values = grid.sweep(const, coefs, const)
    near = grid.near(values, coefs)
    residue = [
        (c - OMEGA * v + n) * d for c, v, n, d in zip(const, values, near, diagonals)
    ]
    coarse_right = grid.restrict(residue, pad_right)
    coarse_perm = [x * 0.125 for x in grid.restrict(perm, pad_perm)]
    update = packed_cycle(grid.coarser(), coarse_right, coarse_perm, level + 1, pads[1:])
    values = [v + e for v, e in zip(values, grid.prolong(update, pad_right))]
    for _ in range(2):
        values = grid.sweep(values, coefs, const)
    return values


def coarse_kernel(
    dom_ref, gathered, coef, const, before, out,
    level, first, pad_right1, pad_perm1, pad_right2, pad_perm2, update,
):
    height = out.shape[0]
    dom = dom_ref[0]
    domains, own, nx, _ = gathered.shape
    ny = LANES // 2
    grid = Packed(domains * own, nx, ny)
    left = iota((nx, LANES), 1) < ny
    right, perm = [], []
    for p in range(grid.planes):
        a = gathered[p // own, p % own]
        q = grid.planes + p
        b = gathered[q // own, q % own]
        right.append(jnp.where(left, a, roll(b, ny, 1)))
        perm.append(jnp.where(left, roll(a, ny, 1), b))
    pads = [(pad_right1, pad_perm1), (pad_right2, pad_perm2)]
    solved = packed_cycle(grid, right, perm, 1, pads)
    for p in range(grid.planes):
        update[p] = solved[p]
    spread = lane_spread(1, LANES, 1, 0)
    for j in range(own + 2):
        layer = jnp.clip(dom * own + j - 1, 0, grid.nz - 1)
        group = layer // grid.planes
        plane = update[lax.rem(layer, grid.planes)]
        plane = jnp.where(group == 0, plane, roll(plane, ny, 1))
        wide = exact_dot(plane, spread)
        pad_perm0 = first.at[0]
        pad_perm0[pl.ds(0, nx, 2), :] = wide
        pad_perm0[pl.ds(1, nx, 2), :] = wide
        whole = first[0]
        level[2 * j] = before[2 * j] + whole
        level[2 * j + 1] = before[2 * j + 1] + whole

    def sweep(source, at, i):
        centre = source[i + 1]
        near = neighbours(
            centre, source[i], source[i + 2], [coef[k, at + i] for k in range(6)]
        )
        return KEEP * centre + (const[at + i] + near)

    def one(i, carry):
        first[i] = sweep(level, 2, i)
        return carry

    lax.fori_loop(0, height + 2, one, 0)

    def two(i, carry):
        out[i] = sweep(first, 3, i)
        return carry

    lax.fori_loop(0, height, two, 0)


def fine_part(dom, perm, source, layers):
    height, nx, ny = perm[0].shape
    field = lambda *lead: pltpu.VMEM(lead + (nx, ny), F32)
    vmem = pl.BlockSpec(memory_space=pltpu.VMEM)
    smem = pl.BlockSpec(memory_space=pltpu.SMEM)
    return pl.pallas_call(
        functools.partial(fine_kernel, layers),
        out_shape=(
            jax.ShapeDtypeStruct((6, height + 6, nx, ny), F32),
            jax.ShapeDtypeStruct((height + 6, nx, ny), F32),
            jax.ShapeDtypeStruct((height + 4, nx, ny), F32),
            jax.ShapeDtypeStruct((height // 2, nx // 2, ny), F32),
        ),
        in_specs=[smem] + [vmem] * 6,
        out_specs=(vmem,) * 4,
        scratch_shapes=[
            field(3 * height),
            field(3 * height),
            field(height + 6),
            field(height // 2),
            field(height // 2),
        ],
        compiler_params=pltpu.CompilerParams(vmem_limit_bytes=VMEM_LIMIT),
        name="fine",
    )(dom, *perm, *source)


def coarse_part(dom, gathered, coefs, const, values, height):
    _, nx, ny = values.shape
    field = lambda *shape: pltpu.VMEM(shape, F32)
    grid1 = Packed(gathered.shape[0] * gathered.shape[1], nx // 2, ny // 2)
    grid2 = grid1.coarser()
    pads1 = field(grid1.planes // 2, grid1.nx, LANES)
    pads2 = field(grid2.planes // 2, grid2.nx, LANES)
    vmem = pl.BlockSpec(memory_space=pltpu.VMEM)
    smem = pl.BlockSpec(memory_space=pltpu.SMEM)
    return pl.pallas_call(
        coarse_kernel,
        out_shape=jax.ShapeDtypeStruct((height, nx, ny), F32),
        in_specs=[smem] + [vmem] * 4,
        out_specs=vmem,
        scratch_shapes=[
            field(*values.shape),
            field(height + 2, nx, ny),
            pads1, pads1, pads2, pads2,
            field(grid1.planes, grid1.nx, LANES),
        ],
        compiler_params=pltpu.CompilerParams(vmem_limit_bytes=VMEM_LIMIT),
        name="coarse",
    )(dom, gathered, coefs, const, values)


def swaps(x, axis, step):
    return lax.ppermute(x, axis, [(i, i ^ step) for i in range(lax.axis_size(axis))])


def pass_on(x):
    count = lax.axis_size("dom")
    ring = [(i, i + 2) for i in range(0, count - 2, 2)] + [(count - 2, count - 1)]
    ring += [(i, i - 2) for i in range(3, count, 2)] + [(1, 0)]
    return lax.ppermute(x, "dom", ring)


def from_accepted(mine, accepted, beside):
    props = lax.axis_size("prop")
    step = props // 2
    offers, order = [mine], [0]
    while step:
        came = [swaps(x, "prop", step) for x in offers]
        if step == props // 2:
            came, beside = lax.optimization_barrier((came, beside))
        offers, order = offers + came, order + [x ^ step for x in order]
        step //= 2
    wanted = lax.axis_index("prop") ^ accepted
    current = offers[0]
    for at, offer in zip(order[1:], offers[1:]):
        current = jnp.where(wanted == at, offer, current)
    return current, beside


def gather_parts(mine):
    domains = lax.axis_size("dom")
    copies = jnp.broadcast_to(mine[None], (domains,) + mine.shape)
    return lax.all_to_all(copies, "dom", 0, 0)


def body(states, accepted, noise, source):
    domains = lax.axis_size("dom")
    height = source.shape[0]
    dom = lax.axis_index("dom").astype(jnp.int32).reshape(1)
    scaled = OMEGA * source
    beside = (scaled, swaps(scaled, "dom", 1))
    current, (scaled, scaled_pair) = from_accepted(states[0], accepted[0], beside)
    sources = (scaled, scaled_pair, pass_on(scaled_pair))
    perm = jnp.exp(SHRINK * current + BETA * noise[0])
    perm_pair = swaps(perm, "dom", 1)
    perms = (perm, perm_pair, pass_on(perm_pair))
    *level, coarse = fine_part(dom, perms, sources, domains * height)
    return coarse_part(dom, gather_parts(coarse), *level, height)[None]


def solution(mesh):
    in_specs = (
        P("prop", "dom", None, None),
        P(),
        P("prop", "dom", None, None),
        P("dom", None, None),
    )
    out_specs = P("prop", "dom", None, None)
    return jax.shard_map(body, mesh=mesh, in_specs=in_specs, out_specs=out_specs, check_vma=False)
```

```python
import functools
import math

import jax
import jax.numpy as jnp
from jax import lax
from jax.experimental import pallas as pl
from jax.experimental.pallas import tpu as pltpu
from jax.sharding import PartitionSpec as P

COARSE_SWEEPS = 64
OMEGA = 0.7
KEEP = 1.0 - OMEGA
BETA = 0.4
SHRINK = math.sqrt(1.0 - BETA * BETA)
ZSCALE = 16.0
LANES = 128
VMEM_LIMIT = 40 * 1024 * 1024
F32 = jnp.float32
WEST, EAST, SOUTH, NORTH, BELOW, ABOVE, CONST = range(7)


def iota(shape, dim):
    return lax.broadcasted_iota(jnp.int32, shape, dim)


def roll(x, amount, axis):
    axis = axis % x.ndim
    return pltpu.roll(x, amount % x.shape[axis], axis)


def inverse_of(x):
    guess = pl.reciprocal(x, approx=True)
    return guess * (2.0 - x * guess)


def harmonic(a, b):
    return (2.0 * a) * b * inverse_of(a + b)


def selector_dot(parts, selector):
    x = jnp.concatenate(parts, axis=0) if len(parts) > 1 else parts[0]
    rows = x.shape[0]
    high = x.astype(jnp.bfloat16).astype(F32)
    rest = x - high
    middle = rest.astype(jnp.bfloat16).astype(F32)
    terms = jnp.concatenate([high, middle, rest - middle], axis=0).astype(jnp.bfloat16)
    y = jnp.dot(terms, selector, preferred_element_type=F32)
    total = y[:rows] + y[rows : 2 * rows] + y[2 * rows :]
    height = parts[0].shape[0]
    return [total[i * height : (i + 1) * height] for i in range(len(parts))]


def face_terms(perm, lower, upper, below_scale, above_scale, ny):
    shape = perm.shape
    rows = iota(shape, 0)
    columns = iota(shape, 1) & (ny - 1)
    west = jnp.where(rows == 0, 0.0, harmonic(perm, roll(perm, 1, 0)))
    east = roll(west, -1, 0)
    south = jnp.where(columns == 0, 0.0, harmonic(perm, roll(perm, 1, 1)))
    north = roll(south, -1, 1)
    below = below_scale * harmonic(perm, lower)
    above = above_scale * harmonic(perm, upper)
    ends = jnp.where(rows == 0, perm, 0.0) + jnp.where(rows == shape[0] - 1, perm, 0.0)
    ends = ends + jnp.where(columns == 0, perm, 0.0) + jnp.where(columns == ny - 1, perm, 0.0)
    diagonal = ((west + east) + (south + north)) + ((below + above) + ends)
    return (west, east, south, north, below, above), diagonal


def stencil(values, lower, upper, coefs, base):
    x = coefs[0] * roll(values, 1, 0) + coefs[1] * roll(values, -1, 0)
    y = coefs[2] * roll(values, 1, 1) + coefs[3] * roll(values, -1, 1)
    z = coefs[4] * lower + coefs[5] * upper
    return (x + y) + (z + base)


def lane_selector(groups, ny, step, spread=False):
    shape = (LANES, step * LANES) if spread else (step * LANES, LANES)
    source, target = iota(shape, int(spread)), iota(shape, 1 - int(spread))
    bits = ny.bit_length() - 1
    lane = source & (LANES - 1)
    group = (lane >> bits) * step + (source >> 7)
    wanted = (group << (bits - 1)) + ((lane & (ny - 1)) >> 1)
    return jnp.where((target == wanted) & (lane < groups * ny), 1.0, 0.0).astype(jnp.bfloat16)


def fine_kernel(
    layers,
    dom_ref,
    per, per_pair, per_other,
    src, src_pair, src_other,
    coef, const, values, coarse_out,
    perm, right, diag, pair_right, pair_perm,
):
    height = per.shape[0]
    dom = dom_ref[0]
    pair_at = jnp.where(lax.rem(dom, 2) == 0, 2 * height, 0)
    other_at = 2 * height - pair_at

    for i in range(height):
        for at, p, s in (
            (height, per, src), (pair_at, per_pair, src_pair), (other_at, per_other, src_other)
        ):
            perm[at + i] = p[i]
            right[at + i] = s[i] if at is height else OMEGA * s[i]

    def build(i, carry):
        z = dom * height + i - 3
        below = jnp.where((z > 0) & (z < layers), ZSCALE, 0.0)
        above = jnp.where((z + 1 > 0) & (z + 1 < layers), ZSCALE, 0.0)
        at = height - 3 + i
        faces, diagonal = face_terms(perm[at], perm[at - 1], perm[at + 1], below, above, LANES)
        inverse = inverse_of(diagonal)
        const[i] = inverse * right[at]
        inverse = OMEGA * inverse
        for k in range(6):
            coef[k, i] = inverse * faces[k]
        diag[i] = diagonal
        return carry

    lax.fori_loop(0, height + 6, build, 0)

    def first(i, carry):
        start = const[i + 1]
        near = [coef[k, i + 1] for k in range(6)]
        values[i] = stencil(start, const[i], const[i + 2], near, (1.0 + KEEP) * start)
        return carry

    lax.fori_loop(0, height + 4, first, 0)

    def residue(i):
        centre = values[i + 2]
        base = const[i + 3] - OMEGA * centre
        near = [coef[k, i + 3] for k in range(6)]
        scaled = stencil(centre, values[i + 1], values[i + 3], near, base)
        return scaled * (diag[i + 3] * (1.0 / OMEGA))

    for m in range(height // 2):
        pair_right[m] = residue(2 * m) + residue(2 * m + 1)
        pair_perm[m] = (perm[height + 2 * m] + perm[height + 2 * m + 1]) * 0.125
    half = pair_right.shape[1] // 2
    rows = []
    for m in range(height // 2):
        both = [x[m, pl.ds(0, half, 2), :] + x[m, pl.ds(1, half, 2), :] for x in (pair_right, pair_perm)]
        rows.append(jnp.concatenate(both, axis=1))
    for m, x in enumerate(selector_dot(rows, lane_selector(1, LANES, 2))):
        coarse_out[m] = x


class Packed:
    def __init__(self, nz, nx, ny):
        self.nz, self.nx, self.ny = nz, nx, ny
        self.groups = min(LANES // ny, nz)
        self.planes = nz // self.groups

    def lower(self, planes, p):
        return planes[p - 1] if p else roll(planes[self.planes - 1], self.ny, 1)

    def upper(self, planes, p):
        return planes[p + 1] if p + 1 < self.planes else roll(planes[0], -self.ny, 1)

    def system(self, right, perm, level):
        lane = iota((self.nx, LANES), 1)
        used = lane < self.groups * self.ny
        if self.groups * self.ny < LANES:
            perm = [jnp.where(used, x, 1.0) for x in perm]
        coefs, const, diagonals = [], [], []
        for p in range(self.planes):
            below, above = ZSCALE, ZSCALE
            if p == 0:
                below = jnp.where(lane < self.ny, 0.0, ZSCALE)
            if p + 1 == self.planes:
                above = jnp.where(lane < (self.groups - 1) * self.ny, ZSCALE, 0.0)
            faces, diagonal = face_terms(
                perm[p], self.lower(perm, p), self.upper(perm, p), below, above, self.ny
            )
            inverse = OMEGA * inverse_of(diagonal)
            coefs.append([inverse * face for face in faces])
            const.append(inverse * right[p] * (4.0**-level))
            diagonals.append(diagonal * (4.0**level / OMEGA))
        return coefs, const, diagonals

    def apply(self, values, coefs, bases):
        return [
            stencil(values[p], self.lower(values, p), self.upper(values, p), coefs[p], bases[p])
            for p in range(self.planes)
        ]

    def sweep(self, values, coefs, const):
        return self.apply(values, coefs, [KEEP * v + c for v, c in zip(values, const)])

    def coarser(self):
        return Packed(self.nz // 2, self.nx // 2, self.ny // 2)

    def restrict(self, fields, pads):
        coarse = self.coarser()
        step = coarse.groups // self.groups
        half = coarse.nx
        parts = []
        for values, pad in zip(fields, pads):
            rows = []
            for m in range(self.planes // 2):
                pad[m] = values[2 * m] + values[2 * m + 1]
                rows.append(pad[m, pl.ds(0, half, 2), :] + pad[m, pl.ds(1, half, 2), :])
            for p in range(coarse.planes):
                blocks = rows[p :: coarse.planes]
                parts.append(jnp.concatenate(blocks, axis=1) if step > 1 else blocks[0])
        sums = selector_dot(parts, lane_selector(self.groups, self.ny, step))
        return [sums[i : i + coarse.planes] for i in range(0, len(sums), coarse.planes)]

    def prolong(self, values, pad):
        coarse = self.coarser()
        step = coarse.groups // self.groups
        half = coarse.nx
        wide = selector_dot(values, lane_selector(self.groups, self.ny, step, spread=True))
        out = []
        for m in range(self.planes // 2):
            j, p = divmod(m, coarse.planes)
            plane = wide[p][:, j * LANES : (j + 1) * LANES]
            pad[m, pl.ds(0, half, 2), :] = plane
            pad[m, pl.ds(1, half, 2), :] = plane
            out += [pad[m], pad[m]]
        return out


def coarsest(grid, right, perm, level):
    coefs, const, _ = grid.system(right, perm, level)
    return lax.fori_loop(
        0,
        COARSE_SWEEPS - 1,
        lambda step, values: tuple(grid.sweep(values, coefs, const)),
        tuple(const),
        unroll=7,
    )


def packed_cycle(grid, right, perm, level, pads):
    if not pads:
        return coarsest(grid, right, perm, level)
    pad_right, pad_perm = pads[0]
    coefs, const, diagonals = grid.system(right, perm, level)
    values = grid.sweep(const, coefs, const)
    scaled = grid.apply(values, coefs, [c - OMEGA * v for c, v in zip(const, values)])
    residue = [r * d for r, d in zip(scaled, diagonals)]
    coarse_right, coarse_perm = grid.restrict((residue, perm), (pad_right, pad_perm))
    coarse_perm = [x * 0.125 for x in coarse_perm]
    update = packed_cycle(grid.coarser(), coarse_right, coarse_perm, level + 1, pads[1:])
    values = [v + e for v, e in zip(values, grid.prolong(update, pad_right))]
    for _ in range(2):
        values = grid.sweep(values, coefs, const)
    return values


def coarse_kernel(
    dom_ref, gathered, coef, const, before, out,
    level, first, pad_right1, pad_perm1, pad_right2, pad_perm2, update,
):
    height = out.shape[0]
    dom = dom_ref[0]
    domains, own, nx, _ = gathered.shape
    ny = LANES // 2
    grid = Packed(domains * own, nx, ny)
    left = iota((nx, LANES), 1) < ny
    right, perm = [], []
    for p in range(grid.planes):
        a = gathered[p // own, p % own]
        q = grid.planes + p
        b = gathered[q // own, q % own]
        right.append(jnp.where(left, a, roll(b, ny, 1)))
        perm.append(jnp.where(left, roll(a, ny, 1), b))
    pads = [(pad_right1, pad_perm1), (pad_right2, pad_perm2)]
    solved = packed_cycle(grid, right, perm, 1, pads)
    for p in range(grid.planes):
        update[p] = solved[p]
    planes, group = [], []
    for j in range(own + 2):
        layer = jnp.clip(dom * own + j - 1, 0, grid.nz - 1)
        group.append(layer // grid.planes)
        planes.append(update[lax.rem(layer, grid.planes)])
    for j, wide in enumerate(selector_dot(planes, lane_selector(1, LANES, 2, spread=True))):
        plane = jnp.where(group[j] == 0, wide[:, :LANES], wide[:, LANES:])
        pad = first.at[0]
        pad[pl.ds(0, nx, 2), :] = plane
        pad[pl.ds(1, nx, 2), :] = plane
        whole = first[0]
        level[2 * j] = before[2 * j] + whole
        level[2 * j + 1] = before[2 * j + 1] + whole

    def sweep(source, at, i):
        centre = source[i + 1]
        near = [coef[k, at + i] for k in range(6)]
        return stencil(centre, source[i], source[i + 2], near, KEEP * centre + const[at + i])

    def one(i, carry):
        first[i] = sweep(level, 2, i)
        return carry

    lax.fori_loop(0, height + 2, one, 0)

    def two(i, carry):
        out[i] = sweep(first, 3, i)
        return carry

    lax.fori_loop(0, height, two, 0)


def fine_part(dom, perm, source, layers):
    height, nx, ny = perm[0].shape
    field = lambda *lead: pltpu.VMEM(lead + (nx, ny), F32)
    vmem = pl.BlockSpec(memory_space=pltpu.VMEM)
    smem = pl.BlockSpec(memory_space=pltpu.SMEM)
    return pl.pallas_call(
        functools.partial(fine_kernel, layers),
        out_shape=(
            jax.ShapeDtypeStruct((6, height + 6, nx, ny), F32),
            jax.ShapeDtypeStruct((height + 6, nx, ny), F32),
            jax.ShapeDtypeStruct((height + 4, nx, ny), F32),
            jax.ShapeDtypeStruct((height // 2, nx // 2, ny), F32),
        ),
        in_specs=[smem] + [vmem] * 6,
        out_specs=(vmem,) * 4,
        scratch_shapes=[
            field(3 * height),
            field(3 * height),
            field(height + 6),
            field(height // 2),
            field(height // 2),
        ],
        compiler_params=pltpu.CompilerParams(vmem_limit_bytes=VMEM_LIMIT),
        name="fine",
    )(dom, *perm, *source)


def coarse_part(dom, gathered, coefs, const, values, height):
    _, nx, ny = values.shape
    field = lambda *shape: pltpu.VMEM(shape, F32)
    grid1 = Packed(gathered.shape[0] * gathered.shape[1], nx // 2, ny // 2)
    grid2 = grid1.coarser()
    pads1 = field(grid1.planes // 2, grid1.nx, LANES)
    pads2 = field(grid2.planes // 2, grid2.nx, LANES)
    vmem = pl.BlockSpec(memory_space=pltpu.VMEM)
    smem = pl.BlockSpec(memory_space=pltpu.SMEM)
    return pl.pallas_call(
        coarse_kernel,
        out_shape=jax.ShapeDtypeStruct((height, nx, ny), F32),
        in_specs=[smem] + [vmem] * 4,
        out_specs=vmem,
        scratch_shapes=[
            field(*values.shape),
            field(height + 2, nx, ny),
            pads1, pads1, pads2, pads2,
            field(grid1.planes, grid1.nx, LANES),
        ],
        compiler_params=pltpu.CompilerParams(vmem_limit_bytes=VMEM_LIMIT),
        name="coarse",
    )(dom, gathered, coefs, const, values)


def swaps(x, axis, step):
    return lax.ppermute(x, axis, [(i, i ^ step) for i in range(lax.axis_size(axis))])


def other_side(x):
    props, domains = lax.axis_size("prop"), lax.axis_size("dom")
    pairs = []
    for p in range(props):
        for d in range(domains):
            end = d in (0, domains - 1)
            partner = ((p ^ 1) * domains + d) if end else (p * domains + ((d + 1) ^ 1) - 1)
            pairs.append((p * domains + d, partner))
    return lax.ppermute(x, ("prop", "dom"), pairs)


def pass_on(x):
    count = lax.axis_size("dom")
    ring = [(i, i + 2) for i in range(0, count - 2, 2)] + [(count - 2, count - 1)]
    ring += [(i, i - 2) for i in range(3, count, 2)] + [(1, 0)]
    return lax.ppermute(x, "dom", ring)


def from_accepted(mine, accepted, beside):
    props = lax.axis_size("prop")
    step = props // 2
    offers, order = [mine], [0]
    while step:
        came = [swaps(x, "prop", step) for x in offers]
        if step == props // 2:
            came, beside = lax.optimization_barrier((came, beside))
        offers, order = offers + came, order + [x ^ step for x in order]
        step //= 2
    wanted = lax.axis_index("prop") ^ accepted
    current = offers[0]
    for at, offer in zip(order[1:], offers[1:]):
        current = jnp.where(wanted == at, offer, current)
    return current, beside


def gather_parts(mine):
    domains = lax.axis_size("dom")
    copies = jnp.broadcast_to(mine[None], (domains,) + mine.shape)
    return lax.all_to_all(copies, "dom", 0, 0)


def body(states, accepted, noise, source):
    domains = lax.axis_size("dom")
    height = source.shape[0]
    dom = lax.axis_index("dom").astype(jnp.int32).reshape(1)
    beside = (OMEGA * source, swaps(source, "dom", 1))
    current, (scaled, source_pair) = from_accepted(states[0], accepted[0], beside)
    sources = (scaled, source_pair, pass_on(source_pair))
    perm = jnp.exp(SHRINK * current + BETA * noise[0])
    perms = (perm, swaps(perm, "dom", 1), other_side(perm))
    *level, coarse = fine_part(dom, perms, sources, domains * height)
    return coarse_part(dom, gather_parts(coarse), *level, height)[None]


def solution(mesh):
    in_specs = (
        P("prop", "dom", None, None),
        P(),
        P("prop", "dom", None, None),
        P("dom", None, None),
    )
    out_specs = P("prop", "dom", None, None)
    return jax.shard_map(body, mesh=mesh, in_specs=in_specs, out_specs=out_specs, check_vma=False)
```

```python
import functools
import math

import jax
import jax.numpy as jnp
from jax import lax
from jax.experimental import pallas as pl
from jax.experimental.pallas import tpu as pltpu
from jax.sharding import PartitionSpec as P

COARSE_SWEEPS = 64
OMEGA = 0.7
KEEP = 1.0 - OMEGA
BETA = 0.4
SHRINK = math.sqrt(1.0 - BETA * BETA)
ZSCALE = 16.0
LANES = 128
VMEM_LIMIT = 40 * 1024 * 1024
F32 = jnp.float32
WEST, EAST, SOUTH, NORTH, BELOW, ABOVE, CONST = range(7)


def iota(shape, dim):
    return lax.broadcasted_iota(jnp.int32, shape, dim)


def roll(x, amount, axis):
    axis = axis % x.ndim
    return pltpu.roll(x, amount % x.shape[axis], axis)


def inverse_of(x):
    guess = pl.reciprocal(x, approx=True)
    return guess * (2.0 - x * guess)


def harmonic(a, b):
    return (2.0 * a) * b * inverse_of(a + b)


def selector_dot(parts, selector):
    x = jnp.concatenate(parts, axis=0) if len(parts) > 1 else parts[0]
    rows = x.shape[0]
    high = x.astype(jnp.bfloat16).astype(F32)
    rest = x - high
    middle = rest.astype(jnp.bfloat16).astype(F32)
    terms = jnp.concatenate([high, middle, rest - middle], axis=0).astype(jnp.bfloat16)
    y = jnp.dot(terms, selector, preferred_element_type=F32)
    total = y[:rows] + y[rows : 2 * rows] + y[2 * rows :]
    height = parts[0].shape[0]
    return [total[i * height : (i + 1) * height] for i in range(len(parts))]


def face_terms(perm, lower, upper, below_scale, above_scale, ny):
    shape = perm.shape
    rows = iota(shape, 0)
    columns = iota(shape, 1) & (ny - 1)
    west = jnp.where(rows == 0, 0.0, harmonic(perm, roll(perm, 1, 0)))
    east = roll(west, -1, 0)
    south = jnp.where(columns == 0, 0.0, harmonic(perm, roll(perm, 1, 1)))
    north = roll(south, -1, 1)
    below = below_scale * harmonic(perm, lower)
    above = above_scale * harmonic(perm, upper)
    ends = jnp.where(rows == 0, perm, 0.0) + jnp.where(rows == shape[0] - 1, perm, 0.0)
    ends = ends + jnp.where(columns == 0, perm, 0.0) + jnp.where(columns == ny - 1, perm, 0.0)
    diagonal = ((west + east) + (south + north)) + ((below + above) + ends)
    return (west, east, south, north, below, above), diagonal


def stencil(values, lower, upper, coefs, base):
    x = coefs[0] * roll(values, 1, 0) + coefs[1] * roll(values, -1, 0)
    y = coefs[2] * roll(values, 1, 1) + coefs[3] * roll(values, -1, 1)
    z = coefs[4] * lower + coefs[5] * upper
    return (x + y) + (z + base)


def lane_selector(groups, ny, step, spread=False):
    shape = (LANES, step * LANES) if spread else (step * LANES, LANES)
    source, target = iota(shape, int(spread)), iota(shape, 1 - int(spread))
    bits = ny.bit_length() - 1
    lane = source & (LANES - 1)
    group = (lane >> bits) * step + (source >> 7)
    wanted = (group << (bits - 1)) + ((lane & (ny - 1)) >> 1)
    return jnp.where((target == wanted) & (lane < groups * ny), 1.0, 0.0).astype(jnp.bfloat16)


def fine_kernel(
    layers,
    dom_ref,
    per, per_pair, per_other,
    src, src_near, src_next,
    coef, const, values, coarse_out,
    perm, right, diag, pair_right, pair_perm,
):
    height = per.shape[0]
    dom = dom_ref[0]
    pair_at = jnp.where(lax.rem(dom, 2) == 0, 2 * height, 0)
    other_at = 2 * height - pair_at

    near_at = jnp.where(lax.rem(dom_ref[1], 2) == 0, pair_at, other_at)
    next_at = 2 * height - near_at
    for i in range(height):
        for at, p in ((height, per), (pair_at, per_pair), (other_at, per_other)):
            perm[at + i] = p[i]
        right[height + i] = src[i]
        right[near_at + i] = OMEGA * src_near[i]
        right[next_at + i] = OMEGA * src_next[i]

    def build(i):
        z = dom * height + i - 3
        below = jnp.where((z > 0) & (z < layers), ZSCALE, 0.0)
        above = jnp.where((z + 1 > 0) & (z + 1 < layers), ZSCALE, 0.0)
        at = height - 3 + i
        faces, diagonal = face_terms(perm[at], perm[at - 1], perm[at + 1], below, above, LANES)
        inverse = inverse_of(diagonal)
        const[i] = inverse * right[at]
        inverse = OMEGA * inverse
        for k in range(6):
            coef[k, i] = inverse * faces[k]
        diag[i] = diagonal

    for i in range(height + 6):
        build(i)

    def first(i):
        start = const[i + 1]
        near = [coef[k, i + 1] for k in range(6)]
        values[i] = stencil(start, const[i], const[i + 2], near, (1.0 + KEEP) * start)

    for i in range(height + 4):
        first(i)

    def residue(i):
        centre = values[i + 2]
        base = const[i + 3] - OMEGA * centre
        near = [coef[k, i + 3] for k in range(6)]
        scaled = stencil(centre, values[i + 1], values[i + 3], near, base)
        return scaled * (diag[i + 3] * (1.0 / OMEGA))

    for m in range(height // 2):
        pair_right[m] = residue(2 * m) + residue(2 * m + 1)
        pair_perm[m] = (perm[height + 2 * m] + perm[height + 2 * m + 1]) * 0.125
    half = pair_right.shape[1] // 2
    rows = []
    for m in range(height // 2):
        both = [x[m, pl.ds(0, half, 2), :] + x[m, pl.ds(1, half, 2), :] for x in (pair_right, pair_perm)]
        rows.append(jnp.concatenate(both, axis=1))
    for m, x in enumerate(selector_dot(rows, lane_selector(1, LANES, 2))):
        coarse_out[m] = x


class Packed:
    def __init__(self, nz, nx, ny):
        self.nz, self.nx, self.ny = nz, nx, ny
        self.groups = min(LANES // ny, nz)
        self.planes = nz // self.groups

    def lower(self, planes, p):
        return planes[p - 1] if p else roll(planes[self.planes - 1], self.ny, 1)

    def upper(self, planes, p):
        return planes[p + 1] if p + 1 < self.planes else roll(planes[0], -self.ny, 1)

    def system(self, right, perm, level):
        lane = iota((self.nx, LANES), 1)
        used = lane < self.groups * self.ny
        if self.groups * self.ny < LANES:
            perm = [jnp.where(used, x, 1.0) for x in perm]
        coefs, const, diagonals = [], [], []
        for p in range(self.planes):
            below, above = ZSCALE, ZSCALE
            if p == 0:
                below = jnp.where(lane < self.ny, 0.0, ZSCALE)
            if p + 1 == self.planes:
                above = jnp.where(lane < (self.groups - 1) * self.ny, ZSCALE, 0.0)
            faces, diagonal = face_terms(
                perm[p], self.lower(perm, p), self.upper(perm, p), below, above, self.ny
            )
            inverse = OMEGA * inverse_of(diagonal)
            coefs.append([inverse * face for face in faces])
            const.append(inverse * right[p] * (4.0**-level))
            diagonals.append(diagonal * (4.0**level / OMEGA))
        return coefs, const, diagonals

    def apply(self, values, coefs, bases):
        return [
            stencil(values[p], self.lower(values, p), self.upper(values, p), coefs[p], bases[p])
            for p in range(self.planes)
        ]

    def sweep(self, values, coefs, const):
        return self.apply(values, coefs, [KEEP * v + c for v, c in zip(values, const)])

    def coarser(self):
        return Packed(self.nz // 2, self.nx // 2, self.ny // 2)

    def restrict(self, fields, pads):
        coarse = self.coarser()
        step = coarse.groups // self.groups
        half = coarse.nx
        parts = []
        for values, pad in zip(fields, pads):
            rows = []
            for m in range(self.planes // 2):
                pad[m] = values[2 * m] + values[2 * m + 1]
                rows.append(pad[m, pl.ds(0, half, 2), :] + pad[m, pl.ds(1, half, 2), :])
            for p in range(coarse.planes):
                blocks = rows[p :: coarse.planes]
                parts.append(jnp.concatenate(blocks, axis=1) if step > 1 else blocks[0])
        sums = selector_dot(parts, lane_selector(self.groups, self.ny, step))
        return [sums[i : i + coarse.planes] for i in range(0, len(sums), coarse.planes)]

    def prolong(self, values, pad):
        coarse = self.coarser()
        step = coarse.groups // self.groups
        half = coarse.nx
        wide = selector_dot(values, lane_selector(self.groups, self.ny, step, spread=True))
        out = []
        for m in range(self.planes // 2):
            j, p = divmod(m, coarse.planes)
            plane = wide[p][:, j * LANES : (j + 1) * LANES]
            pad[m, pl.ds(0, half, 2), :] = plane
            pad[m, pl.ds(1, half, 2), :] = plane
            out += [pad[m], pad[m]]
        return out


def coarsest(grid, right, perm, level):
    coefs, const, _ = grid.system(right, perm, level)
    return lax.fori_loop(
        0,
        COARSE_SWEEPS - 1,
        lambda step, values: tuple(grid.sweep(values, coefs, const)),
        tuple(const),
        unroll=7,
    )


def packed_cycle(grid, right, perm, level, pads):
    if not pads:
        return coarsest(grid, right, perm, level)
    pad_right, pad_perm = pads[0]
    coefs, const, diagonals = grid.system(right, perm, level)
    values = grid.sweep(const, coefs, const)
    scaled = grid.apply(values, coefs, [c - OMEGA * v for c, v in zip(const, values)])
    residue = [r * d for r, d in zip(scaled, diagonals)]
    coarse_right, coarse_perm = grid.restrict((residue, perm), (pad_right, pad_perm))
    coarse_perm = [x * 0.125 for x in coarse_perm]
    update = packed_cycle(grid.coarser(), coarse_right, coarse_perm, level + 1, pads[1:])
    values = [v + e for v, e in zip(values, grid.prolong(update, pad_right))]
    for _ in range(2):
        values = grid.sweep(values, coefs, const)
    return values


def coarse_kernel(
    dom_ref, gathered, coef, const, before, out,
    level, first, pad_right1, pad_perm1, pad_right2, pad_perm2, update,
):
    height = out.shape[0]
    dom = dom_ref[0]
    domains, own, nx, _ = gathered.shape
    ny = LANES // 2
    grid = Packed(domains * own, nx, ny)
    left = iota((nx, LANES), 1) < ny
    right, perm = [], []
    for p in range(grid.planes):
        a = gathered[p // own, p % own]
        q = grid.planes + p
        b = gathered[q // own, q % own]
        right.append(jnp.where(left, a, roll(b, ny, 1)))
        perm.append(jnp.where(left, roll(a, ny, 1), b))
    pads = [(pad_right1, pad_perm1), (pad_right2, pad_perm2)]
    solved = packed_cycle(grid, right, perm, 1, pads)
    for p in range(grid.planes):
        update[p] = solved[p]
    planes, group = [], []
    for j in range(own + 2):
        layer = jnp.clip(dom * own + j - 1, 0, grid.nz - 1)
        group.append(layer // grid.planes)
        planes.append(update[lax.rem(layer, grid.planes)])
    for j, wide in enumerate(selector_dot(planes, lane_selector(1, LANES, 2, spread=True))):
        plane = jnp.where(group[j] == 0, wide[:, :LANES], wide[:, LANES:])
        pad = first.at[0]
        pad[pl.ds(0, nx, 2), :] = plane
        pad[pl.ds(1, nx, 2), :] = plane
        whole = first[0]
        level[2 * j] = before[2 * j] + whole
        level[2 * j + 1] = before[2 * j + 1] + whole

    def sweep(source, at, i):
        centre = source[i + 1]
        near = [coef[k, at + i] for k in range(6)]
        return stencil(centre, source[i], source[i + 2], near, KEEP * centre + const[at + i])

    def one(i):
        first[i] = sweep(level, 2, i)

    for i in range(height + 2):
        one(i)

    def two(i):
        out[i] = sweep(first, 3, i)

    for i in range(height):
        two(i)


def fine_part(dom, perm, source, layers):
    height, nx, ny = perm[0].shape
    field = lambda *lead: pltpu.VMEM(lead + (nx, ny), F32)
    vmem = pl.BlockSpec(memory_space=pltpu.VMEM)
    smem = pl.BlockSpec(memory_space=pltpu.SMEM)
    return pl.pallas_call(
        functools.partial(fine_kernel, layers),
        out_shape=(
            jax.ShapeDtypeStruct((6, height + 6, nx, ny), F32),
            jax.ShapeDtypeStruct((height + 6, nx, ny), F32),
            jax.ShapeDtypeStruct((height + 4, nx, ny), F32),
            jax.ShapeDtypeStruct((height // 2, nx // 2, ny), F32),
        ),
        in_specs=[smem] + [vmem] * 6,
        out_specs=(vmem,) * 4,
        scratch_shapes=[
            field(3 * height),
            field(3 * height),
            field(height + 6),
            field(height // 2),
            field(height // 2),
        ],
        compiler_params=pltpu.CompilerParams(vmem_limit_bytes=VMEM_LIMIT),
        name="fine",
    )(dom, *perm, *source)


def coarse_part(dom, gathered, coefs, const, values, height):
    _, nx, ny = values.shape
    field = lambda *shape: pltpu.VMEM(shape, F32)
    grid1 = Packed(gathered.shape[0] * gathered.shape[1], nx // 2, ny // 2)
    grid2 = grid1.coarser()
    pads1 = field(grid1.planes // 2, grid1.nx, LANES)
    pads2 = field(grid2.planes // 2, grid2.nx, LANES)
    vmem = pl.BlockSpec(memory_space=pltpu.VMEM)
    smem = pl.BlockSpec(memory_space=pltpu.SMEM)
    return pl.pallas_call(
        coarse_kernel,
        out_shape=jax.ShapeDtypeStruct((height, nx, ny), F32),
        in_specs=[smem] + [vmem] * 4,
        out_specs=vmem,
        scratch_shapes=[
            field(*values.shape),
            field(height + 2, nx, ny),
            pads1, pads1, pads2, pads2,
            field(grid1.planes, grid1.nx, LANES),
        ],
        compiler_params=pltpu.CompilerParams(vmem_limit_bytes=VMEM_LIMIT),
        name="coarse",
    )(dom, gathered, coefs, const, values)


def swaps(x, axis, step):
    return lax.ppermute(x, axis, [(i, i ^ step) for i in range(lax.axis_size(axis))])


def other_side(x):
    props, domains = lax.axis_size("prop"), lax.axis_size("dom")
    pairs = []
    for p in range(props):
        for d in range(domains):
            end = d in (0, domains - 1)
            partner = ((p ^ 1) * domains + d) if end else (p * domains + ((d + 1) ^ 1) - 1)
            pairs.append((p * domains + d, partner))
    return lax.ppermute(x, ("prop", "dom"), pairs)


def source_side(x):
    props, domains = lax.axis_size("prop"), lax.axis_size("dom")
    pairs = []
    for p in range(props):
        for d in range(domains):
            if p % 2 == 0:
                partner = p * domains + (d ^ 1)
            elif d in (0, domains - 1):
                partner = (p ^ 2) * domains + d
            else:
                partner = p * domains + ((d + 1) ^ 1) - 1
            pairs.append((p * domains + d, partner))
    return lax.ppermute(x, ("prop", "dom"), pairs)


def from_accepted(mine, accepted, beside):
    props = lax.axis_size("prop")
    step = props // 2
    own = SHRINK * mine
    offers, order = [mine], [0]
    while step:
        came = [swaps(x, "prop", step) for x in offers]
        if step == props // 2:
            came, own, beside = lax.optimization_barrier((came, own, beside))
        offers, order = offers + came, order + [x ^ step for x in order]
        step //= 2
    wanted = lax.axis_index("prop") ^ accepted
    current = offers[1]
    for at, offer in zip(order[2:], offers[2:]):
        current = jnp.where(wanted == at, offer, current)
    return jnp.where(wanted == 0, own, SHRINK * current), beside


def gather_parts(mine):
    domains = lax.axis_size("dom")
    copies = jnp.broadcast_to(mine[None], (domains,) + mine.shape)
    return lax.all_to_all(copies, "dom", 0, 0)


def body(states, accepted, noise, source):
    domains = lax.axis_size("dom")
    height = source.shape[0]
    dom = jnp.stack([lax.axis_index("dom"), lax.axis_index("prop")]).astype(jnp.int32)
    near = source_side(source)
    beside = (OMEGA * source, BETA * noise[0], near)
    current, (scaled, noise_part, near) = from_accepted(states[0], accepted[0], beside)
    perm = jnp.exp(current + noise_part)
    perms = (perm, swaps(perm, "dom", 1), other_side(perm))
    sources = (scaled, near, swaps(near, "prop", 1))
    *level, coarse = fine_part(dom, perms, sources, domains * height)
    return coarse_part(dom, gather_parts(coarse), *level, height)[None]


def solution(mesh):
    in_specs = (
        P("prop", "dom", None, None),
        P(),
        P("prop", "dom", None, None),
        P("dom", None, None),
    )
    out_specs = P("prop", "dom", None, None)
    return jax.shard_map(body, mesh=mesh, in_specs=in_specs, out_specs=out_specs, check_vma=False)
```

```python
import functools
import math

import jax
import jax.numpy as jnp
from jax import lax
from jax.experimental import pallas as pl
from jax.experimental.pallas import tpu as pltpu
from jax.sharding import PartitionSpec as P

COARSE_SWEEPS = 64
OMEGA = 0.7
KEEP = 1.0 - OMEGA
BETA = 0.4
SHRINK = math.sqrt(1.0 - BETA * BETA)
ZSCALE = 16.0
LANES = 128
VMEM_LIMIT = 40 * 1024 * 1024
F32 = jnp.float32
WEST, EAST, SOUTH, NORTH, BELOW, ABOVE, CONST = range(7)


def iota(shape, dim):
    return lax.broadcasted_iota(jnp.int32, shape, dim)


def roll(x, amount, axis):
    axis = axis % x.ndim
    return pltpu.roll(x, amount % x.shape[axis], axis)


def inverse_of(x):
    guess = pl.reciprocal(x, approx=True)
    return guess * (2.0 - x * guess)


def harmonic(a, b):
    return (2.0 * a) * b * inverse_of(a + b)


def selector_dot(parts, selector):
    x = jnp.concatenate(parts, axis=0) if len(parts) > 1 else parts[0]
    rows = x.shape[0]
    high = x.astype(jnp.bfloat16).astype(F32)
    rest = x - high
    middle = rest.astype(jnp.bfloat16).astype(F32)
    terms = jnp.concatenate([high, middle, rest - middle], axis=0).astype(jnp.bfloat16)
    y = jnp.dot(terms, selector, preferred_element_type=F32)
    total = y[:rows] + y[rows : 2 * rows] + y[2 * rows :]
    height = parts[0].shape[0]
    return [total[i * height : (i + 1) * height] for i in range(len(parts))]


def face_terms(perm, lower, upper, below_scale, above_scale, ny):
    shape = perm.shape
    rows = iota(shape, 0)
    columns = iota(shape, 1) & (ny - 1)
    west = jnp.where(rows == 0, 0.0, harmonic(perm, roll(perm, 1, 0)))
    east = roll(west, -1, 0)
    south = jnp.where(columns == 0, 0.0, harmonic(perm, roll(perm, 1, 1)))
    north = roll(south, -1, 1)
    below = below_scale * harmonic(perm, lower)
    above = above_scale * harmonic(perm, upper)
    ends = jnp.where(rows == 0, perm, 0.0) + jnp.where(rows == shape[0] - 1, perm, 0.0)
    ends = ends + jnp.where(columns == 0, perm, 0.0) + jnp.where(columns == ny - 1, perm, 0.0)
    diagonal = ((west + east) + (south + north)) + ((below + above) + ends)
    return (west, east, south, north, below, above), diagonal


def stencil(values, lower, upper, coefs, base):
    x = coefs[0] * roll(values, 1, 0) + coefs[1] * roll(values, -1, 0)
    y = coefs[2] * roll(values, 1, 1) + coefs[3] * roll(values, -1, 1)
    z = coefs[4] * lower + coefs[5] * upper
    return (x + y) + (z + base)


def lane_selector(groups, ny, step, spread=False):
    shape = (LANES, step * LANES) if spread else (step * LANES, LANES)
    source, target = iota(shape, int(spread)), iota(shape, 1 - int(spread))
    bits = ny.bit_length() - 1
    lane = source & (LANES - 1)
    group = (lane >> bits) * step + (source >> 7)
    wanted = (group << (bits - 1)) + ((lane & (ny - 1)) >> 1)
    return jnp.where((target == wanted) & (lane < groups * ny), 1.0, 0.0).astype(jnp.bfloat16)


def fine_kernel(
    layers,
    dom_ref,
    per, per_pair, per_other,
    src, src_near, src_next,
    coef, const, values, coarse_out,
    perm, right, diag, pair_right, pair_perm,
):
    height = per.shape[0]
    dom = dom_ref[0]
    pair_at = jnp.where(lax.rem(dom, 2) == 0, 2 * height, 0)
    other_at = 2 * height - pair_at

    near_at = jnp.where(lax.rem(dom_ref[1], 2) == 0, pair_at, other_at)
    next_at = 2 * height - near_at
    for i in range(height):
        for at, p in ((height, per), (pair_at, per_pair), (other_at, per_other)):
            perm[at + i] = p[i]
        right[height + i] = src[i]
        right[near_at + i] = OMEGA * src_near[i]
        right[next_at + i] = OMEGA * src_next[i]

    def build(i):
        z = dom * height + i - 3
        below = jnp.where((z > 0) & (z < layers), ZSCALE, 0.0)
        above = jnp.where((z + 1 > 0) & (z + 1 < layers), ZSCALE, 0.0)
        at = height - 3 + i
        faces, diagonal = face_terms(perm[at], perm[at - 1], perm[at + 1], below, above, LANES)
        inverse = inverse_of(diagonal)
        const[i] = inverse * right[at]
        inverse = OMEGA * inverse
        for k in range(6):
            coef[k, i] = inverse * faces[k]
        diag[i] = diagonal

    for i in range(height + 6):
        build(i)

    def first(i):
        start = const[i + 1]
        near = [coef[k, i + 1] for k in range(6)]
        values[i] = stencil(start, const[i], const[i + 2], near, (1.0 + KEEP) * start)

    for i in range(height + 4):
        first(i)

    def residue(i):
        centre = values[i + 2]
        base = const[i + 3] - OMEGA * centre
        near = [coef[k, i + 3] for k in range(6)]
        scaled = stencil(centre, values[i + 1], values[i + 3], near, base)
        return scaled * (diag[i + 3] * (1.0 / OMEGA))

    for m in range(height // 2):
        pair_right[m] = residue(2 * m) + residue(2 * m + 1)
        pair_perm[m] = (perm[height + 2 * m] + perm[height + 2 * m + 1]) * 0.125
    half = pair_right.shape[1] // 2
    rows = []
    for m in range(height // 2):
        both = [x[m, pl.ds(0, half, 2), :] + x[m, pl.ds(1, half, 2), :] for x in (pair_right, pair_perm)]
        rows.append(jnp.concatenate(both, axis=1))
    for m, x in enumerate(selector_dot(rows, lane_selector(1, LANES, 2))):
        coarse_out[m] = x


class Packed:
    def __init__(self, nz, nx, ny):
        self.nz, self.nx, self.ny = nz, nx, ny
        self.groups = min(LANES // ny, nz)
        self.planes = nz // self.groups

    def lower(self, planes, p):
        return planes[p - 1] if p else roll(planes[self.planes - 1], self.ny, 1)

    def upper(self, planes, p):
        return planes[p + 1] if p + 1 < self.planes else roll(planes[0], -self.ny, 1)

    def system(self, right, perm, level):
        lane = iota((self.nx, LANES), 1)
        used = lane < self.groups * self.ny
        if self.groups * self.ny < LANES:
            perm = [jnp.where(used, x, 1.0) for x in perm]
        coefs, const, diagonals = [], [], []
        for p in range(self.planes):
            below, above = ZSCALE, ZSCALE
            if p == 0:
                below = jnp.where(lane < self.ny, 0.0, ZSCALE)
            if p + 1 == self.planes:
                above = jnp.where(lane < (self.groups - 1) * self.ny, ZSCALE, 0.0)
            faces, diagonal = face_terms(
                perm[p], self.lower(perm, p), self.upper(perm, p), below, above, self.ny
            )
            inverse = OMEGA * inverse_of(diagonal)
            coefs.append([inverse * face for face in faces])
            const.append(inverse * right[p] * (4.0**-level))
            diagonals.append(diagonal * (4.0**level / OMEGA))
        return coefs, const, diagonals

    def apply(self, values, coefs, bases):
        return [
            stencil(values[p], self.lower(values, p), self.upper(values, p), coefs[p], bases[p])
            for p in range(self.planes)
        ]

    def sweep(self, values, coefs, const):
        return self.apply(values, coefs, [KEEP * v + c for v, c in zip(values, const)])

    def coarser(self):
        return Packed(self.nz // 2, self.nx // 2, self.ny // 2)

    def restrict(self, fields, pads):
        coarse = self.coarser()
        step = coarse.groups // self.groups
        half = coarse.nx
        parts = []
        for values, pad in zip(fields, pads):
            rows = []
            for m in range(self.planes // 2):
                pad[m] = values[2 * m] + values[2 * m + 1]
                rows.append(pad[m, pl.ds(0, half, 2), :] + pad[m, pl.ds(1, half, 2), :])
            for p in range(coarse.planes):
                blocks = rows[p :: coarse.planes]
                parts.append(jnp.concatenate(blocks, axis=1) if step > 1 else blocks[0])
        sums = selector_dot(parts, lane_selector(self.groups, self.ny, step))
        return [sums[i : i + coarse.planes] for i in range(0, len(sums), coarse.planes)]

    def prolong(self, values, pad):
        coarse = self.coarser()
        step = coarse.groups // self.groups
        half = coarse.nx
        wide = selector_dot(values, lane_selector(self.groups, self.ny, step, spread=True))
        out = []
        for m in range(self.planes // 2):
            j, p = divmod(m, coarse.planes)
            plane = wide[p][:, j * LANES : (j + 1) * LANES]
            pad[m, pl.ds(0, half, 2), :] = plane
            pad[m, pl.ds(1, half, 2), :] = plane
            out += [pad[m], pad[m]]
        return out


def coarsest(grid, right, perm, level):
    coefs, const, _ = grid.system(right, perm, level)
    return lax.fori_loop(
        0,
        COARSE_SWEEPS - 1,
        lambda step, values: tuple(grid.sweep(values, coefs, const)),
        tuple(const),
        unroll=7,
    )


def packed_cycle(grid, right, perm, level, pads):
    if not pads:
        return coarsest(grid, right, perm, level)
    pad_right, pad_perm = pads[0]
    coefs, const, diagonals = grid.system(right, perm, level)
    values = grid.sweep(const, coefs, const)
    scaled = grid.apply(values, coefs, [c - OMEGA * v for c, v in zip(const, values)])
    residue = [r * d for r, d in zip(scaled, diagonals)]
    coarse_right, coarse_perm = grid.restrict((residue, perm), (pad_right, pad_perm))
    coarse_perm = [x * 0.125 for x in coarse_perm]
    update = packed_cycle(grid.coarser(), coarse_right, coarse_perm, level + 1, pads[1:])
    values = [v + e for v, e in zip(values, grid.prolong(update, pad_right))]
    for _ in range(2):
        values = grid.sweep(values, coefs, const)
    return values


def coarse_kernel(
    dom_ref, gathered, coef, const, before, out,
    level, first, pad_right1, pad_perm1, pad_right2, pad_perm2, update,
):
    height = out.shape[0]
    dom = dom_ref[0]
    domains, own, nx, _ = gathered.shape
    ny = LANES // 2
    grid = Packed(domains * own, nx, ny)
    left = iota((nx, LANES), 1) < ny
    right, perm = [], []
    for p in range(grid.planes):
        a = gathered[p // own, p % own]
        q = grid.planes + p
        b = gathered[q // own, q % own]
        right.append(jnp.where(left, a, roll(b, ny, 1)))
        perm.append(jnp.where(left, roll(a, ny, 1), b))
    pads = [(pad_right1, pad_perm1), (pad_right2, pad_perm2)]
    solved = packed_cycle(grid, right, perm, 1, pads)
    for p in range(grid.planes):
        update[p] = solved[p]
    planes, group = [], []
    for j in range(own + 2):
        layer = jnp.clip(dom * own + j - 1, 0, grid.nz - 1)
        group.append(layer // grid.planes)
        planes.append(update[lax.rem(layer, grid.planes)])
    for j, wide in enumerate(selector_dot(planes, lane_selector(1, LANES, 2, spread=True))):
        plane = jnp.where(group[j] == 0, wide[:, :LANES], wide[:, LANES:])
        pad = first.at[0]
        pad[pl.ds(0, nx, 2), :] = plane
        pad[pl.ds(1, nx, 2), :] = plane
        whole = first[0]
        level[2 * j] = before[2 * j] + whole
        level[2 * j + 1] = before[2 * j + 1] + whole

    def sweep(source, at, i):
        centre = source[i + 1]
        near = [coef[k, at + i] for k in range(6)]
        return stencil(centre, source[i], source[i + 2], near, KEEP * centre + const[at + i])

    def one(i):
        first[i] = sweep(level, 2, i)

    for i in range(height + 2):
        one(i)

    def two(i):
        out[i] = sweep(first, 3, i)

    for i in range(height):
        two(i)


def fine_part(dom, perm, source, layers):
    height, nx, ny = perm[0].shape
    field = lambda *lead: pltpu.VMEM(lead + (nx, ny), F32)
    vmem = pl.BlockSpec(memory_space=pltpu.VMEM)
    smem = pl.BlockSpec(memory_space=pltpu.SMEM)
    return pl.pallas_call(
        functools.partial(fine_kernel, layers),
        out_shape=(
            jax.ShapeDtypeStruct((6, height + 6, nx, ny), F32),
            jax.ShapeDtypeStruct((height + 6, nx, ny), F32),
            jax.ShapeDtypeStruct((height + 4, nx, ny), F32),
            jax.ShapeDtypeStruct((height // 2, nx // 2, ny), F32),
        ),
        in_specs=[smem] + [vmem] * 6,
        out_specs=(vmem,) * 4,
        scratch_shapes=[
            field(3 * height),
            field(3 * height),
            field(height + 6),
            field(height // 2),
            field(height // 2),
        ],
        compiler_params=pltpu.CompilerParams(vmem_limit_bytes=VMEM_LIMIT),
        name="fine",
    )(dom, *perm, *source)


def coarse_part(dom, gathered, coefs, const, values, height):
    _, nx, ny = values.shape
    field = lambda *shape: pltpu.VMEM(shape, F32)
    grid1 = Packed(gathered.shape[0] * gathered.shape[1], nx // 2, ny // 2)
    grid2 = grid1.coarser()
    pads1 = field(grid1.planes // 2, grid1.nx, LANES)
    pads2 = field(grid2.planes // 2, grid2.nx, LANES)
    vmem = pl.BlockSpec(memory_space=pltpu.VMEM)
    smem = pl.BlockSpec(memory_space=pltpu.SMEM)
    return pl.pallas_call(
        coarse_kernel,
        out_shape=jax.ShapeDtypeStruct((height, nx, ny), F32),
        in_specs=[smem] + [vmem] * 4,
        out_specs=vmem,
        scratch_shapes=[
            field(*values.shape),
            field(height + 2, nx, ny),
            pads1, pads1, pads2, pads2,
            field(grid1.planes, grid1.nx, LANES),
        ],
        compiler_params=pltpu.CompilerParams(vmem_limit_bytes=VMEM_LIMIT),
        name="coarse",
    )(dom, gathered, coefs, const, values)


def swaps(x, axis, step):
    return lax.ppermute(x, axis, [(i, i ^ step) for i in range(lax.axis_size(axis))])


def other_side(x):
    props, domains = lax.axis_size("prop"), lax.axis_size("dom")
    pairs = []
    for p in range(props):
        for d in range(domains):
            end = d in (0, domains - 1)
            partner = ((p ^ 1) * domains + d) if end else (p * domains + ((d + 1) ^ 1) - 1)
            pairs.append((p * domains + d, partner))
    return lax.ppermute(x, ("prop", "dom"), pairs)


def source_side(x):
    props, domains = lax.axis_size("prop"), lax.axis_size("dom")
    pairs = []
    for p in range(props):
        for d in range(domains):
            if p % 2 == 0:
                partner = p * domains + (d ^ 1)
            elif d in (0, domains - 1):
                partner = (p ^ 2) * domains + d
            else:
                partner = p * domains + ((d + 1) ^ 1) - 1
            pairs.append((p * domains + d, partner))
    return lax.ppermute(x, ("prop", "dom"), pairs)


def from_accepted(mine, accepted, beside):
    props = lax.axis_size("prop")
    step = props // 2
    own = SHRINK * mine
    offers, order = [mine], [0]
    while step:
        came = [swaps(x, "prop", step) for x in offers]
        if step == props // 2:
            came, own, beside = lax.optimization_barrier((came, own, beside))
        offers, order = offers + came, order + [x ^ step for x in order]
        step //= 2
    wanted = lax.axis_index("prop") ^ accepted
    current = offers[1]
    for at, offer in zip(order[2:], offers[2:]):
        current = jnp.where(wanted == at, offer, current)
    return jnp.where(wanted == 0, own, SHRINK * current), beside


def gather_parts(mine):
    domains = lax.axis_size("dom")
    copies = jnp.broadcast_to(mine[None], (domains,) + mine.shape)
    return lax.all_to_all(copies, "dom", 0, 0)


def body(states, accepted, noise, source):
    domains = lax.axis_size("dom")
    height = source.shape[0]
    dom = jnp.stack([lax.axis_index("dom"), lax.axis_index("prop")]).astype(jnp.int32)
    near = source_side(source)
    beside = (OMEGA * source, BETA * noise[0])
    current, (scaled, noise_part) = from_accepted(states[0], accepted[0], beside)
    perm = jnp.exp(current + noise_part)
    perms = (perm, swaps(perm, "dom", 1), other_side(perm))
    sources = (scaled, near, swaps(near, "prop", 1))
    *level, coarse = fine_part(dom, perms, sources, domains * height)
    return coarse_part(dom, gather_parts(coarse), *level, height)[None]


def solution(mesh):
    in_specs = (
        P("prop", "dom", None, None),
        P(),
        P("prop", "dom", None, None),
        P("dom", None, None),
    )
    out_specs = P("prop", "dom", None, None)
    return jax.shard_map(body, mesh=mesh, in_specs=in_specs, out_specs=out_specs, check_vma=False)
```

```python
import functools
import math

import jax
import jax.numpy as jnp
from jax import lax
from jax.experimental import pallas as pl
from jax.experimental.pallas import tpu as pltpu
from jax.sharding import PartitionSpec as P

COARSE_SWEEPS = 64
POWER = 2
OMEGA = 0.7
KEEP = 1.0 - OMEGA
BETA = 0.4
SHRINK = math.sqrt(1.0 - BETA * BETA)
ZSCALE = 16.0
LANES = 128
VMEM_LIMIT = 40 * 1024 * 1024
F32 = jnp.float32
WEST, EAST, SOUTH, NORTH, BELOW, ABOVE, CONST = range(7)


def iota(shape, dim):
    return lax.broadcasted_iota(jnp.int32, shape, dim)


def roll(x, amount, axis):
    axis = axis % x.ndim
    return pltpu.roll(x, amount % x.shape[axis], axis)


def inverse_of(x):
    guess = pl.reciprocal(x, approx=True)
    return guess * (2.0 - x * guess)


def harmonic(a, b):
    return (2.0 * a) * b * inverse_of(a + b)


def selector_dot(parts, selector):
    x = jnp.concatenate(parts, axis=0) if len(parts) > 1 else parts[0]
    rows = x.shape[0]
    high = x.astype(jnp.bfloat16).astype(F32)
    rest = x - high
    middle = rest.astype(jnp.bfloat16).astype(F32)
    terms = jnp.concatenate([high, middle, rest - middle], axis=0).astype(jnp.bfloat16)
    y = jnp.dot(terms, selector, preferred_element_type=F32)
    total = y[:rows] + y[rows : 2 * rows] + y[2 * rows :]
    height = parts[0].shape[0]
    return [total[i * height : (i + 1) * height] for i in range(len(parts))]


def face_terms(perm, lower, upper, below_scale, above_scale, ny):
    shape = perm.shape
    rows = iota(shape, 0)
    columns = iota(shape, 1) & (ny - 1)
    west = jnp.where(rows == 0, 0.0, harmonic(perm, roll(perm, 1, 0)))
    east = roll(west, -1, 0)
    south = jnp.where(columns == 0, 0.0, harmonic(perm, roll(perm, 1, 1)))
    north = roll(south, -1, 1)
    below = below_scale * harmonic(perm, lower)
    above = above_scale * harmonic(perm, upper)
    ends = jnp.where(rows == 0, perm, 0.0) + jnp.where(rows == shape[0] - 1, perm, 0.0)
    ends = ends + jnp.where(columns == 0, perm, 0.0) + jnp.where(columns == ny - 1, perm, 0.0)
    diagonal = ((west + east) + (south + north)) + ((below + above) + ends)
    return (west, east, south, north, below, above), diagonal


def stencil(values, lower, upper, coefs, base):
    x = coefs[0] * roll(values, 1, 0) + coefs[1] * roll(values, -1, 0)
    y = coefs[2] * roll(values, 1, 1) + coefs[3] * roll(values, -1, 1)
    z = coefs[4] * lower + coefs[5] * upper
    return (x + y) + (z + base)


def lane_selector(groups, ny, step, spread=False):
    shape = (LANES, step * LANES) if spread else (step * LANES, LANES)
    source, target = iota(shape, int(spread)), iota(shape, 1 - int(spread))
    bits = ny.bit_length() - 1
    lane = source & (LANES - 1)
    group = (lane >> bits) * step + (source >> 7)
    wanted = (group << (bits - 1)) + ((lane & (ny - 1)) >> 1)
    return jnp.where((target == wanted) & (lane < groups * ny), 1.0, 0.0).astype(jnp.bfloat16)


def fine_kernel(
    layers,
    dom_ref,
    per, per_pair, per_other,
    src, src_near, src_next,
    coef, const, values, coarse_out,
    perm, right, diag, pair_right, pair_perm,
):
    height = per.shape[0]
    dom = dom_ref[0]
    pair_at = jnp.where(lax.rem(dom, 2) == 0, 2 * height, 0)
    other_at = 2 * height - pair_at

    near_at = jnp.where(lax.rem(dom_ref[1], 2) == 0, pair_at, other_at)
    next_at = 2 * height - near_at
    for i in range(height):
        for at, p in ((height, per), (pair_at, per_pair), (other_at, per_other)):
            perm[at + i] = p[i]
        right[height + i] = src[i]
        right[near_at + i] = OMEGA * src_near[i]
        right[next_at + i] = OMEGA * src_next[i]

    def build(i):
        z = dom * height + i - 3
        below = jnp.where((z > 0) & (z < layers), ZSCALE, 0.0)
        above = jnp.where((z + 1 > 0) & (z + 1 < layers), ZSCALE, 0.0)
        at = height - 3 + i
        faces, diagonal = face_terms(perm[at], perm[at - 1], perm[at + 1], below, above, LANES)
        inverse = inverse_of(diagonal)
        const[i] = inverse * right[at]
        inverse = OMEGA * inverse
        for k in range(6):
            coef[k, i] = inverse * faces[k]
        diag[i] = diagonal

    for i in range(height + 6):
        build(i)

    def first(i):
        start = const[i + 1]
        near = [coef[k, i + 1] for k in range(6)]
        values[i] = stencil(start, const[i], const[i + 2], near, (1.0 + KEEP) * start)

    for i in range(height + 4):
        first(i)

    def residue(i):
        centre = values[i + 2]
        base = const[i + 3] - OMEGA * centre
        near = [coef[k, i + 3] for k in range(6)]
        scaled = stencil(centre, values[i + 1], values[i + 3], near, base)
        return scaled * (diag[i + 3] * (1.0 / OMEGA))

    for m in range(height // 2):
        pair_right[m] = residue(2 * m) + residue(2 * m + 1)
        pair_perm[m] = (perm[height + 2 * m] + perm[height + 2 * m + 1]) * 0.125
    half = pair_right.shape[1] // 2
    rows = []
    for m in range(height // 2):
        both = [x[m, pl.ds(0, half, 2), :] + x[m, pl.ds(1, half, 2), :] for x in (pair_right, pair_perm)]
        rows.append(jnp.concatenate(both, axis=1))
    for m, x in enumerate(selector_dot(rows, lane_selector(1, LANES, 2))):
        coarse_out[m] = x


class Packed:
    def __init__(self, nz, nx, ny):
        self.nz, self.nx, self.ny = nz, nx, ny
        self.groups = min(LANES // ny, nz)
        self.planes = nz // self.groups

    def lower(self, planes, p):
        return planes[p - 1] if p else roll(planes[self.planes - 1], self.ny, 1)

    def upper(self, planes, p):
        return planes[p + 1] if p + 1 < self.planes else roll(planes[0], -self.ny, 1)

    def system(self, right, perm, level):
        lane = iota((self.nx, LANES), 1)
        used = lane < self.groups * self.ny
        if self.groups * self.ny < LANES:
            perm = [jnp.where(used, x, 1.0) for x in perm]
        coefs, const, diagonals = [], [], []
        for p in range(self.planes):
            below, above = ZSCALE, ZSCALE
            if p == 0:
                below = jnp.where(lane < self.ny, 0.0, ZSCALE)
            if p + 1 == self.planes:
                above = jnp.where(lane < (self.groups - 1) * self.ny, ZSCALE, 0.0)
            faces, diagonal = face_terms(
                perm[p], self.lower(perm, p), self.upper(perm, p), below, above, self.ny
            )
            inverse = OMEGA * inverse_of(diagonal)
            coefs.append([inverse * face for face in faces])
            const.append(inverse * right[p] * (4.0**-level))
            diagonals.append(diagonal * (4.0**level / OMEGA))
        return coefs, const, diagonals

    def apply(self, values, coefs, bases):
        return [
            stencil(values[p], self.lower(values, p), self.upper(values, p), coefs[p], bases[p])
            for p in range(self.planes)
        ]

    def sweep(self, values, coefs, const):
        return self.apply(values, coefs, [KEEP * v + c for v, c in zip(values, const)])

    def coarser(self):
        return Packed(self.nz // 2, self.nx // 2, self.ny // 2)

    def restrict(self, fields, pads):
        coarse = self.coarser()
        step = coarse.groups // self.groups
        half = coarse.nx
        parts = []
        for values, pad in zip(fields, pads):
            rows = []
            for m in range(self.planes // 2):
                pad[m] = values[2 * m] + values[2 * m + 1]
                rows.append(pad[m, pl.ds(0, half, 2), :] + pad[m, pl.ds(1, half, 2), :])
            for p in range(coarse.planes):
                blocks = rows[p :: coarse.planes]
                parts.append(jnp.concatenate(blocks, axis=1) if step > 1 else blocks[0])
        sums = selector_dot(parts, lane_selector(self.groups, self.ny, step))
        return [sums[i : i + coarse.planes] for i in range(0, len(sums), coarse.planes)]

    def prolong(self, values, pad):
        coarse = self.coarser()
        step = coarse.groups // self.groups
        half = coarse.nx
        wide = selector_dot(values, lane_selector(self.groups, self.ny, step, spread=True))
        out = []
        for m in range(self.planes // 2):
            j, p = divmod(m, coarse.planes)
            plane = wide[p][:, j * LANES : (j + 1) * LANES]
            pad[m, pl.ds(0, half, 2), :] = plane
            pad[m, pl.ds(1, half, 2), :] = plane
            out += [pad[m], pad[m]]
        return out


class Flat:
    def __init__(self, finer):
        coarse = finer.coarser()
        self.finer = finer
        self.nz, self.nx, self.ny = coarse.nz, coarse.nx, coarse.ny
        self.pairs = finer.planes // 2

    def selector(self, spread=False):
        wide = self.finer.groups * LANES
        shape = (wide, LANES) if spread else (LANES, wide)
        fine, flat = iota(shape, int(spread)), iota(shape, 1 - int(spread))
        bits = self.finer.ny.bit_length() - 1
        same = (fine >> bits) == (flat >> 7)
        same &= ((fine & (self.finer.ny - 1)) >> 1) == (flat & (self.ny - 1))
        return jnp.where(same, 1.0, 0.0).astype(jnp.bfloat16)

    def diagonal(self):
        shape = (self.nx, LANES)
        return iota(shape, 0) == (iota(shape, 1) >> (self.ny.bit_length() - 1))

    def restrict(self, fields, pads):
        parts = []
        for values, pad in zip(fields, pads):
            for m in range(self.pairs):
                pad[m] = values[2 * m] + values[2 * m + 1]
                parts.append(pad[m, pl.ds(0, self.nx, 2), :] + pad[m, pl.ds(1, self.nx, 2), :])
        sums = selector_dot(parts, self.selector())
        mask = self.diagonal()
        out = []
        for i in range(len(fields)):
            planes = []
            for z in range(self.nz):
                s, m = divmod(z, self.pairs)
                block = sums[i * self.pairs + m][:, s * LANES : (s + 1) * LANES]
                row = jnp.sum(jnp.where(mask, block, 0.0), axis=0, keepdims=True)
                planes.append(jnp.broadcast_to(row, (8, LANES)))
            out.append(planes)
        return out

    def prolong(self, planes, pad):
        mask = self.diagonal()
        parts = []
        for m in range(self.pairs):
            blocks = [
                jnp.where(mask, planes[s * self.pairs + m], 0.0) for s in range(self.finer.groups)
            ]
            parts.append(jnp.concatenate(blocks, axis=1))
        out = []
        for m, wide in enumerate(selector_dot(parts, self.selector(spread=True))):
            pad[m, pl.ds(0, self.nx, 2), :] = wide
            pad[m, pl.ds(1, self.nx, 2), :] = wide
            out += [pad[m], pad[m]]
        return out

    def system(self, right, perm, level):
        lane = iota((8, LANES), 1)
        x, y = lane >> (self.ny.bit_length() - 1), lane & (self.ny - 1)
        keys = ((-1, 0, 0), (1, 0, 0), (0, -1, 0), (0, 1, 0), (0, 0, -1), (0, 0, 1))
        terms = {key: [None] * self.nz for key in keys}
        const = []
        faces = [harmonic(perm[z], perm[z + 1]) * ZSCALE for z in range(self.nz - 1)]
        for z in range(self.nz):
            centre = perm[z]
            west = jnp.where(x == 0, 0.0, harmonic(centre, roll(centre, self.ny, 1)))
            east = roll(west, -self.ny, 1)
            south = jnp.where(y == 0, 0.0, harmonic(centre, roll(centre, 1, 1)))
            north = roll(south, -1, 1)
            below = faces[z - 1] if z else None
            above = faces[z] if z + 1 < self.nz else None
            parts = [west, east, south, north, below, above]
            for end in (x == 0, x == self.nx - 1, y == 0, y == self.ny - 1):
                parts.append(jnp.where(end, centre, 0.0))
            inverse = OMEGA * inverse_of(tree_sum([part for part in parts if part is not None]))
            for key, part in zip(keys, parts):
                if part is not None:
                    terms[key][z] = inverse * part
            const.append(inverse * right[z] * (4.0**-level))
        terms[0, 0, 0] = [jnp.full((8, LANES), KEEP, F32)] * self.nz
        return terms, const

    def shifted(self, planes, key):
        dx, dy, dz = key
        out = []
        for z in range(self.nz):
            plane = planes[z + dz] if 0 <= z + dz < self.nz else None
            moved = dx * self.ny + dy
            out.append(roll(plane, -moved, 1) if plane is not None and moved else plane)
        return out

    def product(self, first, second):
        sums = {}
        for key, coefs in first.items():
            for other, others in second.items():
                moved = self.shifted(others, key)
                total = tuple(a + b for a, b in zip(key, other))
                for z in range(self.nz):
                    if coefs[z] is not None and moved[z] is not None:
                        sums.setdefault(total, [[] for _ in range(self.nz)])[z].append(coefs[z] * moved[z])
        return {
            key: [tree_sum(parts) if parts else None for parts in planes]
            for key, planes in sums.items()
        }

    def apply(self, terms, values, base):
        moved = {}
        parts = [[x] for x in base]
        for (dx, dy, dz), coefs in terms.items():
            if (dx, dy) not in moved:
                moved[dx, dy] = self.shifted(values, (dx, dy, 0))
            for z in range(self.nz):
                if coefs[z] is not None:
                    parts[z].append(coefs[z][...] * moved[dx, dy][z + dz])
        return tuple(tree_sum(x) for x in parts)

    def solve(self, right, perm, level, store):
        terms, const = self.system(right, perm, level)
        power, base, start = terms, const, const
        for _ in range(POWER - 1):
            base = self.apply(terms, base, const)
            power = self.product(terms, power)
        if COARSE_SWEEPS % POWER == 0:
            start = base
        slot = 0
        kept = {}
        for key in sorted(power):
            kept[key] = [None] * self.nz
            for z in range(self.nz):
                if power[key][z] is not None:
                    store[slot] = power[key][z]
                    kept[key][z] = store.at[slot]
                    slot += 1
        assert slot == store.shape[0]
        steps = (COARSE_SWEEPS - 1) // POWER
        assert steps * POWER + (POWER if COARSE_SWEEPS % POWER == 0 else 1) == COARSE_SWEEPS
        return lax.fori_loop(
            0, steps, lambda step, values: self.apply(kept, values, base), tuple(start)
        )

    def count(self):
        total = 0
        for z in range(self.nz):
            for other in range(self.nz):
                reach = POWER - abs(z - other)
                total += 2 * reach * (reach + 1) + 1 if reach >= 0 else 0
        return total


def tree_sum(parts):
    while len(parts) > 1:
        odd = parts[len(parts) // 2 * 2 :]
        parts = [a + b for a, b in zip(parts[::2], parts[1::2])] + odd
    return parts[0]


def packed_cycle(grid, right, perm, level, pads, store):
    pad_right, pad_perm = pads[0]
    coefs, const, diagonals = grid.system(right, perm, level)
    values = grid.sweep(const, coefs, const)
    scaled = grid.apply(values, coefs, [c - OMEGA * v for c, v in zip(const, values)])
    residue = [r * d for r, d in zip(scaled, diagonals)]
    coarse = grid if len(pads) > 1 else Flat(grid)
    coarse_right, coarse_perm = coarse.restrict((residue, perm), (pad_right, pad_perm))
    coarse_perm = [x * 0.125 for x in coarse_perm]
    if len(pads) > 1:
        update = packed_cycle(grid.coarser(), coarse_right, coarse_perm, level + 1, pads[1:], store)
    else:
        update = coarse.solve(coarse_right, coarse_perm, level + 1, store)
    values = [v + e for v, e in zip(values, coarse.prolong(update, pad_right))]
    for _ in range(2):
        values = grid.sweep(values, coefs, const)
    return values


def coarse_kernel(
    dom_ref, gathered, coef, const, before, out,
    level, first, pad_right1, pad_perm1, pad_right2, pad_perm2, update, store,
):
    height = out.shape[0]
    dom = dom_ref[0]
    domains, own, nx, _ = gathered.shape
    ny = LANES // 2
    grid = Packed(domains * own, nx, ny)
    left = iota((nx, LANES), 1) < ny
    right, perm = [], []
    for p in range(grid.planes):
        a = gathered[p // own, p % own]
        q = grid.planes + p
        b = gathered[q // own, q % own]
        right.append(jnp.where(left, a, roll(b, ny, 1)))
        perm.append(jnp.where(left, roll(a, ny, 1), b))
    pads = [(pad_right1, pad_perm1), (pad_right2, pad_perm2)]
    solved = packed_cycle(grid, right, perm, 1, pads, store)
    for p in range(grid.planes):
        update[p] = solved[p]
    planes, group = [], []
    for j in range(own + 2):
        layer = jnp.clip(dom * own + j - 1, 0, grid.nz - 1)
        group.append(layer // grid.planes)
        planes.append(update[lax.rem(layer, grid.planes)])
    for j, wide in enumerate(selector_dot(planes, lane_selector(1, LANES, 2, spread=True))):
        plane = jnp.where(group[j] == 0, wide[:, :LANES], wide[:, LANES:])
        pad = first.at[0]
        pad[pl.ds(0, nx, 2), :] = plane
        pad[pl.ds(1, nx, 2), :] = plane
        whole = first[0]
        level[2 * j] = before[2 * j] + whole
        level[2 * j + 1] = before[2 * j + 1] + whole

    def sweep(source, at, i):
        centre = source[i + 1]
        near = [coef[k, at + i] for k in range(6)]
        return stencil(centre, source[i], source[i + 2], near, KEEP * centre + const[at + i])

    def one(i):
        first[i] = sweep(level, 2, i)

    for i in range(height + 2):
        one(i)

    def two(i):
        out[i] = sweep(first, 3, i)

    for i in range(height):
        two(i)


def fine_part(dom, perm, source, layers):
    height, nx, ny = perm[0].shape
    field = lambda *lead: pltpu.VMEM(lead + (nx, ny), F32)
    vmem = pl.BlockSpec(memory_space=pltpu.VMEM)
    smem = pl.BlockSpec(memory_space=pltpu.SMEM)
    return pl.pallas_call(
        functools.partial(fine_kernel, layers),
        out_shape=(
            jax.ShapeDtypeStruct((6, height + 6, nx, ny), F32),
            jax.ShapeDtypeStruct((height + 6, nx, ny), F32),
            jax.ShapeDtypeStruct((height + 4, nx, ny), F32),
            jax.ShapeDtypeStruct((height // 2, nx // 2, ny), F32),
        ),
        in_specs=[smem] + [vmem] * 6,
        out_specs=(vmem,) * 4,
        scratch_shapes=[
            field(3 * height),
            field(3 * height),
            field(height + 6),
            field(height // 2),
            field(height // 2),
        ],
        compiler_params=pltpu.CompilerParams(vmem_limit_bytes=VMEM_LIMIT),
        name="fine",
    )(dom, *perm, *source)


def coarse_part(dom, gathered, coefs, const, values, height):
    _, nx, ny = values.shape
    field = lambda *shape: pltpu.VMEM(shape, F32)
    grid1 = Packed(gathered.shape[0] * gathered.shape[1], nx // 2, ny // 2)
    grid2 = grid1.coarser()
    pads1 = field(grid1.planes // 2, grid1.nx, LANES)
    pads2 = field(grid2.planes // 2, grid2.nx, LANES)
    vmem = pl.BlockSpec(memory_space=pltpu.VMEM)
    smem = pl.BlockSpec(memory_space=pltpu.SMEM)
    return pl.pallas_call(
        coarse_kernel,
        out_shape=jax.ShapeDtypeStruct((height, nx, ny), F32),
        in_specs=[smem] + [vmem] * 4,
        out_specs=vmem,
        scratch_shapes=[
            field(*values.shape),
            field(height + 2, nx, ny),
            pads1, pads1, pads2, pads2,
            field(grid1.planes, grid1.nx, LANES),
            field(Flat(grid2).count(), 8, LANES),
        ],
        compiler_params=pltpu.CompilerParams(vmem_limit_bytes=VMEM_LIMIT),
        name="coarse",
    )(dom, gathered, coefs, const, values)


def swaps(x, axis, step):
    return lax.ppermute(x, axis, [(i, i ^ step) for i in range(lax.axis_size(axis))])


def other_side(x):
    props, domains = lax.axis_size("prop"), lax.axis_size("dom")
    pairs = []
    for p in range(props):
        for d in range(domains):
            end = d in (0, domains - 1)
            partner = ((p ^ 1) * domains + d) if end else (p * domains + ((d + 1) ^ 1) - 1)
            pairs.append((p * domains + d, partner))
    return lax.ppermute(x, ("prop", "dom"), pairs)


def source_side(x):
    props, domains = lax.axis_size("prop"), lax.axis_size("dom")
    pairs = []
    for p in range(props):
        for d in range(domains):
            if p % 2 == 0:
                partner = p * domains + (d ^ 1)
            elif d in (0, domains - 1):
                partner = (p ^ 2) * domains + d
            else:
                partner = p * domains + ((d + 1) ^ 1) - 1
            pairs.append((p * domains + d, partner))
    return lax.ppermute(x, ("prop", "dom"), pairs)


def from_accepted(mine, accepted, beside):
    props = lax.axis_size("prop")
    step = props // 2
    own = SHRINK * mine
    offers, order = [mine], [0]
    while step:
        came = [swaps(x, "prop", step) for x in offers]
        if step == props // 2:
            came, own, beside = lax.optimization_barrier((came, own, beside))
        offers, order = offers + came, order + [x ^ step for x in order]
        step //= 2
    wanted = lax.axis_index("prop") ^ accepted
    current = offers[1]
    for at, offer in zip(order[2:], offers[2:]):
        current = jnp.where(wanted == at, offer, current)
    return jnp.where(wanted == 0, own, SHRINK * current), beside


def gather_parts(mine):
    domains = lax.axis_size("dom")
    copies = jnp.broadcast_to(mine[None], (domains,) + mine.shape)
    return lax.all_to_all(copies, "dom", 0, 0)


def body(states, accepted, noise, source):
    domains = lax.axis_size("dom")
    height = source.shape[0]
    dom = jnp.stack([lax.axis_index("dom"), lax.axis_index("prop")]).astype(jnp.int32)
    near = source_side(source)
    beside = (OMEGA * source, BETA * noise[0])
    current, (scaled, noise_part) = from_accepted(states[0], accepted[0], beside)
    perm = jnp.exp(current + noise_part)
    perms = (perm, swaps(perm, "dom", 1), other_side(perm))
    sources = (scaled, near, swaps(near, "prop", 1))
    *level, coarse = fine_part(dom, perms, sources, domains * height)
    return coarse_part(dom, gather_parts(coarse), *level, height)[None]


def solution(mesh):
    in_specs = (
        P("prop", "dom", None, None),
        P(),
        P("prop", "dom", None, None),
        P("dom", None, None),
    )
    out_specs = P("prop", "dom", None, None)
    return jax.shard_map(body, mesh=mesh, in_specs=in_specs, out_specs=out_specs, check_vma=False)
```

```python
import functools
import math

import jax
import jax.numpy as jnp
from jax import lax
from jax.experimental import pallas as pl
from jax.experimental.pallas import tpu as pltpu
from jax.sharding import PartitionSpec as P

COARSE_SWEEPS = 64
POWER = 3
OMEGA = 0.7
KEEP = 1.0 - OMEGA
BETA = 0.4
SHRINK = math.sqrt(1.0 - BETA * BETA)
ZSCALE = 16.0
LANES = 128
VMEM_LIMIT = 40 * 1024 * 1024
F32 = jnp.float32
WEST, EAST, SOUTH, NORTH, BELOW, ABOVE, CONST = range(7)


def iota(shape, dim):
    return lax.broadcasted_iota(jnp.int32, shape, dim)


def roll(x, amount, axis):
    axis = axis % x.ndim
    return pltpu.roll(x, amount % x.shape[axis], axis)


def inverse_of(x):
    guess = pl.reciprocal(x, approx=True)
    return guess * (2.0 - x * guess)


def harmonic(a, b):
    return (2.0 * a) * b * inverse_of(a + b)


def selector_dot(parts, selector):
    x = jnp.concatenate(parts, axis=0) if len(parts) > 1 else parts[0]
    rows = x.shape[0]
    high = x.astype(jnp.bfloat16).astype(F32)
    rest = x - high
    middle = rest.astype(jnp.bfloat16).astype(F32)
    terms = jnp.concatenate([high, middle, rest - middle], axis=0).astype(jnp.bfloat16)
    y = jnp.dot(terms, selector, preferred_element_type=F32)
    total = y[:rows] + y[rows : 2 * rows] + y[2 * rows :]
    height = parts[0].shape[0]
    return [total[i * height : (i + 1) * height] for i in range(len(parts))]


def face_terms(perm, lower, upper, below_scale, above_scale, ny):
    shape = perm.shape
    rows = iota(shape, 0)
    columns = iota(shape, 1) & (ny - 1)
    west = jnp.where(rows == 0, 0.0, harmonic(perm, roll(perm, 1, 0)))
    east = roll(west, -1, 0)
    south = jnp.where(columns == 0, 0.0, harmonic(perm, roll(perm, 1, 1)))
    north = roll(south, -1, 1)
    below = below_scale * harmonic(perm, lower)
    above = above_scale * harmonic(perm, upper)
    ends = jnp.where(rows == 0, perm, 0.0) + jnp.where(rows == shape[0] - 1, perm, 0.0)
    ends = ends + jnp.where(columns == 0, perm, 0.0) + jnp.where(columns == ny - 1, perm, 0.0)
    diagonal = ((west + east) + (south + north)) + ((below + above) + ends)
    return (west, east, south, north, below, above), diagonal


def stencil(values, lower, upper, coefs, base):
    x = coefs[0] * roll(values, 1, 0) + coefs[1] * roll(values, -1, 0)
    y = coefs[2] * roll(values, 1, 1) + coefs[3] * roll(values, -1, 1)
    z = coefs[4] * lower + coefs[5] * upper
    return (x + y) + (z + base)


def lane_selector(groups, ny, step, spread=False):
    shape = (LANES, step * LANES) if spread else (step * LANES, LANES)
    source, target = iota(shape, int(spread)), iota(shape, 1 - int(spread))
    bits = ny.bit_length() - 1
    lane = source & (LANES - 1)
    group = (lane >> bits) * step + (source >> 7)
    wanted = (group << (bits - 1)) + ((lane & (ny - 1)) >> 1)
    return jnp.where((target == wanted) & (lane < groups * ny), 1.0, 0.0).astype(jnp.bfloat16)


def fine_kernel(
    layers,
    dom_ref,
    per, per_pair, per_other,
    src, src_near, src_next,
    coef, const, values, coarse_out,
    perm, right, diag, pair_right, pair_perm,
):
    height = per.shape[0]
    dom = dom_ref[0]
    pair_at = jnp.where(lax.rem(dom, 2) == 0, 2 * height, 0)
    other_at = 2 * height - pair_at

    near_at = jnp.where(lax.rem(dom_ref[1], 2) == 0, pair_at, other_at)
    next_at = 2 * height - near_at
    for i in range(height):
        for at, p in ((height, per), (pair_at, per_pair), (other_at, per_other)):
            perm[at + i] = p[i]
        right[height + i] = src[i]
        right[near_at + i] = OMEGA * src_near[i]
        right[next_at + i] = OMEGA * src_next[i]

    def build(i):
        z = dom * height + i - 3
        below = jnp.where((z > 0) & (z < layers), ZSCALE, 0.0)
        above = jnp.where((z + 1 > 0) & (z + 1 < layers), ZSCALE, 0.0)
        at = height - 3 + i
        faces, diagonal = face_terms(perm[at], perm[at - 1], perm[at + 1], below, above, LANES)
        inverse = inverse_of(diagonal)
        const[i] = inverse * right[at]
        inverse = OMEGA * inverse
        for k in range(6):
            coef[k, i] = inverse * faces[k]
        diag[i] = diagonal

    for i in range(height + 6):
        build(i)

    def first(i):
        start = const[i + 1]
        near = [coef[k, i + 1] for k in range(6)]
        values[i] = stencil(start, const[i], const[i + 2], near, (1.0 + KEEP) * start)

    for i in range(height + 4):
        first(i)

    def residue(i):
        centre = values[i + 2]
        base = const[i + 3] - OMEGA * centre
        near = [coef[k, i + 3] for k in range(6)]
        scaled = stencil(centre, values[i + 1], values[i + 3], near, base)
        return scaled * (diag[i + 3] * (1.0 / OMEGA))

    for m in range(height // 2):
        pair_right[m] = residue(2 * m) + residue(2 * m + 1)
        pair_perm[m] = (perm[height + 2 * m] + perm[height + 2 * m + 1]) * 0.125
    half = pair_right.shape[1] // 2
    rows = []
    for m in range(height // 2):
        both = [x[m, pl.ds(0, half, 2), :] + x[m, pl.ds(1, half, 2), :] for x in (pair_right, pair_perm)]
        rows.append(jnp.concatenate(both, axis=1))
    for m, x in enumerate(selector_dot(rows, lane_selector(1, LANES, 2))):
        coarse_out[m] = x


class Packed:
    def __init__(self, nz, nx, ny):
        self.nz, self.nx, self.ny = nz, nx, ny
        self.groups = min(LANES // ny, nz)
        self.planes = nz // self.groups

    def lower(self, planes, p):
        return planes[p - 1] if p else roll(planes[self.planes - 1], self.ny, 1)

    def upper(self, planes, p):
        return planes[p + 1] if p + 1 < self.planes else roll(planes[0], -self.ny, 1)

    def system(self, right, perm, level):
        lane = iota((self.nx, LANES), 1)
        used = lane < self.groups * self.ny
        if self.groups * self.ny < LANES:
            perm = [jnp.where(used, x, 1.0) for x in perm]
        coefs, const, diagonals = [], [], []
        for p in range(self.planes):
            below, above = ZSCALE, ZSCALE
            if p == 0:
                below = jnp.where(lane < self.ny, 0.0, ZSCALE)
            if p + 1 == self.planes:
                above = jnp.where(lane < (self.groups - 1) * self.ny, ZSCALE, 0.0)
            faces, diagonal = face_terms(
                perm[p], self.lower(perm, p), self.upper(perm, p), below, above, self.ny
            )
            inverse = OMEGA * inverse_of(diagonal)
            coefs.append([inverse * face for face in faces])
            const.append(inverse * right[p] * (4.0**-level))
            diagonals.append(diagonal * (4.0**level / OMEGA))
        return coefs, const, diagonals

    def apply(self, values, coefs, bases):
        return [
            stencil(values[p], self.lower(values, p), self.upper(values, p), coefs[p], bases[p])
            for p in range(self.planes)
        ]

    def sweep(self, values, coefs, const):
        return self.apply(values, coefs, [KEEP * v + c for v, c in zip(values, const)])

    def coarser(self):
        return Packed(self.nz // 2, self.nx // 2, self.ny // 2)

    def restrict(self, fields, pads):
        coarse = self.coarser()
        step = coarse.groups // self.groups
        half = coarse.nx
        parts = []
        for values, pad in zip(fields, pads):
            rows = []
            for m in range(self.planes // 2):
                pad[m] = values[2 * m] + values[2 * m + 1]
                rows.append(pad[m, pl.ds(0, half, 2), :] + pad[m, pl.ds(1, half, 2), :])
            for p in range(coarse.planes):
                blocks = rows[p :: coarse.planes]
                parts.append(jnp.concatenate(blocks, axis=1) if step > 1 else blocks[0])
        sums = selector_dot(parts, lane_selector(self.groups, self.ny, step))
        return [sums[i : i + coarse.planes] for i in range(0, len(sums), coarse.planes)]

    def prolong(self, values, pad):
        coarse = self.coarser()
        step = coarse.groups // self.groups
        half = coarse.nx
        wide = selector_dot(values, lane_selector(self.groups, self.ny, step, spread=True))
        out = []
        for m in range(self.planes // 2):
            j, p = divmod(m, coarse.planes)
            plane = wide[p][:, j * LANES : (j + 1) * LANES]
            pad[m, pl.ds(0, half, 2), :] = plane
            pad[m, pl.ds(1, half, 2), :] = plane
            out += [pad[m], pad[m]]
        return out


class Flat:
    def __init__(self, finer):
        coarse = finer.coarser()
        self.finer = finer
        self.nz, self.nx, self.ny = coarse.nz, coarse.nx, coarse.ny
        self.pairs = finer.planes // 2

    def selector(self, spread=False):
        wide = self.finer.groups * LANES
        shape = (wide, LANES) if spread else (LANES, wide)
        fine, flat = iota(shape, int(spread)), iota(shape, 1 - int(spread))
        bits = self.finer.ny.bit_length() - 1
        same = (fine >> bits) == (flat >> 7)
        same &= ((fine & (self.finer.ny - 1)) >> 1) == (flat & (self.ny - 1))
        return jnp.where(same, 1.0, 0.0).astype(jnp.bfloat16)

    def diagonal(self):
        shape = (self.nx, LANES)
        return iota(shape, 0) == (iota(shape, 1) >> (self.ny.bit_length() - 1))

    def restrict(self, fields, pads):
        parts = []
        for values, pad in zip(fields, pads):
            for m in range(self.pairs):
                pad[m] = values[2 * m] + values[2 * m + 1]
                parts.append(pad[m, pl.ds(0, self.nx, 2), :] + pad[m, pl.ds(1, self.nx, 2), :])
        sums = selector_dot(parts, self.selector())
        mask = self.diagonal()
        out = []
        for i in range(len(fields)):
            planes = []
            for z in range(self.nz):
                s, m = divmod(z, self.pairs)
                block = sums[i * self.pairs + m][:, s * LANES : (s + 1) * LANES]
                row = jnp.sum(jnp.where(mask, block, 0.0), axis=0, keepdims=True)
                planes.append(jnp.broadcast_to(row, (8, LANES)))
            out.append(planes)
        return out

    def prolong(self, planes, pad):
        mask = self.diagonal()
        parts = []
        for m in range(self.pairs):
            blocks = [
                jnp.where(mask, planes[s * self.pairs + m], 0.0) for s in range(self.finer.groups)
            ]
            parts.append(jnp.concatenate(blocks, axis=1))
        out = []
        for m, wide in enumerate(selector_dot(parts, self.selector(spread=True))):
            pad[m, pl.ds(0, self.nx, 2), :] = wide
            pad[m, pl.ds(1, self.nx, 2), :] = wide
            out += [pad[m], pad[m]]
        return out

    def system(self, right, perm, level):
        lane = iota((8, LANES), 1)
        x, y = lane >> (self.ny.bit_length() - 1), lane & (self.ny - 1)
        keys = ((-1, 0, 0), (1, 0, 0), (0, -1, 0), (0, 1, 0), (0, 0, -1), (0, 0, 1))
        terms = {key: [None] * self.nz for key in keys}
        const = []
        faces = [harmonic(perm[z], perm[z + 1]) * ZSCALE for z in range(self.nz - 1)]
        for z in range(self.nz):
            centre = perm[z]
            west = jnp.where(x == 0, 0.0, harmonic(centre, roll(centre, self.ny, 1)))
            east = roll(west, -self.ny, 1)
            south = jnp.where(y == 0, 0.0, harmonic(centre, roll(centre, 1, 1)))
            north = roll(south, -1, 1)
            below = faces[z - 1] if z else None
            above = faces[z] if z + 1 < self.nz else None
            parts = [west, east, south, north, below, above]
            for end in (x == 0, x == self.nx - 1, y == 0, y == self.ny - 1):
                parts.append(jnp.where(end, centre, 0.0))
            inverse = OMEGA * inverse_of(tree_sum([part for part in parts if part is not None]))
            for key, part in zip(keys, parts):
                if part is not None:
                    terms[key][z] = inverse * part
            const.append(inverse * right[z] * (4.0**-level))
        terms[0, 0, 0] = [jnp.full((8, LANES), KEEP, F32)] * self.nz
        return terms, const

    def shifted(self, planes, key):
        dx, dy, dz = key
        out = []
        for z in range(self.nz):
            plane = planes[z + dz] if 0 <= z + dz < self.nz else None
            moved = dx * self.ny + dy
            out.append(roll(plane, -moved, 1) if plane is not None and moved else plane)
        return out

    def product(self, first, second):
        sums = {}
        for key, coefs in first.items():
            for other, others in second.items():
                moved = self.shifted(others, key)
                total = tuple(a + b for a, b in zip(key, other))
                for z in range(self.nz):
                    if coefs[z] is not None and moved[z] is not None:
                        sums.setdefault(total, [[] for _ in range(self.nz)])[z].append(coefs[z] * moved[z])
        return {
            key: [tree_sum(parts) if parts else None for parts in planes]
            for key, planes in sums.items()
        }

    def apply(self, terms, values, base):
        moved = {}
        parts = [[x] for x in base]
        for (dx, dy, dz), coefs in terms.items():
            if (dx, dy) not in moved:
                moved[dx, dy] = self.shifted(values, (dx, dy, 0))
            for z in range(self.nz):
                if coefs[z] is not None:
                    parts[z].append(coefs[z][...] * moved[dx, dy][z + dz])
        return tuple(tree_sum(x) for x in parts)

    def solve(self, right, perm, level, store):
        terms, const = self.system(right, perm, level)
        power, base, start = terms, const, const
        for _ in range(POWER - 1):
            base = self.apply(terms, base, const)
            power = self.product(terms, power)
        if COARSE_SWEEPS % POWER == 0:
            start = base
        slot = 0
        kept = {}
        for key in sorted(power):
            kept[key] = [None] * self.nz
            for z in range(self.nz):
                if power[key][z] is not None:
                    store[slot] = power[key][z]
                    kept[key][z] = store.at[slot]
                    slot += 1
        assert slot == store.shape[0]
        steps = (COARSE_SWEEPS - 1) // POWER
        assert steps * POWER + (POWER if COARSE_SWEEPS % POWER == 0 else 1) == COARSE_SWEEPS
        return lax.fori_loop(
            0, steps, lambda step, values: self.apply(kept, values, base), tuple(start)
        )

    def count(self):
        total = 0
        for z in range(self.nz):
            for other in range(self.nz):
                reach = POWER - abs(z - other)
                total += 2 * reach * (reach + 1) + 1 if reach >= 0 else 0
        return total


def tree_sum(parts):
    while len(parts) > 1:
        odd = parts[len(parts) // 2 * 2 :]
        parts = [a + b for a, b in zip(parts[::2], parts[1::2])] + odd
    return parts[0]


def packed_cycle(grid, right, perm, level, pads, store):
    pad_right, pad_perm = pads[0]
    coefs, const, diagonals = grid.system(right, perm, level)
    values = grid.sweep(const, coefs, const)
    scaled = grid.apply(values, coefs, [c - OMEGA * v for c, v in zip(const, values)])
    residue = [r * d for r, d in zip(scaled, diagonals)]
    coarse = grid if len(pads) > 1 else Flat(grid)
    coarse_right, coarse_perm = coarse.restrict((residue, perm), (pad_right, pad_perm))
    coarse_perm = [x * 0.125 for x in coarse_perm]
    if len(pads) > 1:
        update = packed_cycle(grid.coarser(), coarse_right, coarse_perm, level + 1, pads[1:], store)
    else:
        update = coarse.solve(coarse_right, coarse_perm, level + 1, store)
    values = [v + e for v, e in zip(values, coarse.prolong(update, pad_right))]
    for _ in range(2):
        values = grid.sweep(values, coefs, const)
    return values


def coarse_kernel(
    dom_ref, gathered, coef, const, before, out,
    level, first, pad_right1, pad_perm1, pad_right2, pad_perm2, update, store,
):
    height = out.shape[0]
    dom = dom_ref[0]
    domains, own, nx, _ = gathered.shape
    ny = LANES // 2
    grid = Packed(domains * own, nx, ny)
    left = iota((nx, LANES), 1) < ny
    right, perm = [], []
    for p in range(grid.planes):
        a = gathered[p // own, p % own]
        q = grid.planes + p
        b = gathered[q // own, q % own]
        right.append(jnp.where(left, a, roll(b, ny, 1)))
        perm.append(jnp.where(left, roll(a, ny, 1), b))
    pads = [(pad_right1, pad_perm1), (pad_right2, pad_perm2)]
    solved = packed_cycle(grid, right, perm, 1, pads, store)
    for p in range(grid.planes):
        update[p] = solved[p]
    planes, group = [], []
    for j in range(own + 2):
        layer = jnp.clip(dom * own + j - 1, 0, grid.nz - 1)
        group.append(layer // grid.planes)
        planes.append(update[lax.rem(layer, grid.planes)])
    for j, wide in enumerate(selector_dot(planes, lane_selector(1, LANES, 2, spread=True))):
        plane = jnp.where(group[j] == 0, wide[:, :LANES], wide[:, LANES:])
        pad = first.at[0]
        pad[pl.ds(0, nx, 2), :] = plane
        pad[pl.ds(1, nx, 2), :] = plane
        whole = first[0]
        level[2 * j] = before[2 * j] + whole
        level[2 * j + 1] = before[2 * j + 1] + whole

    def sweep(source, at, i):
        centre = source[i + 1]
        near = [coef[k, at + i] for k in range(6)]
        return stencil(centre, source[i], source[i + 2], near, KEEP * centre + const[at + i])

    def one(i):
        first[i] = sweep(level, 2, i)

    for i in range(height + 2):
        one(i)

    def two(i):
        out[i] = sweep(first, 3, i)

    for i in range(height):
        two(i)


def fine_part(dom, perm, source, layers):
    height, nx, ny = perm[0].shape
    field = lambda *lead: pltpu.VMEM(lead + (nx, ny), F32)
    vmem = pl.BlockSpec(memory_space=pltpu.VMEM)
    smem = pl.BlockSpec(memory_space=pltpu.SMEM)
    return pl.pallas_call(
        functools.partial(fine_kernel, layers),
        out_shape=(
            jax.ShapeDtypeStruct((6, height + 6, nx, ny), F32),
            jax.ShapeDtypeStruct((height + 6, nx, ny), F32),
            jax.ShapeDtypeStruct((height + 4, nx, ny), F32),
            jax.ShapeDtypeStruct((height // 2, nx // 2, ny), F32),
        ),
        in_specs=[smem] + [vmem] * 6,
        out_specs=(vmem,) * 4,
        scratch_shapes=[
            field(3 * height),
            field(3 * height),
            field(height + 6),
            field(height // 2),
            field(height // 2),
        ],
        compiler_params=pltpu.CompilerParams(vmem_limit_bytes=VMEM_LIMIT),
        name="fine",
    )(dom, *perm, *source)


def coarse_part(dom, gathered, coefs, const, values, height):
    _, nx, ny = values.shape
    field = lambda *shape: pltpu.VMEM(shape, F32)
    grid1 = Packed(gathered.shape[0] * gathered.shape[1], nx // 2, ny // 2)
    grid2 = grid1.coarser()
    pads1 = field(grid1.planes // 2, grid1.nx, LANES)
    pads2 = field(grid2.planes // 2, grid2.nx, LANES)
    vmem = pl.BlockSpec(memory_space=pltpu.VMEM)
    smem = pl.BlockSpec(memory_space=pltpu.SMEM)
    return pl.pallas_call(
        coarse_kernel,
        out_shape=jax.ShapeDtypeStruct((height, nx, ny), F32),
        in_specs=[smem] + [vmem] * 4,
        out_specs=vmem,
        scratch_shapes=[
            field(*values.shape),
            field(height + 2, nx, ny),
            pads1, pads1, pads2, pads2,
            field(grid1.planes, grid1.nx, LANES),
            field(Flat(grid2).count(), 8, LANES),
        ],
        compiler_params=pltpu.CompilerParams(vmem_limit_bytes=VMEM_LIMIT),
        name="coarse",
    )(dom, gathered, coefs, const, values)


def swaps(x, axis, step):
    return lax.ppermute(x, axis, [(i, i ^ step) for i in range(lax.axis_size(axis))])


def other_side(x):
    props, domains = lax.axis_size("prop"), lax.axis_size("dom")
    pairs = []
    for p in range(props):
        for d in range(domains):
            end = d in (0, domains - 1)
            partner = ((p ^ 1) * domains + d) if end else (p * domains + ((d + 1) ^ 1) - 1)
            pairs.append((p * domains + d, partner))
    return lax.ppermute(x, ("prop", "dom"), pairs)


def source_side(x):
    props, domains = lax.axis_size("prop"), lax.axis_size("dom")
    pairs = []
    for p in range(props):
        for d in range(domains):
            if p % 2 == 0:
                partner = p * domains + (d ^ 1)
            elif d in (0, domains - 1):
                partner = (p ^ 2) * domains + d
            else:
                partner = p * domains + ((d + 1) ^ 1) - 1
            pairs.append((p * domains + d, partner))
    return lax.ppermute(x, ("prop", "dom"), pairs)


def from_accepted(mine, accepted, beside):
    props = lax.axis_size("prop")
    step = props // 2
    own = SHRINK * mine
    offers, order = [mine], [0]
    while step:
        came = [swaps(x, "prop", step) for x in offers]
        if step == props // 2:
            came, own, beside = lax.optimization_barrier((came, own, beside))
        offers, order = offers + came, order + [x ^ step for x in order]
        step //= 2
    wanted = lax.axis_index("prop") ^ accepted
    current = offers[1]
    for at, offer in zip(order[2:], offers[2:]):
        current = jnp.where(wanted == at, offer, current)
    return jnp.where(wanted == 0, own, SHRINK * current), beside


def gather_parts(mine):
    domains = lax.axis_size("dom")
    copies = jnp.broadcast_to(mine[None], (domains,) + mine.shape)
    return lax.all_to_all(copies, "dom", 0, 0)


def body(states, accepted, noise, source):
    domains = lax.axis_size("dom")
    height = source.shape[0]
    dom = jnp.stack([lax.axis_index("dom"), lax.axis_index("prop")]).astype(jnp.int32)
    near = source_side(source)
    beside = (OMEGA * source, BETA * noise[0])
    current, (scaled, noise_part) = from_accepted(states[0], accepted[0], beside)
    perm = jnp.exp(current + noise_part)
    perms = (perm, swaps(perm, "dom", 1), other_side(perm))
    sources = (scaled, near, swaps(near, "prop", 1))
    *level, coarse = fine_part(dom, perms, sources, domains * height)
    return coarse_part(dom, gather_parts(coarse), *level, height)[None]


def solution(mesh):
    in_specs = (
        P("prop", "dom", None, None),
        P(),
        P("prop", "dom", None, None),
        P("dom", None, None),
    )
    out_specs = P("prop", "dom", None, None)
    return jax.shard_map(body, mesh=mesh, in_specs=in_specs, out_specs=out_specs, check_vma=False)
```

```python
import functools
import math

import jax
import jax.numpy as jnp
from jax import lax
from jax.experimental import pallas as pl
from jax.experimental.pallas import tpu as pltpu
from jax.sharding import PartitionSpec as P

COARSE_SWEEPS = 64
POWER = 2
OMEGA = 0.7
KEEP = 1.0 - OMEGA
BETA = 0.4
SHRINK = math.sqrt(1.0 - BETA * BETA)
ZSCALE = 16.0
LANES = 128
VMEM_LIMIT = 40 * 1024 * 1024
F32 = jnp.float32
WEST, EAST, SOUTH, NORTH, BELOW, ABOVE, CONST = range(7)


def iota(shape, dim):
    return lax.broadcasted_iota(jnp.int32, shape, dim)


def roll(x, amount, axis):
    axis = axis % x.ndim
    return pltpu.roll(x, amount % x.shape[axis], axis)


def inverse_of(x):
    guess = pl.reciprocal(x, approx=True)
    return guess * (2.0 - x * guess)


def harmonic(a, b):
    return (2.0 * a) * b * inverse_of(a + b)


def selector_dot(parts, selector):
    x = jnp.concatenate(parts, axis=0) if len(parts) > 1 else parts[0]
    rows = x.shape[0]
    high = x.astype(jnp.bfloat16).astype(F32)
    rest = x - high
    middle = rest.astype(jnp.bfloat16).astype(F32)
    terms = jnp.concatenate([high, middle, rest - middle], axis=0).astype(jnp.bfloat16)
    y = jnp.dot(terms, selector, preferred_element_type=F32)
    total = y[:rows] + y[rows : 2 * rows] + y[2 * rows :]
    height = parts[0].shape[0]
    return [total[i * height : (i + 1) * height] for i in range(len(parts))]


def face_terms(perm, lower, upper, below_scale, above_scale, ny):
    shape = perm.shape
    rows = iota(shape, 0)
    columns = iota(shape, 1) & (ny - 1)
    west = jnp.where(rows == 0, 0.0, harmonic(perm, roll(perm, 1, 0)))
    east = roll(west, -1, 0)
    south = jnp.where(columns == 0, 0.0, harmonic(perm, roll(perm, 1, 1)))
    north = roll(south, -1, 1)
    below = below_scale * harmonic(perm, lower)
    above = above_scale * harmonic(perm, upper)
    ends = jnp.where(rows == 0, perm, 0.0) + jnp.where(rows == shape[0] - 1, perm, 0.0)
    ends = ends + jnp.where(columns == 0, perm, 0.0) + jnp.where(columns == ny - 1, perm, 0.0)
    diagonal = ((west + east) + (south + north)) + ((below + above) + ends)
    return (west, east, south, north, below, above), diagonal


def stencil(values, lower, upper, coefs, base):
    x = coefs[0] * roll(values, 1, 0) + coefs[1] * roll(values, -1, 0)
    y = coefs[2] * roll(values, 1, 1) + coefs[3] * roll(values, -1, 1)
    z = coefs[4] * lower + coefs[5] * upper
    return (x + y) + (z + base)


def lane_selector(groups, ny, step, spread=False):
    shape = (LANES, step * LANES) if spread else (step * LANES, LANES)
    source, target = iota(shape, int(spread)), iota(shape, 1 - int(spread))
    bits = ny.bit_length() - 1
    lane = source & (LANES - 1)
    group = (lane >> bits) * step + (source >> 7)
    wanted = (group << (bits - 1)) + ((lane & (ny - 1)) >> 1)
    return jnp.where((target == wanted) & (lane < groups * ny), 1.0, 0.0).astype(jnp.bfloat16)


def fine_kernel(
    layers,
    dom_ref,
    per, per_pair, per_other,
    src, src_near, src_next,
    coef, const, values, coarse_out,
    perm, right, diag, pair,
):
    height = per.shape[0]
    dom = dom_ref[0]
    pair_at = jnp.where(lax.rem(dom, 2) == 0, 2 * height, 0)
    other_at = 2 * height - pair_at

    near_at = jnp.where(lax.rem(dom_ref[1], 2) == 0, pair_at, other_at)
    next_at = 2 * height - near_at
    for i in range(height):
        for at, p in ((height, per), (pair_at, per_pair), (other_at, per_other)):
            perm[at + i] = p[i]
        right[height + i] = src[i]
        right[near_at + i] = OMEGA * src_near[i]
        right[next_at + i] = OMEGA * src_next[i]

    def build(i):
        z = dom * height + i - 3
        below = jnp.where((z > 0) & (z < layers), ZSCALE, 0.0)
        above = jnp.where((z + 1 > 0) & (z + 1 < layers), ZSCALE, 0.0)
        at = height - 3 + i
        faces, diagonal = face_terms(perm[at], perm[at - 1], perm[at + 1], below, above, LANES)
        inverse = inverse_of(diagonal)
        const[i] = inverse * right[at]
        inverse = OMEGA * inverse
        for k in range(6):
            coef[k, i] = inverse * faces[k]
        diag[i] = diagonal

    for i in range(height + 6):
        build(i)

    def first(i):
        start = const[i + 1]
        near = [coef[k, i + 1] for k in range(6)]
        values[i] = stencil(start, const[i], const[i + 2], near, (1.0 + KEEP) * start)

    for i in range(height + 4):
        first(i)

    def residue(i):
        centre = values[i + 2]
        base = const[i + 3] - OMEGA * centre
        near = [coef[k, i + 3] for k in range(6)]
        scaled = stencil(centre, values[i + 1], values[i + 3], near, base)
        return scaled * (diag[i + 3] * (1.0 / OMEGA))

    for m in range(height // 2):
        pair[m] = residue(2 * m) + residue(2 * m + 1)
    coarse_out[...] = halved(pair)


def mean_kernel(perm, out, pair):
    for m in range(perm.shape[0] // 2):
        pair[m] = (perm[2 * m] + perm[2 * m + 1]) * 0.125
    out[...] = halved(pair)


def halved(pair):
    count, rows, _ = pair.shape
    half = rows // 2
    sums = [pair[m, pl.ds(0, half, 2), :] + pair[m, pl.ds(1, half, 2), :] for m in range(count)]
    return selector_dot([jnp.concatenate(sums, axis=1)], lane_selector(1, LANES, count))[0]


class Packed:
    def __init__(self, nz, nx, ny):
        self.nz, self.nx, self.ny = nz, nx, ny
        self.groups = min(LANES // ny, nz)
        self.planes = nz // self.groups

    def lower(self, planes, p):
        return planes[p - 1] if p else roll(planes[self.planes - 1], self.ny, 1)

    def upper(self, planes, p):
        return planes[p + 1] if p + 1 < self.planes else roll(planes[0], -self.ny, 1)

    def system(self, right, perm, level):
        lane = iota((self.nx, LANES), 1)
        used = lane < self.groups * self.ny
        if self.groups * self.ny < LANES:
            perm = [jnp.where(used, x, 1.0) for x in perm]
        coefs, const, diagonals = [], [], []
        for p in range(self.planes):
            below, above = ZSCALE, ZSCALE
            if p == 0:
                below = jnp.where(lane < self.ny, 0.0, ZSCALE)
            if p + 1 == self.planes:
                above = jnp.where(lane < (self.groups - 1) * self.ny, ZSCALE, 0.0)
            faces, diagonal = face_terms(
                perm[p], self.lower(perm, p), self.upper(perm, p), below, above, self.ny
            )
            inverse = OMEGA * inverse_of(diagonal)
            coefs.append([inverse * face for face in faces])
            const.append(inverse * right[p] * (4.0**-level))
            diagonals.append(diagonal * (4.0**level / OMEGA))
        return coefs, const, diagonals

    def apply(self, values, coefs, bases):
        return [
            stencil(values[p], self.lower(values, p), self.upper(values, p), coefs[p], bases[p])
            for p in range(self.planes)
        ]

    def sweep(self, values, coefs, const):
        return self.apply(values, coefs, [KEEP * v + c for v, c in zip(values, const)])

    def coarser(self):
        return Packed(self.nz // 2, self.nx // 2, self.ny // 2)

    def restrict(self, fields, pads):
        coarse = self.coarser()
        step = coarse.groups // self.groups
        half = coarse.nx
        parts = []
        for values, pad in zip(fields, pads):
            rows = []
            for m in range(self.planes // 2):
                pad[m] = values[2 * m] + values[2 * m + 1]
                rows.append(pad[m, pl.ds(0, half, 2), :] + pad[m, pl.ds(1, half, 2), :])
            for p in range(coarse.planes):
                blocks = rows[p :: coarse.planes]
                parts.append(jnp.concatenate(blocks, axis=1) if step > 1 else blocks[0])
        sums = selector_dot(parts, lane_selector(self.groups, self.ny, step))
        return [sums[i : i + coarse.planes] for i in range(0, len(sums), coarse.planes)]

    def prolong(self, values, pad):
        coarse = self.coarser()
        step = coarse.groups // self.groups
        half = coarse.nx
        wide = selector_dot(values, lane_selector(self.groups, self.ny, step, spread=True))
        out = []
        for m in range(self.planes // 2):
            j, p = divmod(m, coarse.planes)
            plane = wide[p][:, j * LANES : (j + 1) * LANES]
            pad[m, pl.ds(0, half, 2), :] = plane
            pad[m, pl.ds(1, half, 2), :] = plane
            out += [pad[m], pad[m]]
        return out


class Flat:
    def __init__(self, finer):
        coarse = finer.coarser()
        self.finer = finer
        self.nz, self.nx, self.ny = coarse.nz, coarse.nx, coarse.ny
        self.pairs = finer.planes // 2

    def selector(self, spread=False):
        wide = self.finer.groups * LANES
        shape = (wide, LANES) if spread else (LANES, wide)
        fine, flat = iota(shape, int(spread)), iota(shape, 1 - int(spread))
        bits = self.finer.ny.bit_length() - 1
        same = (fine >> bits) == (flat >> 7)
        same &= ((fine & (self.finer.ny - 1)) >> 1) == (flat & (self.ny - 1))
        return jnp.where(same, 1.0, 0.0).astype(jnp.bfloat16)

    def diagonal(self):
        shape = (self.nx, LANES)
        return iota(shape, 0) == (iota(shape, 1) >> (self.ny.bit_length() - 1))

    def restrict(self, fields, pads):
        parts = []
        for values, pad in zip(fields, pads):
            for m in range(self.pairs):
                pad[m] = values[2 * m] + values[2 * m + 1]
                parts.append(pad[m, pl.ds(0, self.nx, 2), :] + pad[m, pl.ds(1, self.nx, 2), :])
        sums = selector_dot(parts, self.selector())
        mask = self.diagonal()
        out = []
        for i in range(len(fields)):
            planes = []
            for z in range(self.nz):
                s, m = divmod(z, self.pairs)
                block = sums[i * self.pairs + m][:, s * LANES : (s + 1) * LANES]
                row = jnp.sum(jnp.where(mask, block, 0.0), axis=0, keepdims=True)
                planes.append(jnp.broadcast_to(row, (8, LANES)))
            out.append(planes)
        return out

    def prolong(self, planes, pad):
        mask = self.diagonal()
        parts = []
        for m in range(self.pairs):
            blocks = [
                jnp.where(mask, planes[s * self.pairs + m], 0.0) for s in range(self.finer.groups)
            ]
            parts.append(jnp.concatenate(blocks, axis=1))
        out = []
        for m, wide in enumerate(selector_dot(parts, self.selector(spread=True))):
            pad[m, pl.ds(0, self.nx, 2), :] = wide
            pad[m, pl.ds(1, self.nx, 2), :] = wide
            out += [pad[m], pad[m]]
        return out

    def system(self, right, perm, level):
        lane = iota((8, LANES), 1)
        x, y = lane >> (self.ny.bit_length() - 1), lane & (self.ny - 1)
        keys = ((-1, 0, 0), (1, 0, 0), (0, -1, 0), (0, 1, 0), (0, 0, -1), (0, 0, 1))
        terms = {key: [None] * self.nz for key in keys}
        const = []
        faces = [harmonic(perm[z], perm[z + 1]) * ZSCALE for z in range(self.nz - 1)]
        for z in range(self.nz):
            centre = perm[z]
            west = jnp.where(x == 0, 0.0, harmonic(centre, roll(centre, self.ny, 1)))
            east = roll(west, -self.ny, 1)
            south = jnp.where(y == 0, 0.0, harmonic(centre, roll(centre, 1, 1)))
            north = roll(south, -1, 1)
            below = faces[z - 1] if z else None
            above = faces[z] if z + 1 < self.nz else None
            parts = [west, east, south, north, below, above]
            for end in (x == 0, x == self.nx - 1, y == 0, y == self.ny - 1):
                parts.append(jnp.where(end, centre, 0.0))
            inverse = OMEGA * inverse_of(tree_sum([part for part in parts if part is not None]))
            for key, part in zip(keys, parts):
                if part is not None:
                    terms[key][z] = inverse * part
            const.append(inverse * right[z] * (4.0**-level))
        terms[0, 0, 0] = [jnp.full((8, LANES), KEEP, F32)] * self.nz
        return terms, const

    def shifted(self, planes, key):
        dx, dy, dz = key
        out = []
        for z in range(self.nz):
            plane = planes[z + dz] if 0 <= z + dz < self.nz else None
            moved = dx * self.ny + dy
            out.append(roll(plane, -moved, 1) if plane is not None and moved else plane)
        return out

    def product(self, first, second):
        sums = {}
        for key, coefs in first.items():
            for other, others in second.items():
                moved = self.shifted(others, key)
                total = tuple(a + b for a, b in zip(key, other))
                for z in range(self.nz):
                    if coefs[z] is not None and moved[z] is not None:
                        sums.setdefault(total, [[] for _ in range(self.nz)])[z].append(coefs[z] * moved[z])
        return {
            key: [tree_sum(parts) if parts else None for parts in planes]
            for key, planes in sums.items()
        }

    def apply(self, terms, values, base):
        moved = {}
        parts = [[x] for x in base]
        for (dx, dy, dz), coefs in terms.items():
            if (dx, dy) not in moved:
                moved[dx, dy] = self.shifted(values, (dx, dy, 0))
            for z in range(self.nz):
                if coefs[z] is not None:
                    parts[z].append(coefs[z][...] * moved[dx, dy][z + dz])
        return tuple(tree_sum(x) for x in parts)

    def solve(self, right, perm, level, store):
        terms, const = self.system(right, perm, level)
        power, base, start = terms, const, const
        for _ in range(POWER - 1):
            base = self.apply(terms, base, const)
            power = self.product(terms, power)
        if COARSE_SWEEPS % POWER == 0:
            start = base
        slot = 0
        kept = {}
        for key in sorted(power):
            kept[key] = [None] * self.nz
            for z in range(self.nz):
                if power[key][z] is not None:
                    store[slot] = power[key][z]
                    kept[key][z] = store.at[slot]
                    slot += 1
        assert slot == store.shape[0]
        steps = (COARSE_SWEEPS - 1) // POWER
        assert steps * POWER + (POWER if COARSE_SWEEPS % POWER == 0 else 1) == COARSE_SWEEPS
        return lax.fori_loop(
            0, steps, lambda step, values: self.apply(kept, values, base), tuple(start)
        )

    def count(self):
        total = 0
        for z in range(self.nz):
            for other in range(self.nz):
                reach = POWER - abs(z - other)
                total += 2 * reach * (reach + 1) + 1 if reach >= 0 else 0
        return total


def tree_sum(parts):
    while len(parts) > 1:
        odd = parts[len(parts) // 2 * 2 :]
        parts = [a + b for a, b in zip(parts[::2], parts[1::2])] + odd
    return parts[0]


def packed_cycle(grid, right, perm, level, pads, store):
    pad_right, pad_perm = pads[0]
    coefs, const, diagonals = grid.system(right, perm, level)
    values = grid.sweep(const, coefs, const)
    scaled = grid.apply(values, coefs, [c - OMEGA * v for c, v in zip(const, values)])
    residue = [r * d for r, d in zip(scaled, diagonals)]
    coarse = grid if len(pads) > 1 else Flat(grid)
    coarse_right, coarse_perm = coarse.restrict((residue, perm), (pad_right, pad_perm))
    coarse_perm = [x * 0.125 for x in coarse_perm]
    if len(pads) > 1:
        update = packed_cycle(grid.coarser(), coarse_right, coarse_perm, level + 1, pads[1:], store)
    else:
        update = coarse.solve(coarse_right, coarse_perm, level + 1, store)
    values = [v + e for v, e in zip(values, coarse.prolong(update, pad_right))]
    for _ in range(2):
        values = grid.sweep(values, coefs, const)
    return values


def coarse_kernel(
    dom_ref, rights, perms, coef, const, before, out,
    level, first, pad_right1, pad_perm1, pad_right2, pad_perm2, update, store,
):
    height = out.shape[0]
    dom = dom_ref[0]
    domains, nx, _ = rights.shape
    ny = LANES // 2
    own = 2
    grid = Packed(domains * own, nx, ny)
    left = iota((nx, LANES), 1) < ny

    def unpacked(parts):
        planes = []
        for p in range(grid.planes):
            low, high = parts[p // own], parts[(grid.planes + p) // own]
            if p % own:
                low = roll(low, ny, 1)
            else:
                high = roll(high, ny, 1)
            planes.append(jnp.where(left, low, high))
        return planes

    right, perm = unpacked(rights), unpacked(perms)
    pads = [(pad_right1, pad_perm1), (pad_right2, pad_perm2)]
    solved = packed_cycle(grid, right, perm, 1, pads, store)
    for p in range(grid.planes):
        update[p] = solved[p]
    planes, group = [], []
    for j in range(own + 2):
        layer = jnp.clip(dom * own + j - 1, 0, grid.nz - 1)
        group.append(layer // grid.planes)
        planes.append(update[lax.rem(layer, grid.planes)])
    for j, wide in enumerate(selector_dot(planes, lane_selector(1, LANES, 2, spread=True))):
        plane = jnp.where(group[j] == 0, wide[:, :LANES], wide[:, LANES:])
        pad = first.at[0]
        pad[pl.ds(0, nx, 2), :] = plane
        pad[pl.ds(1, nx, 2), :] = plane
        whole = first[0]
        level[2 * j] = before[2 * j] + whole
        level[2 * j + 1] = before[2 * j + 1] + whole

    def sweep(source, at, i):
        centre = source[i + 1]
        near = [coef[k, at + i] for k in range(6)]
        return stencil(centre, source[i], source[i + 2], near, KEEP * centre + const[at + i])

    def one(i):
        first[i] = sweep(level, 2, i)

    for i in range(height + 2):
        one(i)

    def two(i):
        out[i] = sweep(first, 3, i)

    for i in range(height):
        two(i)


def fine_part(dom, perm, source, layers):
    height, nx, ny = perm[0].shape
    field = lambda *lead: pltpu.VMEM(lead + (nx, ny), F32)
    vmem = pl.BlockSpec(memory_space=pltpu.VMEM)
    smem = pl.BlockSpec(memory_space=pltpu.SMEM)
    return pl.pallas_call(
        functools.partial(fine_kernel, layers),
        out_shape=(
            jax.ShapeDtypeStruct((6, height + 6, nx, ny), F32),
            jax.ShapeDtypeStruct((height + 6, nx, ny), F32),
            jax.ShapeDtypeStruct((height + 4, nx, ny), F32),
            jax.ShapeDtypeStruct((nx // 2, ny), F32),
        ),
        in_specs=[smem] + [vmem] * 6,
        out_specs=(vmem,) * 4,
        scratch_shapes=[
            field(3 * height),
            field(3 * height),
            field(height + 6),
            field(height // 2),
        ],
        compiler_params=pltpu.CompilerParams(vmem_limit_bytes=VMEM_LIMIT),
        name="fine",
    )(dom, *perm, *source)


def mean_part(perm):
    height, nx, ny = perm.shape
    vmem = pl.BlockSpec(memory_space=pltpu.VMEM)
    return pl.pallas_call(
        mean_kernel,
        out_shape=jax.ShapeDtypeStruct((nx // 2, ny), F32),
        in_specs=[vmem],
        out_specs=vmem,
        scratch_shapes=[pltpu.VMEM((height // 2, nx, ny), F32)],
        compiler_params=pltpu.CompilerParams(vmem_limit_bytes=VMEM_LIMIT),
        name="mean",
    )(perm)


def coarse_part(dom, rights, perms, coefs, const, values, height):
    _, nx, ny = values.shape
    field = lambda *shape: pltpu.VMEM(shape, F32)
    grid1 = Packed(rights.shape[0] * 2, nx // 2, ny // 2)
    grid2 = grid1.coarser()
    pads1 = field(grid1.planes // 2, grid1.nx, LANES)
    pads2 = field(grid2.planes // 2, grid2.nx, LANES)
    vmem = pl.BlockSpec(memory_space=pltpu.VMEM)
    smem = pl.BlockSpec(memory_space=pltpu.SMEM)
    return pl.pallas_call(
        coarse_kernel,
        out_shape=jax.ShapeDtypeStruct((height, nx, ny), F32),
        in_specs=[smem] + [vmem] * 5,
        out_specs=vmem,
        scratch_shapes=[
            field(*values.shape),
            field(height + 2, nx, ny),
            pads1, pads1, pads2, pads2,
            field(grid1.planes, grid1.nx, LANES),
            field(Flat(grid2).count(), 8, LANES),
        ],
        compiler_params=pltpu.CompilerParams(vmem_limit_bytes=VMEM_LIMIT),
        name="coarse",
    )(dom, rights, perms, coefs, const, values)


def swaps(x, axis, step):
    return lax.ppermute(x, axis, [(i, i ^ step) for i in range(lax.axis_size(axis))])


def other_side(x):
    props, domains = lax.axis_size("prop"), lax.axis_size("dom")
    pairs = []
    for p in range(props):
        for d in range(domains):
            end = d in (0, domains - 1)
            partner = ((p ^ 1) * domains + d) if end else (p * domains + ((d + 1) ^ 1) - 1)
            pairs.append((p * domains + d, partner))
    return lax.ppermute(x, ("prop", "dom"), pairs)


def source_side(x):
    props, domains = lax.axis_size("prop"), lax.axis_size("dom")
    pairs = []
    for p in range(props):
        for d in range(domains):
            if p % 2 == 0:
                partner = p * domains + (d ^ 1)
            elif d in (0, domains - 1):
                partner = (p ^ 2) * domains + d
            else:
                partner = p * domains + ((d + 1) ^ 1) - 1
            pairs.append((p * domains + d, partner))
    return lax.ppermute(x, ("prop", "dom"), pairs)


def from_accepted(mine, accepted, beside):
    props = lax.axis_size("prop")
    step = props // 2
    own = SHRINK * mine
    offers, order = [mine], [0]
    while step:
        came = [swaps(x, "prop", step) for x in offers]
        if step == props // 2:
            came, own, beside = lax.optimization_barrier((came, own, beside))
        offers, order = offers + came, order + [x ^ step for x in order]
        step //= 2
    wanted = lax.axis_index("prop") ^ accepted
    current = offers[1]
    for at, offer in zip(order[2:], offers[2:]):
        current = jnp.where(wanted == at, offer, current)
    return jnp.where(wanted == 0, own, SHRINK * current), beside


def gather_parts(mine):
    domains = lax.axis_size("dom")
    copies = jnp.broadcast_to(mine[None], (domains,) + mine.shape)
    return lax.all_to_all(copies, "dom", 0, 0)


def body(states, accepted, noise, source):
    domains = lax.axis_size("dom")
    height = source.shape[0]
    assert height == 4 and source.shape[2] == LANES
    dom = jnp.stack([lax.axis_index("dom"), lax.axis_index("prop")]).astype(jnp.int32)
    near = source_side(source)
    beside = (OMEGA * source, BETA * noise[0])
    current, (scaled, noise_part) = from_accepted(states[0], accepted[0], beside)
    perm = jnp.exp(current + noise_part)
    perms = (perm, swaps(perm, "dom", 1), other_side(perm))
    sources = (scaled, near, swaps(near, "prop", 1))
    coarse_perms = lax.all_gather(mean_part(perm), "dom")
    *level, coarse = fine_part(dom, perms, sources, domains * height)
    return coarse_part(dom, gather_parts(coarse), coarse_perms, *level, height)[None]


def solution(mesh):
    in_specs = (
        P("prop", "dom", None, None),
        P(),
        P("prop", "dom", None, None),
        P("dom", None, None),
    )
    out_specs = P("prop", "dom", None, None)
    return jax.shard_map(body, mesh=mesh, in_specs=in_specs, out_specs=out_specs, check_vma=False)
```

```python
import functools
import itertools
import math

import jax
import jax.numpy as jnp
from jax import lax
from jax.experimental import pallas as pl
from jax.experimental.pallas import tpu as pltpu
from jax.sharding import PartitionSpec as P

COARSE_SWEEPS = 64
POWER = 2
OMEGA = 0.7
KEEP = 1.0 - OMEGA
BETA = 0.4
SHRINK = math.sqrt(1.0 - BETA * BETA)
ZSCALE = 16.0
LANES = 128
VMEM_LIMIT = 40 * 1024 * 1024
F32 = jnp.float32
WEST, EAST, SOUTH, NORTH, BELOW, ABOVE, CONST = range(7)


def iota(shape, dim):
    return lax.broadcasted_iota(jnp.int32, shape, dim)


def roll(x, amount, axis):
    axis = axis % x.ndim
    return pltpu.roll(x, amount % x.shape[axis], axis)


def inverse_of(x):
    guess = pl.reciprocal(x, approx=True)
    return guess * (2.0 - x * guess)


def harmonic(a, b):
    return (2.0 * a) * b * inverse_of(a + b)


def selector_dot(parts, selector):
    x = jnp.concatenate(parts, axis=0) if len(parts) > 1 else parts[0]
    rows = x.shape[0]
    high = x.astype(jnp.bfloat16).astype(F32)
    rest = x - high
    middle = rest.astype(jnp.bfloat16).astype(F32)
    terms = jnp.concatenate([high, middle, rest - middle], axis=0).astype(jnp.bfloat16)
    y = jnp.dot(terms, selector, preferred_element_type=F32)
    total = y[:rows] + y[rows : 2 * rows] + y[2 * rows :]
    height = parts[0].shape[0]
    return [total[i * height : (i + 1) * height] for i in range(len(parts))]


def face_terms(perm, lower, upper, below_scale, above_scale, ny):
    shape = perm.shape
    rows = iota(shape, 0)
    columns = iota(shape, 1) & (ny - 1)
    west = jnp.where(rows == 0, 0.0, harmonic(perm, roll(perm, 1, 0)))
    east = roll(west, -1, 0)
    south = jnp.where(columns == 0, 0.0, harmonic(perm, roll(perm, 1, 1)))
    north = roll(south, -1, 1)
    below = below_scale * harmonic(perm, lower)
    above = above_scale * harmonic(perm, upper)
    ends = jnp.where(rows == 0, perm, 0.0) + jnp.where(rows == shape[0] - 1, perm, 0.0)
    ends = ends + jnp.where(columns == 0, perm, 0.0) + jnp.where(columns == ny - 1, perm, 0.0)
    diagonal = ((west + east) + (south + north)) + ((below + above) + ends)
    return (west, east, south, north, below, above), diagonal


def stencil(values, lower, upper, coefs, base):
    west, east, south, north, below, above = (c[...] for c in coefs)
    x = west * roll(values, 1, 0) + east * roll(values, -1, 0)
    y = south * roll(values, 1, 1) + north * roll(values, -1, 1)
    z = below * lower + above * upper
    return (x + y) + (z + base)


def lane_selector(groups, ny, step, spread=False):
    shape = (LANES, step * LANES) if spread else (step * LANES, LANES)
    source, target = iota(shape, int(spread)), iota(shape, 1 - int(spread))
    bits = ny.bit_length() - 1
    lane = source & (LANES - 1)
    group = (lane >> bits) * step + (source >> 7)
    wanted = (group << (bits - 1)) + ((lane & (ny - 1)) >> 1)
    return jnp.where((target == wanted) & (lane < groups * ny), 1.0, 0.0).astype(jnp.bfloat16)


def fine_kernel(
    layers,
    dom_ref,
    per, per_pair, per_other,
    src, src_near, src_next,
    coef, const, values, coarse_out,
    perm, right, diag, pair,
):
    height = per.shape[0]
    dom = dom_ref[0]
    pair_at = jnp.where(lax.rem(dom, 2) == 0, 2 * height, 0)
    other_at = 2 * height - pair_at

    near_at = jnp.where(lax.rem(dom_ref[1], 2) == 0, pair_at, other_at)
    next_at = 2 * height - near_at
    for i in range(height):
        for at, p in ((height, per), (pair_at, per_pair), (other_at, per_other)):
            perm[at + i] = p[i]
        right[height + i] = src[i]
        right[near_at + i] = OMEGA * src_near[i]
        right[next_at + i] = OMEGA * src_next[i]

    def build(i):
        z = dom * height + i - 3
        below = jnp.where((z > 0) & (z < layers), ZSCALE, 0.0)
        above = jnp.where((z + 1 > 0) & (z + 1 < layers), ZSCALE, 0.0)
        at = height - 3 + i
        faces, diagonal = face_terms(perm[at], perm[at - 1], perm[at + 1], below, above, LANES)
        inverse = inverse_of(diagonal)
        const[i] = inverse * right[at]
        inverse = OMEGA * inverse
        for k in range(6):
            coef[k, i] = inverse * faces[k]
        diag[i] = diagonal

    for i in range(height + 6):
        build(i)

    def first(i):
        start = const[i + 1]
        near = [coef.at[k, i + 1] for k in range(6)]
        values[i] = stencil(start, const[i], const[i + 2], near, (1.0 + KEEP) * start)

    for i in range(height + 4):
        first(i)

    def residue(i):
        centre = values[i + 2]
        base = const[i + 3] - OMEGA * centre
        near = [coef.at[k, i + 3] for k in range(6)]
        scaled = stencil(centre, values[i + 1], values[i + 3], near, base)
        return scaled * (diag[i + 3] * (1.0 / OMEGA))

    for m in range(height // 2):
        pair[m] = residue(2 * m) + residue(2 * m + 1)
    coarse_out[...] = halved(pair)


def mean_kernel(perm, out, pair):
    for m in range(perm.shape[0] // 2):
        pair[m] = (perm[2 * m] + perm[2 * m + 1]) * 0.125
    out[...] = halved(pair)


def halved(pair):
    count, rows, _ = pair.shape
    half = rows // 2
    sums = [pair[m, pl.ds(0, half, 2), :] + pair[m, pl.ds(1, half, 2), :] for m in range(count)]
    return selector_dot([jnp.concatenate(sums, axis=1)], lane_selector(1, LANES, count))[0]


class Packed:
    def __init__(self, nz, nx, ny):
        self.nz, self.nx, self.ny = nz, nx, ny
        self.groups = min(LANES // ny, nz)
        self.planes = nz // self.groups

    def lower(self, planes, p):
        return planes[p - 1] if p else roll(planes[self.planes - 1], self.ny, 1)

    def upper(self, planes, p):
        return planes[p + 1] if p + 1 < self.planes else roll(planes[0], -self.ny, 1)

    def system(self, perm, level, out):
        lane = iota((self.nx, LANES), 1)
        used = lane < self.groups * self.ny
        if self.groups * self.ny < LANES:
            perm = [jnp.where(used, x, 1.0) for x in perm]
        for p in range(self.planes):
            below, above = ZSCALE, ZSCALE
            if p == 0:
                below = jnp.where(lane < self.ny, 0.0, ZSCALE)
            if p + 1 == self.planes:
                above = jnp.where(lane < (self.groups - 1) * self.ny, ZSCALE, 0.0)
            faces, diagonal = face_terms(
                perm[p], self.lower(perm, p), self.upper(perm, p), below, above, self.ny
            )
            inverse = OMEGA * inverse_of(diagonal)
            for k, face in enumerate(faces):
                out[p, k] = inverse * face
            out[p, 6] = inverse * (4.0**-level)
            out[p, 7] = diagonal * (4.0**level / OMEGA)

    def apply(self, values, coefs, bases):
        return [
            stencil(
                values[p], self.lower(values, p), self.upper(values, p),
                [coefs.at[p, k] for k in range(6)], bases[p],
            )
            for p in range(self.planes)
        ]

    def sweep(self, values, coefs, const):
        return self.apply(values, coefs, [KEEP * v + c for v, c in zip(values, const)])

    def coarser(self):
        return Packed(self.nz // 2, self.nx // 2, self.ny // 2)

    def restrict(self, fields, pads):
        coarse = self.coarser()
        step = coarse.groups // self.groups
        half = coarse.nx
        parts = []
        for values, pad in zip(fields, pads):
            rows = []
            for m in range(self.planes // 2):
                pad[m] = values[2 * m] + values[2 * m + 1]
                rows.append(pad[m, pl.ds(0, half, 2), :] + pad[m, pl.ds(1, half, 2), :])
            for p in range(coarse.planes):
                blocks = rows[p :: coarse.planes]
                parts.append(jnp.concatenate(blocks, axis=1) if step > 1 else blocks[0])
        sums = selector_dot(parts, lane_selector(self.groups, self.ny, step))
        return [sums[i : i + coarse.planes] for i in range(0, len(sums), coarse.planes)]

    def prolong(self, values, pad):
        coarse = self.coarser()
        step = coarse.groups // self.groups
        half = coarse.nx
        wide = selector_dot(values, lane_selector(self.groups, self.ny, step, spread=True))
        out = []
        for m in range(self.planes // 2):
            j, p = divmod(m, coarse.planes)
            plane = wide[p][:, j * LANES : (j + 1) * LANES]
            pad[m, pl.ds(0, half, 2), :] = plane
            pad[m, pl.ds(1, half, 2), :] = plane
            out += [pad[m], pad[m]]
        return out


class Flat:
    def __init__(self, finer):
        coarse = finer.coarser()
        self.finer = finer
        self.nz, self.nx, self.ny = coarse.nz, coarse.nx, coarse.ny
        self.pairs = finer.planes // 2

    def selector(self, spread=False):
        wide = self.finer.groups * LANES
        shape = (wide, LANES) if spread else (LANES, wide)
        fine, flat = iota(shape, int(spread)), iota(shape, 1 - int(spread))
        bits = self.finer.ny.bit_length() - 1
        same = (fine >> bits) == (flat >> 7)
        same &= ((fine & (self.finer.ny - 1)) >> 1) == (flat & (self.ny - 1))
        return jnp.where(same, 1.0, 0.0).astype(jnp.bfloat16)

    def diagonal(self):
        shape = (self.nx, LANES)
        return iota(shape, 0) == (iota(shape, 1) >> (self.ny.bit_length() - 1))

    def restrict(self, fields, pads):
        parts = []
        for values, pad in zip(fields, pads):
            for m in range(self.pairs):
                pad[m] = values[2 * m] + values[2 * m + 1]
                parts.append(pad[m, pl.ds(0, self.nx, 2), :] + pad[m, pl.ds(1, self.nx, 2), :])
        sums = selector_dot(parts, self.selector())
        mask = self.diagonal()
        out = []
        for i in range(len(fields)):
            planes = []
            for z in range(self.nz):
                s, m = divmod(z, self.pairs)
                block = sums[i * self.pairs + m][:, s * LANES : (s + 1) * LANES]
                row = jnp.sum(jnp.where(mask, block, 0.0), axis=0, keepdims=True)
                planes.append(jnp.broadcast_to(row, (8, LANES)))
            out.append(planes)
        return out

    def prolong(self, planes, pad):
        mask = self.diagonal()
        parts = []
        for m in range(self.pairs):
            blocks = [
                jnp.where(mask, planes[s * self.pairs + m], 0.0) for s in range(self.finer.groups)
            ]
            parts.append(jnp.concatenate(blocks, axis=1))
        out = []
        for m, wide in enumerate(selector_dot(parts, self.selector(spread=True))):
            pad[m, pl.ds(0, self.nx, 2), :] = wide
            pad[m, pl.ds(1, self.nx, 2), :] = wide
            out += [pad[m], pad[m]]
        return out

    def system(self, perm, level):
        lane = iota((8, LANES), 1)
        x, y = lane >> (self.ny.bit_length() - 1), lane & (self.ny - 1)
        keys = ((-1, 0, 0), (1, 0, 0), (0, -1, 0), (0, 1, 0), (0, 0, -1), (0, 0, 1))
        terms = {key: [None] * self.nz for key in keys}
        factors = []
        faces = [harmonic(perm[z], perm[z + 1]) * ZSCALE for z in range(self.nz - 1)]
        for z in range(self.nz):
            centre = perm[z]
            west = jnp.where(x == 0, 0.0, harmonic(centre, roll(centre, self.ny, 1)))
            east = roll(west, -self.ny, 1)
            south = jnp.where(y == 0, 0.0, harmonic(centre, roll(centre, 1, 1)))
            north = roll(south, -1, 1)
            below = faces[z - 1] if z else None
            above = faces[z] if z + 1 < self.nz else None
            parts = [west, east, south, north, below, above]
            for end in (x == 0, x == self.nx - 1, y == 0, y == self.ny - 1):
                parts.append(jnp.where(end, centre, 0.0))
            inverse = OMEGA * inverse_of(tree_sum([part for part in parts if part is not None]))
            for key, part in zip(keys, parts):
                if part is not None:
                    terms[key][z] = inverse * part
            factors.append(inverse * (4.0**-level))
        terms[0, 0, 0] = [jnp.full((8, LANES), KEEP, F32)] * self.nz
        return terms, factors

    def shifted(self, planes, key):
        dx, dy, dz = key
        out = []
        for z in range(self.nz):
            plane = planes[z + dz] if 0 <= z + dz < self.nz else None
            moved = dx * self.ny + dy
            out.append(roll(plane, -moved, 1) if plane is not None and moved else plane)
        return out

    def product(self, first, second):
        sums = {}
        for key, coefs in first.items():
            for other, others in second.items():
                moved = self.shifted(others, key)
                total = tuple(a + b for a, b in zip(key, other))
                for z in range(self.nz):
                    if coefs[z] is not None and moved[z] is not None:
                        sums.setdefault(total, [[] for _ in range(self.nz)])[z].append(coefs[z] * moved[z])
        return {
            key: [tree_sum(parts) if parts else None for parts in planes]
            for key, planes in sums.items()
        }

    def apply(self, terms, values, base):
        moved = {}
        parts = [[x] for x in base]
        for (dx, dy, dz), coefs in terms.items():
            if (dx, dy) not in moved:
                moved[dx, dy] = self.shifted(values, (dx, dy, 0))
            for z in range(self.nz):
                if coefs[z] is not None:
                    parts[z].append(coefs[z][...] * moved[dx, dy][z + dz])
        return tuple(tree_sum(x) for x in parts)

    def slots(self, power):
        reach = range(-power, power + 1)
        places, slot = {}, 0
        for key in itertools.product(reach, reach, reach):
            if sum(abs(x) for x in key) <= power:
                places[key] = [None] * self.nz
                for z in range(self.nz):
                    if 0 <= z + key[2] < self.nz:
                        places[key][z] = slot
                        slot += 1
        return places, slot

    def count(self, power):
        return self.slots(power)[1]

    def prepare(self, perm, level, sweep_out, power_out, factor_out):
        terms, factors = self.system(perm, level)
        power = terms
        for _ in range(POWER - 1):
            power = self.product(terms, power)
        for which, (operator, out) in enumerate(((terms, sweep_out), (power, power_out))):
            for key, places in self.slots(POWER if which else 1)[0].items():
                for z, slot in enumerate(places):
                    if slot is not None:
                        out[slot] = operator[key][z]
        for z in range(self.nz):
            factor_out[z] = factors[z]

    def stored(self, ref, power):
        return {
            key: [None if slot is None else ref.at[slot] for slot in places]
            for key, places in self.slots(power)[0].items()
        }

    def solve(self, right, sweep_ref, power_ref, factors):
        const = [factors[z] * right[z] for z in range(self.nz)]
        once, many = self.stored(sweep_ref, 1), self.stored(power_ref, POWER)
        base = const
        for _ in range(POWER - 1):
            base = self.apply(once, base, const)
        whole = COARSE_SWEEPS % POWER == 0
        start = base if whole else const
        steps = (COARSE_SWEEPS - 1) // POWER
        assert steps * POWER + (POWER if whole else 1) == COARSE_SWEEPS
        return lax.fori_loop(
            0, steps, lambda step, values: self.apply(many, values, base), tuple(start)
        )


def tree_sum(parts):
    while len(parts) > 1:
        odd = parts[len(parts) // 2 * 2 :]
        parts = [a + b for a, b in zip(parts[::2], parts[1::2])] + odd
    return parts[0]


def packed_cycle(grid, right, systems, flat_system, pads):
    coefs = systems[0]
    const = [coefs[p, 6] * right[p] for p in range(grid.planes)]
    values = grid.sweep(const, coefs, const)
    scaled = grid.apply(values, coefs, [c - OMEGA * v for c, v in zip(const, values)])
    residue = [r * coefs[p, 7] for p, r in enumerate(scaled)]
    if len(systems) > 1:
        (coarse_right,) = grid.restrict([residue], pads[:1])
        update = packed_cycle(grid.coarser(), coarse_right, systems[1:], flat_system, pads[1:])
        update = grid.prolong(update, pads[0])
    else:
        flat = Flat(grid)
        (coarse_right,) = flat.restrict([residue], pads[:1])
        update = flat.prolong(flat.solve(coarse_right, *flat_system), pads[0])
    values = [v + e for v, e in zip(values, update)]
    for _ in range(2):
        values = grid.sweep(values, coefs, const)
    return values


OWN = 2


def unpacked(grid, parts):
    left = iota((grid.nx, LANES), 1) < grid.ny
    planes = []
    for p in range(grid.planes):
        low, high = parts[p // OWN], parts[(grid.planes + p) // OWN]
        if p % OWN:
            low = roll(low, grid.ny, 1)
        else:
            high = roll(high, grid.ny, 1)
        planes.append(jnp.where(left, low, high))
    return planes


def coarse_grid(parts):
    return Packed(parts.shape[0] * OWN, parts.shape[1], LANES // OWN)


def system_kernel(perms, system1, system2, sweep_out, power_out, factor_out, pad1, pad2):
    grid = coarse_grid(perms)
    perm = unpacked(grid, perms)
    grid.system(perm, 1, system1)
    (perm,) = grid.restrict([perm], [pad1])
    perm = [x * 0.125 for x in perm]
    grid = grid.coarser()
    grid.system(perm, 2, system2)
    flat = Flat(grid)
    (perm,) = flat.restrict([perm], [pad2])
    flat.prepare([x * 0.125 for x in perm], 3, sweep_out, power_out, factor_out)


def coarse_kernel(
    dom_ref, rights, system1, system2, sweep_ref, power_ref, factors, coef, const, before, out,
    level, first, pad1, pad2, update,
):
    height = out.shape[0]
    dom = dom_ref[0]
    grid = coarse_grid(rights)
    nx = grid.nx
    flat_system = (sweep_ref, power_ref, factors)
    solved = packed_cycle(
        grid, unpacked(grid, rights), (system1, system2), flat_system, (pad1, pad2)
    )
    for p in range(grid.planes):
        update[p] = solved[p]
    planes, group = [], []
    for j in range(OWN + 2):
        layer = jnp.clip(dom * OWN + j - 1, 0, grid.nz - 1)
        group.append(layer // grid.planes)
        planes.append(update[lax.rem(layer, grid.planes)])
    for j, wide in enumerate(selector_dot(planes, lane_selector(1, LANES, 2, spread=True))):
        plane = jnp.where(group[j] == 0, wide[:, :LANES], wide[:, LANES:])
        pad = first.at[0]
        pad[pl.ds(0, nx, 2), :] = plane
        pad[pl.ds(1, nx, 2), :] = plane
        whole = first[0]
        level[2 * j] = before[2 * j] + whole
        level[2 * j + 1] = before[2 * j + 1] + whole

    def sweep(source, at, i):
        centre = source[i + 1]
        near = [coef.at[k, at + i] for k in range(6)]
        return stencil(centre, source[i], source[i + 2], near, KEEP * centre + const[at + i])

    def one(i):
        first[i] = sweep(level, 2, i)

    for i in range(height + 2):
        one(i)

    def two(i):
        out[i] = sweep(first, 3, i)

    for i in range(height):
        two(i)


def fine_part(dom, perm, source, layers):
    height, nx, ny = perm[0].shape
    field = lambda *lead: pltpu.VMEM(lead + (nx, ny), F32)
    vmem = pl.BlockSpec(memory_space=pltpu.VMEM)
    smem = pl.BlockSpec(memory_space=pltpu.SMEM)
    return pl.pallas_call(
        functools.partial(fine_kernel, layers),
        out_shape=(
            jax.ShapeDtypeStruct((6, height + 6, nx, ny), F32),
            jax.ShapeDtypeStruct((height + 6, nx, ny), F32),
            jax.ShapeDtypeStruct((height + 4, nx, ny), F32),
            jax.ShapeDtypeStruct((nx // 2, ny), F32),
        ),
        in_specs=[smem] + [vmem] * 6,
        out_specs=(vmem,) * 4,
        scratch_shapes=[
            field(3 * height),
            field(3 * height),
            field(height + 6),
            field(height // 2),
        ],
        compiler_params=pltpu.CompilerParams(vmem_limit_bytes=VMEM_LIMIT),
        name="fine",
    )(dom, *perm, *source)


def mean_part(perm):
    height, nx, ny = perm.shape
    vmem = pl.BlockSpec(memory_space=pltpu.VMEM)
    return pl.pallas_call(
        mean_kernel,
        out_shape=jax.ShapeDtypeStruct((nx // 2, ny), F32),
        in_specs=[vmem],
        out_specs=vmem,
        scratch_shapes=[pltpu.VMEM((height // 2, nx, ny), F32)],
        compiler_params=pltpu.CompilerParams(vmem_limit_bytes=VMEM_LIMIT),
        name="mean",
    )(perm)


def system_part(perms):
    field = lambda *shape: jax.ShapeDtypeStruct(shape, F32)
    scratch = lambda grid: pltpu.VMEM((grid.planes // 2, grid.nx, LANES), F32)
    grid1 = coarse_grid(perms)
    grid2 = grid1.coarser()
    flat = Flat(grid2)
    vmem = pl.BlockSpec(memory_space=pltpu.VMEM)
    return pl.pallas_call(
        system_kernel,
        out_shape=(
            field(grid1.planes, 8, grid1.nx, LANES),
            field(grid2.planes, 8, grid2.nx, LANES),
            field(flat.count(1), 8, LANES),
            field(flat.count(POWER), 8, LANES),
            field(flat.nz, 8, LANES),
        ),
        in_specs=[vmem],
        out_specs=(vmem,) * 5,
        scratch_shapes=[scratch(grid1), scratch(grid2)],
        compiler_params=pltpu.CompilerParams(vmem_limit_bytes=VMEM_LIMIT),
        name="system",
    )(perms)


def coarse_part(dom, rights, system, coefs, const, values, height):
    _, nx, ny = values.shape
    field = lambda *shape: pltpu.VMEM(shape, F32)
    grid1 = coarse_grid(rights)
    grid2 = grid1.coarser()
    vmem = pl.BlockSpec(memory_space=pltpu.VMEM)
    smem = pl.BlockSpec(memory_space=pltpu.SMEM)
    return pl.pallas_call(
        coarse_kernel,
        out_shape=jax.ShapeDtypeStruct((height, nx, ny), F32),
        in_specs=[smem] + [vmem] * 9,
        out_specs=vmem,
        scratch_shapes=[
            field(*values.shape),
            field(height + 2, nx, ny),
            field(grid1.planes // 2, grid1.nx, LANES),
            field(grid2.planes // 2, grid2.nx, LANES),
            field(grid1.planes, grid1.nx, LANES),
        ],
        compiler_params=pltpu.CompilerParams(vmem_limit_bytes=VMEM_LIMIT),
        name="coarse",
    )(dom, rights, *system, coefs, const, values)


def swaps(x, axis, step):
    return lax.ppermute(x, axis, [(i, i ^ step) for i in range(lax.axis_size(axis))])


def other_side(x):
    props, domains = lax.axis_size("prop"), lax.axis_size("dom")
    pairs = []
    for p in range(props):
        for d in range(domains):
            end = d in (0, domains - 1)
            partner = ((p ^ 1) * domains + d) if end else (p * domains + ((d + 1) ^ 1) - 1)
            pairs.append((p * domains + d, partner))
    return lax.ppermute(x, ("prop", "dom"), pairs)


def source_side(x):
    props, domains = lax.axis_size("prop"), lax.axis_size("dom")
    pairs = []
    for p in range(props):
        for d in range(domains):
            if p % 2 == 0:
                partner = p * domains + (d ^ 1)
            elif d in (0, domains - 1):
                partner = (p ^ 2) * domains + d
            else:
                partner = p * domains + ((d + 1) ^ 1) - 1
            pairs.append((p * domains + d, partner))
    return lax.ppermute(x, ("prop", "dom"), pairs)


def from_accepted(mine, accepted, beside):
    props = lax.axis_size("prop")
    step = props // 2
    own = SHRINK * mine
    offers, order = [mine], [0]
    while step:
        came = [swaps(x, "prop", step) for x in offers]
        if step == props // 2:
            came, own, beside = lax.optimization_barrier((came, own, beside))
        offers, order = offers + came, order + [x ^ step for x in order]
        step //= 2
    wanted = lax.axis_index("prop") ^ accepted
    current = offers[1]
    for at, offer in zip(order[2:], offers[2:]):
        current = jnp.where(wanted == at, offer, current)
    return jnp.where(wanted == 0, own, SHRINK * current), beside


def gather_parts(mine):
    domains = lax.axis_size("dom")
    copies = jnp.broadcast_to(mine[None], (domains,) + mine.shape)
    return lax.all_to_all(copies, "dom", 0, 0)


def body(states, accepted, noise, source):
    domains = lax.axis_size("dom")
    height = source.shape[0]
    assert height == 4 and source.shape[2] == LANES
    dom = jnp.stack([lax.axis_index("dom"), lax.axis_index("prop")]).astype(jnp.int32)
    near = source_side(source)
    beside = (OMEGA * source, BETA * noise[0])
    current, (scaled, noise_part) = from_accepted(states[0], accepted[0], beside)
    perm = jnp.exp(current + noise_part)
    perms = (perm, swaps(perm, "dom", 1), other_side(perm))
    sources = (scaled, near, swaps(near, "prop", 1))
    coarse_perms = gather_parts(mean_part(perm))
    *level, coarse = fine_part(dom, perms, sources, domains * height)
    system = system_part(coarse_perms)
    return coarse_part(dom, gather_parts(coarse), system, *level, height)[None]


def solution(mesh):
    in_specs = (
        P("prop", "dom", None, None),
        P(),
        P("prop", "dom", None, None),
        P("dom", None, None),
    )
    out_specs = P("prop", "dom", None, None)
    return jax.shard_map(body, mesh=mesh, in_specs=in_specs, out_specs=out_specs, check_vma=False)
```

```python
import functools
import math

import jax
import jax.numpy as jnp
from jax import lax
from jax.experimental import pallas as pl
from jax.experimental.pallas import tpu as pltpu
from jax.sharding import PartitionSpec as P

COARSE_SWEEPS = 64
POWER = 2
OMEGA = 0.7
KEEP = 1.0 - OMEGA
BETA = 0.4
SHRINK = math.sqrt(1.0 - BETA * BETA)
ZSCALE = 16.0
LANES = 128
VMEM_LIMIT = 40 * 1024 * 1024
F32 = jnp.float32
WEST, EAST, SOUTH, NORTH, BELOW, ABOVE, CONST = range(7)


def iota(shape, dim):
    return lax.broadcasted_iota(jnp.int32, shape, dim)


def roll(x, amount, axis):
    axis = axis % x.ndim
    return pltpu.roll(x, amount % x.shape[axis], axis)


def inverse_of(x):
    guess = pl.reciprocal(x, approx=True)
    return guess * (2.0 - x * guess)


def harmonic(a, b):
    return (2.0 * a) * b * inverse_of(a + b)


def selector_dot(parts, selector):
    x = jnp.concatenate(parts, axis=0) if len(parts) > 1 else parts[0]
    rows = x.shape[0]
    high = x.astype(jnp.bfloat16).astype(F32)
    rest = x - high
    middle = rest.astype(jnp.bfloat16).astype(F32)
    terms = jnp.concatenate([high, middle, rest - middle], axis=0).astype(jnp.bfloat16)
    y = jnp.dot(terms, selector, preferred_element_type=F32)
    total = y[:rows] + y[rows : 2 * rows] + y[2 * rows :]
    height = parts[0].shape[0]
    return [total[i * height : (i + 1) * height] for i in range(len(parts))]


def face_terms(perm, lower, upper, below_scale, above_scale, ny):
    shape = perm.shape
    rows = iota(shape, 0)
    columns = iota(shape, 1) & (ny - 1)
    west = jnp.where(rows == 0, 0.0, harmonic(perm, roll(perm, 1, 0)))
    east = roll(west, -1, 0)
    south = jnp.where(columns == 0, 0.0, harmonic(perm, roll(perm, 1, 1)))
    north = roll(south, -1, 1)
    below = below_scale * harmonic(perm, lower)
    above = above_scale * harmonic(perm, upper)
    ends = jnp.where(rows == 0, perm, 0.0) + jnp.where(rows == shape[0] - 1, perm, 0.0)
    ends = ends + jnp.where(columns == 0, perm, 0.0) + jnp.where(columns == ny - 1, perm, 0.0)
    diagonal = ((west + east) + (south + north)) + ((below + above) + ends)
    return (west, east, south, north, below, above), diagonal


def stencil(values, lower, upper, coefs, base):
    x = coefs[0] * roll(values, 1, 0) + coefs[1] * roll(values, -1, 0)
    y = coefs[2] * roll(values, 1, 1) + coefs[3] * roll(values, -1, 1)
    z = coefs[4] * lower + coefs[5] * upper
    return (x + y) + (z + base)


def lane_selector(groups, ny, step, spread=False):
    shape = (LANES, step * LANES) if spread else (step * LANES, LANES)
    source, target = iota(shape, int(spread)), iota(shape, 1 - int(spread))
    bits = ny.bit_length() - 1
    lane = source & (LANES - 1)
    group = (lane >> bits) * step + (source >> 7)
    wanted = (group << (bits - 1)) + ((lane & (ny - 1)) >> 1)
    return jnp.where((target == wanted) & (lane < groups * ny), 1.0, 0.0).astype(jnp.bfloat16)


def fine_kernel(
    layers,
    dom_ref,
    per, per_pair, per_other,
    src, src_near, src_next,
    coef, const, values, coarse_out,
    perm, right, diag, pair_right, pair_perm,
):
    height = per.shape[0]
    dom = dom_ref[0]
    pair_at = jnp.where(lax.rem(dom, 2) == 0, 2 * height, 0)
    other_at = 2 * height - pair_at

    near_at = jnp.where(lax.rem(dom_ref[1], 2) == 0, pair_at, other_at)
    next_at = 2 * height - near_at
    for i in range(height):
        for at, p in ((height, per), (pair_at, per_pair), (other_at, per_other)):
            perm[at + i] = p[i]
        right[height + i] = src[i]
        right[near_at + i] = OMEGA * src_near[i]
        right[next_at + i] = OMEGA * src_next[i]

    def build(i):
        z = dom * height + i - 3
        below = jnp.where((z > 0) & (z < layers), ZSCALE, 0.0)
        above = jnp.where((z + 1 > 0) & (z + 1 < layers), ZSCALE, 0.0)
        at = height - 3 + i
        faces, diagonal = face_terms(perm[at], perm[at - 1], perm[at + 1], below, above, LANES)
        inverse = inverse_of(diagonal)
        const[i] = inverse * right[at]
        inverse = OMEGA * inverse
        for k in range(6):
            coef[k, i] = inverse * faces[k]
        diag[i] = diagonal

    for i in range(height + 6):
        build(i)

    def first(i):
        start = const[i + 1]
        near = [coef[k, i + 1] for k in range(6)]
        values[i] = stencil(start, const[i], const[i + 2], near, (1.0 + KEEP) * start)

    for i in range(height + 4):
        first(i)

    def residue(i):
        centre = values[i + 2]
        base = const[i + 3] - OMEGA * centre
        near = [coef[k, i + 3] for k in range(6)]
        scaled = stencil(centre, values[i + 1], values[i + 3], near, base)
        return scaled * (diag[i + 3] * (1.0 / OMEGA))

    for m in range(height // 2):
        pair_right[m] = residue(2 * m) + residue(2 * m + 1)
        pair_perm[m] = (perm[height + 2 * m] + perm[height + 2 * m + 1]) * 0.125
    half = pair_right.shape[1] // 2
    rows = []
    for m in range(height // 2):
        both = [x[m, pl.ds(0, half, 2), :] + x[m, pl.ds(1, half, 2), :] for x in (pair_right, pair_perm)]
        rows.append(jnp.concatenate(both, axis=1))
    for m, x in enumerate(selector_dot(rows, lane_selector(1, LANES, 2))):
        coarse_out[m] = x


class Packed:
    def __init__(self, nz, nx, ny):
        self.nz, self.nx, self.ny = nz, nx, ny
        self.groups = min(LANES // ny, nz)
        self.planes = nz // self.groups

    def lower(self, planes, p):
        return planes[p - 1] if p else roll(planes[self.planes - 1], self.ny, 1)

    def upper(self, planes, p):
        return planes[p + 1] if p + 1 < self.planes else roll(planes[0], -self.ny, 1)

    def system(self, right, perm, level):
        lane = iota((self.nx, LANES), 1)
        used = lane < self.groups * self.ny
        if self.groups * self.ny < LANES:
            perm = [jnp.where(used, x, 1.0) for x in perm]
        coefs, const, diagonals = [], [], []
        for p in range(self.planes):
            below, above = ZSCALE, ZSCALE
            if p == 0:
                below = jnp.where(lane < self.ny, 0.0, ZSCALE)
            if p + 1 == self.planes:
                above = jnp.where(lane < (self.groups - 1) * self.ny, ZSCALE, 0.0)
            faces, diagonal = face_terms(
                perm[p], self.lower(perm, p), self.upper(perm, p), below, above, self.ny
            )
            inverse = OMEGA * inverse_of(diagonal)
            coefs.append([inverse * face for face in faces])
            const.append(inverse * right[p] * (4.0**-level))
            diagonals.append(diagonal * (4.0**level / OMEGA))
        return coefs, const, diagonals

    def apply(self, values, coefs, bases):
        return [
            stencil(values[p], self.lower(values, p), self.upper(values, p), coefs[p], bases[p])
            for p in range(self.planes)
        ]

    def sweep(self, values, coefs, const):
        return self.apply(values, coefs, [KEEP * v + c for v, c in zip(values, const)])

    def coarser(self):
        return Packed(self.nz // 2, self.nx // 2, self.ny // 2)

    def restrict(self, fields, pads):
        coarse = self.coarser()
        step = coarse.groups // self.groups
        half = coarse.nx
        parts = []
        for values, pad in zip(fields, pads):
            rows = []
            for m in range(self.planes // 2):
                pad[m] = values[2 * m] + values[2 * m + 1]
                rows.append(pad[m, pl.ds(0, half, 2), :] + pad[m, pl.ds(1, half, 2), :])
            for p in range(coarse.planes):
                blocks = rows[p :: coarse.planes]
                parts.append(jnp.concatenate(blocks, axis=1) if step > 1 else blocks[0])
        sums = selector_dot(parts, lane_selector(self.groups, self.ny, step))
        return [sums[i : i + coarse.planes] for i in range(0, len(sums), coarse.planes)]

    def prolong(self, values, pad):
        coarse = self.coarser()
        step = coarse.groups // self.groups
        half = coarse.nx
        wide = selector_dot(values, lane_selector(self.groups, self.ny, step, spread=True))
        out = []
        for m in range(self.planes // 2):
            j, p = divmod(m, coarse.planes)
            plane = wide[p][:, j * LANES : (j + 1) * LANES]
            pad[m, pl.ds(0, half, 2), :] = plane
            pad[m, pl.ds(1, half, 2), :] = plane
            out += [pad[m], pad[m]]
        return out


class Flat:
    def __init__(self, finer):
        coarse = finer.coarser()
        self.finer = finer
        self.nz, self.nx, self.ny = coarse.nz, coarse.nx, coarse.ny
        self.pairs = finer.planes // 2
        self.rows = max(8, self.nz)
        self.shape = (self.rows, LANES)
        self.buffer_rows = 2 * (self.rows + 2 * POWER)

    def selector(self, spread=False):
        wide = self.finer.groups * LANES
        shape = (wide, LANES) if spread else (LANES, wide)
        fine, flat = iota(shape, int(spread)), iota(shape, 1 - int(spread))
        bits = self.finer.ny.bit_length() - 1
        same = (fine >> bits) == (flat >> 7)
        same &= ((fine & (self.finer.ny - 1)) >> 1) == (flat & (self.ny - 1))
        return jnp.where(same, 1.0, 0.0).astype(jnp.bfloat16)

    def diagonal(self):
        shape = (self.nx, LANES)
        return iota(shape, 0) == (iota(shape, 1) >> (self.ny.bit_length() - 1))

    def restrict(self, fields, pads, pack):
        parts = []
        for values, pad in zip(fields, pads):
            for m in range(self.pairs):
                pad[m] = values[2 * m] + values[2 * m + 1]
                parts.append(pad[m, pl.ds(0, self.nx, 2), :] + pad[m, pl.ds(1, self.nx, 2), :])
        sums = selector_dot(parts, self.selector())
        mask = self.diagonal()
        pack[...] = jnp.zeros_like(pack)
        for i in range(len(fields)):
            for z in range(self.nz):
                s, m = divmod(z, self.pairs)
                block = sums[i * self.pairs + m][:, s * LANES : (s + 1) * LANES]
                row = jnp.sum(jnp.where(mask, block, 0.0), axis=0, keepdims=True)
                pack[i, z : z + 1, :] = row
        return [pack[i] for i in range(len(fields))]

    def prolong(self, values, pad, pack):
        mask = self.diagonal()
        pack[0] = values
        parts = []
        for m in range(self.pairs):
            layers = [s * self.pairs + m for s in range(self.finer.groups)]
            spread = [jnp.broadcast_to(pack[0, z : z + 1, :], mask.shape) for z in layers]
            parts.append(jnp.concatenate([jnp.where(mask, x, 0.0) for x in spread], axis=1))
        out = []
        for m, wide in enumerate(selector_dot(parts, self.selector(spread=True))):
            pad[m, pl.ds(0, self.nx, 2), :] = wide
            pad[m, pl.ds(1, self.nx, 2), :] = wide
            out += [pad[m], pad[m]]
        return out

    def system(self, right, perm, level):
        lane, row = iota(self.shape, 1), iota(self.shape, 0)
        x, y = lane >> (self.ny.bit_length() - 1), lane & (self.ny - 1)
        real = row < self.nz
        perm = jnp.where(real, perm, 1.0)
        west = jnp.where(x == 0, 0.0, harmonic(perm, roll(perm, self.ny, 1)))
        east = roll(west, -self.ny, 1)
        south = jnp.where(y == 0, 0.0, harmonic(perm, roll(perm, 1, 1)))
        north = roll(south, -1, 1)
        below = ZSCALE * harmonic(perm, roll(perm, 1, 0))
        below = jnp.where((row > 0) & real, below, 0.0)
        above = roll(below, -1, 0)
        faces = [west, east, south, north, below, above]
        ends = (x == 0, x == self.nx - 1, y == 0, y == self.ny - 1)
        diagonal = tree_sum(faces + [jnp.where(end, perm, 0.0) for end in ends])
        inverse = jnp.where(real, OMEGA * inverse_of(diagonal), 0.0)
        keys = ((-1, 0, 0), (1, 0, 0), (0, -1, 0), (0, 1, 0), (0, 0, -1), (0, 0, 1))
        terms = {key: inverse * face for key, face in zip(keys, faces)}
        terms[0, 0, 0] = jnp.full(self.shape, KEEP, F32)
        return terms, inverse * right * (4.0**-level)

    def product(self, first, second):
        sums = {}
        for (dx, dy, dz), coef in first.items():
            for other, moved in second.items():
                if dz:
                    moved = roll(moved, -dz, 0)
                if dx or dy:
                    moved = roll(moved, -(dx * self.ny + dy), 1)
                total = tuple(a + b for a, b in zip((dx, dy, dz), other))
                sums.setdefault(total, []).append(coef * moved)
        return {key: tree_sum(parts) for key, parts in sums.items()}

    def apply(self, terms, values, base, buffer):
        buffer[pl.ds(2 * POWER, self.rows, 2), :] = values
        moved = {}
        for dx, dy, dz in sorted(terms, key=lambda key: abs(key[2])):
            if (0, 0, dz) not in moved:
                moved[0, 0, dz] = buffer[pl.ds(2 * (POWER + dz), self.rows, 2), :] if dz else values
            if dx or dy:
                moved[dx, dy, dz] = roll(moved[0, 0, dz], -(dx * self.ny + dy), 1)
        return tree_sum([base] + [coef * moved[key] for key, coef in terms.items()])

    def solve(self, right, perm, level, buffer):
        buffer[...] = jnp.zeros_like(buffer)
        terms, const = self.system(right, perm, level)
        power, base = terms, const
        for _ in range(POWER - 1):
            base = self.apply(terms, base, const, buffer)
            power = self.product(terms, power)
        whole = COARSE_SWEEPS % POWER == 0
        start = base if whole else const
        steps = (COARSE_SWEEPS - 1) // POWER
        assert steps * POWER + (POWER if whole else 1) == COARSE_SWEEPS
        return lax.fori_loop(
            0, steps, lambda step, values: self.apply(power, values, base, buffer), start
        )


def tree_sum(parts):
    while len(parts) > 1:
        odd = parts[len(parts) // 2 * 2 :]
        parts = [a + b for a, b in zip(parts[::2], parts[1::2])] + odd
    return parts[0]


def packed_cycle(grid, right, perm, level, pads, store):
    pad_right, pad_perm = pads[0]
    coefs, const, diagonals = grid.system(right, perm, level)
    values = grid.sweep(const, coefs, const)
    scaled = grid.apply(values, coefs, [c - OMEGA * v for c, v in zip(const, values)])
    residue = [r * d for r, d in zip(scaled, diagonals)]
    if len(pads) > 1:
        coarse_right, coarse_perm = grid.restrict((residue, perm), (pad_right, pad_perm))
        coarse_perm = [x * 0.125 for x in coarse_perm]
        update = packed_cycle(grid.coarser(), coarse_right, coarse_perm, level + 1, pads[1:], store)
        update = grid.prolong(update, pad_right)
    else:
        pack, buffer = store
        flat = Flat(grid)
        coarse_right, coarse_perm = flat.restrict((residue, perm), (pad_right, pad_perm), pack)
        update = flat.solve(coarse_right, coarse_perm * 0.125, level + 1, buffer)
        update = flat.prolong(update, pad_right, pack)
    values = [v + e for v, e in zip(values, update)]
    for _ in range(2):
        values = grid.sweep(values, coefs, const)
    return values


def coarse_kernel(
    dom_ref, gathered, coef, const, before, out,
    level, first, pad_right1, pad_perm1, pad_right2, pad_perm2, update, pack, buffer,
):
    height = out.shape[0]
    dom = dom_ref[0]
    domains, own, nx, _ = gathered.shape
    ny = LANES // 2
    grid = Packed(domains * own, nx, ny)
    left = iota((nx, LANES), 1) < ny
    right, perm = [], []
    for p in range(grid.planes):
        a = gathered[p // own, p % own]
        q = grid.planes + p
        b = gathered[q // own, q % own]
        right.append(jnp.where(left, a, roll(b, ny, 1)))
        perm.append(jnp.where(left, roll(a, ny, 1), b))
    pads = [(pad_right1, pad_perm1), (pad_right2, pad_perm2)]
    solved = packed_cycle(grid, right, perm, 1, pads, (pack, buffer))
    for p in range(grid.planes):
        update[p] = solved[p]
    planes, group = [], []
    for j in range(own + 2):
        layer = jnp.clip(dom * own + j - 1, 0, grid.nz - 1)
        group.append(layer // grid.planes)
        planes.append(update[lax.rem(layer, grid.planes)])
    for j, wide in enumerate(selector_dot(planes, lane_selector(1, LANES, 2, spread=True))):
        plane = jnp.where(group[j] == 0, wide[:, :LANES], wide[:, LANES:])
        pad = first.at[0]
        pad[pl.ds(0, nx, 2), :] = plane
        pad[pl.ds(1, nx, 2), :] = plane
        whole = first[0]
        level[2 * j] = before[2 * j] + whole
        level[2 * j + 1] = before[2 * j + 1] + whole

    def sweep(source, at, i):
        centre = source[i + 1]
        near = [coef[k, at + i] for k in range(6)]
        return stencil(centre, source[i], source[i + 2], near, KEEP * centre + const[at + i])

    def one(i):
        first[i] = sweep(level, 2, i)

    for i in range(height + 2):
        one(i)

    def two(i):
        out[i] = sweep(first, 3, i)

    for i in range(height):
        two(i)


def fine_part(dom, perm, source, layers):
    height, nx, ny = perm[0].shape
    field = lambda *lead: pltpu.VMEM(lead + (nx, ny), F32)
    vmem = pl.BlockSpec(memory_space=pltpu.VMEM)
    smem = pl.BlockSpec(memory_space=pltpu.SMEM)
    return pl.pallas_call(
        functools.partial(fine_kernel, layers),
        out_shape=(
            jax.ShapeDtypeStruct((6, height + 6, nx, ny), F32),
            jax.ShapeDtypeStruct((height + 6, nx, ny), F32),
            jax.ShapeDtypeStruct((height + 4, nx, ny), F32),
            jax.ShapeDtypeStruct((height // 2, nx // 2, ny), F32),
        ),
        in_specs=[smem] + [vmem] * 6,
        out_specs=(vmem,) * 4,
        scratch_shapes=[
            field(3 * height),
            field(3 * height),
            field(height + 6),
            field(height // 2),
            field(height // 2),
        ],
        compiler_params=pltpu.CompilerParams(vmem_limit_bytes=VMEM_LIMIT),
        name="fine",
    )(dom, *perm, *source)


def coarse_part(dom, gathered, coefs, const, values, height):
    _, nx, ny = values.shape
    field = lambda *shape: pltpu.VMEM(shape, F32)
    grid1 = Packed(gathered.shape[0] * gathered.shape[1], nx // 2, ny // 2)
    grid2 = grid1.coarser()
    pads1 = field(grid1.planes // 2, grid1.nx, LANES)
    pads2 = field(grid2.planes // 2, grid2.nx, LANES)
    vmem = pl.BlockSpec(memory_space=pltpu.VMEM)
    smem = pl.BlockSpec(memory_space=pltpu.SMEM)
    return pl.pallas_call(
        coarse_kernel,
        out_shape=jax.ShapeDtypeStruct((height, nx, ny), F32),
        in_specs=[smem] + [vmem] * 4,
        out_specs=vmem,
        scratch_shapes=[
            field(*values.shape),
            field(height + 2, nx, ny),
            pads1, pads1, pads2, pads2,
            field(grid1.planes, grid1.nx, LANES),
            field(2, Flat(grid2).rows, LANES),
            field(Flat(grid2).buffer_rows, LANES),
        ],
        compiler_params=pltpu.CompilerParams(vmem_limit_bytes=VMEM_LIMIT),
        name="coarse",
    )(dom, gathered, coefs, const, values)


def swaps(x, axis, step):
    return lax.ppermute(x, axis, [(i, i ^ step) for i in range(lax.axis_size(axis))])


def other_side(x):
    props, domains = lax.axis_size("prop"), lax.axis_size("dom")
    pairs = []
    for p in range(props):
        for d in range(domains):
            end = d in (0, domains - 1)
            partner = ((p ^ 1) * domains + d) if end else (p * domains + ((d + 1) ^ 1) - 1)
            pairs.append((p * domains + d, partner))
    return lax.ppermute(x, ("prop", "dom"), pairs)


def source_side(x):
    props, domains = lax.axis_size("prop"), lax.axis_size("dom")
    pairs = []
    for p in range(props):
        for d in range(domains):
            if p % 2 == 0:
                partner = p * domains + (d ^ 1)
            elif d in (0, domains - 1):
                partner = (p ^ 2) * domains + d
            else:
                partner = p * domains + ((d + 1) ^ 1) - 1
            pairs.append((p * domains + d, partner))
    return lax.ppermute(x, ("prop", "dom"), pairs)


def from_accepted(mine, accepted, beside):
    props = lax.axis_size("prop")
    step = props // 2
    own = SHRINK * mine
    offers, order = [mine], [0]
    while step:
        came = [swaps(x, "prop", step) for x in offers]
        if step == props // 2:
            came, own, beside = lax.optimization_barrier((came, own, beside))
        offers, order = offers + came, order + [x ^ step for x in order]
        step //= 2
    wanted = lax.axis_index("prop") ^ accepted
    current = offers[1]
    for at, offer in zip(order[2:], offers[2:]):
        current = jnp.where(wanted == at, offer, current)
    return jnp.where(wanted == 0, own, SHRINK * current), beside


def gather_parts(mine):
    domains = lax.axis_size("dom")
    copies = jnp.broadcast_to(mine[None], (domains,) + mine.shape)
    return lax.all_to_all(copies, "dom", 0, 0)


def body(states, accepted, noise, source):
    domains = lax.axis_size("dom")
    height = source.shape[0]
    dom = jnp.stack([lax.axis_index("dom"), lax.axis_index("prop")]).astype(jnp.int32)
    near = source_side(source)
    beside = (OMEGA * source, BETA * noise[0])
    current, (scaled, noise_part) = from_accepted(states[0], accepted[0], beside)
    perm = jnp.exp(current + noise_part)
    perms = (perm, swaps(perm, "dom", 1), other_side(perm))
    sources = (scaled, near, swaps(near, "prop", 1))
    *level, coarse = fine_part(dom, perms, sources, domains * height)
    return coarse_part(dom, gather_parts(coarse), *level, height)[None]


def solution(mesh):
    in_specs = (
        P("prop", "dom", None, None),
        P(),
        P("prop", "dom", None, None),
        P("dom", None, None),
    )
    out_specs = P("prop", "dom", None, None)
    return jax.shard_map(body, mesh=mesh, in_specs=in_specs, out_specs=out_specs, check_vma=False)
```

```python
import functools
import math

import jax
import jax.numpy as jnp
from jax import lax
from jax.experimental import pallas as pl
from jax.experimental.pallas import tpu as pltpu
from jax.sharding import PartitionSpec as P

COARSE_SWEEPS = 64
POWER = 4
OMEGA = 0.7
KEEP = 1.0 - OMEGA
BETA = 0.4
SHRINK = math.sqrt(1.0 - BETA * BETA)
ZSCALE = 16.0
LANES = 128
VMEM_LIMIT = 40 * 1024 * 1024
F32 = jnp.float32
WEST, EAST, SOUTH, NORTH, BELOW, ABOVE, CONST = range(7)


def iota(shape, dim):
    return lax.broadcasted_iota(jnp.int32, shape, dim)


def roll(x, amount, axis):
    axis = axis % x.ndim
    return pltpu.roll(x, amount % x.shape[axis], axis)


def inverse_of(x):
    guess = pl.reciprocal(x, approx=True)
    return guess * (2.0 - x * guess)


def harmonic(a, b):
    return (2.0 * a) * b * inverse_of(a + b)


def selector_dot(parts, selector):
    x = jnp.concatenate(parts, axis=0) if len(parts) > 1 else parts[0]
    rows = x.shape[0]
    high = x.astype(jnp.bfloat16).astype(F32)
    rest = x - high
    middle = rest.astype(jnp.bfloat16).astype(F32)
    terms = jnp.concatenate([high, middle, rest - middle], axis=0).astype(jnp.bfloat16)
    y = jnp.dot(terms, selector, preferred_element_type=F32)
    total = y[:rows] + y[rows : 2 * rows] + y[2 * rows :]
    height = parts[0].shape[0]
    return [total[i * height : (i + 1) * height] for i in range(len(parts))]


def face_terms(perm, lower, upper, below_scale, above_scale, ny):
    shape = perm.shape
    rows = iota(shape, 0)
    columns = iota(shape, 1) & (ny - 1)
    west = jnp.where(rows == 0, 0.0, harmonic(perm, roll(perm, 1, 0)))
    east = roll(west, -1, 0)
    south = jnp.where(columns == 0, 0.0, harmonic(perm, roll(perm, 1, 1)))
    north = roll(south, -1, 1)
    below = below_scale * harmonic(perm, lower)
    above = above_scale * harmonic(perm, upper)
    ends = jnp.where(rows == 0, perm, 0.0) + jnp.where(rows == shape[0] - 1, perm, 0.0)
    ends = ends + jnp.where(columns == 0, perm, 0.0) + jnp.where(columns == ny - 1, perm, 0.0)
    diagonal = ((west + east) + (south + north)) + ((below + above) + ends)
    return (west, east, south, north, below, above), diagonal


def stencil(values, lower, upper, coefs, base):
    x = coefs[0] * roll(values, 1, 0) + coefs[1] * roll(values, -1, 0)
    y = coefs[2] * roll(values, 1, 1) + coefs[3] * roll(values, -1, 1)
    z = coefs[4] * lower + coefs[5] * upper
    return (x + y) + (z + base)


def lane_selector(groups, ny, step, spread=False):
    shape = (LANES, step * LANES) if spread else (step * LANES, LANES)
    source, target = iota(shape, int(spread)), iota(shape, 1 - int(spread))
    bits = ny.bit_length() - 1
    lane = source & (LANES - 1)
    group = (lane >> bits) * step + (source >> 7)
    wanted = (group << (bits - 1)) + ((lane & (ny - 1)) >> 1)
    return jnp.where((target == wanted) & (lane < groups * ny), 1.0, 0.0).astype(jnp.bfloat16)


def fine_kernel(
    layers,
    dom_ref,
    per, per_pair, per_other,
    src, src_near, src_next,
    coef, const, values, coarse_out,
    perm, right, diag, pair_right, pair_perm,
):
    height = per.shape[0]
    dom = dom_ref[0]
    pair_at = jnp.where(lax.rem(dom, 2) == 0, 2 * height, 0)
    other_at = 2 * height - pair_at

    near_at = jnp.where(lax.rem(dom_ref[1], 2) == 0, pair_at, other_at)
    next_at = 2 * height - near_at
    for i in range(height):
        for at, p in ((height, per), (pair_at, per_pair), (other_at, per_other)):
            perm[at + i] = p[i]
        right[height + i] = src[i]
        right[near_at + i] = OMEGA * src_near[i]
        right[next_at + i] = OMEGA * src_next[i]

    def build(i):
        z = dom * height + i - 3
        below = jnp.where((z > 0) & (z < layers), ZSCALE, 0.0)
        above = jnp.where((z + 1 > 0) & (z + 1 < layers), ZSCALE, 0.0)
        at = height - 3 + i
        faces, diagonal = face_terms(perm[at], perm[at - 1], perm[at + 1], below, above, LANES)
        inverse = inverse_of(diagonal)
        const[i] = inverse * right[at]
        inverse = OMEGA * inverse
        for k in range(6):
            coef[k, i] = inverse * faces[k]
        diag[i] = diagonal

    for i in range(height + 6):
        build(i)

    def first(i):
        start = const[i + 1]
        near = [coef[k, i + 1] for k in range(6)]
        values[i] = stencil(start, const[i], const[i + 2], near, (1.0 + KEEP) * start)

    for i in range(height + 4):
        first(i)

    def residue(i):
        centre = values[i + 2]
        base = const[i + 3] - OMEGA * centre
        near = [coef[k, i + 3] for k in range(6)]
        scaled = stencil(centre, values[i + 1], values[i + 3], near, base)
        return scaled * (diag[i + 3] * (1.0 / OMEGA))

    for m in range(height // 2):
        pair_right[m] = residue(2 * m) + residue(2 * m + 1)
        pair_perm[m] = (perm[height + 2 * m] + perm[height + 2 * m + 1]) * 0.125
    half = pair_right.shape[1] // 2
    rows = []
    for m in range(height // 2):
        both = [x[m, pl.ds(0, half, 2), :] + x[m, pl.ds(1, half, 2), :] for x in (pair_right, pair_perm)]
        rows.append(jnp.concatenate(both, axis=1))
    for m, x in enumerate(selector_dot(rows, lane_selector(1, LANES, 2))):
        coarse_out[m] = x


class Packed:
    def __init__(self, nz, nx, ny):
        self.nz, self.nx, self.ny = nz, nx, ny
        self.groups = min(LANES // ny, nz)
        self.planes = nz // self.groups

    def lower(self, planes, p):
        return planes[p - 1] if p else roll(planes[self.planes - 1], self.ny, 1)

    def upper(self, planes, p):
        return planes[p + 1] if p + 1 < self.planes else roll(planes[0], -self.ny, 1)

    def system(self, right, perm, level):
        lane = iota((self.nx, LANES), 1)
        used = lane < self.groups * self.ny
        if self.groups * self.ny < LANES:
            perm = [jnp.where(used, x, 1.0) for x in perm]
        coefs, const, diagonals = [], [], []
        for p in range(self.planes):
            below, above = ZSCALE, ZSCALE
            if p == 0:
                below = jnp.where(lane < self.ny, 0.0, ZSCALE)
            if p + 1 == self.planes:
                above = jnp.where(lane < (self.groups - 1) * self.ny, ZSCALE, 0.0)
            faces, diagonal = face_terms(
                perm[p], self.lower(perm, p), self.upper(perm, p), below, above, self.ny
            )
            inverse = OMEGA * inverse_of(diagonal)
            coefs.append([inverse * face for face in faces])
            const.append(inverse * right[p] * (4.0**-level))
            diagonals.append(diagonal * (4.0**level / OMEGA))
        return coefs, const, diagonals

    def apply(self, values, coefs, bases):
        return [
            stencil(values[p], self.lower(values, p), self.upper(values, p), coefs[p], bases[p])
            for p in range(self.planes)
        ]

    def sweep(self, values, coefs, const):
        return self.apply(values, coefs, [KEEP * v + c for v, c in zip(values, const)])

    def coarser(self):
        return Packed(self.nz // 2, self.nx // 2, self.ny // 2)

    def restrict(self, fields, pads):
        coarse = self.coarser()
        step = coarse.groups // self.groups
        half = coarse.nx
        parts = []
        for values, pad in zip(fields, pads):
            rows = []
            for m in range(self.planes // 2):
                pad[m] = values[2 * m] + values[2 * m + 1]
                rows.append(pad[m, pl.ds(0, half, 2), :] + pad[m, pl.ds(1, half, 2), :])
            for p in range(coarse.planes):
                blocks = rows[p :: coarse.planes]
                parts.append(jnp.concatenate(blocks, axis=1) if step > 1 else blocks[0])
        sums = selector_dot(parts, lane_selector(self.groups, self.ny, step))
        return [sums[i : i + coarse.planes] for i in range(0, len(sums), coarse.planes)]

    def prolong(self, values, pad):
        coarse = self.coarser()
        step = coarse.groups // self.groups
        half = coarse.nx
        wide = selector_dot(values, lane_selector(self.groups, self.ny, step, spread=True))
        out = []
        for m in range(self.planes // 2):
            j, p = divmod(m, coarse.planes)
            plane = wide[p][:, j * LANES : (j + 1) * LANES]
            pad[m, pl.ds(0, half, 2), :] = plane
            pad[m, pl.ds(1, half, 2), :] = plane
            out += [pad[m], pad[m]]
        return out


class Flat:
    def __init__(self, finer):
        coarse = finer.coarser()
        self.finer = finer
        self.nz, self.nx, self.ny = coarse.nz, coarse.nx, coarse.ny
        self.pairs = finer.planes // 2
        self.rows = max(8, self.nz)
        self.shape = (self.rows, LANES)
        self.buffer_rows = 2 * (self.rows + 2 * POWER)

    def selector(self, spread=False):
        wide = self.finer.groups * LANES
        shape = (wide, LANES) if spread else (LANES, wide)
        fine, flat = iota(shape, int(spread)), iota(shape, 1 - int(spread))
        bits = self.finer.ny.bit_length() - 1
        same = (fine >> bits) == (flat >> 7)
        same &= ((fine & (self.finer.ny - 1)) >> 1) == (flat & (self.ny - 1))
        return jnp.where(same, 1.0, 0.0).astype(jnp.bfloat16)

    def diagonal(self):
        shape = (self.nx, LANES)
        return iota(shape, 0) == (iota(shape, 1) >> (self.ny.bit_length() - 1))

    def restrict(self, fields, pads, pack):
        parts = []
        for values, pad in zip(fields, pads):
            for m in range(self.pairs):
                pad[m] = values[2 * m] + values[2 * m + 1]
                parts.append(pad[m, pl.ds(0, self.nx, 2), :] + pad[m, pl.ds(1, self.nx, 2), :])
        sums = selector_dot(parts, self.selector())
        mask = self.diagonal()
        pack[...] = jnp.zeros_like(pack)
        for i in range(len(fields)):
            for z in range(self.nz):
                s, m = divmod(z, self.pairs)
                block = sums[i * self.pairs + m][:, s * LANES : (s + 1) * LANES]
                row = jnp.sum(jnp.where(mask, block, 0.0), axis=0, keepdims=True)
                pack[i, z : z + 1, :] = row
        return [pack[i] for i in range(len(fields))]

    def prolong(self, values, pad, pack):
        mask = self.diagonal()
        pack[0] = values
        parts = []
        for m in range(self.pairs):
            layers = [s * self.pairs + m for s in range(self.finer.groups)]
            spread = [jnp.broadcast_to(pack[0, z : z + 1, :], mask.shape) for z in layers]
            parts.append(jnp.concatenate([jnp.where(mask, x, 0.0) for x in spread], axis=1))
        out = []
        for m, wide in enumerate(selector_dot(parts, self.selector(spread=True))):
            pad[m, pl.ds(0, self.nx, 2), :] = wide
            pad[m, pl.ds(1, self.nx, 2), :] = wide
            out += [pad[m], pad[m]]
        return out

    def system(self, right, perm, level):
        lane, row = iota(self.shape, 1), iota(self.shape, 0)
        x, y = lane >> (self.ny.bit_length() - 1), lane & (self.ny - 1)
        real = row < self.nz
        perm = jnp.where(real, perm, 1.0)
        west = jnp.where(x == 0, 0.0, harmonic(perm, roll(perm, self.ny, 1)))
        east = roll(west, -self.ny, 1)
        south = jnp.where(y == 0, 0.0, harmonic(perm, roll(perm, 1, 1)))
        north = roll(south, -1, 1)
        below = ZSCALE * harmonic(perm, roll(perm, 1, 0))
        below = jnp.where((row > 0) & real, below, 0.0)
        above = roll(below, -1, 0)
        faces = [west, east, south, north, below, above]
        ends = (x == 0, x == self.nx - 1, y == 0, y == self.ny - 1)
        diagonal = tree_sum(faces + [jnp.where(end, perm, 0.0) for end in ends])
        inverse = jnp.where(real, OMEGA * inverse_of(diagonal), 0.0)
        keys = ((-1, 0, 0), (1, 0, 0), (0, -1, 0), (0, 1, 0), (0, 0, -1), (0, 0, 1))
        terms = {key: inverse * face for key, face in zip(keys, faces)}
        terms[0, 0, 0] = jnp.full(self.shape, KEEP, F32)
        return terms, inverse * right * (4.0**-level)

    def product(self, first, second):
        sums = {}
        for (dx, dy, dz), coef in first.items():
            for other, moved in second.items():
                if dz:
                    moved = roll(moved, -dz, 0)
                if dx or dy:
                    moved = roll(moved, -(dx * self.ny + dy), 1)
                total = tuple(a + b for a, b in zip((dx, dy, dz), other))
                sums.setdefault(total, []).append(coef * moved)
        return {key: tree_sum(parts) for key, parts in sums.items()}

    def apply(self, terms, values, base, buffer):
        buffer[pl.ds(2 * POWER, self.rows, 2), :] = values
        moved = {}
        for dx, dy, dz in sorted(terms, key=lambda key: abs(key[2])):
            if (0, 0, dz) not in moved:
                moved[0, 0, dz] = buffer[pl.ds(2 * (POWER + dz), self.rows, 2), :] if dz else values
            if dx or dy:
                moved[dx, dy, dz] = roll(moved[0, 0, dz], -(dx * self.ny + dy), 1)
        return tree_sum([base] + [coef * moved[key] for key, coef in terms.items()])

    def solve(self, right, perm, level, buffer):
        buffer[...] = jnp.zeros_like(buffer)
        terms, const = self.system(right, perm, level)
        power, base = terms, const
        for _ in range(POWER - 1):
            base = self.apply(terms, base, const, buffer)
            power = self.product(terms, power)
        whole = COARSE_SWEEPS % POWER == 0
        start = base if whole else const
        steps = (COARSE_SWEEPS - 1) // POWER
        assert steps * POWER + (POWER if whole else 1) == COARSE_SWEEPS
        return lax.fori_loop(
            0, steps, lambda step, values: self.apply(power, values, base, buffer), start
        )


def tree_sum(parts):
    while len(parts) > 1:
        odd = parts[len(parts) // 2 * 2 :]
        parts = [a + b for a, b in zip(parts[::2], parts[1::2])] + odd
    return parts[0]


def packed_cycle(grid, right, perm, level, pads, store):
    pad_right, pad_perm = pads[0]
    coefs, const, diagonals = grid.system(right, perm, level)
    values = grid.sweep(const, coefs, const)
    scaled = grid.apply(values, coefs, [c - OMEGA * v for c, v in zip(const, values)])
    residue = [r * d for r, d in zip(scaled, diagonals)]
    if len(pads) > 1:
        coarse_right, coarse_perm = grid.restrict((residue, perm), (pad_right, pad_perm))
        coarse_perm = [x * 0.125 for x in coarse_perm]
        update = packed_cycle(grid.coarser(), coarse_right, coarse_perm, level + 1, pads[1:], store)
        update = grid.prolong(update, pad_right)
    else:
        pack, buffer = store
        flat = Flat(grid)
        coarse_right, coarse_perm = flat.restrict((residue, perm), (pad_right, pad_perm), pack)
        update = flat.solve(coarse_right, coarse_perm * 0.125, level + 1, buffer)
        update = flat.prolong(update, pad_right, pack)
    values = [v + e for v, e in zip(values, update)]
    for _ in range(2):
        values = grid.sweep(values, coefs, const)
    return values


def coarse_kernel(
    dom_ref, gathered, coef, const, before, out,
    level, first, pad_right1, pad_perm1, pad_right2, pad_perm2, update, pack, buffer,
):
    height = out.shape[0]
    dom = dom_ref[0]
    domains, own, nx, _ = gathered.shape
    ny = LANES // 2
    grid = Packed(domains * own, nx, ny)
    left = iota((nx, LANES), 1) < ny
    right, perm = [], []
    for p in range(grid.planes):
        a = gathered[p // own, p % own]
        q = grid.planes + p
        b = gathered[q // own, q % own]
        right.append(jnp.where(left, a, roll(b, ny, 1)))
        perm.append(jnp.where(left, roll(a, ny, 1), b))
    pads = [(pad_right1, pad_perm1), (pad_right2, pad_perm2)]
    solved = packed_cycle(grid, right, perm, 1, pads, (pack, buffer))
    for p in range(grid.planes):
        update[p] = solved[p]
    planes, group = [], []
    for j in range(own + 2):
        layer = jnp.clip(dom * own + j - 1, 0, grid.nz - 1)
        group.append(layer // grid.planes)
        planes.append(update[lax.rem(layer, grid.planes)])
    for j, wide in enumerate(selector_dot(planes, lane_selector(1, LANES, 2, spread=True))):
        plane = jnp.where(group[j] == 0, wide[:, :LANES], wide[:, LANES:])
        pad = first.at[0]
        pad[pl.ds(0, nx, 2), :] = plane
        pad[pl.ds(1, nx, 2), :] = plane
        whole = first[0]
        level[2 * j] = before[2 * j] + whole
        level[2 * j + 1] = before[2 * j + 1] + whole

    def sweep(source, at, i):
        centre = source[i + 1]
        near = [coef[k, at + i] for k in range(6)]
        return stencil(centre, source[i], source[i + 2], near, KEEP * centre + const[at + i])

    def one(i):
        first[i] = sweep(level, 2, i)

    for i in range(height + 2):
        one(i)

    def two(i):
        out[i] = sweep(first, 3, i)

    for i in range(height):
        two(i)


def fine_part(dom, perm, source, layers):
    height, nx, ny = perm[0].shape
    field = lambda *lead: pltpu.VMEM(lead + (nx, ny), F32)
    vmem = pl.BlockSpec(memory_space=pltpu.VMEM)
    smem = pl.BlockSpec(memory_space=pltpu.SMEM)
    return pl.pallas_call(
        functools.partial(fine_kernel, layers),
        out_shape=(
            jax.ShapeDtypeStruct((6, height + 6, nx, ny), F32),
            jax.ShapeDtypeStruct((height + 6, nx, ny), F32),
            jax.ShapeDtypeStruct((height + 4, nx, ny), F32),
            jax.ShapeDtypeStruct((height // 2, nx // 2, ny), F32),
        ),
        in_specs=[smem] + [vmem] * 6,
        out_specs=(vmem,) * 4,
        scratch_shapes=[
            field(3 * height),
            field(3 * height),
            field(height + 6),
            field(height // 2),
            field(height // 2),
        ],
        compiler_params=pltpu.CompilerParams(vmem_limit_bytes=VMEM_LIMIT),
        name="fine",
    )(dom, *perm, *source)


def coarse_part(dom, gathered, coefs, const, values, height):
    _, nx, ny = values.shape
    field = lambda *shape: pltpu.VMEM(shape, F32)
    grid1 = Packed(gathered.shape[0] * gathered.shape[1], nx // 2, ny // 2)
    grid2 = grid1.coarser()
    pads1 = field(grid1.planes // 2, grid1.nx, LANES)
    pads2 = field(grid2.planes // 2, grid2.nx, LANES)
    vmem = pl.BlockSpec(memory_space=pltpu.VMEM)
    smem = pl.BlockSpec(memory_space=pltpu.SMEM)
    return pl.pallas_call(
        coarse_kernel,
        out_shape=jax.ShapeDtypeStruct((height, nx, ny), F32),
        in_specs=[smem] + [vmem] * 4,
        out_specs=vmem,
        scratch_shapes=[
            field(*values.shape),
            field(height + 2, nx, ny),
            pads1, pads1, pads2, pads2,
            field(grid1.planes, grid1.nx, LANES),
            field(2, Flat(grid2).rows, LANES),
            field(Flat(grid2).buffer_rows, LANES),
        ],
        compiler_params=pltpu.CompilerParams(vmem_limit_bytes=VMEM_LIMIT),
        name="coarse",
    )(dom, gathered, coefs, const, values)


def swaps(x, axis, step):
    return lax.ppermute(x, axis, [(i, i ^ step) for i in range(lax.axis_size(axis))])


def other_side(x):
    props, domains = lax.axis_size("prop"), lax.axis_size("dom")
    pairs = []
    for p in range(props):
        for d in range(domains):
            end = d in (0, domains - 1)
            partner = ((p ^ 1) * domains + d) if end else (p * domains + ((d + 1) ^ 1) - 1)
            pairs.append((p * domains + d, partner))
    return lax.ppermute(x, ("prop", "dom"), pairs)


def source_side(x):
    props, domains = lax.axis_size("prop"), lax.axis_size("dom")
    pairs = []
    for p in range(props):
        for d in range(domains):
            if p % 2 == 0:
                partner = p * domains + (d ^ 1)
            elif d in (0, domains - 1):
                partner = (p ^ 2) * domains + d
            else:
                partner = p * domains + ((d + 1) ^ 1) - 1
            pairs.append((p * domains + d, partner))
    return lax.ppermute(x, ("prop", "dom"), pairs)


def from_accepted(mine, accepted, beside):
    props = lax.axis_size("prop")
    step = props // 2
    own = SHRINK * mine
    offers, order = [mine], [0]
    while step:
        came = [swaps(x, "prop", step) for x in offers]
        if step == props // 2:
            came, own, beside = lax.optimization_barrier((came, own, beside))
        offers, order = offers + came, order + [x ^ step for x in order]
        step //= 2
    wanted = lax.axis_index("prop") ^ accepted
    current = offers[1]
    for at, offer in zip(order[2:], offers[2:]):
        current = jnp.where(wanted == at, offer, current)
    return jnp.where(wanted == 0, own, SHRINK * current), beside


def gather_parts(mine):
    domains = lax.axis_size("dom")
    copies = jnp.broadcast_to(mine[None], (domains,) + mine.shape)
    return lax.all_to_all(copies, "dom", 0, 0)


def body(states, accepted, noise, source):
    domains = lax.axis_size("dom")
    height = source.shape[0]
    dom = jnp.stack([lax.axis_index("dom"), lax.axis_index("prop")]).astype(jnp.int32)
    near = source_side(source)
    beside = (OMEGA * source, BETA * noise[0])
    current, (scaled, noise_part) = from_accepted(states[0], accepted[0], beside)
    perm = jnp.exp(current + noise_part)
    perms = (perm, swaps(perm, "dom", 1), other_side(perm))
    sources = (scaled, near, swaps(near, "prop", 1))
    *level, coarse = fine_part(dom, perms, sources, domains * height)
    return coarse_part(dom, gather_parts(coarse), *level, height)[None]


def solution(mesh):
    in_specs = (
        P("prop", "dom", None, None),
        P(),
        P("prop", "dom", None, None),
        P("dom", None, None),
    )
    out_specs = P("prop", "dom", None, None)
    return jax.shard_map(body, mesh=mesh, in_specs=in_specs, out_specs=out_specs, check_vma=False)
```

```python
import functools
import math

import jax
import jax.numpy as jnp
from jax import lax
from jax.experimental import pallas as pl
from jax.experimental.pallas import tpu as pltpu
from jax.sharding import PartitionSpec as P

COARSE_SWEEPS = 64
POWER = 3
OMEGA = 0.7
KEEP = 1.0 - OMEGA
BETA = 0.4
SHRINK = math.sqrt(1.0 - BETA * BETA)
ZSCALE = 16.0
LANES = 128
VMEM_LIMIT = 40 * 1024 * 1024
F32 = jnp.float32
WEST, EAST, SOUTH, NORTH, BELOW, ABOVE, CONST = range(7)


def iota(shape, dim):
    return lax.broadcasted_iota(jnp.int32, shape, dim)


def roll(x, amount, axis):
    axis = axis % x.ndim
    return pltpu.roll(x, amount % x.shape[axis], axis)


def inverse_of(x):
    guess = pl.reciprocal(x, approx=True)
    return guess * (2.0 - x * guess)


def harmonic(a, b):
    return (2.0 * a) * b * inverse_of(a + b)


def selector_dot(parts, selector):
    x = jnp.concatenate(parts, axis=0) if len(parts) > 1 else parts[0]
    rows = x.shape[0]
    high = x.astype(jnp.bfloat16).astype(F32)
    rest = x - high
    middle = rest.astype(jnp.bfloat16).astype(F32)
    terms = jnp.concatenate([high, middle, rest - middle], axis=0).astype(jnp.bfloat16)
    y = jnp.dot(terms, selector, preferred_element_type=F32)
    total = y[:rows] + y[rows : 2 * rows] + y[2 * rows :]
    height = parts[0].shape[0]
    return [total[i * height : (i + 1) * height] for i in range(len(parts))]


def face_terms(perm, lower, upper, below_scale, above_scale, ny):
    shape = perm.shape
    rows = iota(shape, 0)
    columns = iota(shape, 1) & (ny - 1)
    west = jnp.where(rows == 0, 0.0, harmonic(perm, roll(perm, 1, 0)))
    east = roll(west, -1, 0)
    south = jnp.where(columns == 0, 0.0, harmonic(perm, roll(perm, 1, 1)))
    north = roll(south, -1, 1)
    below = below_scale * harmonic(perm, lower)
    above = above_scale * harmonic(perm, upper)
    ends = jnp.where(rows == 0, perm, 0.0) + jnp.where(rows == shape[0] - 1, perm, 0.0)
    ends = ends + jnp.where(columns == 0, perm, 0.0) + jnp.where(columns == ny - 1, perm, 0.0)
    diagonal = ((west + east) + (south + north)) + ((below + above) + ends)
    return (west, east, south, north, below, above), diagonal


def stencil(values, lower, upper, coefs, base):
    x = coefs[0] * roll(values, 1, 0) + coefs[1] * roll(values, -1, 0)
    y = coefs[2] * roll(values, 1, 1) + coefs[3] * roll(values, -1, 1)
    z = coefs[4] * lower + coefs[5] * upper
    return (x + y) + (z + base)


def lane_selector(groups, ny, step, spread=False):
    shape = (LANES, step * LANES) if spread else (step * LANES, LANES)
    source, target = iota(shape, int(spread)), iota(shape, 1 - int(spread))
    bits = ny.bit_length() - 1
    lane = source & (LANES - 1)
    group = (lane >> bits) * step + (source >> 7)
    wanted = (group << (bits - 1)) + ((lane & (ny - 1)) >> 1)
    return jnp.where((target == wanted) & (lane < groups * ny), 1.0, 0.0).astype(jnp.bfloat16)


def fine_kernel(
    layers,
    dom_ref,
    per, per_pair, per_other,
    src, src_near, src_next,
    coef, const, values, coarse_out,
    perm, right, diag, pair_right, pair_perm,
):
    height = per.shape[0]
    dom = dom_ref[0]
    pair_at = jnp.where(lax.rem(dom, 2) == 0, 2 * height, 0)
    other_at = 2 * height - pair_at

    near_at = jnp.where(lax.rem(dom_ref[1], 2) == 0, pair_at, other_at)
    next_at = 2 * height - near_at
    for i in range(height):
        for at, p in ((height, per), (pair_at, per_pair), (other_at, per_other)):
            perm[at + i] = p[i]
        right[height + i] = src[i]
        right[near_at + i] = OMEGA * src_near[i]
        right[next_at + i] = OMEGA * src_next[i]

    def build(i):
        z = dom * height + i - 3
        below = jnp.where((z > 0) & (z < layers), ZSCALE, 0.0)
        above = jnp.where((z + 1 > 0) & (z + 1 < layers), ZSCALE, 0.0)
        at = height - 3 + i
        faces, diagonal = face_terms(perm[at], perm[at - 1], perm[at + 1], below, above, LANES)
        inverse = inverse_of(diagonal)
        const[i] = inverse * right[at]
        inverse = OMEGA * inverse
        for k in range(6):
            coef[k, i] = inverse * faces[k]
        diag[i] = diagonal

    for i in range(height + 6):
        build(i)

    def first(i):
        start = const[i + 1]
        near = [coef[k, i + 1] for k in range(6)]
        values[i] = stencil(start, const[i], const[i + 2], near, (1.0 + KEEP) * start)

    for i in range(height + 4):
        first(i)

    def residue(i):
        centre = values[i + 2]
        base = const[i + 3] - OMEGA * centre
        near = [coef[k, i + 3] for k in range(6)]
        scaled = stencil(centre, values[i + 1], values[i + 3], near, base)
        return scaled * (diag[i + 3] * (1.0 / OMEGA))

    for m in range(height // 2):
        pair_right[m] = residue(2 * m) + residue(2 * m + 1)
        pair_perm[m] = (perm[height + 2 * m] + perm[height + 2 * m + 1]) * 0.125
    half = pair_right.shape[1] // 2
    rows = []
    for m in range(height // 2):
        both = [x[m, pl.ds(0, half, 2), :] + x[m, pl.ds(1, half, 2), :] for x in (pair_right, pair_perm)]
        rows.append(jnp.concatenate(both, axis=1))
    for m, x in enumerate(selector_dot(rows, lane_selector(1, LANES, 2))):
        coarse_out[m] = x


class Packed:
    def __init__(self, nz, nx, ny):
        self.nz, self.nx, self.ny = nz, nx, ny
        self.groups = min(LANES // ny, nz)
        self.planes = nz // self.groups

    def lower(self, planes, p):
        return planes[p - 1] if p else roll(planes[self.planes - 1], self.ny, 1)

    def upper(self, planes, p):
        return planes[p + 1] if p + 1 < self.planes else roll(planes[0], -self.ny, 1)

    def system(self, right, perm, level):
        lane = iota((self.nx, LANES), 1)
        used = lane < self.groups * self.ny
        if self.groups * self.ny < LANES:
            perm = [jnp.where(used, x, 1.0) for x in perm]
        coefs, const, diagonals = [], [], []
        for p in range(self.planes):
            below, above = ZSCALE, ZSCALE
            if p == 0:
                below = jnp.where(lane < self.ny, 0.0, ZSCALE)
            if p + 1 == self.planes:
                above = jnp.where(lane < (self.groups - 1) * self.ny, ZSCALE, 0.0)
            faces, diagonal = face_terms(
                perm[p], self.lower(perm, p), self.upper(perm, p), below, above, self.ny
            )
            inverse = OMEGA * inverse_of(diagonal)
            coefs.append([inverse * face for face in faces])
            const.append(inverse * right[p] * (4.0**-level))
            diagonals.append(diagonal * (4.0**level / OMEGA))
        return coefs, const, diagonals

    def apply(self, values, coefs, bases):
        return [
            stencil(values[p], self.lower(values, p), self.upper(values, p), coefs[p], bases[p])
            for p in range(self.planes)
        ]

    def sweep(self, values, coefs, const):
        return self.apply(values, coefs, [KEEP * v + c for v, c in zip(values, const)])

    def coarser(self):
        return Packed(self.nz // 2, self.nx // 2, self.ny // 2)

    def restrict(self, fields, pads):
        coarse = self.coarser()
        step = coarse.groups // self.groups
        half = coarse.nx
        parts = []
        for values, pad in zip(fields, pads):
            rows = []
            for m in range(self.planes // 2):
                pad[m] = values[2 * m] + values[2 * m + 1]
                rows.append(pad[m, pl.ds(0, half, 2), :] + pad[m, pl.ds(1, half, 2), :])
            for p in range(coarse.planes):
                blocks = rows[p :: coarse.planes]
                parts.append(jnp.concatenate(blocks, axis=1) if step > 1 else blocks[0])
        sums = selector_dot(parts, lane_selector(self.groups, self.ny, step))
        return [sums[i : i + coarse.planes] for i in range(0, len(sums), coarse.planes)]

    def prolong(self, values, pad):
        coarse = self.coarser()
        step = coarse.groups // self.groups
        half = coarse.nx
        wide = selector_dot(values, lane_selector(self.groups, self.ny, step, spread=True))
        out = []
        for m in range(self.planes // 2):
            j, p = divmod(m, coarse.planes)
            plane = wide[p][:, j * LANES : (j + 1) * LANES]
            pad[m, pl.ds(0, half, 2), :] = plane
            pad[m, pl.ds(1, half, 2), :] = plane
            out += [pad[m], pad[m]]
        return out


class Flat:
    def __init__(self, finer):
        coarse = finer.coarser()
        self.finer = finer
        self.nz, self.nx, self.ny = coarse.nz, coarse.nx, coarse.ny
        self.pairs = finer.planes // 2
        self.rows = max(8, self.nz)
        self.shape = (self.rows, LANES)
        self.buffer_rows = 2 * (self.rows + 2 * POWER)

    def selector(self, spread=False):
        wide = self.finer.groups * LANES
        shape = (wide, LANES) if spread else (LANES, wide)
        fine, flat = iota(shape, int(spread)), iota(shape, 1 - int(spread))
        bits = self.finer.ny.bit_length() - 1
        same = (fine >> bits) == (flat >> 7)
        same &= ((fine & (self.finer.ny - 1)) >> 1) == (flat & (self.ny - 1))
        return jnp.where(same, 1.0, 0.0).astype(jnp.bfloat16)

    def diagonal(self):
        shape = (self.nx, LANES)
        return iota(shape, 0) == (iota(shape, 1) >> (self.ny.bit_length() - 1))

    def restrict(self, fields, pads, pack):
        parts = []
        for values, pad in zip(fields, pads):
            for m in range(self.pairs):
                pad[m] = values[2 * m] + values[2 * m + 1]
                parts.append(pad[m, pl.ds(0, self.nx, 2), :] + pad[m, pl.ds(1, self.nx, 2), :])
        sums = selector_dot(parts, self.selector())
        mask = self.diagonal()
        pack[...] = jnp.zeros_like(pack)
        for i in range(len(fields)):
            for z in range(self.nz):
                s, m = divmod(z, self.pairs)
                block = sums[i * self.pairs + m][:, s * LANES : (s + 1) * LANES]
                row = jnp.sum(jnp.where(mask, block, 0.0), axis=0, keepdims=True)
                pack[i, z : z + 1, :] = row
        return [pack[i] for i in range(len(fields))]

    def prolong(self, values, pad, pack):
        mask = self.diagonal()
        pack[0] = values
        parts = []
        for m in range(self.pairs):
            layers = [s * self.pairs + m for s in range(self.finer.groups)]
            spread = [jnp.broadcast_to(pack[0, z : z + 1, :], mask.shape) for z in layers]
            parts.append(jnp.concatenate([jnp.where(mask, x, 0.0) for x in spread], axis=1))
        out = []
        for m, wide in enumerate(selector_dot(parts, self.selector(spread=True))):
            pad[m, pl.ds(0, self.nx, 2), :] = wide
            pad[m, pl.ds(1, self.nx, 2), :] = wide
            out += [pad[m], pad[m]]
        return out

    def system(self, right, perm, level):
        lane, row = iota(self.shape, 1), iota(self.shape, 0)
        x, y = lane >> (self.ny.bit_length() - 1), lane & (self.ny - 1)
        real = row < self.nz
        perm = jnp.where(real, perm, 1.0)
        west = jnp.where(x == 0, 0.0, harmonic(perm, roll(perm, self.ny, 1)))
        east = roll(west, -self.ny, 1)
        south = jnp.where(y == 0, 0.0, harmonic(perm, roll(perm, 1, 1)))
        north = roll(south, -1, 1)
        below = ZSCALE * harmonic(perm, roll(perm, 1, 0))
        below = jnp.where((row > 0) & real, below, 0.0)
        above = roll(below, -1, 0)
        faces = [west, east, south, north, below, above]
        ends = (x == 0, x == self.nx - 1, y == 0, y == self.ny - 1)
        diagonal = tree_sum(faces + [jnp.where(end, perm, 0.0) for end in ends])
        inverse = jnp.where(real, OMEGA * inverse_of(diagonal), 0.0)
        keys = ((-1, 0, 0), (1, 0, 0), (0, -1, 0), (0, 1, 0), (0, 0, -1), (0, 0, 1))
        terms = {key: inverse * face for key, face in zip(keys, faces)}
        terms[0, 0, 0] = jnp.full(self.shape, KEEP, F32)
        return terms, inverse * right * (4.0**-level)

    def product(self, first, second):
        sums = {}
        for (dx, dy, dz), coef in first.items():
            for other, moved in second.items():
                if dz:
                    moved = roll(moved, -dz, 0)
                if dx or dy:
                    moved = roll(moved, -(dx * self.ny + dy), 1)
                total = tuple(a + b for a, b in zip((dx, dy, dz), other))
                sums.setdefault(total, []).append(coef * moved)
        return {key: tree_sum(parts) for key, parts in sums.items()}

    def apply(self, terms, values, base, buffer):
        buffer[pl.ds(2 * POWER, self.rows, 2), :] = values
        moved = {}
        for dx, dy, dz in sorted(terms, key=lambda key: abs(key[2])):
            if (0, 0, dz) not in moved:
                moved[0, 0, dz] = buffer[pl.ds(2 * (POWER + dz), self.rows, 2), :] if dz else values
            if dx or dy:
                moved[dx, dy, dz] = roll(moved[0, 0, dz], -(dx * self.ny + dy), 1)
        return tree_sum([base] + [coef * moved[key] for key, coef in terms.items()])

    def solve(self, right, perm, level, buffer):
        buffer[...] = jnp.zeros_like(buffer)
        terms, const = self.system(right, perm, level)
        power, base = terms, const
        for _ in range(POWER - 1):
            base = self.apply(terms, base, const, buffer)
            power = self.product(terms, power)
        whole = COARSE_SWEEPS % POWER == 0
        start = base if whole else const
        steps = (COARSE_SWEEPS - 1) // POWER
        assert steps * POWER + (POWER if whole else 1) == COARSE_SWEEPS
        return lax.fori_loop(
            0, steps, lambda step, values: self.apply(power, values, base, buffer), start
        )


def tree_sum(parts):
    while len(parts) > 1:
        odd = parts[len(parts) // 2 * 2 :]
        parts = [a + b for a, b in zip(parts[::2], parts[1::2])] + odd
    return parts[0]


def packed_cycle(grid, right, perm, level, pads, store):
    pad_right, pad_perm = pads[0]
    coefs, const, diagonals = grid.system(right, perm, level)
    values = grid.sweep(const, coefs, const)
    scaled = grid.apply(values, coefs, [c - OMEGA * v for c, v in zip(const, values)])
    residue = [r * d for r, d in zip(scaled, diagonals)]
    if len(pads) > 1:
        coarse_right, coarse_perm = grid.restrict((residue, perm), (pad_right, pad_perm))
        coarse_perm = [x * 0.125 for x in coarse_perm]
        update = packed_cycle(grid.coarser(), coarse_right, coarse_perm, level + 1, pads[1:], store)
        update = grid.prolong(update, pad_right)
    else:
        pack, buffer = store
        flat = Flat(grid)
        coarse_right, coarse_perm = flat.restrict((residue, perm), (pad_right, pad_perm), pack)
        update = flat.solve(coarse_right, coarse_perm * 0.125, level + 1, buffer)
        update = flat.prolong(update, pad_right, pack)
    values = [v + e for v, e in zip(values, update)]
    for _ in range(2):
        values = grid.sweep(values, coefs, const)
    return values


def coarse_kernel(
    dom_ref, gathered, coef, const, before, out,
    level, first, pad_right1, pad_perm1, pad_right2, pad_perm2, update, pack, buffer,
):
    height = out.shape[0]
    dom = dom_ref[0]
    domains, own, nx, _ = gathered.shape
    ny = LANES // 2
    grid = Packed(domains * own, nx, ny)
    left = iota((nx, LANES), 1) < ny
    right, perm = [], []
    for p in range(grid.planes):
        a = gathered[p // own, p % own]
        q = grid.planes + p
        b = gathered[q // own, q % own]
        right.append(jnp.where(left, a, roll(b, ny, 1)))
        perm.append(jnp.where(left, roll(a, ny, 1), b))
    pads = [(pad_right1, pad_perm1), (pad_right2, pad_perm2)]
    solved = packed_cycle(grid, right, perm, 1, pads, (pack, buffer))
    for p in range(grid.planes):
        update[p] = solved[p]
    planes, group = [], []
    for j in range(own + 2):
        layer = jnp.clip(dom * own + j - 1, 0, grid.nz - 1)
        group.append(layer // grid.planes)
        planes.append(update[lax.rem(layer, grid.planes)])
    for j, wide in enumerate(selector_dot(planes, lane_selector(1, LANES, 2, spread=True))):
        plane = jnp.where(group[j] == 0, wide[:, :LANES], wide[:, LANES:])
        pad = first.at[0]
        pad[pl.ds(0, nx, 2), :] = plane
        pad[pl.ds(1, nx, 2), :] = plane
        whole = first[0]
        level[2 * j] = before[2 * j] + whole
        level[2 * j + 1] = before[2 * j + 1] + whole

    def sweep(source, at, i):
        centre = source[i + 1]
        near = [coef[k, at + i] for k in range(6)]
        return stencil(centre, source[i], source[i + 2], near, KEEP * centre + const[at + i])

    def one(i):
        first[i] = sweep(level, 2, i)

    for i in range(height + 2):
        one(i)

    def two(i):
        out[i] = sweep(first, 3, i)

    for i in range(height):
        two(i)


def fine_part(dom, perm, source, layers):
    height, nx, ny = perm[0].shape
    field = lambda *lead: pltpu.VMEM(lead + (nx, ny), F32)
    vmem = pl.BlockSpec(memory_space=pltpu.VMEM)
    smem = pl.BlockSpec(memory_space=pltpu.SMEM)
    return pl.pallas_call(
        functools.partial(fine_kernel, layers),
        out_shape=(
            jax.ShapeDtypeStruct((6, height + 6, nx, ny), F32),
            jax.ShapeDtypeStruct((height + 6, nx, ny), F32),
            jax.ShapeDtypeStruct((height + 4, nx, ny), F32),
            jax.ShapeDtypeStruct((height // 2, nx // 2, ny), F32),
        ),
        in_specs=[smem] + [vmem] * 6,
        out_specs=(vmem,) * 4,
        scratch_shapes=[
            field(3 * height),
            field(3 * height),
            field(height + 6),
            field(height // 2),
            field(height // 2),
        ],
        compiler_params=pltpu.CompilerParams(vmem_limit_bytes=VMEM_LIMIT),
        name="fine",
    )(dom, *perm, *source)


def coarse_part(dom, gathered, coefs, const, values, height):
    _, nx, ny = values.shape
    field = lambda *shape: pltpu.VMEM(shape, F32)
    grid1 = Packed(gathered.shape[0] * gathered.shape[1], nx // 2, ny // 2)
    grid2 = grid1.coarser()
    pads1 = field(grid1.planes // 2, grid1.nx, LANES)
    pads2 = field(grid2.planes // 2, grid2.nx, LANES)
    vmem = pl.BlockSpec(memory_space=pltpu.VMEM)
    smem = pl.BlockSpec(memory_space=pltpu.SMEM)
    return pl.pallas_call(
        coarse_kernel,
        out_shape=jax.ShapeDtypeStruct((height, nx, ny), F32),
        in_specs=[smem] + [vmem] * 4,
        out_specs=vmem,
        scratch_shapes=[
            field(*values.shape),
            field(height + 2, nx, ny),
            pads1, pads1, pads2, pads2,
            field(grid1.planes, grid1.nx, LANES),
            field(2, Flat(grid2).rows, LANES),
            field(Flat(grid2).buffer_rows, LANES),
        ],
        compiler_params=pltpu.CompilerParams(vmem_limit_bytes=VMEM_LIMIT),
        name="coarse",
    )(dom, gathered, coefs, const, values)


def swaps(x, axis, step):
    return lax.ppermute(x, axis, [(i, i ^ step) for i in range(lax.axis_size(axis))])


def other_side(x):
    props, domains = lax.axis_size("prop"), lax.axis_size("dom")
    pairs = []
    for p in range(props):
        for d in range(domains):
            end = d in (0, domains - 1)
            partner = ((p ^ 1) * domains + d) if end else (p * domains + ((d + 1) ^ 1) - 1)
            pairs.append((p * domains + d, partner))
    return lax.ppermute(x, ("prop", "dom"), pairs)


def source_side(x):
    props, domains = lax.axis_size("prop"), lax.axis_size("dom")
    pairs = []
    for p in range(props):
        for d in range(domains):
            if p % 2 == 0:
                partner = p * domains + (d ^ 1)
            elif d in (0, domains - 1):
                partner = (p ^ 2) * domains + d
            else:
                partner = p * domains + ((d + 1) ^ 1) - 1
            pairs.append((p * domains + d, partner))
    return lax.ppermute(x, ("prop", "dom"), pairs)


def from_accepted(mine, accepted, beside):
    props = lax.axis_size("prop")
    step = props // 2
    own = SHRINK * mine
    offers, order = [mine], [0]
    while step:
        came = [swaps(x, "prop", step) for x in offers]
        if step == props // 2:
            came, own, beside = lax.optimization_barrier((came, own, beside))
        offers, order = offers + came, order + [x ^ step for x in order]
        step //= 2
    wanted = lax.axis_index("prop") ^ accepted
    current = offers[1]
    for at, offer in zip(order[2:], offers[2:]):
        current = jnp.where(wanted == at, offer, current)
    return jnp.where(wanted == 0, own, SHRINK * current), beside


def gather_parts(mine):
    domains = lax.axis_size("dom")
    copies = jnp.broadcast_to(mine[None], (domains,) + mine.shape)
    return lax.all_to_all(copies, "dom", 0, 0)


def body(states, accepted, noise, source):
    domains = lax.axis_size("dom")
    height = source.shape[0]
    dom = jnp.stack([lax.axis_index("dom"), lax.axis_index("prop")]).astype(jnp.int32)
    near = source_side(source)
    beside = (OMEGA * source, BETA * noise[0])
    current, (scaled, noise_part) = from_accepted(states[0], accepted[0], beside)
    perm = jnp.exp(current + noise_part)
    perms = (perm, swaps(perm, "dom", 1), other_side(perm))
    sources = (scaled, near, swaps(near, "prop", 1))
    *level, coarse = fine_part(dom, perms, sources, domains * height)
    return coarse_part(dom, gather_parts(coarse), *level, height)[None]


def solution(mesh):
    in_specs = (
        P("prop", "dom", None, None),
        P(),
        P("prop", "dom", None, None),
        P("dom", None, None),
    )
    out_specs = P("prop", "dom", None, None)
    return jax.shard_map(body, mesh=mesh, in_specs=in_specs, out_specs=out_specs, check_vma=False)
```

```python
import functools
import math

import jax
import jax.numpy as jnp
from jax import lax
from jax.experimental import pallas as pl
from jax.experimental.pallas import tpu as pltpu
from jax.sharding import PartitionSpec as P

COARSE_SWEEPS = 64
POWER = 2
OMEGA = 0.7
KEEP = 1.0 - OMEGA
BETA = 0.4
SHRINK = math.sqrt(1.0 - BETA * BETA)
ZSCALE = 16.0
LANES = 128
VMEM_LIMIT = 40 * 1024 * 1024
F32 = jnp.float32
WEST, EAST, SOUTH, NORTH, BELOW, ABOVE, CONST = range(7)


def iota(shape, dim):
    return lax.broadcasted_iota(jnp.int32, shape, dim)


def roll(x, amount, axis):
    axis = axis % x.ndim
    return pltpu.roll(x, amount % x.shape[axis], axis)


def inverse_of(x):
    guess = pl.reciprocal(x, approx=True)
    return guess * (2.0 - x * guess)


def harmonic(a, b):
    return (2.0 * a) * b * inverse_of(a + b)


def selector_dot(parts, selector):
    x = jnp.concatenate(parts, axis=0) if len(parts) > 1 else parts[0]
    rows = x.shape[0]
    high = x.astype(jnp.bfloat16).astype(F32)
    rest = x - high
    middle = rest.astype(jnp.bfloat16).astype(F32)
    terms = jnp.concatenate([high, middle, rest - middle], axis=0).astype(jnp.bfloat16)
    y = jnp.dot(terms, selector, preferred_element_type=F32)
    total = y[:rows] + y[rows : 2 * rows] + y[2 * rows :]
    height = parts[0].shape[0]
    return [total[i * height : (i + 1) * height] for i in range(len(parts))]


def face_terms(perm, lower, upper, below_scale, above_scale, ny):
    shape = perm.shape
    rows = iota(shape, 0)
    columns = iota(shape, 1) & (ny - 1)
    west = jnp.where(rows == 0, 0.0, harmonic(perm, roll(perm, 1, 0)))
    east = roll(west, -1, 0)
    south = jnp.where(columns == 0, 0.0, harmonic(perm, roll(perm, 1, 1)))
    north = roll(south, -1, 1)
    below = below_scale * harmonic(perm, lower)
    above = above_scale * harmonic(perm, upper)
    ends = jnp.where(rows == 0, perm, 0.0) + jnp.where(rows == shape[0] - 1, perm, 0.0)
    ends = ends + jnp.where(columns == 0, perm, 0.0) + jnp.where(columns == ny - 1, perm, 0.0)
    diagonal = ((west + east) + (south + north)) + ((below + above) + ends)
    return (west, east, south, north, below, above), diagonal


def stencil(values, lower, upper, coefs, base):
    x = coefs[0] * roll(values, 1, 0) + coefs[1] * roll(values, -1, 0)
    y = coefs[2] * roll(values, 1, 1) + coefs[3] * roll(values, -1, 1)
    z = coefs[4] * lower + coefs[5] * upper
    return (x + y) + (z + base)


def lane_selector(groups, ny, step, spread=False):
    shape = (LANES, step * LANES) if spread else (step * LANES, LANES)
    source, target = iota(shape, int(spread)), iota(shape, 1 - int(spread))
    bits = ny.bit_length() - 1
    lane = source & (LANES - 1)
    group = (lane >> bits) * step + (source >> 7)
    wanted = (group << (bits - 1)) + ((lane & (ny - 1)) >> 1)
    return jnp.where((target == wanted) & (lane < groups * ny), 1.0, 0.0).astype(jnp.bfloat16)


def fine_kernel(
    layers,
    dom_ref,
    per, per_pair, per_other,
    src, src_near, src_next,
    coef, const, values, coarse_out,
    perm, right, diag, pair_right, pair_perm,
):
    height = per.shape[0]
    dom = dom_ref[0]
    pair_at = jnp.where(lax.rem(dom, 2) == 0, 2 * height, 0)
    other_at = 2 * height - pair_at

    near_at = jnp.where(lax.rem(dom_ref[1], 2) == 0, pair_at, other_at)
    next_at = 2 * height - near_at
    for i in range(height):
        for at, p in ((height, per), (pair_at, per_pair), (other_at, per_other)):
            perm[at + i] = p[i]
        right[height + i] = src[i]
        right[near_at + i] = OMEGA * src_near[i]
        right[next_at + i] = OMEGA * src_next[i]

    def build(i):
        z = dom * height + i - 3
        below = jnp.where((z > 0) & (z < layers), ZSCALE, 0.0)
        above = jnp.where((z + 1 > 0) & (z + 1 < layers), ZSCALE, 0.0)
        at = height - 3 + i
        faces, diagonal = face_terms(perm[at], perm[at - 1], perm[at + 1], below, above, LANES)
        inverse = inverse_of(diagonal)
        const[i] = inverse * right[at]
        inverse = OMEGA * inverse
        for k in range(6):
            coef[k, i] = inverse * faces[k]
        diag[i] = diagonal

    for i in range(height + 6):
        build(i)

    def first(i):
        start = const[i + 1]
        near = [coef[k, i + 1] for k in range(6)]
        values[i] = stencil(start, const[i], const[i + 2], near, (1.0 + KEEP) * start)

    for i in range(height + 4):
        first(i)

    def residue(i):
        centre = values[i + 2]
        base = const[i + 3] - OMEGA * centre
        near = [coef[k, i + 3] for k in range(6)]
        scaled = stencil(centre, values[i + 1], values[i + 3], near, base)
        return scaled * (diag[i + 3] * (1.0 / OMEGA))

    for m in range(height // 2):
        pair_right[m] = residue(2 * m) + residue(2 * m + 1)
        pair_perm[m] = (perm[height + 2 * m] + perm[height + 2 * m + 1]) * 0.125
    half = pair_right.shape[1] // 2
    rows = []
    for m in range(height // 2):
        both = [x[m, pl.ds(0, half, 2), :] + x[m, pl.ds(1, half, 2), :] for x in (pair_right, pair_perm)]
        rows.append(jnp.concatenate(both, axis=1))
    for m, x in enumerate(selector_dot(rows, lane_selector(1, LANES, 2))):
        coarse_out[m] = x


class Packed:
    def __init__(self, nz, nx, ny):
        self.nz, self.nx, self.ny = nz, nx, ny
        self.groups = min(LANES // ny, nz)
        self.planes = nz // self.groups

    def lower(self, planes, p):
        return planes[p - 1] if p else roll(planes[self.planes - 1], self.ny, 1)

    def upper(self, planes, p):
        return planes[p + 1] if p + 1 < self.planes else roll(planes[0], -self.ny, 1)

    def system(self, right, perm, level):
        lane = iota((self.nx, LANES), 1)
        used = lane < self.groups * self.ny
        if self.groups * self.ny < LANES:
            perm = [jnp.where(used, x, 1.0) for x in perm]
        coefs, const, diagonals = [], [], []
        for p in range(self.planes):
            below, above = ZSCALE, ZSCALE
            if p == 0:
                below = jnp.where(lane < self.ny, 0.0, ZSCALE)
            if p + 1 == self.planes:
                above = jnp.where(lane < (self.groups - 1) * self.ny, ZSCALE, 0.0)
            faces, diagonal = face_terms(
                perm[p], self.lower(perm, p), self.upper(perm, p), below, above, self.ny
            )
            inverse = OMEGA * inverse_of(diagonal)
            coefs.append([inverse * face for face in faces])
            const.append(inverse * right[p] * (4.0**-level))
            diagonals.append(diagonal * (4.0**level / OMEGA))
        return coefs, const, diagonals

    def apply(self, values, coefs, bases):
        return [
            stencil(values[p], self.lower(values, p), self.upper(values, p), coefs[p], bases[p])
            for p in range(self.planes)
        ]

    def sweep(self, values, coefs, const):
        return self.apply(values, coefs, [KEEP * v + c for v, c in zip(values, const)])

    def coarser(self):
        return Packed(self.nz // 2, self.nx // 2, self.ny // 2)

    def restrict(self, fields, pads):
        coarse = self.coarser()
        step = coarse.groups // self.groups
        half = coarse.nx
        parts = []
        for values, pad in zip(fields, pads):
            rows = []
            for m in range(self.planes // 2):
                pad[m] = values[2 * m] + values[2 * m + 1]
                rows.append(pad[m, pl.ds(0, half, 2), :] + pad[m, pl.ds(1, half, 2), :])
            for p in range(coarse.planes):
                blocks = rows[p :: coarse.planes]
                parts.append(jnp.concatenate(blocks, axis=1) if step > 1 else blocks[0])
        sums = selector_dot(parts, lane_selector(self.groups, self.ny, step))
        return [sums[i : i + coarse.planes] for i in range(0, len(sums), coarse.planes)]

    def prolong(self, values, pad):
        coarse = self.coarser()
        step = coarse.groups // self.groups
        half = coarse.nx
        wide = selector_dot(values, lane_selector(self.groups, self.ny, step, spread=True))
        out = []
        for m in range(self.planes // 2):
            j, p = divmod(m, coarse.planes)
            plane = wide[p][:, j * LANES : (j + 1) * LANES]
            pad[m, pl.ds(0, half, 2), :] = plane
            pad[m, pl.ds(1, half, 2), :] = plane
            out += [pad[m], pad[m]]
        return out


class Flat:
    def __init__(self, finer):
        coarse = finer.coarser()
        self.finer = finer
        self.nz, self.nx, self.ny = coarse.nz, coarse.nx, coarse.ny
        self.pairs = finer.planes // 2
        self.rows = max(8, self.nz)
        self.shape = (self.rows, LANES)
        self.buffer_rows = 2 * (self.rows + 2 * POWER)

    def selector(self, spread=False):
        wide = self.finer.groups * LANES
        shape = (wide, LANES) if spread else (LANES, wide)
        fine, flat = iota(shape, int(spread)), iota(shape, 1 - int(spread))
        bits = self.finer.ny.bit_length() - 1
        same = (fine >> bits) == (flat >> 7)
        same &= ((fine & (self.finer.ny - 1)) >> 1) == (flat & (self.ny - 1))
        return jnp.where(same, 1.0, 0.0).astype(jnp.bfloat16)

    def diagonal(self):
        shape = (self.nx, LANES)
        return iota(shape, 0) == (iota(shape, 1) >> (self.ny.bit_length() - 1))

    def restrict(self, fields, pads, pack):
        parts = []
        for values, pad in zip(fields, pads):
            for m in range(self.pairs):
                pad[m] = values[2 * m] + values[2 * m + 1]
                parts.append(pad[m, pl.ds(0, self.nx, 2), :] + pad[m, pl.ds(1, self.nx, 2), :])
        sums = selector_dot(parts, self.selector())
        mask = self.diagonal()
        pack[...] = jnp.zeros_like(pack)
        for i in range(len(fields)):
            for z in range(self.nz):
                s, m = divmod(z, self.pairs)
                block = sums[i * self.pairs + m][:, s * LANES : (s + 1) * LANES]
                row = jnp.sum(jnp.where(mask, block, 0.0), axis=0, keepdims=True)
                pack[i, z : z + 1, :] = row
        return [pack[i] for i in range(len(fields))]

    def prolong(self, values, pad, pack):
        mask = self.diagonal()
        pack[0] = values
        parts = []
        for m in range(self.pairs):
            layers = [s * self.pairs + m for s in range(self.finer.groups)]
            spread = [jnp.broadcast_to(pack[0, z : z + 1, :], mask.shape) for z in layers]
            parts.append(jnp.concatenate([jnp.where(mask, x, 0.0) for x in spread], axis=1))
        out = []
        for m, wide in enumerate(selector_dot(parts, self.selector(spread=True))):
            pad[m, pl.ds(0, self.nx, 2), :] = wide
            pad[m, pl.ds(1, self.nx, 2), :] = wide
            out += [pad[m], pad[m]]
        return out

    def system(self, right, perm, level):
        lane, row = iota(self.shape, 1), iota(self.shape, 0)
        x, y = lane >> (self.ny.bit_length() - 1), lane & (self.ny - 1)
        real = row < self.nz
        perm = jnp.where(real, perm, 1.0)
        west = jnp.where(x == 0, 0.0, harmonic(perm, roll(perm, self.ny, 1)))
        east = roll(west, -self.ny, 1)
        south = jnp.where(y == 0, 0.0, harmonic(perm, roll(perm, 1, 1)))
        north = roll(south, -1, 1)
        below = ZSCALE * harmonic(perm, roll(perm, 1, 0))
        below = jnp.where((row > 0) & real, below, 0.0)
        above = roll(below, -1, 0)
        faces = [west, east, south, north, below, above]
        ends = (x == 0, x == self.nx - 1, y == 0, y == self.ny - 1)
        diagonal = tree_sum(faces + [jnp.where(end, perm, 0.0) for end in ends])
        inverse = jnp.where(real, OMEGA * inverse_of(diagonal), 0.0)
        keys = ((-1, 0, 0), (1, 0, 0), (0, -1, 0), (0, 1, 0), (0, 0, -1), (0, 0, 1))
        terms = {key: inverse * face for key, face in zip(keys, faces)}
        terms[0, 0, 0] = jnp.full(self.shape, KEEP, F32)
        return terms, inverse * right * (4.0**-level)

    def product(self, first, second):
        sums = {}
        for (dx, dy, dz), coef in first.items():
            for other, moved in second.items():
                if dz:
                    moved = roll(moved, -dz, 0)
                if dx or dy:
                    moved = roll(moved, -(dx * self.ny + dy), 1)
                total = tuple(a + b for a, b in zip((dx, dy, dz), other))
                sums.setdefault(total, []).append(coef * moved)
        return {key: tree_sum(parts) for key, parts in sums.items()}

    def apply(self, terms, values, base, buffer):
        buffer[pl.ds(2 * POWER, self.rows, 2), :] = values
        moved = {}
        for dx, dy, dz in sorted(terms, key=lambda key: abs(key[2])):
            if (0, 0, dz) not in moved:
                moved[0, 0, dz] = buffer[pl.ds(2 * (POWER + dz), self.rows, 2), :] if dz else values
            if dx or dy:
                moved[dx, dy, dz] = roll(moved[0, 0, dz], -(dx * self.ny + dy), 1)
        return tree_sum([base] + [coef * moved[key] for key, coef in terms.items()])

    def solve(self, right, perm, level, buffer):
        buffer[...] = jnp.zeros_like(buffer)
        terms, const = self.system(right, perm, level)
        power, base = terms, const
        for _ in range(POWER - 1):
            base = self.apply(terms, base, const, buffer)
            power = self.product(terms, power)
        whole = COARSE_SWEEPS % POWER == 0
        start = base if whole else const
        steps = (COARSE_SWEEPS - 1) // POWER
        assert steps * POWER + (POWER if whole else 1) == COARSE_SWEEPS
        return lax.fori_loop(
            0, steps, lambda step, values: self.apply(power, values, base, buffer), start
        )


def tree_sum(parts):
    while len(parts) > 1:
        odd = parts[len(parts) // 2 * 2 :]
        parts = [a + b for a, b in zip(parts[::2], parts[1::2])] + odd
    return parts[0]


def packed_cycle(grid, right, perm, level, pads, store):
    pad_right, pad_perm = pads[0]
    coefs, const, diagonals = grid.system(right, perm, level)
    values = grid.sweep(const, coefs, const)
    scaled = grid.apply(values, coefs, [c - OMEGA * v for c, v in zip(const, values)])
    residue = [r * d for r, d in zip(scaled, diagonals)]
    if len(pads) > 1:
        coarse_right, coarse_perm = grid.restrict((residue, perm), (pad_right, pad_perm))
        coarse_perm = [x * 0.125 for x in coarse_perm]
        update = packed_cycle(grid.coarser(), coarse_right, coarse_perm, level + 1, pads[1:], store)
        update = grid.prolong(update, pad_right)
    else:
        pack, buffer = store
        flat = Flat(grid)
        coarse_right, coarse_perm = flat.restrict((residue, perm), (pad_right, pad_perm), pack)
        update = flat.solve(coarse_right, coarse_perm * 0.125, level + 1, buffer)
        update = flat.prolong(update, pad_right, pack)
    values = [v + e for v, e in zip(values, update)]
    for _ in range(2):
        values = grid.sweep(values, coefs, const)
    return values


def coarse_kernel(
    dom_ref, like, unlike, coef, const, before, out,
    gathered, level, first, pad_right1, pad_perm1, pad_right2, pad_perm2, update, pack, buffer,
):
    height = out.shape[0]
    dom = dom_ref[0]
    domains, own, nx, _ = gathered.shape
    parity = lax.rem(dom, 2)
    for i in range(domains // 2):
        gathered[2 * i + parity] = like[i]
        gathered[2 * i + 1 - parity] = unlike[i]
    ny = LANES // 2
    grid = Packed(domains * own, nx, ny)
    left = iota((nx, LANES), 1) < ny
    right, perm = [], []
    for p in range(grid.planes):
        a = gathered[p // own, p % own]
        q = grid.planes + p
        b = gathered[q // own, q % own]
        right.append(jnp.where(left, a, roll(b, ny, 1)))
        perm.append(jnp.where(left, roll(a, ny, 1), b))
    pads = [(pad_right1, pad_perm1), (pad_right2, pad_perm2)]
    solved = packed_cycle(grid, right, perm, 1, pads, (pack, buffer))
    for p in range(grid.planes):
        update[p] = solved[p]
    planes, group = [], []
    for j in range(own + 2):
        layer = jnp.clip(dom * own + j - 1, 0, grid.nz - 1)
        group.append(layer // grid.planes)
        planes.append(update[lax.rem(layer, grid.planes)])
    for j, wide in enumerate(selector_dot(planes, lane_selector(1, LANES, 2, spread=True))):
        plane = jnp.where(group[j] == 0, wide[:, :LANES], wide[:, LANES:])
        pad = first.at[0]
        pad[pl.ds(0, nx, 2), :] = plane
        pad[pl.ds(1, nx, 2), :] = plane
        whole = first[0]
        level[2 * j] = before[2 * j] + whole
        level[2 * j + 1] = before[2 * j + 1] + whole

    def sweep(source, at, i):
        centre = source[i + 1]
        near = [coef[k, at + i] for k in range(6)]
        return stencil(centre, source[i], source[i + 2], near, KEEP * centre + const[at + i])

    def one(i):
        first[i] = sweep(level, 2, i)

    for i in range(height + 2):
        one(i)

    def two(i):
        out[i] = sweep(first, 3, i)

    for i in range(height):
        two(i)


def fine_part(dom, perm, source, layers):
    height, nx, ny = perm[0].shape
    field = lambda *lead: pltpu.VMEM(lead + (nx, ny), F32)
    vmem = pl.BlockSpec(memory_space=pltpu.VMEM)
    smem = pl.BlockSpec(memory_space=pltpu.SMEM)
    return pl.pallas_call(
        functools.partial(fine_kernel, layers),
        out_shape=(
            jax.ShapeDtypeStruct((6, height + 6, nx, ny), F32),
            jax.ShapeDtypeStruct((height + 6, nx, ny), F32),
            jax.ShapeDtypeStruct((height + 4, nx, ny), F32),
            jax.ShapeDtypeStruct((height // 2, nx // 2, ny), F32),
        ),
        in_specs=[smem] + [vmem] * 6,
        out_specs=(vmem,) * 4,
        scratch_shapes=[
            field(3 * height),
            field(3 * height),
            field(height + 6),
            field(height // 2),
            field(height // 2),
        ],
        compiler_params=pltpu.CompilerParams(vmem_limit_bytes=VMEM_LIMIT),
        name="fine",
    )(dom, *perm, *source)


def coarse_part(dom, like, unlike, coefs, const, values, height):
    _, nx, ny = values.shape
    field = lambda *shape: pltpu.VMEM(shape, F32)
    whole = (2 * like.shape[0],) + like.shape[1:]
    grid1 = Packed(whole[0] * whole[1], nx // 2, ny // 2)
    grid2 = grid1.coarser()
    pads1 = field(grid1.planes // 2, grid1.nx, LANES)
    pads2 = field(grid2.planes // 2, grid2.nx, LANES)
    vmem = pl.BlockSpec(memory_space=pltpu.VMEM)
    smem = pl.BlockSpec(memory_space=pltpu.SMEM)
    return pl.pallas_call(
        coarse_kernel,
        out_shape=jax.ShapeDtypeStruct((height, nx, ny), F32),
        in_specs=[smem] + [vmem] * 5,
        out_specs=vmem,
        scratch_shapes=[
            field(*whole),
            field(*values.shape),
            field(height + 2, nx, ny),
            pads1, pads1, pads2, pads2,
            field(grid1.planes, grid1.nx, LANES),
            field(2, Flat(grid2).rows, LANES),
            field(Flat(grid2).buffer_rows, LANES),
        ],
        compiler_params=pltpu.CompilerParams(vmem_limit_bytes=VMEM_LIMIT),
        name="coarse",
    )(dom, like, unlike, coefs, const, values)


def swaps(x, axis, step):
    return lax.ppermute(x, axis, [(i, i ^ step) for i in range(lax.axis_size(axis))])


def other_side(x):
    props, domains = lax.axis_size("prop"), lax.axis_size("dom")
    pairs = []
    for p in range(props):
        for d in range(domains):
            end = d in (0, domains - 1)
            partner = ((p ^ 1) * domains + d) if end else (p * domains + ((d + 1) ^ 1) - 1)
            pairs.append((p * domains + d, partner))
    return lax.ppermute(x, ("prop", "dom"), pairs)


def source_side(x):
    props, domains = lax.axis_size("prop"), lax.axis_size("dom")
    pairs = []
    for p in range(props):
        for d in range(domains):
            if p % 2 == 0:
                partner = p * domains + (d ^ 1)
            elif d in (0, domains - 1):
                partner = (p ^ 2) * domains + d
            else:
                partner = p * domains + ((d + 1) ^ 1) - 1
            pairs.append((p * domains + d, partner))
    return lax.ppermute(x, ("prop", "dom"), pairs)


def from_accepted(mine, accepted, beside):
    props = lax.axis_size("prop")
    step = props // 2
    own = SHRINK * mine
    offers, order = [mine], [0]
    while step:
        came = [swaps(x, "prop", step) for x in offers]
        if step == props // 2:
            came, own, beside = lax.optimization_barrier((came, own, beside))
        offers, order = offers + came, order + [x ^ step for x in order]
        step //= 2
    wanted = lax.axis_index("prop") ^ accepted
    current = offers[1]
    for at, offer in zip(order[2:], offers[2:]):
        current = jnp.where(wanted == at, offer, current)
    return jnp.where(wanted == 0, own, SHRINK * current), beside


def gather_parts(mine):
    domains = lax.axis_size("dom")
    copies = jnp.broadcast_to(mine[None], (domains // 2,) + mine.shape)
    groups = [list(range(0, domains, 2)), list(range(1, domains, 2))]
    like = lax.all_to_all(copies, "dom", 0, 0, axis_index_groups=groups)
    return like, swaps(like, "dom", 1)


def body(states, accepted, noise, source):
    domains = lax.axis_size("dom")
    height = source.shape[0]
    dom = jnp.stack([lax.axis_index("dom"), lax.axis_index("prop")]).astype(jnp.int32)
    near = source_side(source)
    beside = (OMEGA * source, BETA * noise[0])
    current, (scaled, noise_part) = from_accepted(states[0], accepted[0], beside)
    perm = jnp.exp(current + noise_part)
    perms = (perm, swaps(perm, "dom", 1), other_side(perm))
    sources = (scaled, near, swaps(near, "prop", 1))
    *level, coarse = fine_part(dom, perms, sources, domains * height)
    return coarse_part(dom, *gather_parts(coarse), *level, height)[None]


def solution(mesh):
    in_specs = (
        P("prop", "dom", None, None),
        P(),
        P("prop", "dom", None, None),
        P("dom", None, None),
    )
    out_specs = P("prop", "dom", None, None)
    return jax.shard_map(body, mesh=mesh, in_specs=in_specs, out_specs=out_specs, check_vma=False)
```

```python
import functools
import math

import jax
import jax.numpy as jnp
from jax import lax
from jax.experimental import pallas as pl
from jax.experimental.pallas import tpu as pltpu
from jax.sharding import PartitionSpec as P

COARSE_SWEEPS = 64
POWER = 2
OMEGA = 0.7
KEEP = 1.0 - OMEGA
BETA = 0.4
SHRINK = math.sqrt(1.0 - BETA * BETA)
ZSCALE = 16.0
LANES = 128
VMEM_LIMIT = 40 * 1024 * 1024
F32 = jnp.float32
WEST, EAST, SOUTH, NORTH, BELOW, ABOVE, CONST = range(7)


def iota(shape, dim):
    return lax.broadcasted_iota(jnp.int32, shape, dim)


def roll(x, amount, axis):
    axis = axis % x.ndim
    return pltpu.roll(x, amount % x.shape[axis], axis)


def inverse_of(x):
    guess = pl.reciprocal(x, approx=True)
    return guess * (2.0 - x * guess)


def harmonic(a, b):
    return (2.0 * a) * b * inverse_of(a + b)


def selector_dot(parts, selector):
    x = jnp.concatenate(parts, axis=0) if len(parts) > 1 else parts[0]
    rows = x.shape[0]
    high = x.astype(jnp.bfloat16).astype(F32)
    rest = x - high
    middle = rest.astype(jnp.bfloat16).astype(F32)
    terms = jnp.concatenate([high, middle, rest - middle], axis=0).astype(jnp.bfloat16)
    y = jnp.dot(terms, selector, preferred_element_type=F32)
    total = y[:rows] + y[rows : 2 * rows] + y[2 * rows :]
    height = parts[0].shape[0]
    return [total[i * height : (i + 1) * height] for i in range(len(parts))]


class Rows:
    def __init__(self, ref, nx):
        self.ref, self.nx = ref, nx

    @staticmethod
    def scratch(count, nx):
        return pltpu.VMEM((count, 2 * nx + 4, LANES), F32)

    def clear(self):
        for i in range(self.ref.shape[0]):
            for at in (0, 2 * self.nx + 2):
                self.ref[i, at : at + 1, :] = jnp.zeros((1, LANES), F32)

    def put(self, i, plane):
        self.ref[i, pl.ds(2, self.nx, 2), :] = plane

    def get(self, i, shift=0):
        return self.ref[i, pl.ds(2 + 2 * shift, self.nx, 2), :]


def face_terms(perm, lower, upper, below_scale, above_scale, ny, rows, i, spare):
    shape = perm.shape
    row = iota(shape, 0)
    columns = iota(shape, 1) & (ny - 1)
    west = jnp.where(row == 0, 0.0, harmonic(perm, rows.get(i, -1)))
    rows.put(spare, west)
    east = rows.get(spare, 1)
    south = jnp.where(columns == 0, 0.0, harmonic(perm, roll(perm, 1, 1)))
    north = roll(south, -1, 1)
    below = below_scale * harmonic(perm, lower)
    above = above_scale * harmonic(perm, upper)
    ends = jnp.where(row == 0, perm, 0.0) + jnp.where(row == shape[0] - 1, perm, 0.0)
    ends = ends + jnp.where(columns == 0, perm, 0.0) + jnp.where(columns == ny - 1, perm, 0.0)
    diagonal = ((west + east) + (south + north)) + ((below + above) + ends)
    return (west, east, south, north, below, above), diagonal


def stencil(values, before, after, lower, upper, coefs, base):
    x = coefs[0] * before + coefs[1] * after
    y = coefs[2] * roll(values, 1, 1) + coefs[3] * roll(values, -1, 1)
    z = coefs[4] * lower + coefs[5] * upper
    return (x + y) + (z + base)


def lane_selector(groups, ny, step, spread=False):
    shape = (LANES, step * LANES) if spread else (step * LANES, LANES)
    source, target = iota(shape, int(spread)), iota(shape, 1 - int(spread))
    bits = ny.bit_length() - 1
    lane = source & (LANES - 1)
    group = (lane >> bits) * step + (source >> 7)
    wanted = (group << (bits - 1)) + ((lane & (ny - 1)) >> 1)
    return jnp.where((target == wanted) & (lane < groups * ny), 1.0, 0.0).astype(jnp.bfloat16)


def fine_kernel(
    layers,
    dom_ref,
    per, per_pair, per_other,
    src, src_near, src_next,
    coef, const, values, coarse_out,
    perm, right, diag, pair_right, pair_perm, perm_rows, start_rows, value_rows,
):
    height, nx, _ = per.shape
    perm_rows, start_rows, value_rows = (Rows(x, nx) for x in (perm_rows, start_rows, value_rows))
    for rows in (perm_rows, start_rows, value_rows):
        rows.clear()
    dom = dom_ref[0]
    pair_at = jnp.where(lax.rem(dom, 2) == 0, 2 * height, 0)
    other_at = 2 * height - pair_at

    near_at = jnp.where(lax.rem(dom_ref[1], 2) == 0, pair_at, other_at)
    next_at = 2 * height - near_at
    for i in range(height):
        for at, p in ((height, per), (pair_at, per_pair), (other_at, per_other)):
            perm[at + i] = p[i]
            perm_rows.put(at + i, p[i])
        right[height + i] = src[i]
        right[near_at + i] = OMEGA * src_near[i]
        right[next_at + i] = OMEGA * src_next[i]

    def build(i):
        z = dom * height + i - 3
        below = jnp.where((z > 0) & (z < layers), ZSCALE, 0.0)
        above = jnp.where((z + 1 > 0) & (z + 1 < layers), ZSCALE, 0.0)
        at = height - 3 + i
        faces, diagonal = face_terms(
            perm[at], perm[at - 1], perm[at + 1], below, above, LANES, perm_rows, at, 3 * height + i % 2
        )
        inverse = inverse_of(diagonal)
        const[i] = inverse * right[at]
        start_rows.put(i, const[i])
        inverse = OMEGA * inverse
        for k in range(6):
            coef[k, i] = inverse * faces[k]
        diag[i] = diagonal

    for i in range(height + 6):
        build(i)

    def first(i):
        start = const[i + 1]
        near = [coef[k, i + 1] for k in range(6)]
        beside = start_rows.get(i + 1, -1), start_rows.get(i + 1, 1)
        values[i] = stencil(start, *beside, const[i], const[i + 2], near, (1.0 + KEEP) * start)
        if 2 <= i < height + 2:
            value_rows.put(i - 2, values[i])

    for i in range(height + 4):
        first(i)

    def residue(i):
        centre = values[i + 2]
        base = const[i + 3] - OMEGA * centre
        near = [coef[k, i + 3] for k in range(6)]
        beside = value_rows.get(i, -1), value_rows.get(i, 1)
        scaled = stencil(centre, *beside, values[i + 1], values[i + 3], near, base)
        return scaled * (diag[i + 3] * (1.0 / OMEGA))

    for m in range(height // 2):
        pair_right[m] = residue(2 * m) + residue(2 * m + 1)
        pair_perm[m] = (perm[height + 2 * m] + perm[height + 2 * m + 1]) * 0.125
    half = pair_right.shape[1] // 2
    rows = []
    for m in range(height // 2):
        both = [x[m, pl.ds(0, half, 2), :] + x[m, pl.ds(1, half, 2), :] for x in (pair_right, pair_perm)]
        rows.append(jnp.concatenate(both, axis=1))
    for m, x in enumerate(selector_dot(rows, lane_selector(1, LANES, 2))):
        coarse_out[m] = x


class Packed:
    def __init__(self, nz, nx, ny, rows=()):
        self.nz, self.nx, self.ny = nz, nx, ny
        self.coarser_rows = rows[1:]
        self.rows = Rows(rows[0], nx) if rows else None
        self.groups = min(LANES // ny, nz)
        self.planes = nz // self.groups

    def lower(self, planes, p):
        return planes[p - 1] if p else roll(planes[self.planes - 1], self.ny, 1)

    def upper(self, planes, p):
        return planes[p + 1] if p + 1 < self.planes else roll(planes[0], -self.ny, 1)

    def system(self, right, perm, level):
        lane = iota((self.nx, LANES), 1)
        used = lane < self.groups * self.ny
        if self.groups * self.ny < LANES:
            perm = [jnp.where(used, x, 1.0) for x in perm]
        coefs, const, diagonals = [], [], []
        self.rows.clear()
        for p in range(self.planes):
            self.rows.put(p, perm[p])
        for p in range(self.planes):
            below, above = ZSCALE, ZSCALE
            if p == 0:
                below = jnp.where(lane < self.ny, 0.0, ZSCALE)
            if p + 1 == self.planes:
                above = jnp.where(lane < (self.groups - 1) * self.ny, ZSCALE, 0.0)
            faces, diagonal = face_terms(
                perm[p], self.lower(perm, p), self.upper(perm, p), below, above, self.ny,
                self.rows, p, self.planes + p % 2,
            )
            inverse = OMEGA * inverse_of(diagonal)
            coefs.append([inverse * face for face in faces])
            const.append(inverse * right[p] * (4.0**-level))
            diagonals.append(diagonal * (4.0**level / OMEGA))
        return coefs, const, diagonals

    def apply(self, values, coefs, bases):
        for p in range(self.planes):
            self.rows.put(p, values[p])
        return [
            stencil(
                values[p], self.rows.get(p, -1), self.rows.get(p, 1),
                self.lower(values, p), self.upper(values, p), coefs[p], bases[p],
            )
            for p in range(self.planes)
        ]

    def sweep(self, values, coefs, const):
        return self.apply(values, coefs, [KEEP * v + c for v, c in zip(values, const)])

    def coarser(self):
        return Packed(self.nz // 2, self.nx // 2, self.ny // 2, self.coarser_rows)

    def restrict(self, fields, pads):
        coarse = self.coarser()
        step = coarse.groups // self.groups
        half = coarse.nx
        parts = []
        for values, pad in zip(fields, pads):
            rows = []
            for m in range(self.planes // 2):
                pad[m] = values[2 * m] + values[2 * m + 1]
                rows.append(pad[m, pl.ds(0, half, 2), :] + pad[m, pl.ds(1, half, 2), :])
            for p in range(coarse.planes):
                blocks = rows[p :: coarse.planes]
                parts.append(jnp.concatenate(blocks, axis=1) if step > 1 else blocks[0])
        sums = selector_dot(parts, lane_selector(self.groups, self.ny, step))
        return [sums[i : i + coarse.planes] for i in range(0, len(sums), coarse.planes)]

    def prolong(self, values, pad):
        coarse = self.coarser()
        step = coarse.groups // self.groups
        half = coarse.nx
        wide = selector_dot(values, lane_selector(self.groups, self.ny, step, spread=True))
        out = []
        for m in range(self.planes // 2):
            j, p = divmod(m, coarse.planes)
            plane = wide[p][:, j * LANES : (j + 1) * LANES]
            pad[m, pl.ds(0, half, 2), :] = plane
            pad[m, pl.ds(1, half, 2), :] = plane
            out += [pad[m], pad[m]]
        return out


class Flat:
    def __init__(self, finer):
        coarse = finer.coarser()
        self.finer = finer
        self.nz, self.nx, self.ny = coarse.nz, coarse.nx, coarse.ny
        self.pairs = finer.planes // 2
        self.rows = max(8, self.nz)
        self.shape = (self.rows, LANES)
        self.buffer_rows = 2 * (self.rows + 2 * POWER)

    def selector(self, spread=False):
        wide = self.finer.groups * LANES
        shape = (wide, LANES) if spread else (LANES, wide)
        fine, flat = iota(shape, int(spread)), iota(shape, 1 - int(spread))
        bits = self.finer.ny.bit_length() - 1
        same = (fine >> bits) == (flat >> 7)
        same &= ((fine & (self.finer.ny - 1)) >> 1) == (flat & (self.ny - 1))
        return jnp.where(same, 1.0, 0.0).astype(jnp.bfloat16)

    def diagonal(self):
        shape = (self.nx, LANES)
        return iota(shape, 0) == (iota(shape, 1) >> (self.ny.bit_length() - 1))

    def restrict(self, fields, pads, pack):
        parts = []
        for values, pad in zip(fields, pads):
            for m in range(self.pairs):
                pad[m] = values[2 * m] + values[2 * m + 1]
                parts.append(pad[m, pl.ds(0, self.nx, 2), :] + pad[m, pl.ds(1, self.nx, 2), :])
        sums = selector_dot(parts, self.selector())
        mask = self.diagonal()
        pack[...] = jnp.zeros_like(pack)
        for i in range(len(fields)):
            for z in range(self.nz):
                s, m = divmod(z, self.pairs)
                block = sums[i * self.pairs + m][:, s * LANES : (s + 1) * LANES]
                row = jnp.sum(jnp.where(mask, block, 0.0), axis=0, keepdims=True)
                pack[i, z : z + 1, :] = row
        return [pack[i] for i in range(len(fields))]

    def prolong(self, values, pad, pack):
        mask = self.diagonal()
        pack[0] = values
        parts = []
        for m in range(self.pairs):
            layers = [s * self.pairs + m for s in range(self.finer.groups)]
            spread = [jnp.broadcast_to(pack[0, z : z + 1, :], mask.shape) for z in layers]
            parts.append(jnp.concatenate([jnp.where(mask, x, 0.0) for x in spread], axis=1))
        out = []
        for m, wide in enumerate(selector_dot(parts, self.selector(spread=True))):
            pad[m, pl.ds(0, self.nx, 2), :] = wide
            pad[m, pl.ds(1, self.nx, 2), :] = wide
            out += [pad[m], pad[m]]
        return out

    def system(self, right, perm, level):
        lane, row = iota(self.shape, 1), iota(self.shape, 0)
        x, y = lane >> (self.ny.bit_length() - 1), lane & (self.ny - 1)
        real = row < self.nz
        perm = jnp.where(real, perm, 1.0)
        west = jnp.where(x == 0, 0.0, harmonic(perm, roll(perm, self.ny, 1)))
        east = roll(west, -self.ny, 1)
        south = jnp.where(y == 0, 0.0, harmonic(perm, roll(perm, 1, 1)))
        north = roll(south, -1, 1)
        below = ZSCALE * harmonic(perm, roll(perm, 1, 0))
        below = jnp.where((row > 0) & real, below, 0.0)
        above = roll(below, -1, 0)
        faces = [west, east, south, north, below, above]
        ends = (x == 0, x == self.nx - 1, y == 0, y == self.ny - 1)
        diagonal = tree_sum(faces + [jnp.where(end, perm, 0.0) for end in ends])
        inverse = jnp.where(real, OMEGA * inverse_of(diagonal), 0.0)
        keys = ((-1, 0, 0), (1, 0, 0), (0, -1, 0), (0, 1, 0), (0, 0, -1), (0, 0, 1))
        terms = {key: inverse * face for key, face in zip(keys, faces)}
        terms[0, 0, 0] = jnp.full(self.shape, KEEP, F32)
        return terms, inverse * right * (4.0**-level)

    def product(self, first, second):
        sums = {}
        for (dx, dy, dz), coef in first.items():
            for other, moved in second.items():
                if dz:
                    moved = roll(moved, -dz, 0)
                if dx or dy:
                    moved = roll(moved, -(dx * self.ny + dy), 1)
                total = tuple(a + b for a, b in zip((dx, dy, dz), other))
                sums.setdefault(total, []).append(coef * moved)
        return {key: tree_sum(parts) for key, parts in sums.items()}

    def apply(self, terms, values, base, buffer):
        buffer[pl.ds(2 * POWER, self.rows, 2), :] = values
        moved = {}
        for dx, dy, dz in sorted(terms, key=lambda key: abs(key[2])):
            if (0, 0, dz) not in moved:
                moved[0, 0, dz] = buffer[pl.ds(2 * (POWER + dz), self.rows, 2), :] if dz else values
            if dx or dy:
                moved[dx, dy, dz] = roll(moved[0, 0, dz], -(dx * self.ny + dy), 1)
        return tree_sum([base] + [coef * moved[key] for key, coef in terms.items()])

    def solve(self, right, perm, level, buffer):
        buffer[...] = jnp.zeros_like(buffer)
        terms, const = self.system(right, perm, level)
        power, base = terms, const
        for _ in range(POWER - 1):
            base = self.apply(terms, base, const, buffer)
            power = self.product(terms, power)
        whole = COARSE_SWEEPS % POWER == 0
        start = base if whole else const
        steps = (COARSE_SWEEPS - 1) // POWER
        assert steps * POWER + (POWER if whole else 1) == COARSE_SWEEPS
        return lax.fori_loop(
            0, steps, lambda step, values: self.apply(power, values, base, buffer), start
        )


def tree_sum(parts):
    while len(parts) > 1:
        odd = parts[len(parts) // 2 * 2 :]
        parts = [a + b for a, b in zip(parts[::2], parts[1::2])] + odd
    return parts[0]


def packed_cycle(grid, right, perm, level, pads, store):
    pad_right, pad_perm = pads[0]
    coefs, const, diagonals = grid.system(right, perm, level)
    values = grid.sweep(const, coefs, const)
    scaled = grid.apply(values, coefs, [c - OMEGA * v for c, v in zip(const, values)])
    residue = [r * d for r, d in zip(scaled, diagonals)]
    if len(pads) > 1:
        coarse_right, coarse_perm = grid.restrict((residue, perm), (pad_right, pad_perm))
        coarse_perm = [x * 0.125 for x in coarse_perm]
        update = packed_cycle(grid.coarser(), coarse_right, coarse_perm, level + 1, pads[1:], store)
        update = grid.prolong(update, pad_right)
    else:
        pack, buffer = store
        flat = Flat(grid)
        coarse_right, coarse_perm = flat.restrict((residue, perm), (pad_right, pad_perm), pack)
        update = flat.solve(coarse_right, coarse_perm * 0.125, level + 1, buffer)
        update = flat.prolong(update, pad_right, pack)
    values = [v + e for v, e in zip(values, update)]
    for _ in range(2):
        values = grid.sweep(values, coefs, const)
    return values


def coarse_kernel(
    dom_ref, gathered, coef, const, before, out,
    level, first, pad_right1, pad_perm1, pad_right2, pad_perm2, update, pack, buffer,
    rows0, rows1, rows2,
):
    height = out.shape[0]
    dom = dom_ref[0]
    domains, own, nx, _ = gathered.shape
    ny = LANES // 2
    grid = Packed(domains * own, nx, ny, (rows1, rows2))
    left = iota((nx, LANES), 1) < ny
    right, perm = [], []
    for p in range(grid.planes):
        a = gathered[p // own, p % own]
        q = grid.planes + p
        b = gathered[q // own, q % own]
        right.append(jnp.where(left, a, roll(b, ny, 1)))
        perm.append(jnp.where(left, roll(a, ny, 1), b))
    pads = [(pad_right1, pad_perm1), (pad_right2, pad_perm2)]
    solved = packed_cycle(grid, right, perm, 1, pads, (pack, buffer))
    for p in range(grid.planes):
        update[p] = solved[p]
    rows0 = Rows(rows0, 2 * nx)
    rows0.clear()
    planes, group = [], []
    for j in range(own + 2):
        layer = jnp.clip(dom * own + j - 1, 0, grid.nz - 1)
        group.append(layer // grid.planes)
        planes.append(update[lax.rem(layer, grid.planes)])
    for j, wide in enumerate(selector_dot(planes, lane_selector(1, LANES, 2, spread=True))):
        plane = jnp.where(group[j] == 0, wide[:, :LANES], wide[:, LANES:])
        pad = first.at[0]
        pad[pl.ds(0, nx, 2), :] = plane
        pad[pl.ds(1, nx, 2), :] = plane
        whole = first[0]
        for i in (2 * j, 2 * j + 1):
            level[i] = before[i] + whole
            if 0 < i < height + 3:
                rows0.put(i - 1, level[i])

    def sweep(source, at, i, j):
        centre = source[i + 1]
        near = [coef[k, at + i] for k in range(6)]
        base = KEEP * centre + const[at + i]
        beside = rows0.get(j, -1), rows0.get(j, 1)
        return stencil(centre, *beside, source[i], source[i + 2], near, base)

    def one(i):
        first[i] = sweep(level, 2, i, i)
        if 0 < i < height + 1:
            rows0.put(height + 1 + i, first[i])

    def two(i):
        out[i] = sweep(first, 3, i, height + 2 + i)

    for i in range(height + 2):
        one(i)

    for i in range(height):
        two(i)


def fine_part(dom, perm, source, layers):
    height, nx, ny = perm[0].shape
    field = lambda *lead: pltpu.VMEM(lead + (nx, ny), F32)
    vmem = pl.BlockSpec(memory_space=pltpu.VMEM)
    smem = pl.BlockSpec(memory_space=pltpu.SMEM)
    return pl.pallas_call(
        functools.partial(fine_kernel, layers),
        out_shape=(
            jax.ShapeDtypeStruct((6, height + 6, nx, ny), F32),
            jax.ShapeDtypeStruct((height + 6, nx, ny), F32),
            jax.ShapeDtypeStruct((height + 4, nx, ny), F32),
            jax.ShapeDtypeStruct((height // 2, nx // 2, ny), F32),
        ),
        in_specs=[smem] + [vmem] * 6,
        out_specs=(vmem,) * 4,
        scratch_shapes=[
            field(3 * height),
            field(3 * height),
            field(height + 6),
            field(height // 2),
            field(height // 2),
            Rows.scratch(3 * height + 2, nx),
            Rows.scratch(height + 6, nx),
            Rows.scratch(height, nx),
        ],
        compiler_params=pltpu.CompilerParams(vmem_limit_bytes=VMEM_LIMIT),
        name="fine",
    )(dom, *perm, *source)


def coarse_part(dom, gathered, coefs, const, values, height):
    _, nx, ny = values.shape
    field = lambda *shape: pltpu.VMEM(shape, F32)
    grid1 = Packed(gathered.shape[0] * gathered.shape[1], nx // 2, ny // 2)
    grid2 = grid1.coarser()
    pads1 = field(grid1.planes // 2, grid1.nx, LANES)
    pads2 = field(grid2.planes // 2, grid2.nx, LANES)
    vmem = pl.BlockSpec(memory_space=pltpu.VMEM)
    smem = pl.BlockSpec(memory_space=pltpu.SMEM)
    return pl.pallas_call(
        coarse_kernel,
        out_shape=jax.ShapeDtypeStruct((height, nx, ny), F32),
        in_specs=[smem] + [vmem] * 4,
        out_specs=vmem,
        scratch_shapes=[
            field(*values.shape),
            field(height + 2, nx, ny),
            pads1, pads1, pads2, pads2,
            field(grid1.planes, grid1.nx, LANES),
            field(2, Flat(grid2).rows, LANES),
            field(Flat(grid2).buffer_rows, LANES),
            Rows.scratch(2 * height + 2, nx),
            Rows.scratch(grid1.planes + 2, grid1.nx),
            Rows.scratch(grid2.planes + 2, grid2.nx),
        ],
        compiler_params=pltpu.CompilerParams(vmem_limit_bytes=VMEM_LIMIT),
        name="coarse",
    )(dom, gathered, coefs, const, values)


def swaps(x, axis, step):
    return lax.ppermute(x, axis, [(i, i ^ step) for i in range(lax.axis_size(axis))])


def other_side(x):
    props, domains = lax.axis_size("prop"), lax.axis_size("dom")
    pairs = []
    for p in range(props):
        for d in range(domains):
            end = d in (0, domains - 1)
            partner = ((p ^ 1) * domains + d) if end else (p * domains + ((d + 1) ^ 1) - 1)
            pairs.append((p * domains + d, partner))
    return lax.ppermute(x, ("prop", "dom"), pairs)


def source_side(x):
    props, domains = lax.axis_size("prop"), lax.axis_size("dom")
    pairs = []
    for p in range(props):
        for d in range(domains):
            if p % 2 == 0:
                partner = p * domains + (d ^ 1)
            elif d in (0, domains - 1):
                partner = (p ^ 2) * domains + d
            else:
                partner = p * domains + ((d + 1) ^ 1) - 1
            pairs.append((p * domains + d, partner))
    return lax.ppermute(x, ("prop", "dom"), pairs)


def from_accepted(mine, accepted, beside):
    props = lax.axis_size("prop")
    step = props // 2
    own = SHRINK * mine
    offers, order = [mine], [0]
    while step:
        came = [swaps(x, "prop", step) for x in offers]
        if step == props // 2:
            came, own, beside = lax.optimization_barrier((came, own, beside))
        offers, order = offers + came, order + [x ^ step for x in order]
        step //= 2
    wanted = lax.axis_index("prop") ^ accepted
    current = offers[1]
    for at, offer in zip(order[2:], offers[2:]):
        current = jnp.where(wanted == at, offer, current)
    return jnp.where(wanted == 0, own, SHRINK * current), beside


def gather_parts(mine):
    domains = lax.axis_size("dom")
    copies = jnp.broadcast_to(mine[None], (domains,) + mine.shape)
    return lax.all_to_all(copies, "dom", 0, 0)


def body(states, accepted, noise, source):
    domains = lax.axis_size("dom")
    height = source.shape[0]
    dom = jnp.stack([lax.axis_index("dom"), lax.axis_index("prop")]).astype(jnp.int32)
    near = source_side(source)
    beside = (OMEGA * source, BETA * noise[0])
    current, (scaled, noise_part) = from_accepted(states[0], accepted[0], beside)
    perm = jnp.exp(current + noise_part)
    perms = (perm, swaps(perm, "dom", 1), other_side(perm))
    sources = (scaled, near, swaps(near, "prop", 1))
    *level, coarse = fine_part(dom, perms, sources, domains * height)
    return coarse_part(dom, gather_parts(coarse), *level, height)[None]


def solution(mesh):
    in_specs = (
        P("prop", "dom", None, None),
        P(),
        P("prop", "dom", None, None),
        P("dom", None, None),
    )
    out_specs = P("prop", "dom", None, None)
    return jax.shard_map(body, mesh=mesh, in_specs=in_specs, out_specs=out_specs, check_vma=False)
```

```python
import functools
import math

import jax
import jax.numpy as jnp
from jax import lax
from jax.experimental import pallas as pl
from jax.experimental.pallas import tpu as pltpu
from jax.sharding import PartitionSpec as P

COARSE_SWEEPS = 64
POWER = 2
OMEGA = 0.7
KEEP = 1.0 - OMEGA
BETA = 0.4
SHRINK = math.sqrt(1.0 - BETA * BETA)
ZSCALE = 16.0
LANES = 128
VMEM_LIMIT = 40 * 1024 * 1024
F32 = jnp.float32
WEST, EAST, SOUTH, NORTH, BELOW, ABOVE, CONST = range(7)


def iota(shape, dim):
    return lax.broadcasted_iota(jnp.int32, shape, dim)


def roll(x, amount, axis):
    axis = axis % x.ndim
    return pltpu.roll(x, amount % x.shape[axis], axis)


def inverse_of(x):
    guess = pl.reciprocal(x, approx=True)
    return guess * (2.0 - x * guess)


def harmonic(a, b):
    return (2.0 * a) * b * inverse_of(a + b)


def selector_dot(parts, selector):
    x = jnp.concatenate(parts, axis=0) if len(parts) > 1 else parts[0]
    rows = x.shape[0]
    high = x.astype(jnp.bfloat16).astype(F32)
    rest = x - high
    middle = rest.astype(jnp.bfloat16).astype(F32)
    terms = jnp.concatenate([high, middle, rest - middle], axis=0).astype(jnp.bfloat16)
    y = jnp.dot(terms, selector, preferred_element_type=F32)
    total = y[:rows] + y[rows : 2 * rows] + y[2 * rows :]
    height = parts[0].shape[0]
    return [total[i * height : (i + 1) * height] for i in range(len(parts))]


def face_terms(perm, lower, upper, below_scale, above_scale, ny):
    shape = perm.shape
    rows = iota(shape, 0)
    columns = iota(shape, 1) & (ny - 1)
    west = jnp.where(rows == 0, 0.0, harmonic(perm, roll(perm, 1, 0)))
    east = roll(west, -1, 0)
    south = jnp.where(columns == 0, 0.0, harmonic(perm, roll(perm, 1, 1)))
    north = roll(south, -1, 1)
    below = below_scale * harmonic(perm, lower)
    above = above_scale * harmonic(perm, upper)
    ends = jnp.where(rows == 0, perm, 0.0) + jnp.where(rows == shape[0] - 1, perm, 0.0)
    ends = ends + jnp.where(columns == 0, perm, 0.0) + jnp.where(columns == ny - 1, perm, 0.0)
    diagonal = ((west + east) + (south + north)) + ((below + above) + ends)
    return (west, east, south, north, below, above), diagonal


def stencil(values, lower, upper, coefs, base):
    x = coefs[0] * roll(values, 1, 0) + coefs[1] * roll(values, -1, 0)
    y = coefs[2] * roll(values, 1, 1) + coefs[3] * roll(values, -1, 1)
    z = coefs[4] * lower + coefs[5] * upper
    return (x + y) + (z + base)


def lane_selector(groups, ny, step, spread=False):
    shape = (LANES, step * LANES) if spread else (step * LANES, LANES)
    source, target = iota(shape, int(spread)), iota(shape, 1 - int(spread))
    bits = ny.bit_length() - 1
    lane = source & (LANES - 1)
    group = (lane >> bits) * step + (source >> 7)
    wanted = (group << (bits - 1)) + ((lane & (ny - 1)) >> 1)
    return jnp.where((target == wanted) & (lane < groups * ny), 1.0, 0.0).astype(jnp.bfloat16)


def fine_kernel(
    layers,
    dom_ref,
    per, pair_low, pair_high, other_low, other_high,
    src, src_near, src_next,
    coef, const, values, coarse_out,
    perm, right, diag, pair_right, pair_perm,
):
    height = per.shape[0]
    dom = dom_ref[0]
    pair_at = jnp.where(lax.rem(dom, 2) == 0, 2 * height, 0)
    other_at = 2 * height - pair_at

    near_at = jnp.where(lax.rem(dom_ref[1], 2) == 0, pair_at, other_at)
    next_at = 2 * height - near_at
    for i in range(height):
        perm[height + i] = per[i]
        low = i < height // 2
        perm[pair_at + i] = pair_low[i] if low else pair_high[i - height // 2]
        perm[other_at + i] = other_low[i] if low else other_high[i - height // 2]
        right[height + i] = src[i]
        right[near_at + i] = OMEGA * src_near[i]
        right[next_at + i] = OMEGA * src_next[i]

    def build(i):
        z = dom * height + i - 3
        below = jnp.where((z > 0) & (z < layers), ZSCALE, 0.0)
        above = jnp.where((z + 1 > 0) & (z + 1 < layers), ZSCALE, 0.0)
        at = height - 3 + i
        faces, diagonal = face_terms(perm[at], perm[at - 1], perm[at + 1], below, above, LANES)
        inverse = inverse_of(diagonal)
        const[i] = inverse * right[at]
        inverse = OMEGA * inverse
        for k in range(6):
            coef[k, i] = inverse * faces[k]
        diag[i] = diagonal

    for i in range(height + 6):
        build(i)

    def first(i):
        start = const[i + 1]
        near = [coef[k, i + 1] for k in range(6)]
        values[i] = stencil(start, const[i], const[i + 2], near, (1.0 + KEEP) * start)

    for i in range(height + 4):
        first(i)

    def residue(i):
        centre = values[i + 2]
        base = const[i + 3] - OMEGA * centre
        near = [coef[k, i + 3] for k in range(6)]
        scaled = stencil(centre, values[i + 1], values[i + 3], near, base)
        return scaled * (diag[i + 3] * (1.0 / OMEGA))

    for m in range(height // 2):
        pair_right[m] = residue(2 * m) + residue(2 * m + 1)
        pair_perm[m] = (perm[height + 2 * m] + perm[height + 2 * m + 1]) * 0.125
    half = pair_right.shape[1] // 2
    rows = []
    for m in range(height // 2):
        both = [x[m, pl.ds(0, half, 2), :] + x[m, pl.ds(1, half, 2), :] for x in (pair_right, pair_perm)]
        rows.append(jnp.concatenate(both, axis=1))
    for m, x in enumerate(selector_dot(rows, lane_selector(1, LANES, 2))):
        coarse_out[m] = x


class Packed:
    def __init__(self, nz, nx, ny):
        self.nz, self.nx, self.ny = nz, nx, ny
        self.groups = min(LANES // ny, nz)
        self.planes = nz // self.groups

    def lower(self, planes, p):
        return planes[p - 1] if p else roll(planes[self.planes - 1], self.ny, 1)

    def upper(self, planes, p):
        return planes[p + 1] if p + 1 < self.planes else roll(planes[0], -self.ny, 1)

    def system(self, right, perm, level):
        lane = iota((self.nx, LANES), 1)
        used = lane < self.groups * self.ny
        if self.groups * self.ny < LANES:
            perm = [jnp.where(used, x, 1.0) for x in perm]
        coefs, const, diagonals = [], [], []
        for p in range(self.planes):
            below, above = ZSCALE, ZSCALE
            if p == 0:
                below = jnp.where(lane < self.ny, 0.0, ZSCALE)
            if p + 1 == self.planes:
                above = jnp.where(lane < (self.groups - 1) * self.ny, ZSCALE, 0.0)
            faces, diagonal = face_terms(
                perm[p], self.lower(perm, p), self.upper(perm, p), below, above, self.ny
            )
            inverse = OMEGA * inverse_of(diagonal)
            coefs.append([inverse * face for face in faces])
            const.append(inverse * right[p] * (4.0**-level))
            diagonals.append(diagonal * (4.0**level / OMEGA))
        return coefs, const, diagonals

    def apply(self, values, coefs, bases):
        return [
            stencil(values[p], self.lower(values, p), self.upper(values, p), coefs[p], bases[p])
            for p in range(self.planes)
        ]

    def sweep(self, values, coefs, const):
        return self.apply(values, coefs, [KEEP * v + c for v, c in zip(values, const)])

    def coarser(self):
        return Packed(self.nz // 2, self.nx // 2, self.ny // 2)

    def restrict(self, fields, pads):
        coarse = self.coarser()
        step = coarse.groups // self.groups
        half = coarse.nx
        parts = []
        for values, pad in zip(fields, pads):
            rows = []
            for m in range(self.planes // 2):
                pad[m] = values[2 * m] + values[2 * m + 1]
                rows.append(pad[m, pl.ds(0, half, 2), :] + pad[m, pl.ds(1, half, 2), :])
            for p in range(coarse.planes):
                blocks = rows[p :: coarse.planes]
                parts.append(jnp.concatenate(blocks, axis=1) if step > 1 else blocks[0])
        sums = selector_dot(parts, lane_selector(self.groups, self.ny, step))
        return [sums[i : i + coarse.planes] for i in range(0, len(sums), coarse.planes)]

    def prolong(self, values, pad):
        coarse = self.coarser()
        step = coarse.groups // self.groups
        half = coarse.nx
        wide = selector_dot(values, lane_selector(self.groups, self.ny, step, spread=True))
        out = []
        for m in range(self.planes // 2):
            j, p = divmod(m, coarse.planes)
            plane = wide[p][:, j * LANES : (j + 1) * LANES]
            pad[m, pl.ds(0, half, 2), :] = plane
            pad[m, pl.ds(1, half, 2), :] = plane
            out += [pad[m], pad[m]]
        return out


class Flat:
    def __init__(self, finer):
        coarse = finer.coarser()
        self.finer = finer
        self.nz, self.nx, self.ny = coarse.nz, coarse.nx, coarse.ny
        self.pairs = finer.planes // 2
        self.rows = max(8, self.nz)
        self.shape = (self.rows, LANES)
        self.buffer_rows = 2 * (self.rows + 2 * POWER)

    def selector(self, spread=False):
        wide = self.finer.groups * LANES
        shape = (wide, LANES) if spread else (LANES, wide)
        fine, flat = iota(shape, int(spread)), iota(shape, 1 - int(spread))
        bits = self.finer.ny.bit_length() - 1
        same = (fine >> bits) == (flat >> 7)
        same &= ((fine & (self.finer.ny - 1)) >> 1) == (flat & (self.ny - 1))
        return jnp.where(same, 1.0, 0.0).astype(jnp.bfloat16)

    def diagonal(self):
        shape = (self.nx, LANES)
        return iota(shape, 0) == (iota(shape, 1) >> (self.ny.bit_length() - 1))

    def restrict(self, fields, pads, pack):
        parts = []
        for values, pad in zip(fields, pads):
            for m in range(self.pairs):
                pad[m] = values[2 * m] + values[2 * m + 1]
                parts.append(pad[m, pl.ds(0, self.nx, 2), :] + pad[m, pl.ds(1, self.nx, 2), :])
        sums = selector_dot(parts, self.selector())
        mask = self.diagonal()
        pack[...] = jnp.zeros_like(pack)
        for i in range(len(fields)):
            for z in range(self.nz):
                s, m = divmod(z, self.pairs)
                block = sums[i * self.pairs + m][:, s * LANES : (s + 1) * LANES]
                row = jnp.sum(jnp.where(mask, block, 0.0), axis=0, keepdims=True)
                pack[i, z : z + 1, :] = row
        return [pack[i] for i in range(len(fields))]

    def prolong(self, values, pad, pack):
        mask = self.diagonal()
        pack[0] = values
        parts = []
        for m in range(self.pairs):
            layers = [s * self.pairs + m for s in range(self.finer.groups)]
            spread = [jnp.broadcast_to(pack[0, z : z + 1, :], mask.shape) for z in layers]
            parts.append(jnp.concatenate([jnp.where(mask, x, 0.0) for x in spread], axis=1))
        out = []
        for m, wide in enumerate(selector_dot(parts, self.selector(spread=True))):
            pad[m, pl.ds(0, self.nx, 2), :] = wide
            pad[m, pl.ds(1, self.nx, 2), :] = wide
            out += [pad[m], pad[m]]
        return out

    def system(self, right, perm, level):
        lane, row = iota(self.shape, 1), iota(self.shape, 0)
        x, y = lane >> (self.ny.bit_length() - 1), lane & (self.ny - 1)
        real = row < self.nz
        perm = jnp.where(real, perm, 1.0)
        west = jnp.where(x == 0, 0.0, harmonic(perm, roll(perm, self.ny, 1)))
        east = roll(west, -self.ny, 1)
        south = jnp.where(y == 0, 0.0, harmonic(perm, roll(perm, 1, 1)))
        north = roll(south, -1, 1)
        below = ZSCALE * harmonic(perm, roll(perm, 1, 0))
        below = jnp.where((row > 0) & real, below, 0.0)
        above = roll(below, -1, 0)
        faces = [west, east, south, north, below, above]
        ends = (x == 0, x == self.nx - 1, y == 0, y == self.ny - 1)
        diagonal = tree_sum(faces + [jnp.where(end, perm, 0.0) for end in ends])
        inverse = jnp.where(real, OMEGA * inverse_of(diagonal), 0.0)
        keys = ((-1, 0, 0), (1, 0, 0), (0, -1, 0), (0, 1, 0), (0, 0, -1), (0, 0, 1))
        terms = {key: inverse * face for key, face in zip(keys, faces)}
        terms[0, 0, 0] = jnp.full(self.shape, KEEP, F32)
        return terms, inverse * right * (4.0**-level)

    def product(self, first, second):
        sums = {}
        for (dx, dy, dz), coef in first.items():
            for other, moved in second.items():
                if dz:
                    moved = roll(moved, -dz, 0)
                if dx or dy:
                    moved = roll(moved, -(dx * self.ny + dy), 1)
                total = tuple(a + b for a, b in zip((dx, dy, dz), other))
                sums.setdefault(total, []).append(coef * moved)
        return {key: tree_sum(parts) for key, parts in sums.items()}

    def apply(self, terms, values, base, buffer):
        buffer[pl.ds(2 * POWER, self.rows, 2), :] = values
        moved = {}
        for dx, dy, dz in sorted(terms, key=lambda key: abs(key[2])):
            if (0, 0, dz) not in moved:
                moved[0, 0, dz] = buffer[pl.ds(2 * (POWER + dz), self.rows, 2), :] if dz else values
            if dx or dy:
                moved[dx, dy, dz] = roll(moved[0, 0, dz], -(dx * self.ny + dy), 1)
        return tree_sum([base] + [coef * moved[key] for key, coef in terms.items()])

    def solve(self, right, perm, level, buffer):
        buffer[...] = jnp.zeros_like(buffer)
        terms, const = self.system(right, perm, level)
        power, base = terms, const
        for _ in range(POWER - 1):
            base = self.apply(terms, base, const, buffer)
            power = self.product(terms, power)
        whole = COARSE_SWEEPS % POWER == 0
        start = base if whole else const
        steps = (COARSE_SWEEPS - 1) // POWER
        assert steps * POWER + (POWER if whole else 1) == COARSE_SWEEPS
        return lax.fori_loop(
            0, steps, lambda step, values: self.apply(power, values, base, buffer), start
        )


def tree_sum(parts):
    while len(parts) > 1:
        odd = parts[len(parts) // 2 * 2 :]
        parts = [a + b for a, b in zip(parts[::2], parts[1::2])] + odd
    return parts[0]


def packed_cycle(grid, right, perm, level, pads, store):
    pad_right, pad_perm = pads[0]
    coefs, const, diagonals = grid.system(right, perm, level)
    values = grid.sweep(const, coefs, const)
    scaled = grid.apply(values, coefs, [c - OMEGA * v for c, v in zip(const, values)])
    residue = [r * d for r, d in zip(scaled, diagonals)]
    if len(pads) > 1:
        coarse_right, coarse_perm = grid.restrict((residue, perm), (pad_right, pad_perm))
        coarse_perm = [x * 0.125 for x in coarse_perm]
        update = packed_cycle(grid.coarser(), coarse_right, coarse_perm, level + 1, pads[1:], store)
        update = grid.prolong(update, pad_right)
    else:
        pack, buffer = store
        flat = Flat(grid)
        coarse_right, coarse_perm = flat.restrict((residue, perm), (pad_right, pad_perm), pack)
        update = flat.solve(coarse_right, coarse_perm * 0.125, level + 1, buffer)
        update = flat.prolong(update, pad_right, pack)
    values = [v + e for v, e in zip(values, update)]
    for _ in range(2):
        values = grid.sweep(values, coefs, const)
    return values


def coarse_kernel(
    dom_ref, gathered, coef, const, before, out,
    level, first, pad_right1, pad_perm1, pad_right2, pad_perm2, update, pack, buffer,
):
    height = out.shape[0]
    dom = dom_ref[0]
    domains, own, nx, _ = gathered.shape
    ny = LANES // 2
    grid = Packed(domains * own, nx, ny)
    left = iota((nx, LANES), 1) < ny
    right, perm = [], []
    for p in range(grid.planes):
        a = gathered[p // own, p % own]
        q = grid.planes + p
        b = gathered[q // own, q % own]
        right.append(jnp.where(left, a, roll(b, ny, 1)))
        perm.append(jnp.where(left, roll(a, ny, 1), b))
    pads = [(pad_right1, pad_perm1), (pad_right2, pad_perm2)]
    solved = packed_cycle(grid, right, perm, 1, pads, (pack, buffer))
    for p in range(grid.planes):
        update[p] = solved[p]
    planes, group = [], []
    for j in range(own + 2):
        layer = jnp.clip(dom * own + j - 1, 0, grid.nz - 1)
        group.append(layer // grid.planes)
        planes.append(update[lax.rem(layer, grid.planes)])
    for j, wide in enumerate(selector_dot(planes, lane_selector(1, LANES, 2, spread=True))):
        plane = jnp.where(group[j] == 0, wide[:, :LANES], wide[:, LANES:])
        pad = first.at[0]
        pad[pl.ds(0, nx, 2), :] = plane
        pad[pl.ds(1, nx, 2), :] = plane
        whole = first[0]
        level[2 * j] = before[2 * j] + whole
        level[2 * j + 1] = before[2 * j + 1] + whole

    def sweep(source, at, i):
        centre = source[i + 1]
        near = [coef[k, at + i] for k in range(6)]
        return stencil(centre, source[i], source[i + 2], near, KEEP * centre + const[at + i])

    def one(i):
        first[i] = sweep(level, 2, i)

    for i in range(height + 2):
        one(i)

    def two(i):
        out[i] = sweep(first, 3, i)

    for i in range(height):
        two(i)


def fine_part(dom, perm, source, layers):
    height, nx, ny = perm[0].shape
    field = lambda *lead: pltpu.VMEM(lead + (nx, ny), F32)
    vmem = pl.BlockSpec(memory_space=pltpu.VMEM)
    smem = pl.BlockSpec(memory_space=pltpu.SMEM)
    return pl.pallas_call(
        functools.partial(fine_kernel, layers),
        out_shape=(
            jax.ShapeDtypeStruct((6, height + 6, nx, ny), F32),
            jax.ShapeDtypeStruct((height + 6, nx, ny), F32),
            jax.ShapeDtypeStruct((height + 4, nx, ny), F32),
            jax.ShapeDtypeStruct((height // 2, nx // 2, ny), F32),
        ),
        in_specs=[smem] + [vmem] * 8,
        out_specs=(vmem,) * 4,
        scratch_shapes=[
            field(3 * height),
            field(3 * height),
            field(height + 6),
            field(height // 2),
            field(height // 2),
        ],
        compiler_params=pltpu.CompilerParams(vmem_limit_bytes=VMEM_LIMIT),
        name="fine",
    )(dom, *perm, *source)


def coarse_part(dom, gathered, coefs, const, values, height):
    _, nx, ny = values.shape
    field = lambda *shape: pltpu.VMEM(shape, F32)
    grid1 = Packed(gathered.shape[0] * gathered.shape[1], nx // 2, ny // 2)
    grid2 = grid1.coarser()
    pads1 = field(grid1.planes // 2, grid1.nx, LANES)
    pads2 = field(grid2.planes // 2, grid2.nx, LANES)
    vmem = pl.BlockSpec(memory_space=pltpu.VMEM)
    smem = pl.BlockSpec(memory_space=pltpu.SMEM)
    return pl.pallas_call(
        coarse_kernel,
        out_shape=jax.ShapeDtypeStruct((height, nx, ny), F32),
        in_specs=[smem] + [vmem] * 4,
        out_specs=vmem,
        scratch_shapes=[
            field(*values.shape),
            field(height + 2, nx, ny),
            pads1, pads1, pads2, pads2,
            field(grid1.planes, grid1.nx, LANES),
            field(2, Flat(grid2).rows, LANES),
            field(Flat(grid2).buffer_rows, LANES),
        ],
        compiler_params=pltpu.CompilerParams(vmem_limit_bytes=VMEM_LIMIT),
        name="coarse",
    )(dom, gathered, coefs, const, values)


def swaps(x, axis, step):
    return lax.ppermute(x, axis, [(i, i ^ step) for i in range(lax.axis_size(axis))])


def pass_on(x):
    count = lax.axis_size("dom")
    ring = [(i, i + 2) for i in range(0, count - 2, 2)] + [(count - 2, count - 1)]
    ring += [(i, i - 2) for i in range(3, count, 2)] + [(1, 0)]
    return lax.ppermute(x, "dom", ring)


def source_side(x):
    props, domains = lax.axis_size("prop"), lax.axis_size("dom")
    pairs = []
    for p in range(props):
        for d in range(domains):
            if p % 2 == 0:
                partner = p * domains + (d ^ 1)
            elif d in (0, domains - 1):
                partner = (p ^ 2) * domains + d
            else:
                partner = p * domains + ((d + 1) ^ 1) - 1
            pairs.append((p * domains + d, partner))
    return lax.ppermute(x, ("prop", "dom"), pairs)


def from_accepted(mine, accepted, beside):
    props = lax.axis_size("prop")
    step = props // 2
    own = SHRINK * mine
    offers, order = [mine], [0]
    while step:
        came = [swaps(x, "prop", step) for x in offers]
        if step == props // 2:
            came, own, beside = lax.optimization_barrier((came, own, beside))
        offers, order = offers + came, order + [x ^ step for x in order]
        step //= 2
    wanted = lax.axis_index("prop") ^ accepted
    current = offers[1]
    for at, offer in zip(order[2:], offers[2:]):
        current = jnp.where(wanted == at, offer, current)
    return jnp.where(wanted == 0, own, SHRINK * current), beside


def gather_parts(mine):
    domains = lax.axis_size("dom")
    copies = jnp.broadcast_to(mine[None], (domains,) + mine.shape)
    return lax.all_to_all(copies, "dom", 0, 0)


def body(states, accepted, noise, source):
    domains = lax.axis_size("dom")
    height = source.shape[0]
    dom = jnp.stack([lax.axis_index("dom"), lax.axis_index("prop")]).astype(jnp.int32)
    near = source_side(source)
    beside = (OMEGA * source, BETA * noise[0])
    current, (scaled, noise_part) = from_accepted(states[0], accepted[0], beside)
    perm = jnp.exp(current + noise_part)
    chunks = [perm[: height // 2], perm[height // 2 :]]
    pairs = [swaps(x, "dom", 1) for x in chunks]
    perms = [perm] + pairs + [pass_on(x) for x in pairs]
    sources = (scaled, near, swaps(near, "prop", 1))
    *level, coarse = fine_part(dom, perms, sources, domains * height)
    return coarse_part(dom, gather_parts(coarse), *level, height)[None]


def solution(mesh):
    in_specs = (
        P("prop", "dom", None, None),
        P(),
        P("prop", "dom", None, None),
        P("dom", None, None),
    )
    out_specs = P("prop", "dom", None, None)
    return jax.shard_map(body, mesh=mesh, in_specs=in_specs, out_specs=out_specs, check_vma=False)
```

```python
import functools
import math

import jax
import jax.numpy as jnp
from jax import lax
from jax.experimental import pallas as pl
from jax.experimental.pallas import tpu as pltpu
from jax.sharding import PartitionSpec as P

COARSE_SWEEPS = 64
POWER = 2
OMEGA = 0.7
KEEP = 1.0 - OMEGA
BETA = 0.4
SHRINK = math.sqrt(1.0 - BETA * BETA)
ZSCALE = 16.0
LANES = 128
VMEM_LIMIT = 40 * 1024 * 1024
F32 = jnp.float32
WEST, EAST, SOUTH, NORTH, BELOW, ABOVE, CONST = range(7)


def iota(shape, dim):
    return lax.broadcasted_iota(jnp.int32, shape, dim)


def roll(x, amount, axis):
    axis = axis % x.ndim
    return pltpu.roll(x, amount % x.shape[axis], axis)


def inverse_of(x):
    guess = pl.reciprocal(x, approx=True)
    return guess * (2.0 - x * guess)


def harmonic(a, b):
    return (2.0 * a) * b * inverse_of(a + b)


def selector_dot(parts, selector):
    x = jnp.concatenate(parts, axis=0) if len(parts) > 1 else parts[0]
    rows = x.shape[0]
    high = x.astype(jnp.bfloat16).astype(F32)
    rest = x - high
    middle = rest.astype(jnp.bfloat16).astype(F32)
    terms = jnp.concatenate([high, middle, rest - middle], axis=0).astype(jnp.bfloat16)
    y = jnp.dot(terms, selector, preferred_element_type=F32)
    total = y[:rows] + y[rows : 2 * rows] + y[2 * rows :]
    height = parts[0].shape[0]
    return [total[i * height : (i + 1) * height] for i in range(len(parts))]


def face_terms(perm, lower, upper, below_scale, above_scale, ny):
    shape = perm.shape
    rows = iota(shape, 0)
    columns = iota(shape, 1) & (ny - 1)
    west = jnp.where(rows == 0, 0.0, harmonic(perm, roll(perm, 1, 0)))
    east = roll(west, -1, 0)
    south = jnp.where(columns == 0, 0.0, harmonic(perm, roll(perm, 1, 1)))
    north = roll(south, -1, 1)
    below = below_scale * harmonic(perm, lower)
    above = above_scale * harmonic(perm, upper)
    ends = jnp.where(rows == 0, perm, 0.0) + jnp.where(rows == shape[0] - 1, perm, 0.0)
    ends = ends + jnp.where(columns == 0, perm, 0.0) + jnp.where(columns == ny - 1, perm, 0.0)
    diagonal = ((west + east) + (south + north)) + ((below + above) + ends)
    return (west, east, south, north, below, above), diagonal


def stencil(values, lower, upper, coefs, base):
    x = coefs[0] * roll(values, 1, 0) + coefs[1] * roll(values, -1, 0)
    y = coefs[2] * roll(values, 1, 1) + coefs[3] * roll(values, -1, 1)
    z = coefs[4] * lower + coefs[5] * upper
    return (x + y) + (z + base)


def lane_selector(groups, ny, step, spread=False):
    shape = (LANES, step * LANES) if spread else (step * LANES, LANES)
    source, target = iota(shape, int(spread)), iota(shape, 1 - int(spread))
    bits = ny.bit_length() - 1
    lane = source & (LANES - 1)
    group = (lane >> bits) * step + (source >> 7)
    wanted = (group << (bits - 1)) + ((lane & (ny - 1)) >> 1)
    return jnp.where((target == wanted) & (lane < groups * ny), 1.0, 0.0).astype(jnp.bfloat16)


def fine_kernel(
    layers,
    dom_ref,
    per, per_pair, per_other,
    src, src_near, src_next,
    coef, const, values, coarse_out,
    perm, right, diag, pair_right, pair_perm,
):
    height = per.shape[0]
    dom = dom_ref[0]
    pair_at = jnp.where(lax.rem(dom, 2) == 0, 2 * height, 0)
    other_at = 2 * height - pair_at

    near_at = jnp.where(lax.rem(dom_ref[1], 2) == 0, pair_at, other_at)
    next_at = 2 * height - near_at
    for i in range(height):
        for at, p in ((height, per), (pair_at, per_pair), (other_at, per_other)):
            perm[at + i] = p[i]
        right[height + i] = src[i]
        right[near_at + i] = OMEGA * src_near[i]
        right[next_at + i] = OMEGA * src_next[i]

    def build(i):
        z = dom * height + i - 3
        below = jnp.where((z > 0) & (z < layers), ZSCALE, 0.0)
        above = jnp.where((z + 1 > 0) & (z + 1 < layers), ZSCALE, 0.0)
        at = height - 3 + i
        faces, diagonal = face_terms(perm[at], perm[at - 1], perm[at + 1], below, above, LANES)
        inverse = inverse_of(diagonal)
        const[i] = inverse * right[at]
        inverse = OMEGA * inverse
        for k in range(6):
            coef[k, i] = inverse * faces[k]
        diag[i] = diagonal

    for i in range(height + 6):
        build(i)

    def first(i):
        start = const[i + 1]
        near = [coef[k, i + 1] for k in range(6)]
        values[i] = stencil(start, const[i], const[i + 2], near, (1.0 + KEEP) * start)

    for i in range(height + 4):
        first(i)

    def residue(i):
        centre = values[i + 2]
        base = const[i + 3] - OMEGA * centre
        near = [coef[k, i + 3] for k in range(6)]
        scaled = stencil(centre, values[i + 1], values[i + 3], near, base)
        return scaled * (diag[i + 3] * (1.0 / OMEGA))

    for m in range(height // 2):
        pair_right[m] = residue(2 * m) + residue(2 * m + 1)
        pair_perm[m] = (perm[height + 2 * m] + perm[height + 2 * m + 1]) * 0.125
    half = pair_right.shape[1] // 2
    rows = []
    for m in range(height // 2):
        both = [x[m, pl.ds(0, half, 2), :] + x[m, pl.ds(1, half, 2), :] for x in (pair_right, pair_perm)]
        rows.append(jnp.concatenate(both, axis=1))
    for m, x in enumerate(selector_dot(rows, lane_selector(1, LANES, 2))):
        coarse_out[m] = x


class Packed:
    def __init__(self, nz, nx, ny):
        self.nz, self.nx, self.ny = nz, nx, ny
        self.groups = min(LANES // ny, nz)
        self.planes = nz // self.groups

    def lower(self, planes, p):
        return planes[p - 1] if p else roll(planes[self.planes - 1], self.ny, 1)

    def upper(self, planes, p):
        return planes[p + 1] if p + 1 < self.planes else roll(planes[0], -self.ny, 1)

    def system(self, right, perm, level):
        lane = iota((self.nx, LANES), 1)
        used = lane < self.groups * self.ny
        if self.groups * self.ny < LANES:
            perm = [jnp.where(used, x, 1.0) for x in perm]
        coefs, const, diagonals = [], [], []
        for p in range(self.planes):
            below, above = ZSCALE, ZSCALE
            if p == 0:
                below = jnp.where(lane < self.ny, 0.0, ZSCALE)
            if p + 1 == self.planes:
                above = jnp.where(lane < (self.groups - 1) * self.ny, ZSCALE, 0.0)
            faces, diagonal = face_terms(
                perm[p], self.lower(perm, p), self.upper(perm, p), below, above, self.ny
            )
            inverse = OMEGA * inverse_of(diagonal)
            coefs.append([inverse * face for face in faces])
            const.append(inverse * right[p] * (4.0**-level))
            diagonals.append(diagonal * (4.0**level / OMEGA))
        return coefs, const, diagonals

    def apply(self, values, coefs, bases):
        return [
            stencil(values[p], self.lower(values, p), self.upper(values, p), coefs[p], bases[p])
            for p in range(self.planes)
        ]

    def sweep(self, values, coefs, const):
        return self.apply(values, coefs, [KEEP * v + c for v, c in zip(values, const)])

    def coarser(self):
        return Packed(self.nz // 2, self.nx // 2, self.ny // 2)

    def restrict(self, fields, pads):
        coarse = self.coarser()
        step = coarse.groups // self.groups
        half = coarse.nx
        parts = []
        for values, pad in zip(fields, pads):
            rows = []
            for m in range(self.planes // 2):
                pad[m] = values[2 * m] + values[2 * m + 1]
                rows.append(pad[m, pl.ds(0, half, 2), :] + pad[m, pl.ds(1, half, 2), :])
            for p in range(coarse.planes):
                blocks = rows[p :: coarse.planes]
                parts.append(jnp.concatenate(blocks, axis=1) if step > 1 else blocks[0])
        sums = selector_dot(parts, lane_selector(self.groups, self.ny, step))
        return [sums[i : i + coarse.planes] for i in range(0, len(sums), coarse.planes)]

    def prolong(self, values, pad):
        coarse = self.coarser()
        step = coarse.groups // self.groups
        half = coarse.nx
        wide = selector_dot(values, lane_selector(self.groups, self.ny, step, spread=True))
        out = []
        for m in range(self.planes // 2):
            j, p = divmod(m, coarse.planes)
            plane = wide[p][:, j * LANES : (j + 1) * LANES]
            pad[m, pl.ds(0, half, 2), :] = plane
            pad[m, pl.ds(1, half, 2), :] = plane
            out += [pad[m], pad[m]]
        return out


class Flat:
    def __init__(self, finer):
        coarse = finer.coarser()
        self.finer = finer
        self.nz, self.nx, self.ny = coarse.nz, coarse.nx, coarse.ny
        self.pairs = finer.planes // 2
        self.rows = max(8, self.nz)
        self.shape = (self.rows, LANES)
        self.buffer_rows = 2 * (self.rows + 2 * POWER)

    def selector(self, spread=False):
        wide = self.finer.groups * LANES
        shape = (wide, LANES) if spread else (LANES, wide)
        fine, flat = iota(shape, int(spread)), iota(shape, 1 - int(spread))
        bits = self.finer.ny.bit_length() - 1
        same = (fine >> bits) == (flat >> 7)
        same &= ((fine & (self.finer.ny - 1)) >> 1) == (flat & (self.ny - 1))
        return jnp.where(same, 1.0, 0.0).astype(jnp.bfloat16)

    def diagonal(self):
        shape = (self.nx, LANES)
        return iota(shape, 0) == (iota(shape, 1) >> (self.ny.bit_length() - 1))

    def restrict(self, fields, pads, pack):
        parts = []
        for values, pad in zip(fields, pads):
            for m in range(self.pairs):
                pad[m] = values[2 * m] + values[2 * m + 1]
                parts.append(pad[m, pl.ds(0, self.nx, 2), :] + pad[m, pl.ds(1, self.nx, 2), :])
        sums = selector_dot(parts, self.selector())
        mask = self.diagonal()
        pack[...] = jnp.zeros_like(pack)
        for i in range(len(fields)):
            for z in range(self.nz):
                s, m = divmod(z, self.pairs)
                block = sums[i * self.pairs + m][:, s * LANES : (s + 1) * LANES]
                row = jnp.sum(jnp.where(mask, block, 0.0), axis=0, keepdims=True)
                pack[i, z : z + 1, :] = row
        return [pack[i] for i in range(len(fields))]

    def prolong(self, values, pad, pack):
        mask = self.diagonal()
        pack[0] = values
        parts = []
        for m in range(self.pairs):
            layers = [s * self.pairs + m for s in range(self.finer.groups)]
            spread = [jnp.broadcast_to(pack[0, z : z + 1, :], mask.shape) for z in layers]
            parts.append(jnp.concatenate([jnp.where(mask, x, 0.0) for x in spread], axis=1))
        out = []
        for m, wide in enumerate(selector_dot(parts, self.selector(spread=True))):
            pad[m, pl.ds(0, self.nx, 2), :] = wide
            pad[m, pl.ds(1, self.nx, 2), :] = wide
            out += [pad[m], pad[m]]
        return out

    def system(self, right, perm, level):
        lane, row = iota(self.shape, 1), iota(self.shape, 0)
        x, y = lane >> (self.ny.bit_length() - 1), lane & (self.ny - 1)
        real = row < self.nz
        perm = jnp.where(real, perm, 1.0)
        west = jnp.where(x == 0, 0.0, harmonic(perm, roll(perm, self.ny, 1)))
        east = roll(west, -self.ny, 1)
        south = jnp.where(y == 0, 0.0, harmonic(perm, roll(perm, 1, 1)))
        north = roll(south, -1, 1)
        below = ZSCALE * harmonic(perm, roll(perm, 1, 0))
        below = jnp.where((row > 0) & real, below, 0.0)
        above = roll(below, -1, 0)
        faces = [west, east, south, north, below, above]
        ends = (x == 0, x == self.nx - 1, y == 0, y == self.ny - 1)
        diagonal = tree_sum(faces + [jnp.where(end, perm, 0.0) for end in ends])
        inverse = jnp.where(real, OMEGA * inverse_of(diagonal), 0.0)
        keys = ((-1, 0, 0), (1, 0, 0), (0, -1, 0), (0, 1, 0), (0, 0, -1), (0, 0, 1))
        terms = {key: inverse * face for key, face in zip(keys, faces)}
        terms[0, 0, 0] = jnp.full(self.shape, KEEP, F32)
        return terms, inverse * right * (4.0**-level)

    def product(self, first, second):
        sums = {}
        for (dx, dy, dz), coef in first.items():
            for other, moved in second.items():
                if dz:
                    moved = roll(moved, -dz, 0)
                if dx or dy:
                    moved = roll(moved, -(dx * self.ny + dy), 1)
                total = tuple(a + b for a, b in zip((dx, dy, dz), other))
                sums.setdefault(total, []).append(coef * moved)
        return {key: tree_sum(parts) for key, parts in sums.items()}

    def apply(self, terms, values, base, buffer):
        buffer[pl.ds(2 * POWER, self.rows, 2), :] = values
        moved = {}
        for dx, dy, dz in sorted(terms, key=lambda key: abs(key[2])):
            if (0, 0, dz) not in moved:
                moved[0, 0, dz] = buffer[pl.ds(2 * (POWER + dz), self.rows, 2), :] if dz else values
            if dx or dy:
                moved[dx, dy, dz] = roll(moved[0, 0, dz], -(dx * self.ny + dy), 1)
        return tree_sum([base] + [coef * moved[key] for key, coef in terms.items()])

    def solve(self, right, perm, level, buffer):
        buffer[...] = jnp.zeros_like(buffer)
        terms, const = self.system(right, perm, level)
        power, base = terms, const
        for _ in range(POWER - 1):
            base = self.apply(terms, base, const, buffer)
            power = self.product(terms, power)
        whole = COARSE_SWEEPS % POWER == 0
        start = base if whole else const
        steps = (COARSE_SWEEPS - 1) // POWER
        assert steps * POWER + (POWER if whole else 1) == COARSE_SWEEPS
        return lax.fori_loop(
            0, steps, lambda step, values: self.apply(power, values, base, buffer), start
        )


def tree_sum(parts):
    while len(parts) > 1:
        odd = parts[len(parts) // 2 * 2 :]
        parts = [a + b for a, b in zip(parts[::2], parts[1::2])] + odd
    return parts[0]


def packed_cycle(grid, right, perm, level, pads, store):
    pad_right, pad_perm = pads[0]
    coefs, const, diagonals = grid.system(right, perm, level)
    values = grid.sweep(const, coefs, const)
    scaled = grid.apply(values, coefs, [c - OMEGA * v for c, v in zip(const, values)])
    residue = [r * d for r, d in zip(scaled, diagonals)]
    if len(pads) > 1:
        coarse_right, coarse_perm = grid.restrict((residue, perm), (pad_right, pad_perm))
        coarse_perm = [x * 0.125 for x in coarse_perm]
        update = packed_cycle(grid.coarser(), coarse_right, coarse_perm, level + 1, pads[1:], store)
        update = grid.prolong(update, pad_right)
    else:
        pack, buffer = store
        flat = Flat(grid)
        coarse_right, coarse_perm = flat.restrict((residue, perm), (pad_right, pad_perm), pack)
        update = flat.solve(coarse_right, coarse_perm * 0.125, level + 1, buffer)
        update = flat.prolong(update, pad_right, pack)
    values = [v + e for v, e in zip(values, update)]
    for _ in range(2):
        values = grid.sweep(values, coefs, const)
    return values


def coarse_kernel(
    dom_ref, gathered, coef, const, before, out,
    level, first, pad_right1, pad_perm1, pad_right2, pad_perm2, update, pack, buffer,
):
    height = out.shape[0]
    dom = dom_ref[0]
    domains, own, nx, _ = gathered.shape
    ny = LANES // 2
    grid = Packed(domains * own, nx, ny)
    left = iota((nx, LANES), 1) < ny
    right, perm = [], []
    for p in range(grid.planes):
        a = gathered[p // own, p % own]
        q = grid.planes + p
        b = gathered[q // own, q % own]
        right.append(jnp.where(left, a, roll(b, ny, 1)))
        perm.append(jnp.where(left, roll(a, ny, 1), b))
    pads = [(pad_right1, pad_perm1), (pad_right2, pad_perm2)]
    solved = packed_cycle(grid, right, perm, 1, pads, (pack, buffer))
    for p in range(grid.planes):
        update[p] = solved[p]
    planes, group = [], []
    for j in range(own + 2):
        layer = jnp.clip(dom * own + j - 1, 0, grid.nz - 1)
        group.append(layer // grid.planes)
        planes.append(update[lax.rem(layer, grid.planes)])
    for j, wide in enumerate(selector_dot(planes, lane_selector(1, LANES, 2, spread=True))):
        plane = jnp.where(group[j] == 0, wide[:, :LANES], wide[:, LANES:])
        pad = first.at[0]
        pad[pl.ds(0, nx, 2), :] = plane
        pad[pl.ds(1, nx, 2), :] = plane
        whole = first[0]
        level[2 * j] = before[2 * j] + whole
        level[2 * j + 1] = before[2 * j + 1] + whole

    def sweep(source, at, i):
        centre = source[i + 1]
        near = [coef[k, at + i] for k in range(6)]
        return stencil(centre, source[i], source[i + 2], near, KEEP * centre + const[at + i])

    def one(i):
        first[i] = sweep(level, 2, i)

    for i in range(height + 2):
        one(i)

    def two(i):
        out[i] = sweep(first, 3, i)

    for i in range(height):
        two(i)


def fine_part(dom, perm, source, layers):
    height, nx, ny = perm[0].shape
    field = lambda *lead: pltpu.VMEM(lead + (nx, ny), F32)
    vmem = pl.BlockSpec(memory_space=pltpu.VMEM)
    smem = pl.BlockSpec(memory_space=pltpu.SMEM)
    return pl.pallas_call(
        functools.partial(fine_kernel, layers),
        out_shape=(
            jax.ShapeDtypeStruct((6, height + 6, nx, ny), F32),
            jax.ShapeDtypeStruct((height + 6, nx, ny), F32),
            jax.ShapeDtypeStruct((height + 4, nx, ny), F32),
            jax.ShapeDtypeStruct((height // 2, nx // 2, ny), F32),
        ),
        in_specs=[smem] + [vmem] * 6,
        out_specs=(vmem,) * 4,
        scratch_shapes=[
            field(3 * height),
            field(3 * height),
            field(height + 6),
            field(height // 2),
            field(height // 2),
        ],
        compiler_params=pltpu.CompilerParams(vmem_limit_bytes=VMEM_LIMIT),
        name="fine",
    )(dom, *perm, *source)


def coarse_part(dom, gathered, coefs, const, values, height):
    _, nx, ny = values.shape
    field = lambda *shape: pltpu.VMEM(shape, F32)
    grid1 = Packed(gathered.shape[0] * gathered.shape[1], nx // 2, ny // 2)
    grid2 = grid1.coarser()
    pads1 = field(grid1.planes // 2, grid1.nx, LANES)
    pads2 = field(grid2.planes // 2, grid2.nx, LANES)
    vmem = pl.BlockSpec(memory_space=pltpu.VMEM)
    smem = pl.BlockSpec(memory_space=pltpu.SMEM)
    return pl.pallas_call(
        coarse_kernel,
        out_shape=jax.ShapeDtypeStruct((height, nx, ny), F32),
        in_specs=[smem] + [vmem] * 4,
        out_specs=vmem,
        scratch_shapes=[
            field(*values.shape),
            field(height + 2, nx, ny),
            pads1, pads1, pads2, pads2,
            field(grid1.planes, grid1.nx, LANES),
            field(2, Flat(grid2).rows, LANES),
            field(Flat(grid2).buffer_rows, LANES),
        ],
        compiler_params=pltpu.CompilerParams(vmem_limit_bytes=VMEM_LIMIT),
        name="coarse",
    )(dom, gathered, coefs, const, values)


def swaps(x, axis, step):
    return lax.ppermute(x, axis, [(i, i ^ step) for i in range(lax.axis_size(axis))])


def other_side(x):
    props, domains = lax.axis_size("prop"), lax.axis_size("dom")
    pairs = []
    for p in range(props):
        for d in range(domains):
            end = d in (0, domains - 1)
            partner = ((p ^ 1) * domains + d) if end else (p * domains + ((d + 1) ^ 1) - 1)
            pairs.append((p * domains + d, partner))
    return lax.ppermute(x, ("prop", "dom"), pairs)


def source_side(x):
    props, domains = lax.axis_size("prop"), lax.axis_size("dom")
    pairs = []
    for p in range(props):
        for d in range(domains):
            if p % 2 == 0:
                partner = p * domains + (d ^ 1)
            elif d in (0, domains - 1):
                partner = (p ^ 2) * domains + d
            else:
                partner = p * domains + ((d + 1) ^ 1) - 1
            pairs.append((p * domains + d, partner))
    return lax.ppermute(x, ("prop", "dom"), pairs)


def from_accepted(mine, accepted, beside):
    props = lax.axis_size("prop")
    apart = lax.axis_index("prop") ^ accepted
    own = SHRINK * mine
    step = props // 2
    came = swaps(mine, "prop", step)
    came, own, beside = lax.optimization_barrier((came, own, beside))
    current = jnp.where(apart & step, SHRINK * came, own)
    while step > 1:
        step //= 2
        current = jnp.where(apart & step, swaps(current, "prop", step), current)
    return current, beside


def gather_parts(mine):
    domains = lax.axis_size("dom")
    copies = jnp.broadcast_to(mine[None], (domains,) + mine.shape)
    return lax.all_to_all(copies, "dom", 0, 0)


def body(states, accepted, noise, source):
    domains = lax.axis_size("dom")
    height = source.shape[0]
    dom = jnp.stack([lax.axis_index("dom"), lax.axis_index("prop")]).astype(jnp.int32)
    near = source_side(source)
    beside = (OMEGA * source, BETA * noise[0])
    current, (scaled, noise_part) = from_accepted(states[0], accepted[0], beside)
    perm = jnp.exp(current + noise_part)
    perms = (perm, swaps(perm, "dom", 1), other_side(perm))
    sources = (scaled, near, swaps(near, "prop", 1))
    *level, coarse = fine_part(dom, perms, sources, domains * height)
    return coarse_part(dom, gather_parts(coarse), *level, height)[None]


def solution(mesh):
    in_specs = (
        P("prop", "dom", None, None),
        P(),
        P("prop", "dom", None, None),
        P("dom", None, None),
    )
    out_specs = P("prop", "dom", None, None)
    return jax.shard_map(body, mesh=mesh, in_specs=in_specs, out_specs=out_specs, check_vma=False)
```

```python
import functools
import math

import jax
import jax.numpy as jnp
from jax import lax
from jax.experimental import pallas as pl
from jax.experimental.pallas import tpu as pltpu
from jax.sharding import PartitionSpec as P

COARSE_SWEEPS = 64
POWER = 2
OMEGA = 0.7
KEEP = 1.0 - OMEGA
BETA = 0.4
SHRINK = math.sqrt(1.0 - BETA * BETA)
ZSCALE = 16.0
LANES = 128
VMEM_LIMIT = 40 * 1024 * 1024
F32 = jnp.float32
WEST, EAST, SOUTH, NORTH, BELOW, ABOVE, CONST = range(7)


def iota(shape, dim):
    return lax.broadcasted_iota(jnp.int32, shape, dim)


def roll(x, amount, axis):
    axis = axis % x.ndim
    return pltpu.roll(x, amount % x.shape[axis], axis)


def inverse_of(x):
    guess = pl.reciprocal(x, approx=True)
    return guess * (2.0 - x * guess)


def harmonic(a, b):
    return (2.0 * a) * b * inverse_of(a + b)


def selector_dot(parts, selector):
    x = jnp.concatenate(parts, axis=0) if len(parts) > 1 else parts[0]
    rows = x.shape[0]
    high = x.astype(jnp.bfloat16).astype(F32)
    rest = x - high
    middle = rest.astype(jnp.bfloat16).astype(F32)
    terms = jnp.concatenate([high, middle, rest - middle], axis=0).astype(jnp.bfloat16)
    y = jnp.dot(terms, selector, preferred_element_type=F32)
    total = y[:rows] + y[rows : 2 * rows] + y[2 * rows :]
    height = parts[0].shape[0]
    return [total[i * height : (i + 1) * height] for i in range(len(parts))]


def face_terms(perm, lower, upper, below_scale, above_scale, ny):
    shape = perm.shape
    rows = iota(shape, 0)
    columns = iota(shape, 1) & (ny - 1)
    west = jnp.where(rows == 0, 0.0, harmonic(perm, roll(perm, 1, 0)))
    east = roll(west, -1, 0)
    south = jnp.where(columns == 0, 0.0, harmonic(perm, roll(perm, 1, 1)))
    north = roll(south, -1, 1)
    below = below_scale * harmonic(perm, lower)
    above = above_scale * harmonic(perm, upper)
    ends = jnp.where(rows == 0, perm, 0.0) + jnp.where(rows == shape[0] - 1, perm, 0.0)
    ends = ends + jnp.where(columns == 0, perm, 0.0) + jnp.where(columns == ny - 1, perm, 0.0)
    diagonal = ((west + east) + (south + north)) + ((below + above) + ends)
    return (west, east, south, north, below, above), diagonal


def stencil(values, lower, upper, coefs, base):
    x = coefs[0] * roll(values, 1, 0) + coefs[1] * roll(values, -1, 0)
    y = coefs[2] * roll(values, 1, 1) + coefs[3] * roll(values, -1, 1)
    z = coefs[4] * lower + coefs[5] * upper
    return (x + y) + (z + base)


def lane_selector(groups, ny, step, spread=False):
    shape = (LANES, step * LANES) if spread else (step * LANES, LANES)
    source, target = iota(shape, int(spread)), iota(shape, 1 - int(spread))
    bits = ny.bit_length() - 1
    lane = source & (LANES - 1)
    group = (lane >> bits) * step + (source >> 7)
    wanted = (group << (bits - 1)) + ((lane & (ny - 1)) >> 1)
    return jnp.where((target == wanted) & (lane < groups * ny), 1.0, 0.0).astype(jnp.bfloat16)


def fine_kernel(
    layers,
    dom_ref,
    per, per_pair, per_other,
    src, src_near, src_next,
    coef, const, values, coarse_out,
    perm, right, diag, pair_right, pair_perm,
):
    height = per.shape[0]
    dom = dom_ref[0]
    pair_at = jnp.where(lax.rem(dom, 2) == 0, 2 * height, 0)
    other_at = 2 * height - pair_at

    near_at = jnp.where(lax.rem(dom_ref[1], 2) == 0, pair_at, other_at)
    next_at = 2 * height - near_at
    for i in range(height):
        for at, p in ((height, per), (pair_at, per_pair), (other_at, per_other)):
            perm[at + i] = p[i]
        right[height + i] = src[i]
        right[near_at + i] = OMEGA * src_near[i]
        right[next_at + i] = OMEGA * src_next[i]

    def build(i):
        z = dom * height + i - 3
        below = jnp.where((z > 0) & (z < layers), ZSCALE, 0.0)
        above = jnp.where((z + 1 > 0) & (z + 1 < layers), ZSCALE, 0.0)
        at = height - 3 + i
        faces, diagonal = face_terms(perm[at], perm[at - 1], perm[at + 1], below, above, LANES)
        inverse = inverse_of(diagonal)
        const[i] = inverse * right[at]
        inverse = OMEGA * inverse
        for k in range(6):
            coef[k, i] = inverse * faces[k]
        diag[i] = diagonal

    for i in range(height + 6):
        build(i)

    def first(i):
        start = const[i + 1]
        near = [coef[k, i + 1] for k in range(6)]
        values[i] = stencil(start, const[i], const[i + 2], near, (1.0 + KEEP) * start)

    for i in range(height + 4):
        first(i)

    def residue(i):
        centre = values[i + 2]
        base = const[i + 3] - OMEGA * centre
        near = [coef[k, i + 3] for k in range(6)]
        scaled = stencil(centre, values[i + 1], values[i + 3], near, base)
        return scaled * (diag[i + 3] * (1.0 / OMEGA))

    for m in range(height // 2):
        pair_right[m] = residue(2 * m) + residue(2 * m + 1)
        pair_perm[m] = (perm[height + 2 * m] + perm[height + 2 * m + 1]) * 0.125
    half = pair_right.shape[1] // 2
    rows = []
    for m in range(height // 2):
        both = [x[m, pl.ds(0, half, 2), :] + x[m, pl.ds(1, half, 2), :] for x in (pair_right, pair_perm)]
        rows.append(jnp.concatenate(both, axis=1))
    for m, x in enumerate(selector_dot(rows, lane_selector(1, LANES, 2))):
        coarse_out[m] = x


class Packed:
    def __init__(self, nz, nx, ny):
        self.nz, self.nx, self.ny = nz, nx, ny
        self.groups = min(LANES // ny, nz)
        self.planes = nz // self.groups

    def lower(self, planes, p):
        return planes[p - 1] if p else roll(planes[self.planes - 1], self.ny, 1)

    def upper(self, planes, p):
        return planes[p + 1] if p + 1 < self.planes else roll(planes[0], -self.ny, 1)

    def system(self, right, perm, level):
        lane = iota((self.nx, LANES), 1)
        used = lane < self.groups * self.ny
        if self.groups * self.ny < LANES:
            perm = [jnp.where(used, x, 1.0) for x in perm]
        coefs, const, diagonals = [], [], []
        for p in range(self.planes):
            below, above = ZSCALE, ZSCALE
            if p == 0:
                below = jnp.where(lane < self.ny, 0.0, ZSCALE)
            if p + 1 == self.planes:
                above = jnp.where(lane < (self.groups - 1) * self.ny, ZSCALE, 0.0)
            faces, diagonal = face_terms(
                perm[p], self.lower(perm, p), self.upper(perm, p), below, above, self.ny
            )
            inverse = OMEGA * inverse_of(diagonal)
            coefs.append([inverse * face for face in faces])
            const.append(inverse * right[p] * (4.0**-level))
            diagonals.append(diagonal * (4.0**level / OMEGA))
        return coefs, const, diagonals

    def apply(self, values, coefs, bases):
        return [
            stencil(values[p], self.lower(values, p), self.upper(values, p), coefs[p], bases[p])
            for p in range(self.planes)
        ]

    def sweep(self, values, coefs, const):
        return self.apply(values, coefs, [KEEP * v + c for v, c in zip(values, const)])

    def coarser(self):
        return Packed(self.nz // 2, self.nx // 2, self.ny // 2)

    def restrict(self, fields, pads):
        coarse = self.coarser()
        step = coarse.groups // self.groups
        half = coarse.nx
        parts = []
        for values, pad in zip(fields, pads):
            rows = []
            for m in range(self.planes // 2):
                pad[m] = values[2 * m] + values[2 * m + 1]
                rows.append(pad[m, pl.ds(0, half, 2), :] + pad[m, pl.ds(1, half, 2), :])
            for p in range(coarse.planes):
                blocks = rows[p :: coarse.planes]
                parts.append(jnp.concatenate(blocks, axis=1) if step > 1 else blocks[0])
        sums = selector_dot(parts, lane_selector(self.groups, self.ny, step))
        return [sums[i : i + coarse.planes] for i in range(0, len(sums), coarse.planes)]

    def prolong(self, values, pad):
        coarse = self.coarser()
        step = coarse.groups // self.groups
        half = coarse.nx
        wide = selector_dot(values, lane_selector(self.groups, self.ny, step, spread=True))
        out = []
        for m in range(self.planes // 2):
            j, p = divmod(m, coarse.planes)
            plane = wide[p][:, j * LANES : (j + 1) * LANES]
            pad[m, pl.ds(0, half, 2), :] = plane
            pad[m, pl.ds(1, half, 2), :] = plane
            out += [pad[m], pad[m]]
        return out


class Flat:
    def __init__(self, finer):
        coarse = finer.coarser()
        self.finer = finer
        self.nz, self.nx, self.ny = coarse.nz, coarse.nx, coarse.ny
        self.pairs = finer.planes // 2
        self.rows = max(8, self.nz)
        self.shape = (self.rows, LANES)
        self.buffer_rows = 2 * (self.rows + 2 * POWER)

    def selector(self, spread=False):
        wide = self.finer.groups * LANES
        shape = (wide, LANES) if spread else (LANES, wide)
        fine, flat = iota(shape, int(spread)), iota(shape, 1 - int(spread))
        bits = self.finer.ny.bit_length() - 1
        same = (fine >> bits) == (flat >> 7)
        same &= ((fine & (self.finer.ny - 1)) >> 1) == (flat & (self.ny - 1))
        return jnp.where(same, 1.0, 0.0).astype(jnp.bfloat16)

    def diagonal(self):
        shape = (self.nx, LANES)
        return iota(shape, 0) == (iota(shape, 1) >> (self.ny.bit_length() - 1))

    def restrict(self, fields, pads, pack):
        parts = []
        for values, pad in zip(fields, pads):
            for m in range(self.pairs):
                pad[m] = values[2 * m] + values[2 * m + 1]
                parts.append(pad[m, pl.ds(0, self.nx, 2), :] + pad[m, pl.ds(1, self.nx, 2), :])
        sums = selector_dot(parts, self.selector())
        mask = self.diagonal()
        pack[...] = jnp.zeros_like(pack)
        for i in range(len(fields)):
            for z in range(self.nz):
                s, m = divmod(z, self.pairs)
                block = sums[i * self.pairs + m][:, s * LANES : (s + 1) * LANES]
                row = jnp.sum(jnp.where(mask, block, 0.0), axis=0, keepdims=True)
                pack[i, z : z + 1, :] = row
        return [pack[i] for i in range(len(fields))]

    def prolong(self, values, pad, pack):
        mask = self.diagonal()
        pack[0] = values
        parts = []
        for m in range(self.pairs):
            layers = [s * self.pairs + m for s in range(self.finer.groups)]
            spread = [jnp.broadcast_to(pack[0, z : z + 1, :], mask.shape) for z in layers]
            parts.append(jnp.concatenate([jnp.where(mask, x, 0.0) for x in spread], axis=1))
        out = []
        for m, wide in enumerate(selector_dot(parts, self.selector(spread=True))):
            pad[m, pl.ds(0, self.nx, 2), :] = wide
            pad[m, pl.ds(1, self.nx, 2), :] = wide
            out += [pad[m], pad[m]]
        return out

    def system(self, right, perm, level):
        lane, row = iota(self.shape, 1), iota(self.shape, 0)
        x, y = lane >> (self.ny.bit_length() - 1), lane & (self.ny - 1)
        real = row < self.nz
        perm = jnp.where(real, perm, 1.0)
        west = jnp.where(x == 0, 0.0, harmonic(perm, roll(perm, self.ny, 1)))
        east = roll(west, -self.ny, 1)
        south = jnp.where(y == 0, 0.0, harmonic(perm, roll(perm, 1, 1)))
        north = roll(south, -1, 1)
        below = ZSCALE * harmonic(perm, roll(perm, 1, 0))
        below = jnp.where((row > 0) & real, below, 0.0)
        above = roll(below, -1, 0)
        faces = [west, east, south, north, below, above]
        ends = (x == 0, x == self.nx - 1, y == 0, y == self.ny - 1)
        diagonal = tree_sum(faces + [jnp.where(end, perm, 0.0) for end in ends])
        inverse = jnp.where(real, OMEGA * inverse_of(diagonal), 0.0)
        keys = ((-1, 0, 0), (1, 0, 0), (0, -1, 0), (0, 1, 0), (0, 0, -1), (0, 0, 1))
        terms = {key: inverse * face for key, face in zip(keys, faces)}
        terms[0, 0, 0] = jnp.full(self.shape, KEEP, F32)
        return terms, inverse * right * (4.0**-level)

    def product(self, first, second):
        sums = {}
        for (dx, dy, dz), coef in first.items():
            for other, moved in second.items():
                if dz:
                    moved = roll(moved, -dz, 0)
                if dx or dy:
                    moved = roll(moved, -(dx * self.ny + dy), 1)
                total = tuple(a + b for a, b in zip((dx, dy, dz), other))
                sums.setdefault(total, []).append(coef * moved)
        return {key: tree_sum(parts) for key, parts in sums.items()}

    def apply(self, terms, values, base, buffer):
        buffer[pl.ds(2 * POWER, self.rows, 2), :] = values
        moved = {}
        for dx, dy, dz in sorted(terms, key=lambda key: abs(key[2])):
            if (0, 0, dz) not in moved:
                moved[0, 0, dz] = buffer[pl.ds(2 * (POWER + dz), self.rows, 2), :] if dz else values
            if dx or dy:
                moved[dx, dy, dz] = roll(moved[0, 0, dz], -(dx * self.ny + dy), 1)
        return tree_sum([base] + [coef * moved[key] for key, coef in terms.items()])

    def solve(self, right, perm, level, buffer):
        buffer[...] = jnp.zeros_like(buffer)
        terms, const = self.system(right, perm, level)
        power, base = terms, const
        for _ in range(POWER - 1):
            base = self.apply(terms, base, const, buffer)
            power = self.product(terms, power)
        whole = COARSE_SWEEPS % POWER == 0
        start = base if whole else const
        steps = (COARSE_SWEEPS - 1) // POWER
        assert steps * POWER + (POWER if whole else 1) == COARSE_SWEEPS
        return lax.fori_loop(
            0, steps, lambda step, values: self.apply(power, values, base, buffer), start
        )


def tree_sum(parts):
    while len(parts) > 1:
        odd = parts[len(parts) // 2 * 2 :]
        parts = [a + b for a, b in zip(parts[::2], parts[1::2])] + odd
    return parts[0]


def packed_cycle(grid, right, perm, level, pads, store):
    pad_right, pad_perm = pads[0]
    coefs, const, diagonals = grid.system(right, perm, level)
    values = grid.sweep(const, coefs, const)
    scaled = grid.apply(values, coefs, [c - OMEGA * v for c, v in zip(const, values)])
    residue = [r * d for r, d in zip(scaled, diagonals)]
    if len(pads) > 1:
        coarse_right, coarse_perm = grid.restrict((residue, perm), (pad_right, pad_perm))
        coarse_perm = [x * 0.125 for x in coarse_perm]
        update = packed_cycle(grid.coarser(), coarse_right, coarse_perm, level + 1, pads[1:], store)
        update = grid.prolong(update, pad_right)
    else:
        pack, buffer = store
        flat = Flat(grid)
        coarse_right, coarse_perm = flat.restrict((residue, perm), (pad_right, pad_perm), pack)
        update = flat.solve(coarse_right, coarse_perm * 0.125, level + 1, buffer)
        update = flat.prolong(update, pad_right, pack)
    values = [v + e for v, e in zip(values, update)]
    for _ in range(2):
        values = grid.sweep(values, coefs, const)
    return values


def coarse_kernel(
    dom_ref, gathered, coef, const, before, out,
    level, first, pad_right1, pad_perm1, pad_right2, pad_perm2, update, pack, buffer,
):
    height = out.shape[0]
    dom = dom_ref[0]
    domains, own, nx, _ = gathered.shape
    ny = LANES // 2
    grid = Packed(domains * own, nx, ny)
    left = iota((nx, LANES), 1) < ny
    right, perm = [], []
    for p in range(grid.planes):
        a = gathered[p // own, p % own]
        q = grid.planes + p
        b = gathered[q // own, q % own]
        right.append(jnp.where(left, a, roll(b, ny, 1)))
        perm.append(jnp.where(left, roll(a, ny, 1), b))
    pads = [(pad_right1, pad_perm1), (pad_right2, pad_perm2)]
    solved = packed_cycle(grid, right, perm, 1, pads, (pack, buffer))
    for p in range(grid.planes):
        update[p] = solved[p]
    planes, group = [], []
    for j in range(own + 2):
        layer = jnp.clip(dom * own + j - 1, 0, grid.nz - 1)
        group.append(layer // grid.planes)
        planes.append(update[lax.rem(layer, grid.planes)])
    for j, wide in enumerate(selector_dot(planes, lane_selector(1, LANES, 2, spread=True))):
        plane = jnp.where(group[j] == 0, wide[:, :LANES], wide[:, LANES:])
        pad = first.at[0]
        pad[pl.ds(0, nx, 2), :] = plane
        pad[pl.ds(1, nx, 2), :] = plane
        whole = first[0]
        level[2 * j] = before[2 * j] + whole
        level[2 * j + 1] = before[2 * j + 1] + whole

    def sweep(source, at, i):
        centre = source[i + 1]
        near = [coef[k, at + i] for k in range(6)]
        return stencil(centre, source[i], source[i + 2], near, KEEP * centre + const[at + i])

    def one(i):
        first[i] = sweep(level, 2, i)

    for i in range(height + 2):
        one(i)

    def two(i):
        out[i] = sweep(first, 3, i)

    for i in range(height):
        two(i)


def fine_part(dom, perm, source, layers):
    height, nx, ny = perm[0].shape
    field = lambda *lead: pltpu.VMEM(lead + (nx, ny), F32)
    vmem = pl.BlockSpec(memory_space=pltpu.VMEM)
    smem = pl.BlockSpec(memory_space=pltpu.SMEM)
    return pl.pallas_call(
        functools.partial(fine_kernel, layers),
        out_shape=(
            jax.ShapeDtypeStruct((6, height + 6, nx, ny), F32),
            jax.ShapeDtypeStruct((height + 6, nx, ny), F32),
            jax.ShapeDtypeStruct((height + 4, nx, ny), F32),
            jax.ShapeDtypeStruct((height // 2, nx // 2, ny), F32),
        ),
        in_specs=[smem] + [vmem] * 6,
        out_specs=(vmem,) * 4,
        scratch_shapes=[
            field(3 * height),
            field(3 * height),
            field(height + 6),
            field(height // 2),
            field(height // 2),
        ],
        compiler_params=pltpu.CompilerParams(vmem_limit_bytes=VMEM_LIMIT),
        name="fine",
    )(dom, *perm, *source)


def coarse_part(dom, gathered, coefs, const, values, height):
    _, nx, ny = values.shape
    field = lambda *shape: pltpu.VMEM(shape, F32)
    grid1 = Packed(gathered.shape[0] * gathered.shape[1], nx // 2, ny // 2)
    grid2 = grid1.coarser()
    pads1 = field(grid1.planes // 2, grid1.nx, LANES)
    pads2 = field(grid2.planes // 2, grid2.nx, LANES)
    vmem = pl.BlockSpec(memory_space=pltpu.VMEM)
    smem = pl.BlockSpec(memory_space=pltpu.SMEM)
    return pl.pallas_call(
        coarse_kernel,
        out_shape=jax.ShapeDtypeStruct((height, nx, ny), F32),
        in_specs=[smem] + [vmem] * 4,
        out_specs=vmem,
        scratch_shapes=[
            field(*values.shape),
            field(height + 2, nx, ny),
            pads1, pads1, pads2, pads2,
            field(grid1.planes, grid1.nx, LANES),
            field(2, Flat(grid2).rows, LANES),
            field(Flat(grid2).buffer_rows, LANES),
        ],
        compiler_params=pltpu.CompilerParams(vmem_limit_bytes=VMEM_LIMIT),
        name="coarse",
    )(dom, gathered, coefs, const, values)


def swaps(x, axis, step):
    return lax.ppermute(x, axis, [(i, i ^ step) for i in range(lax.axis_size(axis))])


def other_side(x):
    props, domains = lax.axis_size("prop"), lax.axis_size("dom")
    pairs = []
    for p in range(props):
        for d in range(domains):
            end = d in (0, domains - 1)
            partner = ((p ^ 1) * domains + d) if end else (p * domains + ((d + 1) ^ 1) - 1)
            pairs.append((p * domains + d, partner))
    return lax.ppermute(x, ("prop", "dom"), pairs)


def source_side(x):
    props, domains = lax.axis_size("prop"), lax.axis_size("dom")
    pairs = []
    for p in range(props):
        for d in range(domains):
            if p % 2 == 0:
                partner = p * domains + (d ^ 1)
            elif d in (0, domains - 1):
                partner = (p ^ 2) * domains + d
            else:
                partner = p * domains + ((d + 1) ^ 1) - 1
            pairs.append((p * domains + d, partner))
    return lax.ppermute(x, ("prop", "dom"), pairs)


def from_accepted(mine, accepted, beside):
    props = lax.axis_size("prop")
    apart = lax.axis_index("prop") ^ accepted
    own = SHRINK * mine
    step = props // 2
    came = swaps(mine, "prop", step)
    came, own, beside = lax.optimization_barrier((came, own, beside))
    current = jnp.where(apart & step, SHRINK * came, own)
    while step > 1:
        step //= 2
        current = jnp.where(apart & step, swaps(current, "prop", step), current)
    return current, beside


def gather_parts(mine):
    domains = lax.axis_size("dom")
    copies = jnp.broadcast_to(mine[None], (domains,) + mine.shape)
    return lax.all_to_all(copies, "dom", 0, 0)


def body(states, accepted, noise, source):
    domains = lax.axis_size("dom")
    height = source.shape[0]
    dom = jnp.stack([lax.axis_index("dom"), lax.axis_index("prop")]).astype(jnp.int32)
    near = source_side(source)
    current, noise_part = from_accepted(states[0], accepted[0], BETA * noise[0])
    perm, source = lax.optimization_barrier((jnp.exp(current + noise_part), source))
    perms = (perm, swaps(perm, "dom", 1), other_side(perm))
    sources = (OMEGA * source, near, swaps(near, "prop", 1))
    *level, coarse = fine_part(dom, perms, sources, domains * height)
    return coarse_part(dom, gather_parts(coarse), *level, height)[None]


def solution(mesh):
    in_specs = (
        P("prop", "dom", None, None),
        P(),
        P("prop", "dom", None, None),
        P("dom", None, None),
    )
    out_specs = P("prop", "dom", None, None)
    return jax.shard_map(body, mesh=mesh, in_specs=in_specs, out_specs=out_specs, check_vma=False)
```

```python
import functools
import math

import jax
import jax.numpy as jnp
from jax import lax
from jax.experimental import pallas as pl
from jax.experimental.pallas import tpu as pltpu
from jax.sharding import PartitionSpec as P

COARSE_SWEEPS = 64
POWER = 2
OMEGA = 0.7
KEEP = 1.0 - OMEGA
BETA = 0.4
SHRINK = math.sqrt(1.0 - BETA * BETA)
ZSCALE = 16.0
LANES = 128
VMEM_LIMIT = 40 * 1024 * 1024
F32 = jnp.float32
WEST, EAST, SOUTH, NORTH, BELOW, ABOVE, CONST = range(7)


def iota(shape, dim):
    return lax.broadcasted_iota(jnp.int32, shape, dim)


def roll(x, amount, axis):
    axis = axis % x.ndim
    return pltpu.roll(x, amount % x.shape[axis], axis)


def inverse_of(x):
    guess = pl.reciprocal(x, approx=True)
    return guess * (2.0 - x * guess)


def harmonic(a, b):
    return (2.0 * a) * b * inverse_of(a + b)


def selector_dot(parts, selector):
    x = jnp.concatenate(parts, axis=0) if len(parts) > 1 else parts[0]
    rows = x.shape[0]
    high = x.astype(jnp.bfloat16).astype(F32)
    rest = x - high
    middle = rest.astype(jnp.bfloat16).astype(F32)
    terms = jnp.concatenate([high, middle, rest - middle], axis=0).astype(jnp.bfloat16)
    y = jnp.dot(terms, selector, preferred_element_type=F32)
    total = y[:rows] + y[rows : 2 * rows] + y[2 * rows :]
    height = parts[0].shape[0]
    return [total[i * height : (i + 1) * height] for i in range(len(parts))]


def face_terms(perm, lower, upper, below_scale, above_scale, ny):
    shape = perm.shape
    rows = iota(shape, 0)
    columns = iota(shape, 1) & (ny - 1)
    west = jnp.where(rows == 0, 0.0, harmonic(perm, roll(perm, 1, 0)))
    east = roll(west, -1, 0)
    south = jnp.where(columns == 0, 0.0, harmonic(perm, roll(perm, 1, 1)))
    north = roll(south, -1, 1)
    below = below_scale * harmonic(perm, lower)
    above = above_scale * harmonic(perm, upper)
    ends = jnp.where(rows == 0, perm, 0.0) + jnp.where(rows == shape[0] - 1, perm, 0.0)
    ends = ends + jnp.where(columns == 0, perm, 0.0) + jnp.where(columns == ny - 1, perm, 0.0)
    diagonal = ((west + east) + (south + north)) + ((below + above) + ends)
    return (west, east, south, north, below, above), diagonal


def stencil(values, lower, upper, coefs, base):
    x = coefs[0] * roll(values, 1, 0) + coefs[1] * roll(values, -1, 0)
    y = coefs[2] * roll(values, 1, 1) + coefs[3] * roll(values, -1, 1)
    z = coefs[4] * lower + coefs[5] * upper
    return (x + y) + (z + base)


def lane_selector(groups, ny, step, spread=False):
    shape = (LANES, step * LANES) if spread else (step * LANES, LANES)
    source, target = iota(shape, int(spread)), iota(shape, 1 - int(spread))
    bits = ny.bit_length() - 1
    lane = source & (LANES - 1)
    group = (lane >> bits) * step + (source >> 7)
    wanted = (group << (bits - 1)) + ((lane & (ny - 1)) >> 1)
    return jnp.where((target == wanted) & (lane < groups * ny), 1.0, 0.0).astype(jnp.bfloat16)


def fine_kernel(
    layers,
    dom_ref,
    per, per_pair, per_other,
    src, src_near, src_next,
    coef, const, values, coarse_out,
    perm, right, diag, pair_right, pair_perm,
):
    height = per.shape[0]
    dom = dom_ref[0]
    pair_at = jnp.where(lax.rem(dom, 2) == 0, 2 * height, 0)
    other_at = 2 * height - pair_at

    near_at = jnp.where(lax.rem(dom_ref[1], 2) == 0, pair_at, other_at)
    next_at = 2 * height - near_at
    for i in range(height):
        for at, p in ((height, per), (pair_at, per_pair), (other_at, per_other)):
            perm[at + i] = p[i]
        right[height + i] = src[i]
        right[near_at + i] = OMEGA * src_near[i]
        right[next_at + i] = OMEGA * src_next[i]

    def build(i):
        z = dom * height + i - 3
        below = jnp.where((z > 0) & (z < layers), ZSCALE, 0.0)
        above = jnp.where((z + 1 > 0) & (z + 1 < layers), ZSCALE, 0.0)
        at = height - 3 + i
        faces, diagonal = face_terms(perm[at], perm[at - 1], perm[at + 1], below, above, LANES)
        inverse = inverse_of(diagonal)
        const[i] = inverse * right[at]
        inverse = OMEGA * inverse
        for k in range(6):
            coef[k, i] = inverse * faces[k]
        diag[i] = diagonal

    for i in range(height + 6):
        build(i)

    def first(i):
        start = const[i + 1]
        near = [coef[k, i + 1] for k in range(6)]
        values[i] = stencil(start, const[i], const[i + 2], near, (1.0 + KEEP) * start)

    for i in range(height + 4):
        first(i)

    def residue(i):
        centre = values[i + 2]
        base = const[i + 3] - OMEGA * centre
        near = [coef[k, i + 3] for k in range(6)]
        scaled = stencil(centre, values[i + 1], values[i + 3], near, base)
        return scaled * (diag[i + 3] * (1.0 / OMEGA))

    for m in range(height // 2):
        pair_right[m] = residue(2 * m) + residue(2 * m + 1)
        pair_perm[m] = (perm[height + 2 * m] + perm[height + 2 * m + 1]) * 0.125
    half = pair_right.shape[1] // 2
    rows = []
    for m in range(height // 2):
        both = [x[m, pl.ds(0, half, 2), :] + x[m, pl.ds(1, half, 2), :] for x in (pair_right, pair_perm)]
        rows.append(jnp.concatenate(both, axis=1))
    for m, x in enumerate(selector_dot(rows, lane_selector(1, LANES, 2))):
        coarse_out[m] = x


class Packed:
    def __init__(self, nz, nx, ny):
        self.nz, self.nx, self.ny = nz, nx, ny
        self.groups = min(LANES // ny, nz)
        self.planes = nz // self.groups

    def lower(self, planes, p):
        return planes[p - 1] if p else roll(planes[self.planes - 1], self.ny, 1)

    def upper(self, planes, p):
        return planes[p + 1] if p + 1 < self.planes else roll(planes[0], -self.ny, 1)

    def system(self, perm, level):
        lane = iota((self.nx, LANES), 1)
        used = lane < self.groups * self.ny
        if self.groups * self.ny < LANES:
            perm = [jnp.where(used, x, 1.0) for x in perm]
        coefs, factors, diagonals = [], [], []
        for p in range(self.planes):
            below, above = ZSCALE, ZSCALE
            if p == 0:
                below = jnp.where(lane < self.ny, 0.0, ZSCALE)
            if p + 1 == self.planes:
                above = jnp.where(lane < (self.groups - 1) * self.ny, ZSCALE, 0.0)
            faces, diagonal = face_terms(
                perm[p], self.lower(perm, p), self.upper(perm, p), below, above, self.ny
            )
            inverse = OMEGA * inverse_of(diagonal)
            coefs.append([inverse * face for face in faces])
            factors.append(inverse * (4.0**-level))
            diagonals.append(diagonal * (4.0**level / OMEGA))
        return coefs, factors, diagonals

    def apply(self, values, coefs, bases):
        return [
            stencil(values[p], self.lower(values, p), self.upper(values, p), coefs[p], bases[p])
            for p in range(self.planes)
        ]

    def sweep(self, values, coefs, const):
        return self.apply(values, coefs, [KEEP * v + c for v, c in zip(values, const)])

    def coarser(self):
        return Packed(self.nz // 2, self.nx // 2, self.ny // 2)

    def restrict(self, fields, pads):
        coarse = self.coarser()
        step = coarse.groups // self.groups
        half = coarse.nx
        parts = []
        for values, pad in zip(fields, pads):
            rows = []
            for m in range(self.planes // 2):
                pad[m] = values[2 * m] + values[2 * m + 1]
                rows.append(pad[m, pl.ds(0, half, 2), :] + pad[m, pl.ds(1, half, 2), :])
            for p in range(coarse.planes):
                blocks = rows[p :: coarse.planes]
                parts.append(jnp.concatenate(blocks, axis=1) if step > 1 else blocks[0])
        sums = selector_dot(parts, lane_selector(self.groups, self.ny, step))
        return [sums[i : i + coarse.planes] for i in range(0, len(sums), coarse.planes)]

    def prolong(self, values, pad):
        coarse = self.coarser()
        step = coarse.groups // self.groups
        half = coarse.nx
        wide = selector_dot(values, lane_selector(self.groups, self.ny, step, spread=True))
        out = []
        for m in range(self.planes // 2):
            j, p = divmod(m, coarse.planes)
            plane = wide[p][:, j * LANES : (j + 1) * LANES]
            pad[m, pl.ds(0, half, 2), :] = plane
            pad[m, pl.ds(1, half, 2), :] = plane
            out += [pad[m], pad[m]]
        return out


class Flat:
    def __init__(self, finer):
        coarse = finer.coarser()
        self.finer = finer
        self.nz, self.nx, self.ny = coarse.nz, coarse.nx, coarse.ny
        self.pairs = finer.planes // 2
        self.rows = max(8, self.nz)
        self.shape = (self.rows, LANES)
        self.buffer_rows = 2 * (self.rows + 2 * POWER)

    def selector(self, spread=False):
        wide = self.finer.groups * LANES
        shape = (wide, LANES) if spread else (LANES, wide)
        fine, flat = iota(shape, int(spread)), iota(shape, 1 - int(spread))
        bits = self.finer.ny.bit_length() - 1
        same = (fine >> bits) == (flat >> 7)
        same &= ((fine & (self.finer.ny - 1)) >> 1) == (flat & (self.ny - 1))
        return jnp.where(same, 1.0, 0.0).astype(jnp.bfloat16)

    def diagonal(self):
        shape = (self.nx, LANES)
        return iota(shape, 0) == (iota(shape, 1) >> (self.ny.bit_length() - 1))

    def restrict(self, fields, pads, pack):
        parts = []
        for values, pad in zip(fields, pads):
            for m in range(self.pairs):
                pad[m] = values[2 * m] + values[2 * m + 1]
                parts.append(pad[m, pl.ds(0, self.nx, 2), :] + pad[m, pl.ds(1, self.nx, 2), :])
        sums = selector_dot(parts, self.selector())
        mask = self.diagonal()
        pack[...] = jnp.zeros_like(pack)
        for i in range(len(fields)):
            for z in range(self.nz):
                s, m = divmod(z, self.pairs)
                block = sums[i * self.pairs + m][:, s * LANES : (s + 1) * LANES]
                row = jnp.sum(jnp.where(mask, block, 0.0), axis=0, keepdims=True)
                pack[i, z : z + 1, :] = row
        return [pack[i] for i in range(len(fields))]

    def prolong(self, values, pad, pack):
        mask = self.diagonal()
        pack[0] = values
        parts = []
        for m in range(self.pairs):
            layers = [s * self.pairs + m for s in range(self.finer.groups)]
            spread = [jnp.broadcast_to(pack[0, z : z + 1, :], mask.shape) for z in layers]
            parts.append(jnp.concatenate([jnp.where(mask, x, 0.0) for x in spread], axis=1))
        out = []
        for m, wide in enumerate(selector_dot(parts, self.selector(spread=True))):
            pad[m, pl.ds(0, self.nx, 2), :] = wide
            pad[m, pl.ds(1, self.nx, 2), :] = wide
            out += [pad[m], pad[m]]
        return out

    def system(self, perm, level):
        lane, row = iota(self.shape, 1), iota(self.shape, 0)
        x, y = lane >> (self.ny.bit_length() - 1), lane & (self.ny - 1)
        real = row < self.nz
        perm = jnp.where(real, perm, 1.0)
        west = jnp.where(x == 0, 0.0, harmonic(perm, roll(perm, self.ny, 1)))
        east = roll(west, -self.ny, 1)
        south = jnp.where(y == 0, 0.0, harmonic(perm, roll(perm, 1, 1)))
        north = roll(south, -1, 1)
        below = ZSCALE * harmonic(perm, roll(perm, 1, 0))
        below = jnp.where((row > 0) & real, below, 0.0)
        above = roll(below, -1, 0)
        faces = [west, east, south, north, below, above]
        ends = (x == 0, x == self.nx - 1, y == 0, y == self.ny - 1)
        diagonal = tree_sum(faces + [jnp.where(end, perm, 0.0) for end in ends])
        inverse = jnp.where(real, OMEGA * inverse_of(diagonal), 0.0)
        keys = ((-1, 0, 0), (1, 0, 0), (0, -1, 0), (0, 1, 0), (0, 0, -1), (0, 0, 1))
        terms = {key: inverse * face for key, face in zip(keys, faces)}
        terms[0, 0, 0] = jnp.full(self.shape, KEEP, F32)
        return terms, inverse * (4.0**-level)

    def product(self, first, second):
        sums = {}
        for (dx, dy, dz), coef in first.items():
            for other, moved in second.items():
                if dz:
                    moved = roll(moved, -dz, 0)
                if dx or dy:
                    moved = roll(moved, -(dx * self.ny + dy), 1)
                total = tuple(a + b for a, b in zip((dx, dy, dz), other))
                sums.setdefault(total, []).append(coef * moved)
        return {key: tree_sum(parts) for key, parts in sums.items()}

    def apply(self, terms, values, base, buffer):
        buffer[pl.ds(2 * POWER, self.rows, 2), :] = values
        moved = {}
        for dx, dy, dz in sorted(terms, key=lambda key: abs(key[2])):
            if (0, 0, dz) not in moved:
                moved[0, 0, dz] = buffer[pl.ds(2 * (POWER + dz), self.rows, 2), :] if dz else values
            if dx or dy:
                moved[dx, dy, dz] = roll(moved[0, 0, dz], -(dx * self.ny + dy), 1)
        return tree_sum([base] + [coef * moved[key] for key, coef in terms.items()])

    def prepare(self, perm, level):
        terms, factor = self.system(perm, level)
        power = terms
        for _ in range(POWER - 1):
            power = self.product(terms, power)
        return terms, power, factor

    def solve(self, right, prepared, buffer):
        terms, power, factor = prepared
        const = factor * right
        buffer[...] = jnp.zeros_like(buffer)
        base = const
        for _ in range(POWER - 1):
            base = self.apply(terms, base, const, buffer)
        whole = COARSE_SWEEPS % POWER == 0
        values = base if whole else const
        steps = (COARSE_SWEEPS - 1) // POWER
        assert steps * POWER + (POWER if whole else 1) == COARSE_SWEEPS
        for _ in range(steps):
            values = self.apply(power, values, base, buffer)
        return values


def tree_sum(parts):
    while len(parts) > 1:
        odd = parts[len(parts) // 2 * 2 :]
        parts = [a + b for a, b in zip(parts[::2], parts[1::2])] + odd
    return parts[0]


def systems_of(grid, perm, level, pads, pack):
    system = grid.system(perm, level)
    if len(pads) > 1:
        (coarse,) = grid.restrict([perm], pads[:1])
        coarse = [x * 0.125 for x in coarse]
        return [system] + systems_of(grid.coarser(), coarse, level + 1, pads[1:], pack)
    flat = Flat(grid)
    (coarse,) = flat.restrict([perm], pads, pack)
    return [system, flat.prepare(coarse * 0.125, level + 1)]


def packed_cycle(grid, right, systems, pads, pack, buffer):
    coefs, factors, diagonals = systems[0]
    const = [f * r for f, r in zip(factors, right)]
    values = grid.sweep(const, coefs, const)
    scaled = grid.apply(values, coefs, [c - OMEGA * v for c, v in zip(const, values)])
    residue = [r * d for r, d in zip(scaled, diagonals)]
    if len(pads) > 1:
        (coarse_right,) = grid.restrict([residue], pads[:1])
        update = packed_cycle(grid.coarser(), coarse_right, systems[1:], pads[1:], pack, buffer)
        update = grid.prolong(update, pads[0])
    else:
        flat = Flat(grid)
        (coarse_right,) = flat.restrict([residue], pads, pack)
        update = flat.prolong(flat.solve(coarse_right, systems[1], buffer), pads[0], pack)
    values = [v + e for v, e in zip(values, update)]
    for _ in range(2):
        values = grid.sweep(values, coefs, const)
    return values


def coarse_kernel(
    dom_ref, gathered, coef, const, before, out,
    level, first, pad_right1, pad_perm1, pad_right2, pad_perm2, update, pack, pack_perm, buffer,
    done, sems,
):
    height = out.shape[0]
    dom = dom_ref[0]
    domains, own, nx, _ = gathered.shape
    ny = LANES // 2
    grid = Packed(domains * own, nx, ny)
    left = iota((nx, LANES), 1) < ny
    right, perm = [], []
    for p in range(grid.planes):
        a = gathered[p // own, p % own]
        q = grid.planes + p
        b = gathered[q // own, q % own]
        right.append(jnp.where(left, a, roll(b, ny, 1)))
        perm.append(jnp.where(left, roll(a, ny, 1), b))
    systems = systems_of(grid, perm, 1, [pad_perm1, pad_perm2], pack_perm)
    solved = packed_cycle(grid, right, systems, [pad_right1, pad_right2], pack, buffer)
    for p in range(grid.planes):
        update[p] = solved[p]
    planes, group = [], []
    for j in range(own + 2):
        layer = jnp.clip(dom * own + j - 1, 0, grid.nz - 1)
        group.append(layer // grid.planes)
        planes.append(update[lax.rem(layer, grid.planes)])
    for j, wide in enumerate(selector_dot(planes, lane_selector(1, LANES, 2, spread=True))):
        plane = jnp.where(group[j] == 0, wide[:, :LANES], wide[:, LANES:])
        pad = first.at[0]
        pad[pl.ds(0, nx, 2), :] = plane
        pad[pl.ds(1, nx, 2), :] = plane
        whole = first[0]
        level[2 * j] = before[2 * j] + whole
        level[2 * j + 1] = before[2 * j + 1] + whole

    def sweep(source, at, i):
        centre = source[i + 1]
        near = [coef[k, at + i] for k in range(6)]
        return stencil(centre, source[i], source[i + 2], near, KEEP * centre + const[at + i])

    def one(i):
        first[i] = sweep(level, 2, i)

    for i in range(height + 2):
        one(i)

    copies = []
    for i in range(height):
        done[i] = sweep(first, 3, i)
        copies.append(pltpu.make_async_copy(done.at[i], out.at[i], sems.at[i]))
        copies[-1].start()
    for copy in copies:
        copy.wait()


def fine_part(dom, perm, source, layers):
    height, nx, ny = perm[0].shape
    field = lambda *lead: pltpu.VMEM(lead + (nx, ny), F32)
    vmem = pl.BlockSpec(memory_space=pltpu.VMEM)
    smem = pl.BlockSpec(memory_space=pltpu.SMEM)
    return pl.pallas_call(
        functools.partial(fine_kernel, layers),
        out_shape=(
            jax.ShapeDtypeStruct((6, height + 6, nx, ny), F32),
            jax.ShapeDtypeStruct((height + 6, nx, ny), F32),
            jax.ShapeDtypeStruct((height + 4, nx, ny), F32),
            jax.ShapeDtypeStruct((height // 2, nx // 2, ny), F32),
        ),
        in_specs=[smem] + [vmem] * 6,
        out_specs=(vmem,) * 4,
        scratch_shapes=[
            field(3 * height),
            field(3 * height),
            field(height + 6),
            field(height // 2),
            field(height // 2),
        ],
        compiler_params=pltpu.CompilerParams(vmem_limit_bytes=VMEM_LIMIT),
        name="fine",
    )(dom, *perm, *source)


def coarse_part(dom, gathered, coefs, const, values, height):
    _, nx, ny = values.shape
    field = lambda *shape: pltpu.VMEM(shape, F32)
    grid1 = Packed(gathered.shape[0] * gathered.shape[1], nx // 2, ny // 2)
    grid2 = grid1.coarser()
    pads1 = field(grid1.planes // 2, grid1.nx, LANES)
    pads2 = field(grid2.planes // 2, grid2.nx, LANES)
    vmem = pl.BlockSpec(memory_space=pltpu.VMEM)
    smem = pl.BlockSpec(memory_space=pltpu.SMEM)
    return pl.pallas_call(
        coarse_kernel,
        out_shape=jax.ShapeDtypeStruct((height, nx, ny), F32),
        in_specs=[smem] + [vmem] * 4,
        out_specs=pl.BlockSpec(memory_space=pl.ANY),
        scratch_shapes=[
            field(*values.shape),
            field(height + 2, nx, ny),
            pads1, pads1, pads2, pads2,
            field(grid1.planes, grid1.nx, LANES),
            field(1, Flat(grid2).rows, LANES),
            field(1, Flat(grid2).rows, LANES),
            field(Flat(grid2).buffer_rows, LANES),
            field(height, nx, ny),
            pltpu.SemaphoreType.DMA((height,)),
        ],
        compiler_params=pltpu.CompilerParams(vmem_limit_bytes=VMEM_LIMIT),
        name="coarse",
    )(dom, gathered, coefs, const, values)


def swaps(x, axis, step):
    return lax.ppermute(x, axis, [(i, i ^ step) for i in range(lax.axis_size(axis))])


def other_side(x):
    props, domains = lax.axis_size("prop"), lax.axis_size("dom")
    pairs = []
    for p in range(props):
        for d in range(domains):
            end = d in (0, domains - 1)
            partner = ((p ^ 1) * domains + d) if end else (p * domains + ((d + 1) ^ 1) - 1)
            pairs.append((p * domains + d, partner))
    return lax.ppermute(x, ("prop", "dom"), pairs)


def source_side(x):
    props, domains = lax.axis_size("prop"), lax.axis_size("dom")
    pairs = []
    for p in range(props):
        for d in range(domains):
            if p % 2 == 0:
                partner = p * domains + (d ^ 1)
            elif d in (0, domains - 1):
                partner = (p ^ 2) * domains + d
            else:
                partner = p * domains + ((d + 1) ^ 1) - 1
            pairs.append((p * domains + d, partner))
    return lax.ppermute(x, ("prop", "dom"), pairs)


def from_accepted(mine, accepted, beside):
    props = lax.axis_size("prop")
    apart = lax.axis_index("prop") ^ accepted
    own = SHRINK * mine
    step = props // 2
    came = swaps(mine, "prop", step)
    came, own, beside = lax.optimization_barrier((came, own, beside))
    current = jnp.where(apart & step, SHRINK * came, own)
    while step > 1:
        step //= 2
        current = jnp.where(apart & step, swaps(current, "prop", step), current)
    return current, beside


def gather_parts(mine):
    domains = lax.axis_size("dom")
    copies = jnp.broadcast_to(mine[None], (domains,) + mine.shape)
    return lax.all_to_all(copies, "dom", 0, 0)


def body(states, accepted, noise, source):
    domains = lax.axis_size("dom")
    height = source.shape[0]
    dom = jnp.stack([lax.axis_index("dom"), lax.axis_index("prop")]).astype(jnp.int32)
    near = source_side(source)
    current, noise_part = from_accepted(states[0], accepted[0], BETA * noise[0])
    perm, source = lax.optimization_barrier((jnp.exp(current + noise_part), source))
    perms = (perm, swaps(perm, "dom", 1), other_side(perm))
    sources = (OMEGA * source, near, swaps(near, "prop", 1))
    *level, coarse = fine_part(dom, perms, sources, domains * height)
    return coarse_part(dom, gather_parts(coarse), *level, height)[None]


def solution(mesh):
    in_specs = (
        P("prop", "dom", None, None),
        P(),
        P("prop", "dom", None, None),
        P("dom", None, None),
    )
    out_specs = P("prop", "dom", None, None)
    return jax.shard_map(body, mesh=mesh, in_specs=in_specs, out_specs=out_specs, check_vma=False)
```

```python
import functools
import math

import jax
import jax.numpy as jnp
from jax import lax
from jax.experimental import pallas as pl
from jax.experimental.pallas import tpu as pltpu
from jax.sharding import PartitionSpec as P

COARSE_SWEEPS = 64
POWER = 3
OMEGA = 0.7
KEEP = 1.0 - OMEGA
BETA = 0.4
SHRINK = math.sqrt(1.0 - BETA * BETA)
ZSCALE = 16.0
LANES = 128
VMEM_LIMIT = 40 * 1024 * 1024
F32 = jnp.float32
WEST, EAST, SOUTH, NORTH, BELOW, ABOVE, CONST = range(7)


def iota(shape, dim):
    return lax.broadcasted_iota(jnp.int32, shape, dim)


def roll(x, amount, axis):
    axis = axis % x.ndim
    return pltpu.roll(x, amount % x.shape[axis], axis)


def inverse_of(x):
    guess = pl.reciprocal(x, approx=True)
    return guess * (2.0 - x * guess)


def harmonic(a, b):
    return (2.0 * a) * b * inverse_of(a + b)


def selector_dot(parts, selector):
    x = jnp.concatenate(parts, axis=0) if len(parts) > 1 else parts[0]
    rows = x.shape[0]
    high = x.astype(jnp.bfloat16).astype(F32)
    rest = x - high
    middle = rest.astype(jnp.bfloat16).astype(F32)
    terms = jnp.concatenate([high, middle, rest - middle], axis=0).astype(jnp.bfloat16)
    y = jnp.dot(terms, selector, preferred_element_type=F32)
    total = y[:rows] + y[rows : 2 * rows] + y[2 * rows :]
    height = parts[0].shape[0]
    return [total[i * height : (i + 1) * height] for i in range(len(parts))]


def face_terms(perm, lower, upper, below_scale, above_scale, ny):
    shape = perm.shape
    rows = iota(shape, 0)
    columns = iota(shape, 1) & (ny - 1)
    west = jnp.where(rows == 0, 0.0, harmonic(perm, roll(perm, 1, 0)))
    east = roll(west, -1, 0)
    south = jnp.where(columns == 0, 0.0, harmonic(perm, roll(perm, 1, 1)))
    north = roll(south, -1, 1)
    below = below_scale * harmonic(perm, lower)
    above = above_scale * harmonic(perm, upper)
    ends = jnp.where(rows == 0, perm, 0.0) + jnp.where(rows == shape[0] - 1, perm, 0.0)
    ends = ends + jnp.where(columns == 0, perm, 0.0) + jnp.where(columns == ny - 1, perm, 0.0)
    diagonal = ((west + east) + (south + north)) + ((below + above) + ends)
    return (west, east, south, north, below, above), diagonal


def stencil(values, lower, upper, coefs, base):
    x = coefs[0] * roll(values, 1, 0) + coefs[1] * roll(values, -1, 0)
    y = coefs[2] * roll(values, 1, 1) + coefs[3] * roll(values, -1, 1)
    z = coefs[4] * lower + coefs[5] * upper
    return (x + y) + (z + base)


def lane_selector(groups, ny, step, spread=False):
    shape = (LANES, step * LANES) if spread else (step * LANES, LANES)
    source, target = iota(shape, int(spread)), iota(shape, 1 - int(spread))
    bits = ny.bit_length() - 1
    lane = source & (LANES - 1)
    group = (lane >> bits) * step + (source >> 7)
    wanted = (group << (bits - 1)) + ((lane & (ny - 1)) >> 1)
    return jnp.where((target == wanted) & (lane < groups * ny), 1.0, 0.0).astype(jnp.bfloat16)


def fine_kernel(
    layers,
    dom_ref,
    per, per_pair, per_other,
    src, src_near, src_next,
    coef, const, values, coarse_out,
    perm, right, diag, pair_right, pair_perm,
):
    height = per.shape[0]
    dom = dom_ref[0]
    pair_at = jnp.where(lax.rem(dom, 2) == 0, 2 * height, 0)
    other_at = 2 * height - pair_at

    near_at = jnp.where(lax.rem(dom_ref[1], 2) == 0, pair_at, other_at)
    next_at = 2 * height - near_at
    for i in range(height):
        for at, p in ((height, per), (pair_at, per_pair), (other_at, per_other)):
            perm[at + i] = p[i]
        right[height + i] = src[i]
        right[near_at + i] = OMEGA * src_near[i]
        right[next_at + i] = OMEGA * src_next[i]

    def build(i):
        z = dom * height + i - 3
        below = jnp.where((z > 0) & (z < layers), ZSCALE, 0.0)
        above = jnp.where((z + 1 > 0) & (z + 1 < layers), ZSCALE, 0.0)
        at = height - 3 + i
        faces, diagonal = face_terms(perm[at], perm[at - 1], perm[at + 1], below, above, LANES)
        inverse = inverse_of(diagonal)
        const[i] = inverse * right[at]
        inverse = OMEGA * inverse
        for k in range(6):
            coef[k, i] = inverse * faces[k]
        diag[i] = diagonal

    for i in range(height + 6):
        build(i)

    def first(i):
        start = const[i + 1]
        near = [coef[k, i + 1] for k in range(6)]
        values[i] = stencil(start, const[i], const[i + 2], near, (1.0 + KEEP) * start)

    for i in range(height + 4):
        first(i)

    def residue(i):
        centre = values[i + 2]
        base = const[i + 3] - OMEGA * centre
        near = [coef[k, i + 3] for k in range(6)]
        scaled = stencil(centre, values[i + 1], values[i + 3], near, base)
        return scaled * (diag[i + 3] * (1.0 / OMEGA))

    for m in range(height // 2):
        pair_right[m] = residue(2 * m) + residue(2 * m + 1)
        pair_perm[m] = (perm[height + 2 * m] + perm[height + 2 * m + 1]) * 0.125
    half = pair_right.shape[1] // 2
    rows = []
    for m in range(height // 2):
        both = [x[m, pl.ds(0, half, 2), :] + x[m, pl.ds(1, half, 2), :] for x in (pair_right, pair_perm)]
        rows.append(jnp.concatenate(both, axis=1))
    for m, x in enumerate(selector_dot(rows, lane_selector(1, LANES, 2))):
        coarse_out[m] = x


class Packed:
    def __init__(self, nz, nx, ny):
        self.nz, self.nx, self.ny = nz, nx, ny
        self.groups = min(LANES // ny, nz)
        self.planes = nz // self.groups

    def lower(self, planes, p):
        return planes[p - 1] if p else roll(planes[self.planes - 1], self.ny, 1)

    def upper(self, planes, p):
        return planes[p + 1] if p + 1 < self.planes else roll(planes[0], -self.ny, 1)

    def system(self, perm, level):
        lane = iota((self.nx, LANES), 1)
        used = lane < self.groups * self.ny
        if self.groups * self.ny < LANES:
            perm = [jnp.where(used, x, 1.0) for x in perm]
        coefs, factors, diagonals = [], [], []
        for p in range(self.planes):
            below, above = ZSCALE, ZSCALE
            if p == 0:
                below = jnp.where(lane < self.ny, 0.0, ZSCALE)
            if p + 1 == self.planes:
                above = jnp.where(lane < (self.groups - 1) * self.ny, ZSCALE, 0.0)
            faces, diagonal = face_terms(
                perm[p], self.lower(perm, p), self.upper(perm, p), below, above, self.ny
            )
            inverse = OMEGA * inverse_of(diagonal)
            coefs.append([inverse * face for face in faces])
            factors.append(inverse * (4.0**-level))
            diagonals.append(diagonal * (4.0**level / OMEGA))
        return coefs, factors, diagonals

    def apply(self, values, coefs, bases):
        return [
            stencil(values[p], self.lower(values, p), self.upper(values, p), coefs[p], bases[p])
            for p in range(self.planes)
        ]

    def sweep(self, values, coefs, const):
        return self.apply(values, coefs, [KEEP * v + c for v, c in zip(values, const)])

    def coarser(self):
        return Packed(self.nz // 2, self.nx // 2, self.ny // 2)

    def restrict(self, fields, pads):
        coarse = self.coarser()
        step = coarse.groups // self.groups
        half = coarse.nx
        parts = []
        for values, pad in zip(fields, pads):
            rows = []
            for m in range(self.planes // 2):
                pad[m] = values[2 * m] + values[2 * m + 1]
                rows.append(pad[m, pl.ds(0, half, 2), :] + pad[m, pl.ds(1, half, 2), :])
            for p in range(coarse.planes):
                blocks = rows[p :: coarse.planes]
                parts.append(jnp.concatenate(blocks, axis=1) if step > 1 else blocks[0])
        sums = selector_dot(parts, lane_selector(self.groups, self.ny, step))
        return [sums[i : i + coarse.planes] for i in range(0, len(sums), coarse.planes)]

    def prolong(self, values, pad):
        coarse = self.coarser()
        step = coarse.groups // self.groups
        half = coarse.nx
        wide = selector_dot(values, lane_selector(self.groups, self.ny, step, spread=True))
        out = []
        for m in range(self.planes // 2):
            j, p = divmod(m, coarse.planes)
            plane = wide[p][:, j * LANES : (j + 1) * LANES]
            pad[m, pl.ds(0, half, 2), :] = plane
            pad[m, pl.ds(1, half, 2), :] = plane
            out += [pad[m], pad[m]]
        return out


class Flat:
    def __init__(self, finer):
        coarse = finer.coarser()
        self.finer = finer
        self.nz, self.nx, self.ny = coarse.nz, coarse.nx, coarse.ny
        self.pairs = finer.planes // 2
        self.rows = max(8, self.nz)
        self.shape = (self.rows, LANES)
        self.buffer_rows = 2 * (self.rows + 2 * POWER)

    def selector(self, spread=False):
        wide = self.finer.groups * LANES
        shape = (wide, LANES) if spread else (LANES, wide)
        fine, flat = iota(shape, int(spread)), iota(shape, 1 - int(spread))
        bits = self.finer.ny.bit_length() - 1
        same = (fine >> bits) == (flat >> 7)
        same &= ((fine & (self.finer.ny - 1)) >> 1) == (flat & (self.ny - 1))
        return jnp.where(same, 1.0, 0.0).astype(jnp.bfloat16)

    def diagonal(self):
        shape = (self.nx, LANES)
        return iota(shape, 0) == (iota(shape, 1) >> (self.ny.bit_length() - 1))

    def restrict(self, fields, pads, pack):
        parts = []
        for values, pad in zip(fields, pads):
            for m in range(self.pairs):
                pad[m] = values[2 * m] + values[2 * m + 1]
                parts.append(pad[m, pl.ds(0, self.nx, 2), :] + pad[m, pl.ds(1, self.nx, 2), :])
        sums = selector_dot(parts, self.selector())
        mask = self.diagonal()
        pack[...] = jnp.zeros_like(pack)
        for i in range(len(fields)):
            for z in range(self.nz):
                s, m = divmod(z, self.pairs)
                block = sums[i * self.pairs + m][:, s * LANES : (s + 1) * LANES]
                row = jnp.sum(jnp.where(mask, block, 0.0), axis=0, keepdims=True)
                pack[i, z : z + 1, :] = row
        return [pack[i] for i in range(len(fields))]

    def prolong(self, values, pad, pack):
        mask = self.diagonal()
        pack[0] = values
        parts = []
        for m in range(self.pairs):
            layers = [s * self.pairs + m for s in range(self.finer.groups)]
            spread = [jnp.broadcast_to(pack[0, z : z + 1, :], mask.shape) for z in layers]
            parts.append(jnp.concatenate([jnp.where(mask, x, 0.0) for x in spread], axis=1))
        out = []
        for m, wide in enumerate(selector_dot(parts, self.selector(spread=True))):
            pad[m, pl.ds(0, self.nx, 2), :] = wide
            pad[m, pl.ds(1, self.nx, 2), :] = wide
            out += [pad[m], pad[m]]
        return out

    def system(self, perm, level):
        lane, row = iota(self.shape, 1), iota(self.shape, 0)
        x, y = lane >> (self.ny.bit_length() - 1), lane & (self.ny - 1)
        real = row < self.nz
        perm = jnp.where(real, perm, 1.0)
        west = jnp.where(x == 0, 0.0, harmonic(perm, roll(perm, self.ny, 1)))
        east = roll(west, -self.ny, 1)
        south = jnp.where(y == 0, 0.0, harmonic(perm, roll(perm, 1, 1)))
        north = roll(south, -1, 1)
        below = ZSCALE * harmonic(perm, roll(perm, 1, 0))
        below = jnp.where((row > 0) & real, below, 0.0)
        above = roll(below, -1, 0)
        faces = [west, east, south, north, below, above]
        ends = (x == 0, x == self.nx - 1, y == 0, y == self.ny - 1)
        diagonal = tree_sum(faces + [jnp.where(end, perm, 0.0) for end in ends])
        inverse = jnp.where(real, OMEGA * inverse_of(diagonal), 0.0)
        keys = ((-1, 0, 0), (1, 0, 0), (0, -1, 0), (0, 1, 0), (0, 0, -1), (0, 0, 1))
        terms = {key: inverse * face for key, face in zip(keys, faces)}
        terms[0, 0, 0] = jnp.full(self.shape, KEEP, F32)
        return terms, inverse * (4.0**-level)

    def product(self, first, second):
        sums = {}
        for (dx, dy, dz), coef in first.items():
            for other, moved in second.items():
                if dz:
                    moved = roll(moved, -dz, 0)
                if dx or dy:
                    moved = roll(moved, -(dx * self.ny + dy), 1)
                total = tuple(a + b for a, b in zip((dx, dy, dz), other))
                sums.setdefault(total, []).append(coef * moved)
        return {key: tree_sum(parts) for key, parts in sums.items()}

    def apply(self, terms, values, base, buffer):
        buffer[pl.ds(2 * POWER, self.rows, 2), :] = values
        moved = {}
        for dx, dy, dz in sorted(terms, key=lambda key: abs(key[2])):
            if (0, 0, dz) not in moved:
                moved[0, 0, dz] = buffer[pl.ds(2 * (POWER + dz), self.rows, 2), :] if dz else values
            if dx or dy:
                moved[dx, dy, dz] = roll(moved[0, 0, dz], -(dx * self.ny + dy), 1)
        return tree_sum([base] + [coef * moved[key] for key, coef in terms.items()])

    def prepare(self, perm, level):
        terms, factor = self.system(perm, level)
        power = terms
        for _ in range(POWER - 1):
            power = self.product(terms, power)
        return terms, power, factor

    def solve(self, right, prepared, buffer):
        terms, power, factor = prepared
        const = factor * right
        buffer[...] = jnp.zeros_like(buffer)
        base = const
        for _ in range(POWER - 1):
            base = self.apply(terms, base, const, buffer)
        whole = COARSE_SWEEPS % POWER == 0
        values = base if whole else const
        steps = (COARSE_SWEEPS - 1) // POWER
        assert steps * POWER + (POWER if whole else 1) == COARSE_SWEEPS
        for _ in range(steps):
            values = self.apply(power, values, base, buffer)
        return values


def tree_sum(parts):
    while len(parts) > 1:
        odd = parts[len(parts) // 2 * 2 :]
        parts = [a + b for a, b in zip(parts[::2], parts[1::2])] + odd
    return parts[0]


def systems_of(grid, perm, level, pads, pack):
    system = grid.system(perm, level)
    if len(pads) > 1:
        (coarse,) = grid.restrict([perm], pads[:1])
        coarse = [x * 0.125 for x in coarse]
        return [system] + systems_of(grid.coarser(), coarse, level + 1, pads[1:], pack)
    flat = Flat(grid)
    (coarse,) = flat.restrict([perm], pads, pack)
    return [system, flat.prepare(coarse * 0.125, level + 1)]


def packed_cycle(grid, right, systems, pads, pack, buffer):
    coefs, factors, diagonals = systems[0]
    const = [f * r for f, r in zip(factors, right)]
    values = grid.sweep(const, coefs, const)
    scaled = grid.apply(values, coefs, [c - OMEGA * v for c, v in zip(const, values)])
    residue = [r * d for r, d in zip(scaled, diagonals)]
    if len(pads) > 1:
        (coarse_right,) = grid.restrict([residue], pads[:1])
        update = packed_cycle(grid.coarser(), coarse_right, systems[1:], pads[1:], pack, buffer)
        update = grid.prolong(update, pads[0])
    else:
        flat = Flat(grid)
        (coarse_right,) = flat.restrict([residue], pads, pack)
        update = flat.prolong(flat.solve(coarse_right, systems[1], buffer), pads[0], pack)
    values = [v + e for v, e in zip(values, update)]
    for _ in range(2):
        values = grid.sweep(values, coefs, const)
    return values


def coarse_kernel(
    dom_ref, gathered, coef, const, before, out,
    level, first, pad_right1, pad_perm1, pad_right2, pad_perm2, update, pack, pack_perm, buffer,
    done, sems,
):
    height = out.shape[0]
    dom = dom_ref[0]
    domains, own, nx, _ = gathered.shape
    ny = LANES // 2
    grid = Packed(domains * own, nx, ny)
    left = iota((nx, LANES), 1) < ny
    right, perm = [], []
    for p in range(grid.planes):
        a = gathered[p // own, p % own]
        q = grid.planes + p
        b = gathered[q // own, q % own]
        right.append(jnp.where(left, a, roll(b, ny, 1)))
        perm.append(jnp.where(left, roll(a, ny, 1), b))
    systems = systems_of(grid, perm, 1, [pad_perm1, pad_perm2], pack_perm)
    solved = packed_cycle(grid, right, systems, [pad_right1, pad_right2], pack, buffer)
    for p in range(grid.planes):
        update[p] = solved[p]
    planes, group = [], []
    for j in range(own + 2):
        layer = jnp.clip(dom * own + j - 1, 0, grid.nz - 1)
        group.append(layer // grid.planes)
        planes.append(update[lax.rem(layer, grid.planes)])
    for j, wide in enumerate(selector_dot(planes, lane_selector(1, LANES, 2, spread=True))):
        plane = jnp.where(group[j] == 0, wide[:, :LANES], wide[:, LANES:])
        pad = first.at[0]
        pad[pl.ds(0, nx, 2), :] = plane
        pad[pl.ds(1, nx, 2), :] = plane
        whole = first[0]
        level[2 * j] = before[2 * j] + whole
        level[2 * j + 1] = before[2 * j + 1] + whole

    def sweep(source, at, i):
        centre = source[i + 1]
        near = [coef[k, at + i] for k in range(6)]
        return stencil(centre, source[i], source[i + 2], near, KEEP * centre + const[at + i])

    def one(i):
        first[i] = sweep(level, 2, i)

    for i in range(height + 2):
        one(i)

    copies = []
    for i in range(height):
        done[i] = sweep(first, 3, i)
        copies.append(pltpu.make_async_copy(done.at[i], out.at[i], sems.at[i]))
        copies[-1].start()
    for copy in copies:
        copy.wait()


def fine_part(dom, perm, source, layers):
    height, nx, ny = perm[0].shape
    field = lambda *lead: pltpu.VMEM(lead + (nx, ny), F32)
    vmem = pl.BlockSpec(memory_space=pltpu.VMEM)
    smem = pl.BlockSpec(memory_space=pltpu.SMEM)
    return pl.pallas_call(
        functools.partial(fine_kernel, layers),
        out_shape=(
            jax.ShapeDtypeStruct((6, height + 6, nx, ny), F32),
            jax.ShapeDtypeStruct((height + 6, nx, ny), F32),
            jax.ShapeDtypeStruct((height + 4, nx, ny), F32),
            jax.ShapeDtypeStruct((height // 2, nx // 2, ny), F32),
        ),
        in_specs=[smem] + [vmem] * 6,
        out_specs=(vmem,) * 4,
        scratch_shapes=[
            field(3 * height),
            field(3 * height),
            field(height + 6),
            field(height // 2),
            field(height // 2),
        ],
        compiler_params=pltpu.CompilerParams(vmem_limit_bytes=VMEM_LIMIT),
        name="fine",
    )(dom, *perm, *source)


def coarse_part(dom, gathered, coefs, const, values, height):
    _, nx, ny = values.shape
    field = lambda *shape: pltpu.VMEM(shape, F32)
    grid1 = Packed(gathered.shape[0] * gathered.shape[1], nx // 2, ny // 2)
    grid2 = grid1.coarser()
    pads1 = field(grid1.planes // 2, grid1.nx, LANES)
    pads2 = field(grid2.planes // 2, grid2.nx, LANES)
    vmem = pl.BlockSpec(memory_space=pltpu.VMEM)
    smem = pl.BlockSpec(memory_space=pltpu.SMEM)
    return pl.pallas_call(
        coarse_kernel,
        out_shape=jax.ShapeDtypeStruct((height, nx, ny), F32),
        in_specs=[smem] + [vmem] * 4,
        out_specs=pl.BlockSpec(memory_space=pl.ANY),
        scratch_shapes=[
            field(*values.shape),
            field(height + 2, nx, ny),
            pads1, pads1, pads2, pads2,
            field(grid1.planes, grid1.nx, LANES),
            field(1, Flat(grid2).rows, LANES),
            field(1, Flat(grid2).rows, LANES),
            field(Flat(grid2).buffer_rows, LANES),
            field(height, nx, ny),
            pltpu.SemaphoreType.DMA((height,)),
        ],
        compiler_params=pltpu.CompilerParams(vmem_limit_bytes=VMEM_LIMIT),
        name="coarse",
    )(dom, gathered, coefs, const, values)


def swaps(x, axis, step):
    return lax.ppermute(x, axis, [(i, i ^ step) for i in range(lax.axis_size(axis))])


def other_side(x):
    props, domains = lax.axis_size("prop"), lax.axis_size("dom")
    pairs = []
    for p in range(props):
        for d in range(domains):
            end = d in (0, domains - 1)
            partner = ((p ^ 1) * domains + d) if end else (p * domains + ((d + 1) ^ 1) - 1)
            pairs.append((p * domains + d, partner))
    return lax.ppermute(x, ("prop", "dom"), pairs)


def source_side(x):
    props, domains = lax.axis_size("prop"), lax.axis_size("dom")
    pairs = []
    for p in range(props):
        for d in range(domains):
            if p % 2 == 0:
                partner = p * domains + (d ^ 1)
            elif d in (0, domains - 1):
                partner = (p ^ 2) * domains + d
            else:
                partner = p * domains + ((d + 1) ^ 1) - 1
            pairs.append((p * domains + d, partner))
    return lax.ppermute(x, ("prop", "dom"), pairs)


def from_accepted(mine, accepted, beside):
    props = lax.axis_size("prop")
    apart = lax.axis_index("prop") ^ accepted
    own = SHRINK * mine
    step = props // 2
    came = swaps(mine, "prop", step)
    came, own, beside = lax.optimization_barrier((came, own, beside))
    current = jnp.where(apart & step, SHRINK * came, own)
    while step > 1:
        step //= 2
        current = jnp.where(apart & step, swaps(current, "prop", step), current)
    return current, beside


def gather_parts(mine):
    domains = lax.axis_size("dom")
    copies = jnp.broadcast_to(mine[None], (domains,) + mine.shape)
    return lax.all_to_all(copies, "dom", 0, 0)


def body(states, accepted, noise, source):
    domains = lax.axis_size("dom")
    height = source.shape[0]
    dom = jnp.stack([lax.axis_index("dom"), lax.axis_index("prop")]).astype(jnp.int32)
    near = source_side(source)
    current, noise_part = from_accepted(states[0], accepted[0], BETA * noise[0])
    perm, source = lax.optimization_barrier((jnp.exp(current + noise_part), source))
    perms = (perm, swaps(perm, "dom", 1), other_side(perm))
    sources = (OMEGA * source, near, swaps(near, "prop", 1))
    *level, coarse = fine_part(dom, perms, sources, domains * height)
    return coarse_part(dom, gather_parts(coarse), *level, height)[None]


def solution(mesh):
    in_specs = (
        P("prop", "dom", None, None),
        P(),
        P("prop", "dom", None, None),
        P("dom", None, None),
    )
    out_specs = P("prop", "dom", None, None)
    return jax.shard_map(body, mesh=mesh, in_specs=in_specs, out_specs=out_specs, check_vma=False)
```

```python
import functools
import math

import jax
import jax.numpy as jnp
from jax import lax
from jax.experimental import pallas as pl
from jax.experimental.pallas import tpu as pltpu
from jax.sharding import PartitionSpec as P

COARSE_SWEEPS = 64
POWER = 3
OMEGA = 0.7
KEEP = 1.0 - OMEGA
BETA = 0.4
SHRINK = math.sqrt(1.0 - BETA * BETA)
ZSCALE = 16.0
LANES = 128
VMEM_LIMIT = 40 * 1024 * 1024
F32 = jnp.float32
WEST, EAST, SOUTH, NORTH, BELOW, ABOVE, CONST = range(7)


def iota(shape, dim):
    return lax.broadcasted_iota(jnp.int32, shape, dim)


def roll(x, amount, axis):
    axis = axis % x.ndim
    return pltpu.roll(x, amount % x.shape[axis], axis)


def inverse_of(x):
    guess = pl.reciprocal(x, approx=True)
    return guess * (2.0 - x * guess)


def harmonic(a, b):
    return (2.0 * a) * b * inverse_of(a + b)


def selector_dot(parts, selector):
    x = jnp.concatenate(parts, axis=0) if len(parts) > 1 else parts[0]
    rows = x.shape[0]
    high = x.astype(jnp.bfloat16).astype(F32)
    rest = x - high
    middle = rest.astype(jnp.bfloat16).astype(F32)
    terms = jnp.concatenate([high, middle, rest - middle], axis=0).astype(jnp.bfloat16)
    y = jnp.dot(terms, selector, preferred_element_type=F32)
    total = y[:rows] + y[rows : 2 * rows] + y[2 * rows :]
    height = parts[0].shape[0]
    return [total[i * height : (i + 1) * height] for i in range(len(parts))]


def face_terms(perm, lower, upper, below_scale, above_scale, ny):
    shape = perm.shape
    rows = iota(shape, 0)
    columns = iota(shape, 1) & (ny - 1)
    west = jnp.where(rows == 0, 0.0, harmonic(perm, roll(perm, 1, 0)))
    east = roll(west, -1, 0)
    south = jnp.where(columns == 0, 0.0, harmonic(perm, roll(perm, 1, 1)))
    north = roll(south, -1, 1)
    below = below_scale * harmonic(perm, lower)
    above = above_scale * harmonic(perm, upper)
    ends = jnp.where(rows == 0, perm, 0.0) + jnp.where(rows == shape[0] - 1, perm, 0.0)
    ends = ends + jnp.where(columns == 0, perm, 0.0) + jnp.where(columns == ny - 1, perm, 0.0)
    diagonal = ((west + east) + (south + north)) + ((below + above) + ends)
    return (west, east, south, north, below, above), diagonal


def stencil(values, lower, upper, coefs, base):
    x = coefs[0] * roll(values, 1, 0) + coefs[1] * roll(values, -1, 0)
    y = coefs[2] * roll(values, 1, 1) + coefs[3] * roll(values, -1, 1)
    z = coefs[4] * lower + coefs[5] * upper
    return (x + y) + (z + base)


def lane_selector(groups, ny, step, spread=False):
    shape = (LANES, step * LANES) if spread else (step * LANES, LANES)
    source, target = iota(shape, int(spread)), iota(shape, 1 - int(spread))
    bits = ny.bit_length() - 1
    lane = source & (LANES - 1)
    group = (lane >> bits) * step + (source >> 7)
    wanted = (group << (bits - 1)) + ((lane & (ny - 1)) >> 1)
    return jnp.where((target == wanted) & (lane < groups * ny), 1.0, 0.0).astype(jnp.bfloat16)


def fine_kernel(
    layers,
    dom_ref,
    per, per_pair, per_other,
    src, src_near, src_next,
    coef, const, values, coarse_out,
    perm, right, diag, pair_right, pair_perm,
):
    height = per.shape[0]
    dom = dom_ref[0]
    pair_at = jnp.where(lax.rem(dom, 2) == 0, 2 * height, 0)
    other_at = 2 * height - pair_at

    near_at = jnp.where(lax.rem(dom_ref[1], 2) == 0, pair_at, other_at)
    next_at = 2 * height - near_at
    for i in range(height):
        for at, p in ((height, per), (pair_at, per_pair), (other_at, per_other)):
            perm[at + i] = p[i]
        right[height + i] = src[i]
        right[near_at + i] = OMEGA * src_near[i]
        right[next_at + i] = OMEGA * src_next[i]

    def build(i):
        z = dom * height + i - 3
        below = jnp.where((z > 0) & (z < layers), ZSCALE, 0.0)
        above = jnp.where((z + 1 > 0) & (z + 1 < layers), ZSCALE, 0.0)
        at = height - 3 + i
        faces, diagonal = face_terms(perm[at], perm[at - 1], perm[at + 1], below, above, LANES)
        inverse = inverse_of(diagonal)
        const[i] = inverse * right[at]
        inverse = OMEGA * inverse
        for k in range(6):
            coef[k, i] = inverse * faces[k]
        diag[i] = diagonal

    for i in range(height + 6):
        build(i)

    def first(i):
        start = const[i + 1]
        near = [coef[k, i + 1] for k in range(6)]
        values[i] = stencil(start, const[i], const[i + 2], near, (1.0 + KEEP) * start)

    for i in range(height + 4):
        first(i)

    def residue(i):
        centre = values[i + 2]
        base = const[i + 3] - OMEGA * centre
        near = [coef[k, i + 3] for k in range(6)]
        scaled = stencil(centre, values[i + 1], values[i + 3], near, base)
        return scaled * (diag[i + 3] * (1.0 / OMEGA))

    for m in range(height // 2):
        pair_right[m] = residue(2 * m) + residue(2 * m + 1)
        pair_perm[m] = (perm[height + 2 * m] + perm[height + 2 * m + 1]) * 0.125
    half = pair_right.shape[1] // 2
    rows = []
    for m in range(height // 2):
        both = [x[m, pl.ds(0, half, 2), :] + x[m, pl.ds(1, half, 2), :] for x in (pair_right, pair_perm)]
        rows.append(jnp.concatenate(both, axis=1))
    for m, x in enumerate(selector_dot(rows, lane_selector(1, LANES, 2))):
        coarse_out[m] = x


class Packed:
    def __init__(self, nz, nx, ny):
        self.nz, self.nx, self.ny = nz, nx, ny
        self.groups = min(LANES // ny, nz)
        self.planes = nz // self.groups

    def lower(self, planes, p):
        return planes[p - 1] if p else roll(planes[self.planes - 1], self.ny, 1)

    def upper(self, planes, p):
        return planes[p + 1] if p + 1 < self.planes else roll(planes[0], -self.ny, 1)

    def system(self, perm, level):
        lane = iota((self.nx, LANES), 1)
        used = lane < self.groups * self.ny
        if self.groups * self.ny < LANES:
            perm = [jnp.where(used, x, 1.0) for x in perm]
        coefs, factors, diagonals = [], [], []
        for p in range(self.planes):
            below, above = ZSCALE, ZSCALE
            if p == 0:
                below = jnp.where(lane < self.ny, 0.0, ZSCALE)
            if p + 1 == self.planes:
                above = jnp.where(lane < (self.groups - 1) * self.ny, ZSCALE, 0.0)
            faces, diagonal = face_terms(
                perm[p], self.lower(perm, p), self.upper(perm, p), below, above, self.ny
            )
            inverse = OMEGA * inverse_of(diagonal)
            coefs.append([inverse * face for face in faces])
            factors.append(inverse * (4.0**-level))
            diagonals.append(diagonal * (4.0**level / OMEGA))
        return coefs, factors, diagonals

    def apply(self, values, coefs, bases):
        return [
            stencil(values[p], self.lower(values, p), self.upper(values, p), coefs[p], bases[p])
            for p in range(self.planes)
        ]

    def sweep(self, values, coefs, const):
        return self.apply(values, coefs, [KEEP * v + c for v, c in zip(values, const)])

    def coarser(self):
        return Packed(self.nz // 2, self.nx // 2, self.ny // 2)

    def restrict(self, fields, pads):
        coarse = self.coarser()
        step = coarse.groups // self.groups
        half = coarse.nx
        parts = []
        for values, pad in zip(fields, pads):
            rows = []
            for m in range(self.planes // 2):
                pad[m] = values[2 * m] + values[2 * m + 1]
                rows.append(pad[m, pl.ds(0, half, 2), :] + pad[m, pl.ds(1, half, 2), :])
            for p in range(coarse.planes):
                blocks = rows[p :: coarse.planes]
                parts.append(jnp.concatenate(blocks, axis=1) if step > 1 else blocks[0])
        sums = selector_dot(parts, lane_selector(self.groups, self.ny, step))
        return [sums[i : i + coarse.planes] for i in range(0, len(sums), coarse.planes)]

    def prolong(self, values, pad):
        coarse = self.coarser()
        step = coarse.groups // self.groups
        half = coarse.nx
        wide = selector_dot(values, lane_selector(self.groups, self.ny, step, spread=True))
        out = []
        for m in range(self.planes // 2):
            j, p = divmod(m, coarse.planes)
            plane = wide[p][:, j * LANES : (j + 1) * LANES]
            pad[m, pl.ds(0, half, 2), :] = plane
            pad[m, pl.ds(1, half, 2), :] = plane
            out += [pad[m], pad[m]]
        return out


class Flat:
    def __init__(self, finer):
        coarse = finer.coarser()
        self.finer = finer
        self.nz, self.nx, self.ny = coarse.nz, coarse.nx, coarse.ny
        self.pairs = finer.planes // 2
        self.rows = max(8, self.nz)
        self.shape = (self.rows, LANES)
        self.buffer_rows = 2 * (self.rows + 2 * POWER)

    def selector(self, spread=False):
        wide = self.finer.groups * LANES
        shape = (wide, LANES) if spread else (LANES, wide)
        fine, flat = iota(shape, int(spread)), iota(shape, 1 - int(spread))
        bits = self.finer.ny.bit_length() - 1
        same = (fine >> bits) == (flat >> 7)
        same &= ((fine & (self.finer.ny - 1)) >> 1) == (flat & (self.ny - 1))
        return jnp.where(same, 1.0, 0.0).astype(jnp.bfloat16)

    def diagonal(self):
        shape = (self.nx, LANES)
        return iota(shape, 0) == (iota(shape, 1) >> (self.ny.bit_length() - 1))

    def restrict(self, fields, pads, pack):
        parts = []
        for values, pad in zip(fields, pads):
            for m in range(self.pairs):
                pad[m] = values[2 * m] + values[2 * m + 1]
                parts.append(pad[m, pl.ds(0, self.nx, 2), :] + pad[m, pl.ds(1, self.nx, 2), :])
        sums = selector_dot(parts, self.selector())
        mask = self.diagonal()
        pack[...] = jnp.zeros_like(pack)
        for i in range(len(fields)):
            for z in range(self.nz):
                s, m = divmod(z, self.pairs)
                block = sums[i * self.pairs + m][:, s * LANES : (s + 1) * LANES]
                row = jnp.sum(jnp.where(mask, block, 0.0), axis=0, keepdims=True)
                pack[i, z : z + 1, :] = row
        return [pack[i] for i in range(len(fields))]

    def prolong(self, values, pad, pack):
        mask = self.diagonal()
        pack[0] = values
        parts = []
        for m in range(self.pairs):
            layers = [s * self.pairs + m for s in range(self.finer.groups)]
            spread = [jnp.broadcast_to(pack[0, z : z + 1, :], mask.shape) for z in layers]
            parts.append(jnp.concatenate([jnp.where(mask, x, 0.0) for x in spread], axis=1))
        out = []
        for m, wide in enumerate(selector_dot(parts, self.selector(spread=True))):
            pad[m, pl.ds(0, self.nx, 2), :] = wide
            pad[m, pl.ds(1, self.nx, 2), :] = wide
            out += [pad[m], pad[m]]
        return out

    def system(self, perm, level):
        lane, row = iota(self.shape, 1), iota(self.shape, 0)
        x, y = lane >> (self.ny.bit_length() - 1), lane & (self.ny - 1)
        real = row < self.nz
        perm = jnp.where(real, perm, 1.0)
        west = jnp.where(x == 0, 0.0, harmonic(perm, roll(perm, self.ny, 1)))
        east = roll(west, -self.ny, 1)
        south = jnp.where(y == 0, 0.0, harmonic(perm, roll(perm, 1, 1)))
        north = roll(south, -1, 1)
        below = ZSCALE * harmonic(perm, roll(perm, 1, 0))
        below = jnp.where((row > 0) & real, below, 0.0)
        above = roll(below, -1, 0)
        faces = [west, east, south, north, below, above]
        ends = (x == 0, x == self.nx - 1, y == 0, y == self.ny - 1)
        diagonal = tree_sum(faces + [jnp.where(end, perm, 0.0) for end in ends])
        inverse = jnp.where(real, OMEGA * inverse_of(diagonal), 0.0)
        keys = ((-1, 0, 0), (1, 0, 0), (0, -1, 0), (0, 1, 0), (0, 0, -1), (0, 0, 1))
        terms = {key: inverse * face for key, face in zip(keys, faces)}
        terms[0, 0, 0] = jnp.full(self.shape, KEEP, F32)
        return terms, inverse * (4.0**-level)

    def product(self, first, second):
        sums = {}
        for (dx, dy, dz), coef in first.items():
            for other, moved in second.items():
                if dz:
                    moved = roll(moved, -dz, 0)
                if dx or dy:
                    moved = roll(moved, -(dx * self.ny + dy), 1)
                total = tuple(a + b for a, b in zip((dx, dy, dz), other))
                sums.setdefault(total, []).append(coef * moved)
        return {key: tree_sum(parts) for key, parts in sums.items()}

    def apply(self, terms, values, base, buffer):
        buffer[pl.ds(2 * POWER, self.rows, 2), :] = values
        moved = {}
        for dx, dy, dz in sorted(terms, key=lambda key: abs(key[2])):
            if (0, 0, dz) not in moved:
                moved[0, 0, dz] = buffer[pl.ds(2 * (POWER + dz), self.rows, 2), :] if dz else values
            if dx or dy:
                moved[dx, dy, dz] = roll(moved[0, 0, dz], -(dx * self.ny + dy), 1)
        return tree_sum([base] + [coef * moved[key] for key, coef in terms.items()])

    def prepare(self, perm, level):
        terms, factor = self.system(perm, level)
        power = terms
        for _ in range(POWER - 1):
            power = self.product(terms, power)
        return terms, power, factor

    def solve(self, right, prepared, buffer):
        terms, power, factor = prepared
        const = factor * right
        buffer[...] = jnp.zeros_like(buffer)
        base = const
        for _ in range(POWER - 1):
            base = self.apply(terms, base, const, buffer)
        whole = COARSE_SWEEPS % POWER == 0
        values = base if whole else const
        steps = (COARSE_SWEEPS - 1) // POWER
        assert steps * POWER + (POWER if whole else 1) == COARSE_SWEEPS
        for _ in range(steps):
            values = self.apply(power, values, base, buffer)
        return values


def tree_sum(parts):
    while len(parts) > 1:
        odd = parts[len(parts) // 2 * 2 :]
        parts = [a + b for a, b in zip(parts[::2], parts[1::2])] + odd
    return parts[0]


def systems_of(grid, perm, level, pads, pack):
    system = grid.system(perm, level)
    if len(pads) > 1:
        (coarse,) = grid.restrict([perm], pads[:1])
        coarse = [x * 0.125 for x in coarse]
        return [system] + systems_of(grid.coarser(), coarse, level + 1, pads[1:], pack)
    flat = Flat(grid)
    (coarse,) = flat.restrict([perm], pads, pack)
    return [system, flat.prepare(coarse * 0.125, level + 1)]


def packed_cycle(grid, right, systems, pads, pack, buffer):
    coefs, factors, diagonals = systems[0]
    const = [f * r for f, r in zip(factors, right)]
    values = grid.sweep(const, coefs, const)
    scaled = grid.apply(values, coefs, [c - OMEGA * v for c, v in zip(const, values)])
    residue = [r * d for r, d in zip(scaled, diagonals)]
    if len(pads) > 1:
        (coarse_right,) = grid.restrict([residue], pads[:1])
        update = packed_cycle(grid.coarser(), coarse_right, systems[1:], pads[1:], pack, buffer)
        update = grid.prolong(update, pads[0])
    else:
        flat = Flat(grid)
        (coarse_right,) = flat.restrict([residue], pads, pack)
        update = flat.prolong(flat.solve(coarse_right, systems[1], buffer), pads[0], pack)
    values = [v + e for v, e in zip(values, update)]
    for _ in range(2):
        values = grid.sweep(values, coefs, const)
    return values


def coarse_kernel(
    dom_ref, gathered, coef, const, before, out,
    level, first, pad_right1, pad_perm1, pad_right2, pad_perm2, update, pack, pack_perm, buffer,
    done, sems,
):
    height = out.shape[0]
    dom = dom_ref[0]
    domains, own, nx, _ = gathered.shape
    ny = LANES // 2
    grid = Packed(domains * own, nx, ny)
    left = iota((nx, LANES), 1) < ny
    right, perm = [], []
    for p in range(grid.planes):
        a = gathered[p // own, p % own]
        q = grid.planes + p
        b = gathered[q // own, q % own]
        right.append(jnp.where(left, a, roll(b, ny, 1)))
        perm.append(jnp.where(left, roll(a, ny, 1), b))
    systems = systems_of(grid, perm, 1, [pad_perm1, pad_perm2], pack_perm)
    solved = packed_cycle(grid, right, systems, [pad_right1, pad_right2], pack, buffer)
    for p in range(grid.planes):
        update[p] = solved[p]
    planes, group = [], []
    for j in range(own + 2):
        layer = jnp.clip(dom * own + j - 1, 0, grid.nz - 1)
        group.append(layer // grid.planes)
        planes.append(update[lax.rem(layer, grid.planes)])
    for j, wide in enumerate(selector_dot(planes, lane_selector(1, LANES, 2, spread=True))):
        plane = jnp.where(group[j] == 0, wide[:, :LANES], wide[:, LANES:])
        pad = first.at[0]
        pad[pl.ds(0, nx, 2), :] = plane
        pad[pl.ds(1, nx, 2), :] = plane
        whole = first[0]
        level[2 * j] = before[2 * j] + whole
        level[2 * j + 1] = before[2 * j + 1] + whole

    def sweep(source, at, i):
        centre = source[i + 1]
        near = [coef[k, at + i] for k in range(6)]
        return stencil(centre, source[i], source[i + 2], near, KEEP * centre + const[at + i])

    def one(i):
        first[i] = sweep(level, 2, i)

    for i in range(height + 2):
        one(i)

    copies = []
    for i in range(height):
        done[i] = sweep(first, 3, i)
        copies.append(pltpu.make_async_copy(done.at[i], out.at[i], sems.at[i]))
        copies[-1].start()
    for copy in copies:
        copy.wait()


def fine_part(dom, perm, source, layers):
    height, nx, ny = perm[0].shape
    field = lambda *lead: pltpu.VMEM(lead + (nx, ny), F32)
    vmem = pl.BlockSpec(memory_space=pltpu.VMEM)
    smem = pl.BlockSpec(memory_space=pltpu.SMEM)
    return pl.pallas_call(
        functools.partial(fine_kernel, layers),
        out_shape=(
            jax.ShapeDtypeStruct((6, height + 6, nx, ny), F32),
            jax.ShapeDtypeStruct((height + 6, nx, ny), F32),
            jax.ShapeDtypeStruct((height + 4, nx, ny), F32),
            jax.ShapeDtypeStruct((height // 2, nx // 2, ny), F32),
        ),
        in_specs=[smem] + [vmem] * 6,
        out_specs=(vmem,) * 4,
        scratch_shapes=[
            field(3 * height),
            field(3 * height),
            field(height + 6),
            field(height // 2),
            field(height // 2),
        ],
        compiler_params=pltpu.CompilerParams(vmem_limit_bytes=VMEM_LIMIT),
        name="fine",
    )(dom, *perm, *source)


def coarse_part(dom, gathered, coefs, const, values, height):
    _, nx, ny = values.shape
    field = lambda *shape: pltpu.VMEM(shape, F32)
    grid1 = Packed(gathered.shape[0] * gathered.shape[1], nx // 2, ny // 2)
    grid2 = grid1.coarser()
    pads1 = field(grid1.planes // 2, grid1.nx, LANES)
    pads2 = field(grid2.planes // 2, grid2.nx, LANES)
    vmem = pl.BlockSpec(memory_space=pltpu.VMEM)
    smem = pl.BlockSpec(memory_space=pltpu.SMEM)
    return pl.pallas_call(
        coarse_kernel,
        out_shape=jax.ShapeDtypeStruct((height, nx, ny), F32),
        in_specs=[smem] + [vmem] * 4,
        out_specs=pl.BlockSpec(memory_space=pl.ANY),
        scratch_shapes=[
            field(*values.shape),
            field(height + 2, nx, ny),
            pads1, pads1, pads2, pads2,
            field(grid1.planes, grid1.nx, LANES),
            field(1, Flat(grid2).rows, LANES),
            field(1, Flat(grid2).rows, LANES),
            field(Flat(grid2).buffer_rows, LANES),
            field(height, nx, ny),
            pltpu.SemaphoreType.DMA((height,)),
        ],
        compiler_params=pltpu.CompilerParams(vmem_limit_bytes=VMEM_LIMIT),
        name="coarse",
    )(dom, gathered, coefs, const, values)


def swaps(x, axis, step):
    return lax.ppermute(x, axis, [(i, i ^ step) for i in range(lax.axis_size(axis))])


def other_side(x):
    props, domains = lax.axis_size("prop"), lax.axis_size("dom")
    pairs = []
    for p in range(props):
        for d in range(domains):
            end = d in (0, domains - 1)
            partner = ((p ^ 1) * domains + d) if end else (p * domains + ((d + 1) ^ 1) - 1)
            pairs.append((p * domains + d, partner))
    return lax.ppermute(x, ("prop", "dom"), pairs)


def source_side(x):
    props, domains = lax.axis_size("prop"), lax.axis_size("dom")
    pairs = []
    for p in range(props):
        for d in range(domains):
            if p % 2 == 0:
                partner = p * domains + (d ^ 1)
            elif d in (0, domains - 1):
                partner = (p ^ 2) * domains + d
            else:
                partner = p * domains + ((d + 1) ^ 1) - 1
            pairs.append((p * domains + d, partner))
    return lax.ppermute(x, ("prop", "dom"), pairs)


def from_accepted(mine, accepted, beside):
    props = lax.axis_size("prop")
    apart = lax.axis_index("prop") ^ accepted
    own = SHRINK * mine
    step = props // 2
    came = swaps(mine, "prop", step)
    came, own, beside = lax.optimization_barrier((came, own, beside))
    current = jnp.where(apart & step, SHRINK * came, own)
    while step > 1:
        step //= 2
        current = jnp.where(apart & step, swaps(current, "prop", step), current)
    return current, beside


def gather_parts(mine):
    domains = lax.axis_size("dom")
    copies = jnp.broadcast_to(mine[None], (domains,) + mine.shape)
    return lax.all_to_all(copies, "dom", 0, 0)


def body(states, accepted, noise, source):
    domains = lax.axis_size("dom")
    height = source.shape[0]
    dom = jnp.stack([lax.axis_index("dom"), lax.axis_index("prop")]).astype(jnp.int32)
    near = source_side(source)
    current, noise_part = from_accepted(states[0], accepted[0], BETA * noise[0])
    perm, source = lax.optimization_barrier((jnp.exp(current + noise_part), source))
    other = other_side(perm)
    perms = (perm, swaps(perm, "dom", 1), other)
    sources = (OMEGA * source, near, swaps(near, "prop", 1))
    *level, coarse = fine_part(dom, perms, sources, domains * height)
    return coarse_part(dom, gather_parts(coarse), *level, height)[None]


def solution(mesh):
    in_specs = (
        P("prop", "dom", None, None),
        P(),
        P("prop", "dom", None, None),
        P("dom", None, None),
    )
    out_specs = P("prop", "dom", None, None)
    return jax.shard_map(body, mesh=mesh, in_specs=in_specs, out_specs=out_specs, check_vma=False)
```

```python
import functools
import math

import jax
import jax.numpy as jnp
from jax import lax
from jax.experimental import pallas as pl
from jax.experimental.pallas import tpu as pltpu
from jax.sharding import PartitionSpec as P

COARSE_SWEEPS = 64
POWER = 3
OMEGA = 0.7
KEEP = 1.0 - OMEGA
BETA = 0.4
SHRINK = math.sqrt(1.0 - BETA * BETA)
ZSCALE = 16.0
LANES = 128
VMEM_LIMIT = 40 * 1024 * 1024
F32 = jnp.float32
WEST, EAST, SOUTH, NORTH, BELOW, ABOVE, CONST = range(7)


def iota(shape, dim):
    return lax.broadcasted_iota(jnp.int32, shape, dim)


def roll(x, amount, axis):
    axis = axis % x.ndim
    return pltpu.roll(x, amount % x.shape[axis], axis)


def inverse_of(x):
    guess = pl.reciprocal(x, approx=True)
    return guess * (2.0 - x * guess)


def harmonic(a, b):
    return (2.0 * a) * b * inverse_of(a + b)


def selector_dot(parts, selector):
    x = jnp.concatenate(parts, axis=0) if len(parts) > 1 else parts[0]
    rows = x.shape[0]
    high = x.astype(jnp.bfloat16).astype(F32)
    rest = x - high
    middle = rest.astype(jnp.bfloat16).astype(F32)
    terms = jnp.concatenate([high, middle, rest - middle], axis=0).astype(jnp.bfloat16)
    y = jnp.dot(terms, selector, preferred_element_type=F32)
    total = y[:rows] + y[rows : 2 * rows] + y[2 * rows :]
    height = parts[0].shape[0]
    return [total[i * height : (i + 1) * height] for i in range(len(parts))]


def face_terms(perm, lower, upper, below_scale, above_scale, ny):
    shape = perm.shape
    rows = iota(shape, 0)
    columns = iota(shape, 1) & (ny - 1)
    west = jnp.where(rows == 0, 0.0, harmonic(perm, roll(perm, 1, 0)))
    east = roll(west, -1, 0)
    south = jnp.where(columns == 0, 0.0, harmonic(perm, roll(perm, 1, 1)))
    north = roll(south, -1, 1)
    below = below_scale * harmonic(perm, lower)
    above = above_scale * harmonic(perm, upper)
    ends = jnp.where(rows == 0, perm, 0.0) + jnp.where(rows == shape[0] - 1, perm, 0.0)
    ends = ends + jnp.where(columns == 0, perm, 0.0) + jnp.where(columns == ny - 1, perm, 0.0)
    diagonal = ((west + east) + (south + north)) + ((below + above) + ends)
    return (west, east, south, north, below, above), diagonal


def stencil(values, lower, upper, coefs, base):
    x = coefs[0] * roll(values, 1, 0) + coefs[1] * roll(values, -1, 0)
    y = coefs[2] * roll(values, 1, 1) + coefs[3] * roll(values, -1, 1)
    z = coefs[4] * lower + coefs[5] * upper
    return (x + y) + (z + base)


def lane_selector(groups, ny, step, spread=False):
    shape = (LANES, step * LANES) if spread else (step * LANES, LANES)
    source, target = iota(shape, int(spread)), iota(shape, 1 - int(spread))
    bits = ny.bit_length() - 1
    lane = source & (LANES - 1)
    group = (lane >> bits) * step + (source >> 7)
    wanted = (group << (bits - 1)) + ((lane & (ny - 1)) >> 1)
    return jnp.where((target == wanted) & (lane < groups * ny), 1.0, 0.0).astype(jnp.bfloat16)


def fine_kernel(
    layers,
    dom_ref,
    per, per_other, per_pair,
    src, src_near, src_next,
    coef, const, values, coarse_out,
    perm, right, diag, pair_right, pair_perm,
):
    height = per.shape[0]
    dom = dom_ref[0]
    pair_at = jnp.where(lax.rem(dom, 2) == 0, 2 * height, 0)
    other_at = 2 * height - pair_at

    near_at = jnp.where(lax.rem(dom_ref[1], 2) == 0, pair_at, other_at)
    next_at = 2 * height - near_at
    for i in range(height):
        for at, p in ((height, per), (pair_at, per_pair), (other_at, per_other)):
            perm[at + i] = p[i]
        right[height + i] = src[i]
        right[near_at + i] = OMEGA * src_near[i]
        right[next_at + i] = OMEGA * src_next[i]

    def build(i):
        z = dom * height + i - 3
        below = jnp.where((z > 0) & (z < layers), ZSCALE, 0.0)
        above = jnp.where((z + 1 > 0) & (z + 1 < layers), ZSCALE, 0.0)
        at = height - 3 + i
        faces, diagonal = face_terms(perm[at], perm[at - 1], perm[at + 1], below, above, LANES)
        inverse = inverse_of(diagonal)
        const[i] = inverse * right[at]
        inverse = OMEGA * inverse
        for k in range(6):
            coef[k, i] = inverse * faces[k]
        diag[i] = diagonal

    for i in range(height + 6):
        build(i)

    def first(i):
        start = const[i + 1]
        near = [coef[k, i + 1] for k in range(6)]
        values[i] = stencil(start, const[i], const[i + 2], near, (1.0 + KEEP) * start)

    for i in range(height + 4):
        first(i)

    def residue(i):
        centre = values[i + 2]
        base = const[i + 3] - OMEGA * centre
        near = [coef[k, i + 3] for k in range(6)]
        scaled = stencil(centre, values[i + 1], values[i + 3], near, base)
        return scaled * (diag[i + 3] * (1.0 / OMEGA))

    for m in range(height // 2):
        pair_right[m] = residue(2 * m) + residue(2 * m + 1)
        pair_perm[m] = (perm[height + 2 * m] + perm[height + 2 * m + 1]) * 0.125
    half = pair_right.shape[1] // 2
    rows = []
    for m in range(height // 2):
        both = [x[m, pl.ds(0, half, 2), :] + x[m, pl.ds(1, half, 2), :] for x in (pair_right, pair_perm)]
        rows.append(jnp.concatenate(both, axis=1))
    for m, x in enumerate(selector_dot(rows, lane_selector(1, LANES, 2))):
        coarse_out[m] = x


class Packed:
    def __init__(self, nz, nx, ny):
        self.nz, self.nx, self.ny = nz, nx, ny
        self.groups = min(LANES // ny, nz)
        self.planes = nz // self.groups

    def lower(self, planes, p):
        return planes[p - 1] if p else roll(planes[self.planes - 1], self.ny, 1)

    def upper(self, planes, p):
        return planes[p + 1] if p + 1 < self.planes else roll(planes[0], -self.ny, 1)

    def system(self, perm, level):
        lane = iota((self.nx, LANES), 1)
        used = lane < self.groups * self.ny
        if self.groups * self.ny < LANES:
            perm = [jnp.where(used, x, 1.0) for x in perm]
        coefs, factors, diagonals = [], [], []
        for p in range(self.planes):
            below, above = ZSCALE, ZSCALE
            if p == 0:
                below = jnp.where(lane < self.ny, 0.0, ZSCALE)
            if p + 1 == self.planes:
                above = jnp.where(lane < (self.groups - 1) * self.ny, ZSCALE, 0.0)
            faces, diagonal = face_terms(
                perm[p], self.lower(perm, p), self.upper(perm, p), below, above, self.ny
            )
            inverse = OMEGA * inverse_of(diagonal)
            coefs.append([inverse * face for face in faces])
            factors.append(inverse * (4.0**-level))
            diagonals.append(diagonal * (4.0**level / OMEGA))
        return coefs, factors, diagonals

    def apply(self, values, coefs, bases):
        return [
            stencil(values[p], self.lower(values, p), self.upper(values, p), coefs[p], bases[p])
            for p in range(self.planes)
        ]

    def sweep(self, values, coefs, const):
        return self.apply(values, coefs, [KEEP * v + c for v, c in zip(values, const)])

    def coarser(self):
        return Packed(self.nz // 2, self.nx // 2, self.ny // 2)

    def restrict(self, fields, pads):
        coarse = self.coarser()
        step = coarse.groups // self.groups
        half = coarse.nx
        parts = []
        for values, pad in zip(fields, pads):
            rows = []
            for m in range(self.planes // 2):
                pad[m] = values[2 * m] + values[2 * m + 1]
                rows.append(pad[m, pl.ds(0, half, 2), :] + pad[m, pl.ds(1, half, 2), :])
            for p in range(coarse.planes):
                blocks = rows[p :: coarse.planes]
                parts.append(jnp.concatenate(blocks, axis=1) if step > 1 else blocks[0])
        sums = selector_dot(parts, lane_selector(self.groups, self.ny, step))
        return [sums[i : i + coarse.planes] for i in range(0, len(sums), coarse.planes)]

    def prolong(self, values, pad):
        coarse = self.coarser()
        step = coarse.groups // self.groups
        half = coarse.nx
        wide = selector_dot(values, lane_selector(self.groups, self.ny, step, spread=True))
        out = []
        for m in range(self.planes // 2):
            j, p = divmod(m, coarse.planes)
            plane = wide[p][:, j * LANES : (j + 1) * LANES]
            pad[m, pl.ds(0, half, 2), :] = plane
            pad[m, pl.ds(1, half, 2), :] = plane
            out += [pad[m], pad[m]]
        return out


class Flat:
    def __init__(self, finer):
        coarse = finer.coarser()
        self.finer = finer
        self.nz, self.nx, self.ny = coarse.nz, coarse.nx, coarse.ny
        self.pairs = finer.planes // 2
        self.rows = max(8, self.nz)
        self.shape = (self.rows, LANES)
        self.buffer_rows = 2 * (self.rows + 2 * POWER)

    def selector(self, spread=False):
        wide = self.finer.groups * LANES
        shape = (wide, LANES) if spread else (LANES, wide)
        fine, flat = iota(shape, int(spread)), iota(shape, 1 - int(spread))
        bits = self.finer.ny.bit_length() - 1
        same = (fine >> bits) == (flat >> 7)
        same &= ((fine & (self.finer.ny - 1)) >> 1) == (flat & (self.ny - 1))
        return jnp.where(same, 1.0, 0.0).astype(jnp.bfloat16)

    def diagonal(self):
        shape = (self.nx, LANES)
        return iota(shape, 0) == (iota(shape, 1) >> (self.ny.bit_length() - 1))

    def restrict(self, fields, pads, pack):
        parts = []
        for values, pad in zip(fields, pads):
            for m in range(self.pairs):
                pad[m] = values[2 * m] + values[2 * m + 1]
                parts.append(pad[m, pl.ds(0, self.nx, 2), :] + pad[m, pl.ds(1, self.nx, 2), :])
        sums = selector_dot(parts, self.selector())
        mask = self.diagonal()
        pack[...] = jnp.zeros_like(pack)
        for i in range(len(fields)):
            for z in range(self.nz):
                s, m = divmod(z, self.pairs)
                block = sums[i * self.pairs + m][:, s * LANES : (s + 1) * LANES]
                row = jnp.sum(jnp.where(mask, block, 0.0), axis=0, keepdims=True)
                pack[i, z : z + 1, :] = row
        return [pack[i] for i in range(len(fields))]

    def prolong(self, values, pad, pack):
        mask = self.diagonal()
        pack[0] = values
        parts = []
        for m in range(self.pairs):
            layers = [s * self.pairs + m for s in range(self.finer.groups)]
            spread = [jnp.broadcast_to(pack[0, z : z + 1, :], mask.shape) for z in layers]
            parts.append(jnp.concatenate([jnp.where(mask, x, 0.0) for x in spread], axis=1))
        out = []
        for m, wide in enumerate(selector_dot(parts, self.selector(spread=True))):
            pad[m, pl.ds(0, self.nx, 2), :] = wide
            pad[m, pl.ds(1, self.nx, 2), :] = wide
            out += [pad[m], pad[m]]
        return out

    def system(self, perm, level):
        lane, row = iota(self.shape, 1), iota(self.shape, 0)
        x, y = lane >> (self.ny.bit_length() - 1), lane & (self.ny - 1)
        real = row < self.nz
        perm = jnp.where(real, perm, 1.0)
        west = jnp.where(x == 0, 0.0, harmonic(perm, roll(perm, self.ny, 1)))
        east = roll(west, -self.ny, 1)
        south = jnp.where(y == 0, 0.0, harmonic(perm, roll(perm, 1, 1)))
        north = roll(south, -1, 1)
        below = ZSCALE * harmonic(perm, roll(perm, 1, 0))
        below = jnp.where((row > 0) & real, below, 0.0)
        above = roll(below, -1, 0)
        faces = [west, east, south, north, below, above]
        ends = (x == 0, x == self.nx - 1, y == 0, y == self.ny - 1)
        diagonal = tree_sum(faces + [jnp.where(end, perm, 0.0) for end in ends])
        inverse = jnp.where(real, OMEGA * inverse_of(diagonal), 0.0)
        keys = ((-1, 0, 0), (1, 0, 0), (0, -1, 0), (0, 1, 0), (0, 0, -1), (0, 0, 1))
        terms = {key: inverse * face for key, face in zip(keys, faces)}
        terms[0, 0, 0] = jnp.full(self.shape, KEEP, F32)
        return terms, inverse * (4.0**-level)

    def product(self, first, second):
        sums = {}
        for (dx, dy, dz), coef in first.items():
            for other, moved in second.items():
                if dz:
                    moved = roll(moved, -dz, 0)
                if dx or dy:
                    moved = roll(moved, -(dx * self.ny + dy), 1)
                total = tuple(a + b for a, b in zip((dx, dy, dz), other))
                sums.setdefault(total, []).append(coef * moved)
        return {key: tree_sum(parts) for key, parts in sums.items()}

    def apply(self, terms, values, base, buffer):
        buffer[pl.ds(2 * POWER, self.rows, 2), :] = values
        moved = {}
        for dx, dy, dz in sorted(terms, key=lambda key: abs(key[2])):
            if (0, 0, dz) not in moved:
                moved[0, 0, dz] = buffer[pl.ds(2 * (POWER + dz), self.rows, 2), :] if dz else values
            if dx or dy:
                moved[dx, dy, dz] = roll(moved[0, 0, dz], -(dx * self.ny + dy), 1)
        return tree_sum([base] + [coef * moved[key] for key, coef in terms.items()])

    def prepare(self, perm, level):
        terms, factor = self.system(perm, level)
        power = terms
        for _ in range(POWER - 1):
            power = self.product(terms, power)
        return terms, power, factor

    def solve(self, right, prepared, buffer):
        terms, power, factor = prepared
        const = factor * right
        buffer[...] = jnp.zeros_like(buffer)
        base = const
        for _ in range(POWER - 1):
            base = self.apply(terms, base, const, buffer)
        whole = COARSE_SWEEPS % POWER == 0
        values = base if whole else const
        steps = (COARSE_SWEEPS - 1) // POWER
        assert steps * POWER + (POWER if whole else 1) == COARSE_SWEEPS
        for _ in range(steps):
            values = self.apply(power, values, base, buffer)
        return values


def tree_sum(parts):
    while len(parts) > 1:
        odd = parts[len(parts) // 2 * 2 :]
        parts = [a + b for a, b in zip(parts[::2], parts[1::2])] + odd
    return parts[0]


def systems_of(grid, perm, level, pads, pack):
    system = grid.system(perm, level)
    if len(pads) > 1:
        (coarse,) = grid.restrict([perm], pads[:1])
        coarse = [x * 0.125 for x in coarse]
        return [system] + systems_of(grid.coarser(), coarse, level + 1, pads[1:], pack)
    flat = Flat(grid)
    (coarse,) = flat.restrict([perm], pads, pack)
    return [system, flat.prepare(coarse * 0.125, level + 1)]


def packed_cycle(grid, right, systems, pads, pack, buffer):
    coefs, factors, diagonals = systems[0]
    const = [f * r for f, r in zip(factors, right)]
    values = grid.sweep(const, coefs, const)
    scaled = grid.apply(values, coefs, [c - OMEGA * v for c, v in zip(const, values)])
    residue = [r * d for r, d in zip(scaled, diagonals)]
    if len(pads) > 1:
        (coarse_right,) = grid.restrict([residue], pads[:1])
        update = packed_cycle(grid.coarser(), coarse_right, systems[1:], pads[1:], pack, buffer)
        update = grid.prolong(update, pads[0])
    else:
        flat = Flat(grid)
        (coarse_right,) = flat.restrict([residue], pads, pack)
        update = flat.prolong(flat.solve(coarse_right, systems[1], buffer), pads[0], pack)
    values = [v + e for v, e in zip(values, update)]
    for _ in range(2):
        values = grid.sweep(values, coefs, const)
    return values


def coarse_kernel(
    dom_ref, gathered, coef, const, before, out,
    level, first, pad_right1, pad_perm1, pad_right2, pad_perm2, update, pack, pack_perm, buffer,
    done, sems,
):
    height = out.shape[0]
    dom = dom_ref[0]
    domains, own, nx, _ = gathered.shape
    ny = LANES // 2
    grid = Packed(domains * own, nx, ny)
    left = iota((nx, LANES), 1) < ny
    right, perm = [], []
    for p in range(grid.planes):
        a = gathered[p // own, p % own]
        q = grid.planes + p
        b = gathered[q // own, q % own]
        right.append(jnp.where(left, a, roll(b, ny, 1)))
        perm.append(jnp.where(left, roll(a, ny, 1), b))
    systems = systems_of(grid, perm, 1, [pad_perm1, pad_perm2], pack_perm)
    solved = packed_cycle(grid, right, systems, [pad_right1, pad_right2], pack, buffer)
    for p in range(grid.planes):
        update[p] = solved[p]
    planes, group = [], []
    for j in range(own + 2):
        layer = jnp.clip(dom * own + j - 1, 0, grid.nz - 1)
        group.append(layer // grid.planes)
        planes.append(update[lax.rem(layer, grid.planes)])
    for j, wide in enumerate(selector_dot(planes, lane_selector(1, LANES, 2, spread=True))):
        plane = jnp.where(group[j] == 0, wide[:, :LANES], wide[:, LANES:])
        pad = first.at[0]
        pad[pl.ds(0, nx, 2), :] = plane
        pad[pl.ds(1, nx, 2), :] = plane
        whole = first[0]
        level[2 * j] = before[2 * j] + whole
        level[2 * j + 1] = before[2 * j + 1] + whole

    def sweep(source, at, i):
        centre = source[i + 1]
        near = [coef[k, at + i] for k in range(6)]
        return stencil(centre, source[i], source[i + 2], near, KEEP * centre + const[at + i])

    def one(i):
        first[i] = sweep(level, 2, i)

    for i in range(height + 2):
        one(i)

    copies = []
    for i in range(height):
        done[i] = sweep(first, 3, i)
        copies.append(pltpu.make_async_copy(done.at[i], out.at[i], sems.at[i]))
        copies[-1].start()
    for copy in copies:
        copy.wait()


def fine_part(dom, perm, source, layers):
    height, nx, ny = perm[0].shape
    field = lambda *lead: pltpu.VMEM(lead + (nx, ny), F32)
    vmem = pl.BlockSpec(memory_space=pltpu.VMEM)
    smem = pl.BlockSpec(memory_space=pltpu.SMEM)
    return pl.pallas_call(
        functools.partial(fine_kernel, layers),
        out_shape=(
            jax.ShapeDtypeStruct((6, height + 6, nx, ny), F32),
            jax.ShapeDtypeStruct((height + 6, nx, ny), F32),
            jax.ShapeDtypeStruct((height + 4, nx, ny), F32),
            jax.ShapeDtypeStruct((height // 2, nx // 2, ny), F32),
        ),
        in_specs=[smem] + [vmem] * 6,
        out_specs=(vmem,) * 4,
        scratch_shapes=[
            field(3 * height),
            field(3 * height),
            field(height + 6),
            field(height // 2),
            field(height // 2),
        ],
        compiler_params=pltpu.CompilerParams(vmem_limit_bytes=VMEM_LIMIT),
        name="fine",
    )(dom, *perm, *source)


def coarse_part(dom, gathered, coefs, const, values, height):
    _, nx, ny = values.shape
    field = lambda *shape: pltpu.VMEM(shape, F32)
    grid1 = Packed(gathered.shape[0] * gathered.shape[1], nx // 2, ny // 2)
    grid2 = grid1.coarser()
    pads1 = field(grid1.planes // 2, grid1.nx, LANES)
    pads2 = field(grid2.planes // 2, grid2.nx, LANES)
    vmem = pl.BlockSpec(memory_space=pltpu.VMEM)
    smem = pl.BlockSpec(memory_space=pltpu.SMEM)
    return pl.pallas_call(
        coarse_kernel,
        out_shape=jax.ShapeDtypeStruct((height, nx, ny), F32),
        in_specs=[smem] + [vmem] * 4,
        out_specs=pl.BlockSpec(memory_space=pl.ANY),
        scratch_shapes=[
            field(*values.shape),
            field(height + 2, nx, ny),
            pads1, pads1, pads2, pads2,
            field(grid1.planes, grid1.nx, LANES),
            field(1, Flat(grid2).rows, LANES),
            field(1, Flat(grid2).rows, LANES),
            field(Flat(grid2).buffer_rows, LANES),
            field(height, nx, ny),
            pltpu.SemaphoreType.DMA((height,)),
        ],
        compiler_params=pltpu.CompilerParams(vmem_limit_bytes=VMEM_LIMIT),
        name="coarse",
    )(dom, gathered, coefs, const, values)


def swaps(x, axis, step):
    return lax.ppermute(x, axis, [(i, i ^ step) for i in range(lax.axis_size(axis))])


def other_side(x):
    props, domains = lax.axis_size("prop"), lax.axis_size("dom")
    pairs = []
    for p in range(props):
        for d in range(domains):
            end = d in (0, domains - 1)
            partner = ((p ^ 1) * domains + d) if end else (p * domains + ((d + 1) ^ 1) - 1)
            pairs.append((p * domains + d, partner))
    return lax.ppermute(x, ("prop", "dom"), pairs)


def source_side(x):
    props, domains = lax.axis_size("prop"), lax.axis_size("dom")
    pairs = []
    for p in range(props):
        for d in range(domains):
            if p % 2 == 0:
                partner = p * domains + (d ^ 1)
            elif d in (0, domains - 1):
                partner = (p ^ 2) * domains + d
            else:
                partner = p * domains + ((d + 1) ^ 1) - 1
            pairs.append((p * domains + d, partner))
    return lax.ppermute(x, ("prop", "dom"), pairs)


def from_accepted(mine, accepted, beside):
    props = lax.axis_size("prop")
    apart = lax.axis_index("prop") ^ accepted
    own = SHRINK * mine
    step = props // 2
    came = swaps(mine, "prop", step)
    came, own, beside = lax.optimization_barrier((came, own, beside))
    current = jnp.where(apart & step, SHRINK * came, own)
    while step > 1:
        step //= 2
        current = jnp.where(apart & step, swaps(current, "prop", step), current)
    return current, beside


def gather_parts(mine):
    domains = lax.axis_size("dom")
    copies = jnp.broadcast_to(mine[None], (domains,) + mine.shape)
    return lax.all_to_all(copies, "dom", 0, 0)


def body(states, accepted, noise, source):
    domains = lax.axis_size("dom")
    height = source.shape[0]
    dom = jnp.stack([lax.axis_index("dom"), lax.axis_index("prop")]).astype(jnp.int32)
    near = source_side(source)
    current, noise_part = from_accepted(states[0], accepted[0], BETA * noise[0])
    perm, source = lax.optimization_barrier((jnp.exp(current + noise_part), source))
    perms = (perm, other_side(perm), swaps(perm, "dom", 1))
    sources = (OMEGA * source, near, swaps(near, "prop", 1))
    *level, coarse = fine_part(dom, perms, sources, domains * height)
    return coarse_part(dom, gather_parts(coarse), *level, height)[None]


def solution(mesh):
    in_specs = (
        P("prop", "dom", None, None),
        P(),
        P("prop", "dom", None, None),
        P("dom", None, None),
    )
    out_specs = P("prop", "dom", None, None)
    return jax.shard_map(body, mesh=mesh, in_specs=in_specs, out_specs=out_specs, check_vma=False)
```

```python
import functools
import math

import jax
import jax.numpy as jnp
from jax import lax
from jax.experimental import pallas as pl
from jax.experimental.pallas import tpu as pltpu
from jax.sharding import PartitionSpec as P

COARSE_SWEEPS = 64
POWER = 3
OMEGA = 0.7
KEEP = 1.0 - OMEGA
BETA = 0.4
SHRINK = math.sqrt(1.0 - BETA * BETA)
ZSCALE = 16.0
LANES = 128
VMEM_LIMIT = 40 * 1024 * 1024
F32 = jnp.float32
WEST, EAST, SOUTH, NORTH, BELOW, ABOVE, CONST = range(7)


def iota(shape, dim):
    return lax.broadcasted_iota(jnp.int32, shape, dim)


def roll(x, amount, axis):
    axis = axis % x.ndim
    return pltpu.roll(x, amount % x.shape[axis], axis)


def inverse_of(x):
    guess = pl.reciprocal(x, approx=True)
    return guess * (2.0 - x * guess)


def harmonic(a, b):
    return (2.0 * a) * b * inverse_of(a + b)


def selector_dot(parts, selector):
    x = jnp.concatenate(parts, axis=0) if len(parts) > 1 else parts[0]
    rows = x.shape[0]
    high = x.astype(jnp.bfloat16).astype(F32)
    rest = x - high
    middle = rest.astype(jnp.bfloat16).astype(F32)
    terms = jnp.concatenate([high, middle, rest - middle], axis=0).astype(jnp.bfloat16)
    y = jnp.dot(terms, selector, preferred_element_type=F32)
    total = y[:rows] + y[rows : 2 * rows] + y[2 * rows :]
    height = parts[0].shape[0]
    return [total[i * height : (i + 1) * height] for i in range(len(parts))]


def face_terms(perm, below, above, ny):
    shape = perm.shape
    rows = iota(shape, 0)
    columns = iota(shape, 1) & (ny - 1)
    west = jnp.where(rows == 0, 0.0, harmonic(perm, roll(perm, 1, 0)))
    east = roll(west, -1, 0)
    south = jnp.where(columns == 0, 0.0, harmonic(perm, roll(perm, 1, 1)))
    north = roll(south, -1, 1)
    ends = jnp.where(rows == 0, perm, 0.0) + jnp.where(rows == shape[0] - 1, perm, 0.0)
    ends = ends + jnp.where(columns == 0, perm, 0.0) + jnp.where(columns == ny - 1, perm, 0.0)
    diagonal = ((west + east) + (south + north)) + ((below + above) + ends)
    return (west, east, south, north, below, above), diagonal


def stencil(values, lower, upper, coefs, base):
    x = coefs[0] * roll(values, 1, 0) + coefs[1] * roll(values, -1, 0)
    y = coefs[2] * roll(values, 1, 1) + coefs[3] * roll(values, -1, 1)
    z = coefs[4] * lower + coefs[5] * upper
    return (x + y) + (z + base)


def lane_selector(groups, ny, step, spread=False):
    shape = (LANES, step * LANES) if spread else (step * LANES, LANES)
    source, target = iota(shape, int(spread)), iota(shape, 1 - int(spread))
    bits = ny.bit_length() - 1
    lane = source & (LANES - 1)
    group = (lane >> bits) * step + (source >> 7)
    wanted = (group << (bits - 1)) + ((lane & (ny - 1)) >> 1)
    return jnp.where((target == wanted) & (lane < groups * ny), 1.0, 0.0).astype(jnp.bfloat16)


def fine_kernel(
    layers,
    dom_ref,
    per, per_other, per_pair,
    src, src_near, src_next,
    coef, const, values, coarse_out,
    perm, right, diag, pair_right, pair_perm,
):
    height = per.shape[0]
    dom = dom_ref[0]
    pair_at = jnp.where(lax.rem(dom, 2) == 0, 2 * height, 0)
    other_at = 2 * height - pair_at

    near_at = jnp.where(lax.rem(dom_ref[1], 2) == 0, pair_at, other_at)
    next_at = 2 * height - near_at
    for i in range(height):
        for at, p in ((height, per), (pair_at, per_pair), (other_at, per_other)):
            perm[at + i] = p[i]
        right[height + i] = src[i]
        right[near_at + i] = OMEGA * src_near[i]
        right[next_at + i] = OMEGA * src_next[i]

    def face(i):
        z = dom * height + i - 3
        scale = jnp.where((z > 0) & (z < layers), ZSCALE, 0.0)
        at = height - 3 + i
        return scale * harmonic(perm[at - 1], perm[at])

    above = face(0)
    for i in range(height + 6):
        at = height - 3 + i
        below, above = above, face(i + 1)
        faces, diagonal = face_terms(perm[at], below, above, LANES)
        inverse = inverse_of(diagonal)
        const[i] = inverse * right[at]
        if 0 < i < height + 5:
            inverse = OMEGA * inverse
            for k in range(6):
                coef[k, i] = inverse * faces[k]
        if 3 <= i < height + 3:
            diag[i] = diagonal

    def first(i):
        start = const[i + 1]
        near = [coef[k, i + 1] for k in range(6)]
        values[i] = stencil(start, const[i], const[i + 2], near, (1.0 + KEEP) * start)

    for i in range(height + 4):
        first(i)

    def residue(i):
        centre = values[i + 2]
        base = const[i + 3] - OMEGA * centre
        near = [coef[k, i + 3] for k in range(6)]
        scaled = stencil(centre, values[i + 1], values[i + 3], near, base)
        return scaled * (diag[i + 3] * (1.0 / OMEGA))

    for m in range(height // 2):
        pair_right[m] = residue(2 * m) + residue(2 * m + 1)
        pair_perm[m] = (perm[height + 2 * m] + perm[height + 2 * m + 1]) * 0.125
    half = pair_right.shape[1] // 2
    rows = []
    for m in range(height // 2):
        both = [x[m, pl.ds(0, half, 2), :] + x[m, pl.ds(1, half, 2), :] for x in (pair_right, pair_perm)]
        rows.append(jnp.concatenate(both, axis=1))
    for m, x in enumerate(selector_dot(rows, lane_selector(1, LANES, 2))):
        coarse_out[m] = x


class Packed:
    def __init__(self, nz, nx, ny):
        self.nz, self.nx, self.ny = nz, nx, ny
        self.groups = min(LANES // ny, nz)
        self.planes = nz // self.groups

    def lower(self, planes, p):
        return planes[p - 1] if p else roll(planes[self.planes - 1], self.ny, 1)

    def upper(self, planes, p):
        return planes[p + 1] if p + 1 < self.planes else roll(planes[0], -self.ny, 1)

    def system(self, perm, level):
        lane = iota((self.nx, LANES), 1)
        used = lane < self.groups * self.ny
        if self.groups * self.ny < LANES:
            perm = [jnp.where(used, x, 1.0) for x in perm]
        coefs, factors, diagonals = [], [], []
        inner = [ZSCALE * harmonic(a, b) for a, b in zip(perm[:-1], perm[1:])]
        wrapped = ZSCALE * harmonic(perm[-1], roll(perm[0], -self.ny, 1))
        last = jnp.where(lane < (self.groups - 1) * self.ny, wrapped, 0.0)
        z_faces = [roll(last, self.ny, 1)] + inner + [last]
        for p in range(self.planes):
            faces, diagonal = face_terms(perm[p], z_faces[p], z_faces[p + 1], self.ny)
            inverse = OMEGA * inverse_of(diagonal)
            coefs.append([inverse * face for face in faces])
            factors.append(inverse * (4.0**-level))
            diagonals.append(diagonal * (4.0**level / OMEGA))
        return coefs, factors, diagonals

    def apply(self, values, coefs, bases):
        return [
            stencil(values[p], self.lower(values, p), self.upper(values, p), coefs[p], bases[p])
            for p in range(self.planes)
        ]

    def sweep(self, values, coefs, const):
        return self.apply(values, coefs, [KEEP * v + c for v, c in zip(values, const)])

    def coarser(self):
        return Packed(self.nz // 2, self.nx // 2, self.ny // 2)

    def restrict(self, fields, pads):
        coarse = self.coarser()
        step = coarse.groups // self.groups
        half = coarse.nx
        parts = []
        for values, pad in zip(fields, pads):
            rows = []
            for m in range(self.planes // 2):
                pad[m] = values[2 * m] + values[2 * m + 1]
                rows.append(pad[m, pl.ds(0, half, 2), :] + pad[m, pl.ds(1, half, 2), :])
            for p in range(coarse.planes):
                blocks = rows[p :: coarse.planes]
                parts.append(jnp.concatenate(blocks, axis=1) if step > 1 else blocks[0])
        sums = selector_dot(parts, lane_selector(self.groups, self.ny, step))
        return [sums[i : i + coarse.planes] for i in range(0, len(sums), coarse.planes)]

    def prolong(self, values, pad):
        coarse = self.coarser()
        step = coarse.groups // self.groups
        half = coarse.nx
        wide = selector_dot(values, lane_selector(self.groups, self.ny, step, spread=True))
        out = []
        for m in range(self.planes // 2):
            j, p = divmod(m, coarse.planes)
            plane = wide[p][:, j * LANES : (j + 1) * LANES]
            pad[m, pl.ds(0, half, 2), :] = plane
            pad[m, pl.ds(1, half, 2), :] = plane
            out += [pad[m], pad[m]]
        return out


class Flat:
    def __init__(self, finer):
        coarse = finer.coarser()
        self.finer = finer
        self.nz, self.nx, self.ny = coarse.nz, coarse.nx, coarse.ny
        self.pairs = finer.planes // 2
        self.rows = max(8, self.nz)
        self.shape = (self.rows, LANES)
        self.buffer_rows = 2 * (self.rows + 2 * POWER)

    def selector(self, spread=False):
        wide = self.finer.groups * LANES
        shape = (wide, LANES) if spread else (LANES, wide)
        fine, flat = iota(shape, int(spread)), iota(shape, 1 - int(spread))
        bits = self.finer.ny.bit_length() - 1
        same = (fine >> bits) == (flat >> 7)
        same &= ((fine & (self.finer.ny - 1)) >> 1) == (flat & (self.ny - 1))
        return jnp.where(same, 1.0, 0.0).astype(jnp.bfloat16)

    def diagonal(self):
        shape = (self.nx, LANES)
        return iota(shape, 0) == (iota(shape, 1) >> (self.ny.bit_length() - 1))

    def restrict(self, fields, pads, pack):
        parts = []
        for values, pad in zip(fields, pads):
            for m in range(self.pairs):
                pad[m] = values[2 * m] + values[2 * m + 1]
                parts.append(pad[m, pl.ds(0, self.nx, 2), :] + pad[m, pl.ds(1, self.nx, 2), :])
        sums = selector_dot(parts, self.selector())
        mask = self.diagonal()
        pack[...] = jnp.zeros_like(pack)
        for i in range(len(fields)):
            for z in range(self.nz):
                s, m = divmod(z, self.pairs)
                block = sums[i * self.pairs + m][:, s * LANES : (s + 1) * LANES]
                row = jnp.sum(jnp.where(mask, block, 0.0), axis=0, keepdims=True)
                pack[i, z : z + 1, :] = row
        return [pack[i] for i in range(len(fields))]

    def prolong(self, values, pad, pack):
        mask = self.diagonal()
        pack[0] = values
        parts = []
        for m in range(self.pairs):
            layers = [s * self.pairs + m for s in range(self.finer.groups)]
            spread = [jnp.broadcast_to(pack[0, z : z + 1, :], mask.shape) for z in layers]
            parts.append(jnp.concatenate([jnp.where(mask, x, 0.0) for x in spread], axis=1))
        out = []
        for m, wide in enumerate(selector_dot(parts, self.selector(spread=True))):
            pad[m, pl.ds(0, self.nx, 2), :] = wide
            pad[m, pl.ds(1, self.nx, 2), :] = wide
            out += [pad[m], pad[m]]
        return out

    def system(self, perm, level):
        lane, row = iota(self.shape, 1), iota(self.shape, 0)
        x, y = lane >> (self.ny.bit_length() - 1), lane & (self.ny - 1)
        real = row < self.nz
        perm = jnp.where(real, perm, 1.0)
        west = jnp.where(x == 0, 0.0, harmonic(perm, roll(perm, self.ny, 1)))
        east = roll(west, -self.ny, 1)
        south = jnp.where(y == 0, 0.0, harmonic(perm, roll(perm, 1, 1)))
        north = roll(south, -1, 1)
        below = ZSCALE * harmonic(perm, roll(perm, 1, 0))
        below = jnp.where((row > 0) & real, below, 0.0)
        above = roll(below, -1, 0)
        faces = [west, east, south, north, below, above]
        ends = (x == 0, x == self.nx - 1, y == 0, y == self.ny - 1)
        diagonal = tree_sum(faces + [jnp.where(end, perm, 0.0) for end in ends])
        inverse = jnp.where(real, OMEGA * inverse_of(diagonal), 0.0)
        keys = ((-1, 0, 0), (1, 0, 0), (0, -1, 0), (0, 1, 0), (0, 0, -1), (0, 0, 1))
        terms = {key: inverse * face for key, face in zip(keys, faces)}
        terms[0, 0, 0] = jnp.full(self.shape, KEEP, F32)
        return terms, inverse * (4.0**-level)

    def product(self, first, second):
        sums = {}
        for (dx, dy, dz), coef in first.items():
            for other, moved in second.items():
                if dz:
                    moved = roll(moved, -dz, 0)
                if dx or dy:
                    moved = roll(moved, -(dx * self.ny + dy), 1)
                total = tuple(a + b for a, b in zip((dx, dy, dz), other))
                sums.setdefault(total, []).append(coef * moved)
        return {key: tree_sum(parts) for key, parts in sums.items()}

    def apply(self, terms, values, base, buffer):
        buffer[pl.ds(2 * POWER, self.rows, 2), :] = values
        moved = {}
        for dx, dy, dz in sorted(terms, key=lambda key: abs(key[2])):
            if (0, 0, dz) not in moved:
                moved[0, 0, dz] = buffer[pl.ds(2 * (POWER + dz), self.rows, 2), :] if dz else values
            if dx or dy:
                moved[dx, dy, dz] = roll(moved[0, 0, dz], -(dx * self.ny + dy), 1)
        return tree_sum([base] + [coef * moved[key] for key, coef in terms.items()])

    def prepare(self, perm, level):
        terms, factor = self.system(perm, level)
        power = terms
        for _ in range(POWER - 1):
            power = self.product(terms, power)
        return terms, power, factor

    def solve(self, right, prepared, buffer):
        terms, power, factor = prepared
        const = factor * right
        buffer[...] = jnp.zeros_like(buffer)
        base = const
        for _ in range(POWER - 1):
            base = self.apply(terms, base, const, buffer)
        whole = COARSE_SWEEPS % POWER == 0
        values = base if whole else const
        steps = (COARSE_SWEEPS - 1) // POWER
        assert steps * POWER + (POWER if whole else 1) == COARSE_SWEEPS
        for _ in range(steps):
            values = self.apply(power, values, base, buffer)
        return values


def tree_sum(parts):
    while len(parts) > 1:
        odd = parts[len(parts) // 2 * 2 :]
        parts = [a + b for a, b in zip(parts[::2], parts[1::2])] + odd
    return parts[0]


def packed_cycle(grid, right, perm, level, pads, packs, buffer):
    pad_right, pad_perm = pads[0]
    coefs, factors, diagonals = grid.system(perm, level)
    if len(pads) > 1:
        (coarse_perm,) = grid.restrict([perm], [pad_perm])
    else:
        flat = Flat(grid)
        (coarse_perm,) = flat.restrict([perm], [pad_perm], packs[1])
        prepared = flat.prepare(coarse_perm * 0.125, level + 1)
    const = [f * r for f, r in zip(factors, right)]
    values = grid.sweep(const, coefs, const)
    scaled = grid.apply(values, coefs, [c - OMEGA * v for c, v in zip(const, values)])
    residue = [r * d for r, d in zip(scaled, diagonals)]
    if len(pads) > 1:
        (coarse_right,) = grid.restrict([residue], [pad_right])
        coarse_perm = [x * 0.125 for x in coarse_perm]
        update = packed_cycle(
            grid.coarser(), coarse_right, coarse_perm, level + 1, pads[1:], packs, buffer
        )
        update = grid.prolong(update, pad_right)
    else:
        (coarse_right,) = flat.restrict([residue], [pad_right], packs[0])
        update = flat.prolong(flat.solve(coarse_right, prepared, buffer), pad_right, packs[0])
    values = [v + e for v, e in zip(values, update)]
    for _ in range(2):
        values = grid.sweep(values, coefs, const)
    return values


def coarse_kernel(
    dom_ref, gathered, coef, const, before, out,
    level, first, pad_right1, pad_perm1, pad_right2, pad_perm2, update, pack, pack_perm, buffer,
    done, sems,
):
    height = out.shape[0]
    dom = dom_ref[0]
    domains, own, nx, _ = gathered.shape
    ny = LANES // 2
    grid = Packed(domains * own, nx, ny)
    left = iota((nx, LANES), 1) < ny
    right, perm = [], []
    for p in range(grid.planes):
        a = gathered[p // own, p % own]
        q = grid.planes + p
        b = gathered[q // own, q % own]
        right.append(jnp.where(left, a, roll(b, ny, 1)))
        perm.append(jnp.where(left, roll(a, ny, 1), b))
    pads = [(pad_right1, pad_perm1), (pad_right2, pad_perm2)]
    solved = packed_cycle(grid, right, perm, 1, pads, (pack, pack_perm), buffer)
    for p in range(grid.planes):
        update[p] = solved[p]
    planes, group = [], []
    for j in range(own + 2):
        layer = jnp.clip(dom * own + j - 1, 0, grid.nz - 1)
        group.append(layer // grid.planes)
        planes.append(update[lax.rem(layer, grid.planes)])
    for j, wide in enumerate(selector_dot(planes, lane_selector(1, LANES, 2, spread=True))):
        plane = jnp.where(group[j] == 0, wide[:, :LANES], wide[:, LANES:])
        pad = first.at[0]
        pad[pl.ds(0, nx, 2), :] = plane
        pad[pl.ds(1, nx, 2), :] = plane
        whole = first[0]
        level[2 * j] = before[2 * j] + whole
        level[2 * j + 1] = before[2 * j + 1] + whole

    def sweep(source, at, i):
        centre = source[i + 1]
        near = [coef[k, at + i] for k in range(6)]
        return stencil(centre, source[i], source[i + 2], near, KEEP * centre + const[at + i])

    def one(i):
        first[i] = sweep(level, 2, i)

    for i in range(height + 2):
        one(i)

    copies = []
    for i in range(height):
        done[i] = sweep(first, 3, i)
        copies.append(pltpu.make_async_copy(done.at[i], out.at[i], sems.at[i]))
        copies[-1].start()
    for copy in copies:
        copy.wait()


def fine_part(dom, perm, source, layers):
    height, nx, ny = perm[0].shape
    field = lambda *lead: pltpu.VMEM(lead + (nx, ny), F32)
    vmem = pl.BlockSpec(memory_space=pltpu.VMEM)
    smem = pl.BlockSpec(memory_space=pltpu.SMEM)
    return pl.pallas_call(
        functools.partial(fine_kernel, layers),
        out_shape=(
            jax.ShapeDtypeStruct((6, height + 6, nx, ny), F32),
            jax.ShapeDtypeStruct((height + 6, nx, ny), F32),
            jax.ShapeDtypeStruct((height + 4, nx, ny), F32),
            jax.ShapeDtypeStruct((height // 2, nx // 2, ny), F32),
        ),
        in_specs=[smem] + [vmem] * 6,
        out_specs=(vmem,) * 4,
        scratch_shapes=[
            field(3 * height),
            field(3 * height),
            field(height + 6),
            field(height // 2),
            field(height // 2),
        ],
        compiler_params=pltpu.CompilerParams(vmem_limit_bytes=VMEM_LIMIT),
        name="fine",
    )(dom, *perm, *source)


def coarse_part(dom, gathered, coefs, const, values, height):
    _, nx, ny = values.shape
    field = lambda *shape: pltpu.VMEM(shape, F32)
    grid1 = Packed(gathered.shape[0] * gathered.shape[1], nx // 2, ny // 2)
    grid2 = grid1.coarser()
    pads1 = field(grid1.planes // 2, grid1.nx, LANES)
    pads2 = field(grid2.planes // 2, grid2.nx, LANES)
    vmem = pl.BlockSpec(memory_space=pltpu.VMEM)
    smem = pl.BlockSpec(memory_space=pltpu.SMEM)
    return pl.pallas_call(
        coarse_kernel,
        out_shape=jax.ShapeDtypeStruct((height, nx, ny), F32),
        in_specs=[smem] + [vmem] * 4,
        out_specs=pl.BlockSpec(memory_space=pl.ANY),
        scratch_shapes=[
            field(*values.shape),
            field(height + 2, nx, ny),
            pads1, pads1, pads2, pads2,
            field(grid1.planes, grid1.nx, LANES),
            field(1, Flat(grid2).rows, LANES),
            field(1, Flat(grid2).rows, LANES),
            field(Flat(grid2).buffer_rows, LANES),
            field(height, nx, ny),
            pltpu.SemaphoreType.DMA((height,)),
        ],
        compiler_params=pltpu.CompilerParams(vmem_limit_bytes=VMEM_LIMIT),
        name="coarse",
    )(dom, gathered, coefs, const, values)


def swaps(x, axis, step):
    return lax.ppermute(x, axis, [(i, i ^ step) for i in range(lax.axis_size(axis))])


def other_side(x):
    props, domains = lax.axis_size("prop"), lax.axis_size("dom")
    pairs = []
    for p in range(props):
        for d in range(domains):
            end = d in (0, domains - 1)
            partner = ((p ^ 1) * domains + d) if end else (p * domains + ((d + 1) ^ 1) - 1)
            pairs.append((p * domains + d, partner))
    return lax.ppermute(x, ("prop", "dom"), pairs)


def source_side(x):
    props, domains = lax.axis_size("prop"), lax.axis_size("dom")
    pairs = []
    for p in range(props):
        for d in range(domains):
            if p % 2 == 0:
                partner = p * domains + (d ^ 1)
            elif d in (0, domains - 1):
                partner = (p ^ 2) * domains + d
            else:
                partner = p * domains + ((d + 1) ^ 1) - 1
            pairs.append((p * domains + d, partner))
    return lax.ppermute(x, ("prop", "dom"), pairs)


def from_accepted(mine, accepted, beside):
    props = lax.axis_size("prop")
    apart = lax.axis_index("prop") ^ accepted
    own = SHRINK * mine
    step = props // 2
    came = swaps(mine, "prop", step)
    came, own, beside = lax.optimization_barrier((came, own, beside))
    current = jnp.where(apart & step, SHRINK * came, own)
    while step > 1:
        step //= 2
        current = jnp.where(apart & step, swaps(current, "prop", step), current)
    return current, beside


def gather_parts(mine):
    domains = lax.axis_size("dom")
    copies = jnp.broadcast_to(mine[None], (domains,) + mine.shape)
    return lax.all_to_all(copies, "dom", 0, 0)


def body(states, accepted, noise, source):
    domains = lax.axis_size("dom")
    height = source.shape[0]
    dom = jnp.stack([lax.axis_index("dom"), lax.axis_index("prop")]).astype(jnp.int32)
    near = source_side(source)
    current, noise_part = from_accepted(states[0], accepted[0], BETA * noise[0])
    perm, source = lax.optimization_barrier((jnp.exp(current + noise_part), source))
    perms = (perm, other_side(perm), swaps(perm, "dom", 1))
    sources = (OMEGA * source, near, swaps(near, "prop", 1))
    *level, coarse = fine_part(dom, perms, sources, domains * height)
    return coarse_part(dom, gather_parts(coarse), *level, height)[None]


def solution(mesh):
    in_specs = (
        P("prop", "dom", None, None),
        P(),
        P("prop", "dom", None, None),
        P("dom", None, None),
    )
    out_specs = P("prop", "dom", None, None)
    return jax.shard_map(body, mesh=mesh, in_specs=in_specs, out_specs=out_specs, check_vma=False)
```

```python
import functools
import math

import jax
import jax.numpy as jnp
from jax import lax
from jax.experimental import pallas as pl
from jax.experimental.pallas import tpu as pltpu
from jax.sharding import PartitionSpec as P

COARSE_SWEEPS = 64
POWER = 3
OMEGA = 0.7
KEEP = 1.0 - OMEGA
BETA = 0.4
SHRINK = math.sqrt(1.0 - BETA * BETA)
ZSCALE = 16.0
LANES = 128
VMEM_LIMIT = 40 * 1024 * 1024
F32 = jnp.float32
WEST, EAST, SOUTH, NORTH, BELOW, ABOVE, CONST = range(7)


def iota(shape, dim):
    return lax.broadcasted_iota(jnp.int32, shape, dim)


def roll(x, amount, axis):
    axis = axis % x.ndim
    return pltpu.roll(x, amount % x.shape[axis], axis)


def inverse_of(x):
    guess = pl.reciprocal(x, approx=True)
    return guess * (2.0 - x * guess)


def harmonic(a, b):
    return (2.0 * a) * b * inverse_of(a + b)


def selector_dot(parts, selector):
    x = jnp.concatenate(parts, axis=0) if len(parts) > 1 else parts[0]
    rows = x.shape[0]
    high = x.astype(jnp.bfloat16).astype(F32)
    rest = x - high
    middle = rest.astype(jnp.bfloat16).astype(F32)
    terms = jnp.concatenate([high, middle, rest - middle], axis=0).astype(jnp.bfloat16)
    y = jnp.dot(terms, selector, preferred_element_type=F32)
    total = y[:rows] + y[rows : 2 * rows] + y[2 * rows :]
    height = parts[0].shape[0]
    return [total[i * height : (i + 1) * height] for i in range(len(parts))]


def face_terms(perm, below, above, ny):
    shape = perm.shape
    rows = iota(shape, 0)
    columns = iota(shape, 1) & (ny - 1)
    west = jnp.where(rows == 0, 0.0, harmonic(perm, roll(perm, 1, 0)))
    east = roll(west, -1, 0)
    south = jnp.where(columns == 0, 0.0, harmonic(perm, roll(perm, 1, 1)))
    north = roll(south, -1, 1)
    ends = jnp.where(rows == 0, perm, 0.0) + jnp.where(rows == shape[0] - 1, perm, 0.0)
    ends = ends + jnp.where(columns == 0, perm, 0.0) + jnp.where(columns == ny - 1, perm, 0.0)
    diagonal = ((west + east) + (south + north)) + ((below + above) + ends)
    return (west, east, south, north, below, above), diagonal


def stencil(values, lower, upper, coefs, base):
    x = coefs[0] * roll(values, 1, 0) + coefs[1] * roll(values, -1, 0)
    y = coefs[2] * roll(values, 1, 1) + coefs[3] * roll(values, -1, 1)
    z = coefs[4] * lower + coefs[5] * upper
    return (x + y) + (z + base)


def lane_selector(groups, ny, step, spread=False):
    shape = (LANES, step * LANES) if spread else (step * LANES, LANES)
    source, target = iota(shape, int(spread)), iota(shape, 1 - int(spread))
    bits = ny.bit_length() - 1
    lane = source & (LANES - 1)
    group = (lane >> bits) * step + (source >> 7)
    wanted = (group << (bits - 1)) + ((lane & (ny - 1)) >> 1)
    return jnp.where((target == wanted) & (lane < groups * ny), 1.0, 0.0).astype(jnp.bfloat16)


def fine_kernel(
    layers,
    dom_ref,
    per, per_other, per_pair,
    src, src_near, src_next,
    coef, const, values, coarse_out,
    perm, right, diag, pair_right, pair_perm,
):
    height = per.shape[0]
    dom = dom_ref[0]
    pair_at = jnp.where(lax.rem(dom, 2) == 0, 2 * height, 0)
    other_at = 2 * height - pair_at

    near_at = jnp.where(lax.rem(dom_ref[1], 2) == 0, pair_at, other_at)
    next_at = 2 * height - near_at
    for i in range(height):
        for at, p in ((height, per), (pair_at, per_pair), (other_at, per_other)):
            perm[at + i] = p[i]
        right[height + i] = src[i]
        right[near_at + i] = OMEGA * src_near[i]
        right[next_at + i] = OMEGA * src_next[i]

    def face(i):
        z = dom * height + i - 3
        scale = jnp.where((z > 0) & (z < layers), ZSCALE, 0.0)
        at = height - 3 + i
        return scale * harmonic(perm[at - 1], perm[at])

    above = face(0)
    for i in range(height + 6):
        at = height - 3 + i
        below, above = above, face(i + 1)
        faces, diagonal = face_terms(perm[at], below, above, LANES)
        inverse = inverse_of(diagonal)
        const[i] = inverse * right[at]
        if 0 < i < height + 5:
            inverse = OMEGA * inverse
            for k in range(6):
                coef[k, i] = inverse * faces[k]
        if 3 <= i < height + 3:
            diag[i] = diagonal

    def first(i):
        start = const[i + 1]
        near = [coef[k, i + 1] for k in range(6)]
        values[i] = stencil(start, const[i], const[i + 2], near, (1.0 + KEEP) * start)

    for i in range(height + 4):
        first(i)

    def residue(i):
        centre = values[i + 2]
        base = const[i + 3] - OMEGA * centre
        near = [coef[k, i + 3] for k in range(6)]
        scaled = stencil(centre, values[i + 1], values[i + 3], near, base)
        return scaled * (diag[i + 3] * (1.0 / OMEGA))

    for m in range(height // 2):
        pair_right[m] = residue(2 * m) + residue(2 * m + 1)
        pair_perm[m] = (perm[height + 2 * m] + perm[height + 2 * m + 1]) * 0.125
    half = pair_right.shape[1] // 2
    rows = []
    for m in range(height // 2):
        both = [x[m, pl.ds(0, half, 2), :] + x[m, pl.ds(1, half, 2), :] for x in (pair_right, pair_perm)]
        rows.append(jnp.concatenate(both, axis=1))
    for m, x in enumerate(selector_dot(rows, lane_selector(1, LANES, 2))):
        coarse_out[m] = x


class Packed:
    def __init__(self, nz, nx, ny):
        self.nz, self.nx, self.ny = nz, nx, ny
        self.groups = min(LANES // ny, nz)
        self.planes = nz // self.groups

    def lower(self, planes, p):
        return planes[p - 1] if p else roll(planes[self.planes - 1], self.ny, 1)

    def upper(self, planes, p):
        return planes[p + 1] if p + 1 < self.planes else roll(planes[0], -self.ny, 1)

    def system(self, perm, level):
        lane = iota((self.nx, LANES), 1)
        used = lane < self.groups * self.ny
        if self.groups * self.ny < LANES:
            perm = [jnp.where(used, x, 1.0) for x in perm]
        coefs, factors, diagonals = [], [], []
        inner = [ZSCALE * harmonic(a, b) for a, b in zip(perm[:-1], perm[1:])]
        wrapped = ZSCALE * harmonic(perm[-1], roll(perm[0], -self.ny, 1))
        last = jnp.where(lane < (self.groups - 1) * self.ny, wrapped, 0.0)
        z_faces = [roll(last, self.ny, 1)] + inner + [last]
        for p in range(self.planes):
            faces, diagonal = face_terms(perm[p], z_faces[p], z_faces[p + 1], self.ny)
            inverse = OMEGA * inverse_of(diagonal)
            coefs.append([inverse * face for face in faces])
            factors.append(inverse * (4.0**-level))
            diagonals.append(diagonal * (4.0**level / OMEGA))
        return coefs, factors, diagonals

    def apply(self, values, coefs, bases):
        return [
            stencil(values[p], self.lower(values, p), self.upper(values, p), coefs[p], bases[p])
            for p in range(self.planes)
        ]

    def sweep(self, values, coefs, const):
        return self.apply(values, coefs, [KEEP * v + c for v, c in zip(values, const)])

    def coarser(self):
        return Packed(self.nz // 2, self.nx // 2, self.ny // 2)

    def restrict(self, fields, pads):
        coarse = self.coarser()
        step = coarse.groups // self.groups
        half = coarse.nx
        parts = []
        for values, pad in zip(fields, pads):
            rows = []
            for m in range(self.planes // 2):
                pad[m] = values[2 * m] + values[2 * m + 1]
                rows.append(pad[m, pl.ds(0, half, 2), :] + pad[m, pl.ds(1, half, 2), :])
            for p in range(coarse.planes):
                blocks = rows[p :: coarse.planes]
                parts.append(jnp.concatenate(blocks, axis=1) if step > 1 else blocks[0])
        sums = selector_dot(parts, lane_selector(self.groups, self.ny, step))
        return [sums[i : i + coarse.planes] for i in range(0, len(sums), coarse.planes)]

    def prolong(self, values, pad):
        coarse = self.coarser()
        step = coarse.groups // self.groups
        half = coarse.nx
        wide = selector_dot(values, lane_selector(self.groups, self.ny, step, spread=True))
        out = []
        for m in range(self.planes // 2):
            j, p = divmod(m, coarse.planes)
            plane = wide[p][:, j * LANES : (j + 1) * LANES]
            pad[m, pl.ds(0, half, 2), :] = plane
            pad[m, pl.ds(1, half, 2), :] = plane
            out += [pad[m], pad[m]]
        return out


class Flat:
    def __init__(self, finer):
        coarse = finer.coarser()
        self.finer = finer
        self.nz, self.nx, self.ny = coarse.nz, coarse.nx, coarse.ny
        self.pairs = finer.planes // 2
        self.rows = max(8, self.nz)
        self.shape = (self.rows, LANES)
        self.buffer_rows = 2 * (self.rows + 2 * POWER)

    def selector(self, spread=False):
        wide = self.finer.groups * LANES
        shape = (wide, LANES) if spread else (LANES, wide)
        fine, flat = iota(shape, int(spread)), iota(shape, 1 - int(spread))
        bits = self.finer.ny.bit_length() - 1
        same = (fine >> bits) == (flat >> 7)
        same &= ((fine & (self.finer.ny - 1)) >> 1) == (flat & (self.ny - 1))
        return jnp.where(same, 1.0, 0.0).astype(jnp.bfloat16)

    def diagonal(self):
        shape = (self.nx, LANES)
        return iota(shape, 0) == (iota(shape, 1) >> (self.ny.bit_length() - 1))

    def restrict(self, fields, pads, pack):
        parts = []
        for values, pad in zip(fields, pads):
            for m in range(self.pairs):
                pad[m] = values[2 * m] + values[2 * m + 1]
                parts.append(pad[m, pl.ds(0, self.nx, 2), :] + pad[m, pl.ds(1, self.nx, 2), :])
        sums = selector_dot(parts, self.selector())
        mask = self.diagonal()
        pack[...] = jnp.zeros_like(pack)
        for i in range(len(fields)):
            for z in range(self.nz):
                s, m = divmod(z, self.pairs)
                block = sums[i * self.pairs + m][:, s * LANES : (s + 1) * LANES]
                row = jnp.sum(jnp.where(mask, block, 0.0), axis=0, keepdims=True)
                pack[i, z : z + 1, :] = row
        return [pack[i] for i in range(len(fields))]

    def prolong(self, values, pad, pack):
        mask = self.diagonal()
        pack[0] = values
        parts = []
        for m in range(self.pairs):
            layers = [s * self.pairs + m for s in range(self.finer.groups)]
            spread = [jnp.broadcast_to(pack[0, z : z + 1, :], mask.shape) for z in layers]
            parts.append(jnp.concatenate([jnp.where(mask, x, 0.0) for x in spread], axis=1))
        out = []
        for m, wide in enumerate(selector_dot(parts, self.selector(spread=True))):
            pad[m, pl.ds(0, self.nx, 2), :] = wide
            pad[m, pl.ds(1, self.nx, 2), :] = wide
            out += [pad[m], pad[m]]
        return out

    def system(self, perm, level):
        lane, row = iota(self.shape, 1), iota(self.shape, 0)
        x, y = lane >> (self.ny.bit_length() - 1), lane & (self.ny - 1)
        real = row < self.nz
        perm = jnp.where(real, perm, 1.0)
        west = jnp.where(x == 0, 0.0, harmonic(perm, roll(perm, self.ny, 1)))
        east = roll(west, -self.ny, 1)
        south = jnp.where(y == 0, 0.0, harmonic(perm, roll(perm, 1, 1)))
        north = roll(south, -1, 1)
        below = ZSCALE * harmonic(perm, roll(perm, 1, 0))
        below = jnp.where((row > 0) & real, below, 0.0)
        above = roll(below, -1, 0)
        faces = [west, east, south, north, below, above]
        ends = (x == 0, x == self.nx - 1, y == 0, y == self.ny - 1)
        diagonal = tree_sum(faces + [jnp.where(end, perm, 0.0) for end in ends])
        inverse = jnp.where(real, OMEGA * inverse_of(diagonal), 0.0)
        keys = ((-1, 0, 0), (1, 0, 0), (0, -1, 0), (0, 1, 0), (0, 0, -1), (0, 0, 1))
        terms = {key: inverse * face for key, face in zip(keys, faces)}
        terms[0, 0, 0] = jnp.full(self.shape, KEEP, F32)
        return terms, inverse * (4.0**-level)

    def product(self, first, second):
        sums = {}
        for (dx, dy, dz), coef in first.items():
            for other, moved in second.items():
                if dz:
                    moved = roll(moved, -dz, 0)
                if dx or dy:
                    moved = roll(moved, -(dx * self.ny + dy), 1)
                total = tuple(a + b for a, b in zip((dx, dy, dz), other))
                sums.setdefault(total, []).append(coef * moved)
        return {key: tree_sum(parts) for key, parts in sums.items()}

    def apply(self, terms, values, base, buffer):
        buffer[pl.ds(2 * POWER, self.rows, 2), :] = values
        moved = {}
        for dx, dy, dz in sorted(terms, key=lambda key: abs(key[2])):
            if (0, 0, dz) not in moved:
                moved[0, 0, dz] = buffer[pl.ds(2 * (POWER + dz), self.rows, 2), :] if dz else values
            if dx or dy:
                moved[dx, dy, dz] = roll(moved[0, 0, dz], -(dx * self.ny + dy), 1)
        return tree_sum([base] + [coef * moved[key] for key, coef in terms.items()])

    def prepare(self, perm, level):
        terms, factor = self.system(perm, level)
        power = terms
        for _ in range(POWER - 1):
            power = self.product(terms, power)
        return terms, power, factor

    def solve(self, right, prepared, buffer):
        terms, power, factor = prepared
        const = factor * right
        buffer[...] = jnp.zeros_like(buffer)
        base = const
        for _ in range(POWER - 1):
            base = self.apply(terms, base, const, buffer)
        whole = COARSE_SWEEPS % POWER == 0
        values = base if whole else const
        steps = (COARSE_SWEEPS - 1) // POWER
        assert steps * POWER + (POWER if whole else 1) == COARSE_SWEEPS
        for _ in range(steps):
            values = self.apply(power, values, base, buffer)
        return values


def tree_sum(parts):
    while len(parts) > 1:
        odd = parts[len(parts) // 2 * 2 :]
        parts = [a + b for a, b in zip(parts[::2], parts[1::2])] + odd
    return parts[0]


def packed_cycle(grid, right, perm, level, pads, packs, buffer):
    pad_right, pad_perm = pads[0]
    coefs, factors, diagonals = grid.system(perm, level)
    if len(pads) > 1:
        (coarse_perm,) = grid.restrict([perm], [pad_perm])
    else:
        flat = Flat(grid)
        (coarse_perm,) = flat.restrict([perm], [pad_perm], packs[1])
        prepared = flat.prepare(coarse_perm * 0.125, level + 1)
    const = [f * r for f, r in zip(factors, right)]
    values = grid.sweep(const, coefs, const)
    scaled = grid.apply(values, coefs, [c - OMEGA * v for c, v in zip(const, values)])
    residue = [r * d for r, d in zip(scaled, diagonals)]
    if len(pads) > 1:
        (coarse_right,) = grid.restrict([residue], [pad_right])
        coarse_perm = [x * 0.125 for x in coarse_perm]
        update = packed_cycle(
            grid.coarser(), coarse_right, coarse_perm, level + 1, pads[1:], packs, buffer
        )
        update = grid.prolong(update, pad_right)
    else:
        (coarse_right,) = flat.restrict([residue], [pad_right], packs[0])
        update = flat.prolong(flat.solve(coarse_right, prepared, buffer), pad_right, packs[0])
    values = [v + e for v, e in zip(values, update)]
    for _ in range(2):
        values = grid.sweep(values, coefs, const)
    return values


def coarse_kernel(
    dom_ref, gathered, coef, const, before, out,
    level, first, pad_right1, pad_perm1, pad_right2, pad_perm2, update, pack, pack_perm, buffer,
    done, sems,
):
    height = out.shape[0]
    dom = dom_ref[0]
    domains, own, nx, _ = gathered.shape
    ny = LANES // 2
    grid = Packed(domains * own, nx, ny)
    left = iota((nx, LANES), 1) < ny
    right, perm = [], []
    for p in range(grid.planes):
        a = gathered[p // own, p % own]
        q = grid.planes + p
        b = gathered[q // own, q % own]
        right.append(jnp.where(left, a, roll(b, ny, 1)))
        perm.append(jnp.where(left, roll(a, ny, 1), b))
    pads = [(pad_right1, pad_perm1), (pad_right2, pad_perm2)]
    solved = packed_cycle(grid, right, perm, 1, pads, (pack, pack_perm), buffer)
    for p in range(grid.planes):
        update[p] = solved[p]
    planes, group = [], []
    for j in range(own + 2):
        layer = jnp.clip(dom * own + j - 1, 0, grid.nz - 1)
        group.append(layer // grid.planes)
        planes.append(update[lax.rem(layer, grid.planes)])
    for j, wide in enumerate(selector_dot(planes, lane_selector(1, LANES, 2, spread=True))):
        plane = jnp.where(group[j] == 0, wide[:, :LANES], wide[:, LANES:])
        pad = first.at[0]
        pad[pl.ds(0, nx, 2), :] = plane
        pad[pl.ds(1, nx, 2), :] = plane
        whole = first[0]
        level[2 * j] = before[2 * j] + whole
        level[2 * j + 1] = before[2 * j + 1] + whole

    def sweep(source, at, i):
        centre = source[i + 1]
        near = [coef[k, at + i] for k in range(6)]
        return stencil(centre, source[i], source[i + 2], near, KEEP * centre + const[at + i])

    def one(i):
        first[i] = sweep(level, 2, i)

    for i in range(height + 2):
        one(i)

    copies = []
    for i in range(height):
        done[i] = sweep(first, 3, i)
        copies.append(pltpu.make_async_copy(done.at[i], out.at[i], sems.at[i]))
        copies[-1].start()
    for copy in copies:
        copy.wait()


def fine_part(dom, perm, source, layers):
    height, nx, ny = perm[0].shape
    field = lambda *lead: pltpu.VMEM(lead + (nx, ny), F32)
    vmem = pl.BlockSpec(memory_space=pltpu.VMEM)
    smem = pl.BlockSpec(memory_space=pltpu.SMEM)
    return pl.pallas_call(
        functools.partial(fine_kernel, layers),
        out_shape=(
            jax.ShapeDtypeStruct((6, height + 6, nx, ny), F32),
            jax.ShapeDtypeStruct((height + 6, nx, ny), F32),
            jax.ShapeDtypeStruct((height + 4, nx, ny), F32),
            jax.ShapeDtypeStruct((height // 2, nx // 2, ny), F32),
        ),
        in_specs=[smem] + [vmem] * 6,
        out_specs=(vmem,) * 4,
        scratch_shapes=[
            field(3 * height),
            field(3 * height),
            field(height + 6),
            field(height // 2),
            field(height // 2),
        ],
        compiler_params=pltpu.CompilerParams(vmem_limit_bytes=VMEM_LIMIT),
        name="fine",
    )(dom, *perm, *source)


def coarse_part(dom, gathered, coefs, const, values, height):
    _, nx, ny = values.shape
    field = lambda *shape: pltpu.VMEM(shape, F32)
    grid1 = Packed(gathered.shape[0] * gathered.shape[1], nx // 2, ny // 2)
    grid2 = grid1.coarser()
    pads1 = field(grid1.planes // 2, grid1.nx, LANES)
    pads2 = field(grid2.planes // 2, grid2.nx, LANES)
    vmem = pl.BlockSpec(memory_space=pltpu.VMEM)
    smem = pl.BlockSpec(memory_space=pltpu.SMEM)
    return pl.pallas_call(
        coarse_kernel,
        out_shape=jax.ShapeDtypeStruct((height, nx, ny), F32),
        in_specs=[smem] + [vmem] * 4,
        out_specs=pl.BlockSpec(memory_space=pl.ANY),
        scratch_shapes=[
            field(*values.shape),
            field(height + 2, nx, ny),
            pads1, pads1, pads2, pads2,
            field(grid1.planes, grid1.nx, LANES),
            field(1, Flat(grid2).rows, LANES),
            field(1, Flat(grid2).rows, LANES),
            field(Flat(grid2).buffer_rows, LANES),
            field(height, nx, ny),
            pltpu.SemaphoreType.DMA((height,)),
        ],
        compiler_params=pltpu.CompilerParams(vmem_limit_bytes=VMEM_LIMIT),
        name="coarse",
    )(dom, gathered, coefs, const, values)


def swaps(x, axis, step):
    return lax.ppermute(x, axis, [(i, i ^ step) for i in range(lax.axis_size(axis))])


def other_side(x):
    props, domains = lax.axis_size("prop"), lax.axis_size("dom")
    pairs = []
    for p in range(props):
        for d in range(domains):
            end = d in (0, domains - 1)
            partner = ((p ^ 1) * domains + d) if end else (p * domains + ((d + 1) ^ 1) - 1)
            pairs.append((p * domains + d, partner))
    return lax.ppermute(x, ("prop", "dom"), pairs)


def source_side(x):
    props, domains = lax.axis_size("prop"), lax.axis_size("dom")
    pairs = []
    for p in range(props):
        for d in range(domains):
            if p % 2 == 0:
                partner = p * domains + (d ^ 1)
            elif d in (0, domains - 1):
                partner = (p ^ 2) * domains + d
            else:
                partner = p * domains + ((d + 1) ^ 1) - 1
            pairs.append((p * domains + d, partner))
    return lax.ppermute(x, ("prop", "dom"), pairs)


def from_accepted(mine, accepted, beside):
    props = lax.axis_size("prop")
    apart = lax.axis_index("prop") ^ accepted
    own = SHRINK * mine
    step = props // 2
    came = swaps(mine, "prop", step)
    came, own, beside = lax.optimization_barrier((came, own, beside))
    current = jnp.where(apart & step, SHRINK * came, own)
    while step > 1:
        step //= 2
        came = jnp.concatenate([swaps(x, "prop", step) for x in jnp.split(current, 2)])
        current = jnp.where(apart & step, came, current)
    return current, beside


def gather_parts(mine):
    domains = lax.axis_size("dom")
    copies = jnp.broadcast_to(mine[None], (domains,) + mine.shape)
    return lax.all_to_all(copies, "dom", 0, 0)


def body(states, accepted, noise, source):
    domains = lax.axis_size("dom")
    height = source.shape[0]
    dom = jnp.stack([lax.axis_index("dom"), lax.axis_index("prop")]).astype(jnp.int32)
    near = source_side(source)
    current, noise_part = from_accepted(states[0], accepted[0], BETA * noise[0])
    perm = jnp.exp(current + noise_part)
    _, source, near = lax.optimization_barrier((perm, source, near))
    perms = (perm, other_side(perm), swaps(perm, "dom", 1))
    sources = (OMEGA * source, near, swaps(near, "prop", 1))
    *level, coarse = fine_part(dom, perms, sources, domains * height)
    return coarse_part(dom, gather_parts(coarse), *level, height)[None]


def solution(mesh):
    in_specs = (
        P("prop", "dom", None, None),
        P(),
        P("prop", "dom", None, None),
        P("dom", None, None),
    )
    out_specs = P("prop", "dom", None, None)
    return jax.shard_map(body, mesh=mesh, in_specs=in_specs, out_specs=out_specs, check_vma=False)
```

```python
import functools
import math

import jax
import jax.numpy as jnp
from jax import lax
from jax.experimental import pallas as pl
from jax.experimental.pallas import tpu as pltpu
from jax.sharding import PartitionSpec as P

COARSE_SWEEPS = 64
POWER = 3
OMEGA = 0.7
KEEP = 1.0 - OMEGA
BETA = 0.4
SHRINK = math.sqrt(1.0 - BETA * BETA)
ZSCALE = 16.0
LANES = 128
VMEM_LIMIT = 40 * 1024 * 1024
F32 = jnp.float32
WEST, EAST, SOUTH, NORTH, BELOW, ABOVE, CONST = range(7)


def iota(shape, dim):
    return lax.broadcasted_iota(jnp.int32, shape, dim)


def roll(x, amount, axis):
    axis = axis % x.ndim
    return pltpu.roll(x, amount % x.shape[axis], axis)


def inverse_of(x):
    guess = pl.reciprocal(x, approx=True)
    return guess * (2.0 - x * guess)


def harmonic(a, b):
    return (2.0 * a) * b * inverse_of(a + b)


def selector_dot(parts, selector):
    x = jnp.concatenate(parts, axis=0) if len(parts) > 1 else parts[0]
    rows = x.shape[0]
    high = x.astype(jnp.bfloat16).astype(F32)
    rest = x - high
    middle = rest.astype(jnp.bfloat16).astype(F32)
    terms = jnp.concatenate([high, middle, rest - middle], axis=0).astype(jnp.bfloat16)
    y = jnp.dot(terms, selector, preferred_element_type=F32)
    total = y[:rows] + y[rows : 2 * rows] + y[2 * rows :]
    height = parts[0].shape[0]
    return [total[i * height : (i + 1) * height] for i in range(len(parts))]


def face_terms(perm, below, above, ny):
    shape = perm.shape
    rows = iota(shape, 0)
    columns = iota(shape, 1) & (ny - 1)
    west = jnp.where(rows == 0, 0.0, harmonic(perm, roll(perm, 1, 0)))
    east = roll(west, -1, 0)
    south = jnp.where(columns == 0, 0.0, harmonic(perm, roll(perm, 1, 1)))
    north = roll(south, -1, 1)
    ends = jnp.where(rows == 0, perm, 0.0) + jnp.where(rows == shape[0] - 1, perm, 0.0)
    ends = ends + jnp.where(columns == 0, perm, 0.0) + jnp.where(columns == ny - 1, perm, 0.0)
    diagonal = ((west + east) + (south + north)) + ((below + above) + ends)
    return (west, east, south, north, below, above), diagonal


def stencil(values, lower, upper, coefs, base):
    x = coefs[0] * roll(values, 1, 0) + coefs[1] * roll(values, -1, 0)
    y = coefs[2] * roll(values, 1, 1) + coefs[3] * roll(values, -1, 1)
    z = coefs[4] * lower + coefs[5] * upper
    return (x + y) + (z + base)


def lane_selector(groups, ny, step, spread=False):
    shape = (LANES, step * LANES) if spread else (step * LANES, LANES)
    source, target = iota(shape, int(spread)), iota(shape, 1 - int(spread))
    bits = ny.bit_length() - 1
    lane = source & (LANES - 1)
    group = (lane >> bits) * step + (source >> 7)
    wanted = (group << (bits - 1)) + ((lane & (ny - 1)) >> 1)
    return jnp.where((target == wanted) & (lane < groups * ny), 1.0, 0.0).astype(jnp.bfloat16)


def fine_kernel(
    layers,
    dom_ref,
    per, per_other, per_pair,
    src, src_near, src_next,
    coef, const, values, coarse_out,
    perm, right, diag, pair_right, pair_perm,
):
    height = per.shape[0]
    dom = dom_ref[0]
    pair_at = jnp.where(lax.rem(dom, 2) == 0, 2 * height, 0)
    other_at = 2 * height - pair_at

    near_at = jnp.where(lax.rem(dom_ref[1], 2) == 0, pair_at, other_at)
    next_at = 2 * height - near_at
    for i in range(height):
        for at, p in ((height, per), (pair_at, per_pair), (other_at, per_other)):
            perm[at + i] = p[i]
        right[height + i] = src[i]
        right[near_at + i] = OMEGA * src_near[i]
        right[next_at + i] = OMEGA * src_next[i]

    def face(i):
        z = dom * height + i - 3
        scale = jnp.where((z > 0) & (z < layers), ZSCALE, 0.0)
        at = height - 3 + i
        return scale * harmonic(perm[at - 1], perm[at])

    above = face(0)
    for i in range(height + 6):
        at = height - 3 + i
        below, above = above, face(i + 1)
        faces, diagonal = face_terms(perm[at], below, above, LANES)
        inverse = inverse_of(diagonal)
        const[i] = inverse * right[at]
        if 0 < i < height + 5:
            inverse = OMEGA * inverse
            for k in range(6):
                coef[k, i] = inverse * faces[k]
        if 3 <= i < height + 3:
            diag[i] = diagonal

    def first(i):
        start = const[i + 1]
        near = [coef[k, i + 1] for k in range(6)]
        values[i] = stencil(start, const[i], const[i + 2], near, (1.0 + KEEP) * start)

    for i in range(height + 4):
        first(i)

    def residue(i):
        centre = values[i + 2]
        base = const[i + 3] - OMEGA * centre
        near = [coef[k, i + 3] for k in range(6)]
        scaled = stencil(centre, values[i + 1], values[i + 3], near, base)
        return scaled * (diag[i + 3] * (1.0 / OMEGA))

    for m in range(height // 2):
        pair_right[m] = residue(2 * m) + residue(2 * m + 1)
        pair_perm[m] = (perm[height + 2 * m] + perm[height + 2 * m + 1]) * 0.125
    half = pair_right.shape[1] // 2
    rows = []
    for m in range(height // 2):
        both = [x[m, pl.ds(0, half, 2), :] + x[m, pl.ds(1, half, 2), :] for x in (pair_right, pair_perm)]
        rows.append(jnp.concatenate(both, axis=1))
    for m, x in enumerate(selector_dot(rows, lane_selector(1, LANES, 2))):
        coarse_out[m] = x


class Packed:
    def __init__(self, nz, nx, ny):
        self.nz, self.nx, self.ny = nz, nx, ny
        self.groups = min(LANES // ny, nz)
        self.planes = nz // self.groups

    def lower(self, planes, p):
        return planes[p - 1] if p else roll(planes[self.planes - 1], self.ny, 1)

    def upper(self, planes, p):
        return planes[p + 1] if p + 1 < self.planes else roll(planes[0], -self.ny, 1)

    def system(self, perm, level):
        lane = iota((self.nx, LANES), 1)
        used = lane < self.groups * self.ny
        if self.groups * self.ny < LANES:
            perm = [jnp.where(used, x, 1.0) for x in perm]
        coefs, factors, diagonals = [], [], []
        inner = [ZSCALE * harmonic(a, b) for a, b in zip(perm[:-1], perm[1:])]
        wrapped = ZSCALE * harmonic(perm[-1], roll(perm[0], -self.ny, 1))
        last = jnp.where(lane < (self.groups - 1) * self.ny, wrapped, 0.0)
        z_faces = [roll(last, self.ny, 1)] + inner + [last]
        for p in range(self.planes):
            faces, diagonal = face_terms(perm[p], z_faces[p], z_faces[p + 1], self.ny)
            inverse = OMEGA * inverse_of(diagonal)
            coefs.append([inverse * face for face in faces])
            factors.append(inverse * (4.0**-level))
            diagonals.append(diagonal * (4.0**level / OMEGA))
        return coefs, factors, diagonals

    def apply(self, values, coefs, bases):
        return [
            stencil(values[p], self.lower(values, p), self.upper(values, p), coefs[p], bases[p])
            for p in range(self.planes)
        ]

    def sweep(self, values, coefs, const):
        return self.apply(values, coefs, [KEEP * v + c for v, c in zip(values, const)])

    def coarser(self):
        return Packed(self.nz // 2, self.nx // 2, self.ny // 2)

    def restrict(self, fields, pads):
        coarse = self.coarser()
        step = coarse.groups // self.groups
        half = coarse.nx
        parts = []
        for values, pad in zip(fields, pads):
            rows = []
            for m in range(self.planes // 2):
                pad[m] = values[2 * m] + values[2 * m + 1]
                rows.append(pad[m, pl.ds(0, half, 2), :] + pad[m, pl.ds(1, half, 2), :])
            for p in range(coarse.planes):
                blocks = rows[p :: coarse.planes]
                parts.append(jnp.concatenate(blocks, axis=1) if step > 1 else blocks[0])
        sums = selector_dot(parts, lane_selector(self.groups, self.ny, step))
        return [sums[i : i + coarse.planes] for i in range(0, len(sums), coarse.planes)]

    def prolong(self, values, pad):
        coarse = self.coarser()
        step = coarse.groups // self.groups
        half = coarse.nx
        wide = selector_dot(values, lane_selector(self.groups, self.ny, step, spread=True))
        out = []
        for m in range(self.planes // 2):
            j, p = divmod(m, coarse.planes)
            plane = wide[p][:, j * LANES : (j + 1) * LANES]
            pad[m, pl.ds(0, half, 2), :] = plane
            pad[m, pl.ds(1, half, 2), :] = plane
            out += [pad[m], pad[m]]
        return out


class Flat:
    def __init__(self, finer):
        coarse = finer.coarser()
        self.finer = finer
        self.nz, self.nx, self.ny = coarse.nz, coarse.nx, coarse.ny
        self.pairs = finer.planes // 2
        self.rows = max(8, self.nz)
        self.shape = (self.rows, LANES)
        self.buffer_rows = 2 * (self.rows + 2 * POWER)

    def selector(self, spread=False):
        wide = self.finer.groups * LANES
        shape = (wide, LANES) if spread else (LANES, wide)
        fine, flat = iota(shape, int(spread)), iota(shape, 1 - int(spread))
        bits = self.finer.ny.bit_length() - 1
        same = (fine >> bits) == (flat >> 7)
        same &= ((fine & (self.finer.ny - 1)) >> 1) == (flat & (self.ny - 1))
        return jnp.where(same, 1.0, 0.0).astype(jnp.bfloat16)

    def diagonal(self):
        shape = (self.nx, LANES)
        return iota(shape, 0) == (iota(shape, 1) >> (self.ny.bit_length() - 1))

    def restrict(self, fields, pads, pack):
        parts = []
        for values, pad in zip(fields, pads):
            for m in range(self.pairs):
                pad[m] = values[2 * m] + values[2 * m + 1]
                parts.append(pad[m, pl.ds(0, self.nx, 2), :] + pad[m, pl.ds(1, self.nx, 2), :])
        sums = selector_dot(parts, self.selector())
        mask = self.diagonal()
        pack[...] = jnp.zeros_like(pack)
        for i in range(len(fields)):
            for z in range(self.nz):
                s, m = divmod(z, self.pairs)
                block = sums[i * self.pairs + m][:, s * LANES : (s + 1) * LANES]
                row = jnp.sum(jnp.where(mask, block, 0.0), axis=0, keepdims=True)
                pack[i, z : z + 1, :] = row
        return [pack[i] for i in range(len(fields))]

    def prolong(self, values, pad, pack):
        mask = self.diagonal()
        pack[0] = values
        parts = []
        for m in range(self.pairs):
            layers = [s * self.pairs + m for s in range(self.finer.groups)]
            spread = [jnp.broadcast_to(pack[0, z : z + 1, :], mask.shape) for z in layers]
            parts.append(jnp.concatenate([jnp.where(mask, x, 0.0) for x in spread], axis=1))
        out = []
        for m, wide in enumerate(selector_dot(parts, self.selector(spread=True))):
            pad[m, pl.ds(0, self.nx, 2), :] = wide
            pad[m, pl.ds(1, self.nx, 2), :] = wide
            out += [pad[m], pad[m]]
        return out

    def system(self, perm, level):
        lane, row = iota(self.shape, 1), iota(self.shape, 0)
        x, y = lane >> (self.ny.bit_length() - 1), lane & (self.ny - 1)
        real = row < self.nz
        perm = jnp.where(real, perm, 1.0)
        west = jnp.where(x == 0, 0.0, harmonic(perm, roll(perm, self.ny, 1)))
        east = roll(west, -self.ny, 1)
        south = jnp.where(y == 0, 0.0, harmonic(perm, roll(perm, 1, 1)))
        north = roll(south, -1, 1)
        below = ZSCALE * harmonic(perm, roll(perm, 1, 0))
        below = jnp.where((row > 0) & real, below, 0.0)
        above = roll(below, -1, 0)
        faces = [west, east, south, north, below, above]
        ends = (x == 0, x == self.nx - 1, y == 0, y == self.ny - 1)
        diagonal = tree_sum(faces + [jnp.where(end, perm, 0.0) for end in ends])
        inverse = jnp.where(real, OMEGA * inverse_of(diagonal), 0.0)
        keys = ((-1, 0, 0), (1, 0, 0), (0, -1, 0), (0, 1, 0), (0, 0, -1), (0, 0, 1))
        terms = {key: inverse * face for key, face in zip(keys, faces)}
        terms[0, 0, 0] = jnp.full(self.shape, KEEP, F32)
        return terms, inverse * (4.0**-level)

    def product(self, first, second):
        sums = {}
        for (dx, dy, dz), coef in first.items():
            for other, moved in second.items():
                if dz:
                    moved = roll(moved, -dz, 0)
                if dx or dy:
                    moved = roll(moved, -(dx * self.ny + dy), 1)
                total = tuple(a + b for a, b in zip((dx, dy, dz), other))
                sums.setdefault(total, []).append(coef * moved)
        return {key: tree_sum(parts) for key, parts in sums.items()}

    def apply(self, terms, values, base, buffer):
        buffer[pl.ds(2 * POWER, self.rows, 2), :] = values
        moved = {}
        for dx, dy, dz in sorted(terms, key=lambda key: abs(key[2])):
            if (0, 0, dz) not in moved:
                moved[0, 0, dz] = buffer[pl.ds(2 * (POWER + dz), self.rows, 2), :] if dz else values
            if dx or dy:
                moved[dx, dy, dz] = roll(moved[0, 0, dz], -(dx * self.ny + dy), 1)
        return tree_sum([base] + [coef * moved[key] for key, coef in terms.items()])

    def prepare(self, perm, level):
        terms, factor = self.system(perm, level)
        power = terms
        for _ in range(POWER - 1):
            power = self.product(terms, power)
        return terms, power, factor

    def solve(self, right, prepared, buffer):
        terms, power, factor = prepared
        const = factor * right
        buffer[...] = jnp.zeros_like(buffer)
        base = const
        for _ in range(POWER - 1):
            base = self.apply(terms, base, const, buffer)
        whole = COARSE_SWEEPS % POWER == 0
        values = base if whole else const
        steps = (COARSE_SWEEPS - 1) // POWER
        assert steps * POWER + (POWER if whole else 1) == COARSE_SWEEPS
        for _ in range(steps):
            values = self.apply(power, values, base, buffer)
        return values


def tree_sum(parts):
    while len(parts) > 1:
        odd = parts[len(parts) // 2 * 2 :]
        parts = [a + b for a, b in zip(parts[::2], parts[1::2])] + odd
    return parts[0]


def packed_cycle(grid, right, perm, level, pads, packs, buffer):
    pad_right, pad_perm = pads[0]
    coefs, factors, diagonals = grid.system(perm, level)
    if len(pads) > 1:
        (coarse_perm,) = grid.restrict([perm], [pad_perm])
    else:
        flat = Flat(grid)
        (coarse_perm,) = flat.restrict([perm], [pad_perm], packs[1])
        prepared = flat.prepare(coarse_perm * 0.125, level + 1)
    const = [f * r for f, r in zip(factors, right)]
    values = grid.sweep(const, coefs, const)
    scaled = grid.apply(values, coefs, [c - OMEGA * v for c, v in zip(const, values)])
    residue = [r * d for r, d in zip(scaled, diagonals)]
    if len(pads) > 1:
        (coarse_right,) = grid.restrict([residue], [pad_right])
        coarse_perm = [x * 0.125 for x in coarse_perm]
        update = packed_cycle(
            grid.coarser(), coarse_right, coarse_perm, level + 1, pads[1:], packs, buffer
        )
        update = grid.prolong(update, pad_right)
    else:
        (coarse_right,) = flat.restrict([residue], [pad_right], packs[0])
        update = flat.prolong(flat.solve(coarse_right, prepared, buffer), pad_right, packs[0])
    values = [v + e for v, e in zip(values, update)]
    for _ in range(2):
        values = grid.sweep(values, coefs, const)
    return values


def coarse_kernel(
    dom_ref, gathered, coef, const, before, out,
    level, first, pad_right1, pad_perm1, pad_right2, pad_perm2, update, pack, pack_perm, buffer,
    done, sems,
):
    height = out.shape[0]
    dom = dom_ref[0]
    domains, own, nx, _ = gathered.shape
    ny = LANES // 2
    grid = Packed(domains * own, nx, ny)
    left = iota((nx, LANES), 1) < ny
    right, perm = [], []
    for p in range(grid.planes):
        a = gathered[p // own, p % own]
        q = grid.planes + p
        b = gathered[q // own, q % own]
        right.append(jnp.where(left, a, roll(b, ny, 1)))
        perm.append(jnp.where(left, roll(a, ny, 1), b))
    pads = [(pad_right1, pad_perm1), (pad_right2, pad_perm2)]
    solved = packed_cycle(grid, right, perm, 1, pads, (pack, pack_perm), buffer)
    for p in range(grid.planes):
        update[p] = solved[p]
    planes, group = [], []
    for j in range(own + 2):
        layer = jnp.clip(dom * own + j - 1, 0, grid.nz - 1)
        group.append(layer // grid.planes)
        planes.append(update[lax.rem(layer, grid.planes)])
    for j, wide in enumerate(selector_dot(planes, lane_selector(1, LANES, 2, spread=True))):
        plane = jnp.where(group[j] == 0, wide[:, :LANES], wide[:, LANES:])
        pad = first.at[0]
        pad[pl.ds(0, nx, 2), :] = plane
        pad[pl.ds(1, nx, 2), :] = plane
        whole = first[0]
        level[2 * j] = before[2 * j] + whole
        level[2 * j + 1] = before[2 * j + 1] + whole

    def sweep(source, at, i):
        centre = source[i + 1]
        near = [coef[k, at + i] for k in range(6)]
        return stencil(centre, source[i], source[i + 2], near, KEEP * centre + const[at + i])

    def one(i):
        first[i] = sweep(level, 2, i)

    for i in range(height + 2):
        one(i)

    copies = []
    for i in range(height):
        done[i] = sweep(first, 3, i)
        copies.append(pltpu.make_async_copy(done.at[i], out.at[i], sems.at[i]))
        copies[-1].start()
    for copy in copies:
        copy.wait()


def fine_part(dom, perm, source, layers):
    height, nx, ny = perm[0].shape
    field = lambda *lead: pltpu.VMEM(lead + (nx, ny), F32)
    vmem = pl.BlockSpec(memory_space=pltpu.VMEM)
    smem = pl.BlockSpec(memory_space=pltpu.SMEM)
    return pl.pallas_call(
        functools.partial(fine_kernel, layers),
        out_shape=(
            jax.ShapeDtypeStruct((6, height + 6, nx, ny), F32),
            jax.ShapeDtypeStruct((height + 6, nx, ny), F32),
            jax.ShapeDtypeStruct((height + 4, nx, ny), F32),
            jax.ShapeDtypeStruct((height // 2, nx // 2, ny), F32),
        ),
        in_specs=[smem] + [vmem] * 6,
        out_specs=(vmem,) * 4,
        scratch_shapes=[
            field(3 * height),
            field(3 * height),
            field(height + 6),
            field(height // 2),
            field(height // 2),
        ],
        compiler_params=pltpu.CompilerParams(vmem_limit_bytes=VMEM_LIMIT),
        name="fine",
    )(dom, *perm, *source)


def coarse_part(dom, gathered, coefs, const, values, height):
    _, nx, ny = values.shape
    field = lambda *shape: pltpu.VMEM(shape, F32)
    grid1 = Packed(gathered.shape[0] * gathered.shape[1], nx // 2, ny // 2)
    grid2 = grid1.coarser()
    pads1 = field(grid1.planes // 2, grid1.nx, LANES)
    pads2 = field(grid2.planes // 2, grid2.nx, LANES)
    vmem = pl.BlockSpec(memory_space=pltpu.VMEM)
    smem = pl.BlockSpec(memory_space=pltpu.SMEM)
    return pl.pallas_call(
        coarse_kernel,
        out_shape=jax.ShapeDtypeStruct((height, nx, ny), F32),
        in_specs=[smem] + [vmem] * 4,
        out_specs=pl.BlockSpec(memory_space=pl.ANY),
        scratch_shapes=[
            field(*values.shape),
            field(height + 2, nx, ny),
            pads1, pads1, pads2, pads2,
            field(grid1.planes, grid1.nx, LANES),
            field(1, Flat(grid2).rows, LANES),
            field(1, Flat(grid2).rows, LANES),
            field(Flat(grid2).buffer_rows, LANES),
            field(height, nx, ny),
            pltpu.SemaphoreType.DMA((height,)),
        ],
        compiler_params=pltpu.CompilerParams(vmem_limit_bytes=VMEM_LIMIT),
        name="coarse",
    )(dom, gathered, coefs, const, values)


def swaps(x, axis, step):
    return lax.ppermute(x, axis, [(i, i ^ step) for i in range(lax.axis_size(axis))])


def other_side(x):
    props, domains = lax.axis_size("prop"), lax.axis_size("dom")
    pairs = []
    for p in range(props):
        for d in range(domains):
            end = d in (0, domains - 1)
            partner = ((p ^ 1) * domains + d) if end else (p * domains + ((d + 1) ^ 1) - 1)
            pairs.append((p * domains + d, partner))
    return lax.ppermute(x, ("prop", "dom"), pairs)


def source_side(x):
    props, domains = lax.axis_size("prop"), lax.axis_size("dom")
    pairs = []
    for p in range(props):
        for d in range(domains):
            if d in (0, domains - 1):
                target = (p ^ 1) * domains + (d if p % 2 == 0 else d ^ 1)
            elif p % 2 == 0:
                target = p * domains + (d ^ 1)
            else:
                target = p * domains + ((d + 1) ^ 1) - 1
            pairs.append((p * domains + d, target))
    return lax.ppermute(x, ("prop", "dom"), pairs)


def from_accepted(mine, accepted, beside):
    props = lax.axis_size("prop")
    apart = lax.axis_index("prop") ^ accepted
    own = SHRINK * mine
    step = props // 2
    came = swaps(mine, "prop", step)
    came, own, beside = lax.optimization_barrier((came, own, beside))
    current = jnp.where(apart & step, SHRINK * came, own)
    while step > 1:
        step //= 2
        came = jnp.concatenate([swaps(x, "prop", step) for x in jnp.split(current, 2)])
        current = jnp.where(apart & step, came, current)
    return current, beside


def gather_parts(mine):
    domains = lax.axis_size("dom")
    copies = jnp.broadcast_to(mine[None], (domains,) + mine.shape)
    return lax.all_to_all(copies, "dom", 0, 0)


def body(states, accepted, noise, source):
    domains = lax.axis_size("dom")
    height = source.shape[0]
    dom = jnp.stack([lax.axis_index("dom"), lax.axis_index("prop")]).astype(jnp.int32)
    near = source_side(source)
    current, noise_part = from_accepted(states[0], accepted[0], BETA * noise[0])
    perm = jnp.exp(current + noise_part)
    _, source, near = lax.optimization_barrier((perm, source, near))
    perms = (perm, other_side(perm), swaps(perm, "dom", 1))
    sources = (OMEGA * source, near, swaps(near, "prop", 1))
    *level, coarse = fine_part(dom, perms, sources, domains * height)
    return coarse_part(dom, gather_parts(coarse), *level, height)[None]


def solution(mesh):
    in_specs = (
        P("prop", "dom", None, None),
        P(),
        P("prop", "dom", None, None),
        P("dom", None, None),
    )
    out_specs = P("prop", "dom", None, None)
    return jax.shard_map(body, mesh=mesh, in_specs=in_specs, out_specs=out_specs, check_vma=False)
```

```python
import functools
import math

import jax
import jax.numpy as jnp
from jax import lax
from jax.experimental import pallas as pl
from jax.experimental.pallas import tpu as pltpu
from jax.sharding import PartitionSpec as P

COARSE_SWEEPS = 64
POWER = 3
OMEGA = 0.7
KEEP = 1.0 - OMEGA
BETA = 0.4
SHRINK = math.sqrt(1.0 - BETA * BETA)
ZSCALE = 16.0
LANES = 128
VMEM_LIMIT = 40 * 1024 * 1024
F32 = jnp.float32
WEST, EAST, SOUTH, NORTH, BELOW, ABOVE, CONST = range(7)


def iota(shape, dim):
    return lax.broadcasted_iota(jnp.int32, shape, dim)


def roll(x, amount, axis):
    axis = axis % x.ndim
    return pltpu.roll(x, amount % x.shape[axis], axis)


def inverse_of(x):
    guess = pl.reciprocal(x, approx=True)
    return guess * (2.0 - x * guess)


def harmonic(a, b):
    return (2.0 * a) * b * inverse_of(a + b)


def selector_dot(parts, selector):
    x = jnp.concatenate(parts, axis=0) if len(parts) > 1 else parts[0]
    rows = x.shape[0]
    high = x.astype(jnp.bfloat16).astype(F32)
    rest = x - high
    middle = rest.astype(jnp.bfloat16).astype(F32)
    terms = jnp.concatenate([high, middle, rest - middle], axis=0).astype(jnp.bfloat16)
    y = jnp.dot(terms, selector, preferred_element_type=F32)
    total = y[:rows] + y[rows : 2 * rows] + y[2 * rows :]
    height = parts[0].shape[0]
    return [total[i * height : (i + 1) * height] for i in range(len(parts))]


def side_faces(perm, ny):
    shape = perm.shape
    rows = iota(shape, 0)
    columns = iota(shape, 1) & (ny - 1)
    west = jnp.where(rows == 0, 0.0, harmonic(perm, roll(perm, 1, 0)))
    east = roll(west, -1, 0)
    south = jnp.where(columns == 0, 0.0, harmonic(perm, roll(perm, 1, 1)))
    north = roll(south, -1, 1)
    ends = jnp.where(rows == 0, perm, 0.0) + jnp.where(rows == shape[0] - 1, perm, 0.0)
    ends = ends + jnp.where(columns == 0, perm, 0.0) + jnp.where(columns == ny - 1, perm, 0.0)
    return west, east, south, north, ((west + east) + (south + north)) + ends


def face_terms(perm, below, above, ny):
    *sides, total = side_faces(perm, ny)
    return (*sides, below, above), total + (below + above)


def stencil(values, lower, upper, coefs, base):
    x = coefs[0] * roll(values, 1, 0) + coefs[1] * roll(values, -1, 0)
    y = coefs[2] * roll(values, 1, 1) + coefs[3] * roll(values, -1, 1)
    z = coefs[4] * lower + coefs[5] * upper
    return (x + y) + (z + base)


def lane_selector(groups, ny, step, spread=False):
    shape = (LANES, step * LANES) if spread else (step * LANES, LANES)
    source, target = iota(shape, int(spread)), iota(shape, 1 - int(spread))
    bits = ny.bit_length() - 1
    lane = source & (LANES - 1)
    group = (lane >> bits) * step + (source >> 7)
    wanted = (group << (bits - 1)) + ((lane & (ny - 1)) >> 1)
    return jnp.where((target == wanted) & (lane < groups * ny), 1.0, 0.0).astype(jnp.bfloat16)


def side_kernel(perm, out):
    for i in range(perm.shape[0]):
        for k, x in enumerate(side_faces(perm[i], LANES)):
            out[k, i] = x


def fine_kernel(
    layers,
    dom_ref, sides,
    per, per_other, per_pair,
    src, src_near, src_next,
    coef, const, values, coarse_out,
    perm, right, diag, pair_right, pair_perm,
):
    height = per.shape[0]
    dom = dom_ref[0]
    pair_at = jnp.where(lax.rem(dom, 2) == 0, 2 * height, 0)
    other_at = 2 * height - pair_at

    near_at = jnp.where(lax.rem(dom_ref[1], 2) == 0, pair_at, other_at)
    next_at = 2 * height - near_at
    for i in range(height):
        for at, p in ((height, per), (pair_at, per_pair), (other_at, per_other)):
            perm[at + i] = p[i]
        right[height + i] = src[i]
        right[near_at + i] = OMEGA * src_near[i]
        right[next_at + i] = OMEGA * src_next[i]

    def face(i):
        z = dom * height + i - 3
        scale = jnp.where((z > 0) & (z < layers), ZSCALE, 0.0)
        at = height - 3 + i
        return scale * harmonic(perm[at - 1], perm[at])

    above = face(0)
    for i in range(height + 6):
        at = height - 3 + i
        below, above = above, face(i + 1)
        if 3 <= i < height + 3:
            faces = tuple(sides[k, i - 3] for k in range(4)) + (below, above)
            diagonal = sides[4, i - 3] + (below + above)
        else:
            faces, diagonal = face_terms(perm[at], below, above, LANES)
        inverse = inverse_of(diagonal)
        const[i] = inverse * right[at]
        if 0 < i < height + 5:
            inverse = OMEGA * inverse
            for k in range(6):
                coef[k, i] = inverse * faces[k]
        if 3 <= i < height + 3:
            diag[i] = diagonal

    def first(i):
        start = const[i + 1]
        near = [coef[k, i + 1] for k in range(6)]
        values[i] = stencil(start, const[i], const[i + 2], near, (1.0 + KEEP) * start)

    for i in range(height + 4):
        first(i)

    def residue(i):
        centre = values[i + 2]
        base = const[i + 3] - OMEGA * centre
        near = [coef[k, i + 3] for k in range(6)]
        scaled = stencil(centre, values[i + 1], values[i + 3], near, base)
        return scaled * (diag[i + 3] * (1.0 / OMEGA))

    for m in range(height // 2):
        pair_right[m] = residue(2 * m) + residue(2 * m + 1)
        pair_perm[m] = (perm[height + 2 * m] + perm[height + 2 * m + 1]) * 0.125
    half = pair_right.shape[1] // 2
    rows = []
    for m in range(height // 2):
        both = [x[m, pl.ds(0, half, 2), :] + x[m, pl.ds(1, half, 2), :] for x in (pair_right, pair_perm)]
        rows.append(jnp.concatenate(both, axis=1))
    for m, x in enumerate(selector_dot(rows, lane_selector(1, LANES, 2))):
        coarse_out[m] = x


class Packed:
    def __init__(self, nz, nx, ny):
        self.nz, self.nx, self.ny = nz, nx, ny
        self.groups = min(LANES // ny, nz)
        self.planes = nz // self.groups

    def lower(self, planes, p):
        return planes[p - 1] if p else roll(planes[self.planes - 1], self.ny, 1)

    def upper(self, planes, p):
        return planes[p + 1] if p + 1 < self.planes else roll(planes[0], -self.ny, 1)

    def system(self, perm, level):
        lane = iota((self.nx, LANES), 1)
        used = lane < self.groups * self.ny
        if self.groups * self.ny < LANES:
            perm = [jnp.where(used, x, 1.0) for x in perm]
        coefs, factors, diagonals = [], [], []
        inner = [ZSCALE * harmonic(a, b) for a, b in zip(perm[:-1], perm[1:])]
        wrapped = ZSCALE * harmonic(perm[-1], roll(perm[0], -self.ny, 1))
        last = jnp.where(lane < (self.groups - 1) * self.ny, wrapped, 0.0)
        z_faces = [roll(last, self.ny, 1)] + inner + [last]
        for p in range(self.planes):
            faces, diagonal = face_terms(perm[p], z_faces[p], z_faces[p + 1], self.ny)
            inverse = OMEGA * inverse_of(diagonal)
            coefs.append([inverse * face for face in faces])
            factors.append(inverse * (4.0**-level))
            diagonals.append(diagonal * (4.0**level / OMEGA))
        return coefs, factors, diagonals

    def apply(self, values, coefs, bases):
        return [
            stencil(values[p], self.lower(values, p), self.upper(values, p), coefs[p], bases[p])
            for p in range(self.planes)
        ]

    def sweep(self, values, coefs, const):
        return self.apply(values, coefs, [KEEP * v + c for v, c in zip(values, const)])

    def coarser(self):
        return Packed(self.nz // 2, self.nx // 2, self.ny // 2)

    def restrict(self, fields, pads):
        coarse = self.coarser()
        step = coarse.groups // self.groups
        half = coarse.nx
        parts = []
        for values, pad in zip(fields, pads):
            rows = []
            for m in range(self.planes // 2):
                pad[m] = values[2 * m] + values[2 * m + 1]
                rows.append(pad[m, pl.ds(0, half, 2), :] + pad[m, pl.ds(1, half, 2), :])
            for p in range(coarse.planes):
                blocks = rows[p :: coarse.planes]
                parts.append(jnp.concatenate(blocks, axis=1) if step > 1 else blocks[0])
        sums = selector_dot(parts, lane_selector(self.groups, self.ny, step))
        return [sums[i : i + coarse.planes] for i in range(0, len(sums), coarse.planes)]

    def prolong(self, values, pad):
        coarse = self.coarser()
        step = coarse.groups // self.groups
        half = coarse.nx
        wide = selector_dot(values, lane_selector(self.groups, self.ny, step, spread=True))
        out = []
        for m in range(self.planes // 2):
            j, p = divmod(m, coarse.planes)
            plane = wide[p][:, j * LANES : (j + 1) * LANES]
            pad[m, pl.ds(0, half, 2), :] = plane
            pad[m, pl.ds(1, half, 2), :] = plane
            out += [pad[m], pad[m]]
        return out


class Flat:
    def __init__(self, finer):
        coarse = finer.coarser()
        self.finer = finer
        self.nz, self.nx, self.ny = coarse.nz, coarse.nx, coarse.ny
        self.pairs = finer.planes // 2
        self.rows = max(8, self.nz)
        self.shape = (self.rows, LANES)
        self.buffer_rows = 2 * (self.rows + 2 * POWER)

    def selector(self, spread=False):
        wide = self.finer.groups * LANES
        shape = (wide, LANES) if spread else (LANES, wide)
        fine, flat = iota(shape, int(spread)), iota(shape, 1 - int(spread))
        bits = self.finer.ny.bit_length() - 1
        same = (fine >> bits) == (flat >> 7)
        same &= ((fine & (self.finer.ny - 1)) >> 1) == (flat & (self.ny - 1))
        return jnp.where(same, 1.0, 0.0).astype(jnp.bfloat16)

    def diagonal(self):
        shape = (self.nx, LANES)
        return iota(shape, 0) == (iota(shape, 1) >> (self.ny.bit_length() - 1))

    def restrict(self, fields, pads, pack):
        parts = []
        for values, pad in zip(fields, pads):
            for m in range(self.pairs):
                pad[m] = values[2 * m] + values[2 * m + 1]
                parts.append(pad[m, pl.ds(0, self.nx, 2), :] + pad[m, pl.ds(1, self.nx, 2), :])
        sums = selector_dot(parts, self.selector())
        mask = self.diagonal()
        pack[...] = jnp.zeros_like(pack)
        for i in range(len(fields)):
            for z in range(self.nz):
                s, m = divmod(z, self.pairs)
                block = sums[i * self.pairs + m][:, s * LANES : (s + 1) * LANES]
                row = jnp.sum(jnp.where(mask, block, 0.0), axis=0, keepdims=True)
                pack[i, z : z + 1, :] = row
        return [pack[i] for i in range(len(fields))]

    def prolong(self, values, pad, pack):
        mask = self.diagonal()
        pack[0] = values
        parts = []
        for m in range(self.pairs):
            layers = [s * self.pairs + m for s in range(self.finer.groups)]
            spread = [jnp.broadcast_to(pack[0, z : z + 1, :], mask.shape) for z in layers]
            parts.append(jnp.concatenate([jnp.where(mask, x, 0.0) for x in spread], axis=1))
        out = []
        for m, wide in enumerate(selector_dot(parts, self.selector(spread=True))):
            pad[m, pl.ds(0, self.nx, 2), :] = wide
            pad[m, pl.ds(1, self.nx, 2), :] = wide
            out += [pad[m], pad[m]]
        return out

    def system(self, perm, level):
        lane, row = iota(self.shape, 1), iota(self.shape, 0)
        x, y = lane >> (self.ny.bit_length() - 1), lane & (self.ny - 1)
        real = row < self.nz
        perm = jnp.where(real, perm, 1.0)
        west = jnp.where(x == 0, 0.0, harmonic(perm, roll(perm, self.ny, 1)))
        east = roll(west, -self.ny, 1)
        south = jnp.where(y == 0, 0.0, harmonic(perm, roll(perm, 1, 1)))
        north = roll(south, -1, 1)
        below = ZSCALE * harmonic(perm, roll(perm, 1, 0))
        below = jnp.where((row > 0) & real, below, 0.0)
        above = roll(below, -1, 0)
        faces = [west, east, south, north, below, above]
        ends = (x == 0, x == self.nx - 1, y == 0, y == self.ny - 1)
        diagonal = tree_sum(faces + [jnp.where(end, perm, 0.0) for end in ends])
        inverse = jnp.where(real, OMEGA * inverse_of(diagonal), 0.0)
        keys = ((-1, 0, 0), (1, 0, 0), (0, -1, 0), (0, 1, 0), (0, 0, -1), (0, 0, 1))
        terms = {key: inverse * face for key, face in zip(keys, faces)}
        terms[0, 0, 0] = jnp.full(self.shape, KEEP, F32)
        return terms, inverse * (4.0**-level)

    def product(self, first, second):
        sums = {}
        for (dx, dy, dz), coef in first.items():
            for other, moved in second.items():
                if dz:
                    moved = roll(moved, -dz, 0)
                if dx or dy:
                    moved = roll(moved, -(dx * self.ny + dy), 1)
                total = tuple(a + b for a, b in zip((dx, dy, dz), other))
                sums.setdefault(total, []).append(coef * moved)
        return {key: tree_sum(parts) for key, parts in sums.items()}

    def apply(self, terms, values, base, buffer):
        buffer[pl.ds(2 * POWER, self.rows, 2), :] = values
        moved = {}
        for dx, dy, dz in sorted(terms, key=lambda key: abs(key[2])):
            if (0, 0, dz) not in moved:
                moved[0, 0, dz] = buffer[pl.ds(2 * (POWER + dz), self.rows, 2), :] if dz else values
            if dx or dy:
                moved[dx, dy, dz] = roll(moved[0, 0, dz], -(dx * self.ny + dy), 1)
        return tree_sum([base] + [coef * moved[key] for key, coef in terms.items()])

    def prepare(self, perm, level):
        terms, factor = self.system(perm, level)
        power = terms
        for _ in range(POWER - 1):
            power = self.product(terms, power)
        return terms, power, factor

    def solve(self, right, prepared, buffer):
        terms, power, factor = prepared
        const = factor * right
        buffer[...] = jnp.zeros_like(buffer)
        base = const
        for _ in range(POWER - 1):
            base = self.apply(terms, base, const, buffer)
        whole = COARSE_SWEEPS % POWER == 0
        values = base if whole else const
        steps = (COARSE_SWEEPS - 1) // POWER
        assert steps * POWER + (POWER if whole else 1) == COARSE_SWEEPS
        for _ in range(steps):
            values = self.apply(power, values, base, buffer)
        return values


def tree_sum(parts):
    while len(parts) > 1:
        odd = parts[len(parts) // 2 * 2 :]
        parts = [a + b for a, b in zip(parts[::2], parts[1::2])] + odd
    return parts[0]


def packed_cycle(grid, right, perm, level, pads, packs, buffer):
    pad_right, pad_perm = pads[0]
    coefs, factors, diagonals = grid.system(perm, level)
    if len(pads) > 1:
        (coarse_perm,) = grid.restrict([perm], [pad_perm])
    else:
        flat = Flat(grid)
        (coarse_perm,) = flat.restrict([perm], [pad_perm], packs[1])
        prepared = flat.prepare(coarse_perm * 0.125, level + 1)
    const = [f * r for f, r in zip(factors, right)]
    values = grid.sweep(const, coefs, const)
    scaled = grid.apply(values, coefs, [c - OMEGA * v for c, v in zip(const, values)])
    residue = [r * d for r, d in zip(scaled, diagonals)]
    if len(pads) > 1:
        (coarse_right,) = grid.restrict([residue], [pad_right])
        coarse_perm = [x * 0.125 for x in coarse_perm]
        update = packed_cycle(
            grid.coarser(), coarse_right, coarse_perm, level + 1, pads[1:], packs, buffer
        )
        update = grid.prolong(update, pad_right)
    else:
        (coarse_right,) = flat.restrict([residue], [pad_right], packs[0])
        update = flat.prolong(flat.solve(coarse_right, prepared, buffer), pad_right, packs[0])
    values = [v + e for v, e in zip(values, update)]
    for _ in range(2):
        values = grid.sweep(values, coefs, const)
    return values


def coarse_kernel(
    dom_ref, gathered, coef, const, before, out,
    level, first, pad_right1, pad_perm1, pad_right2, pad_perm2, update, pack, pack_perm, buffer,
    done, sems,
):
    height = out.shape[0]
    dom = dom_ref[0]
    domains, own, nx, _ = gathered.shape
    ny = LANES // 2
    grid = Packed(domains * own, nx, ny)
    left = iota((nx, LANES), 1) < ny
    right, perm = [], []
    for p in range(grid.planes):
        a = gathered[p // own, p % own]
        q = grid.planes + p
        b = gathered[q // own, q % own]
        right.append(jnp.where(left, a, roll(b, ny, 1)))
        perm.append(jnp.where(left, roll(a, ny, 1), b))
    pads = [(pad_right1, pad_perm1), (pad_right2, pad_perm2)]
    solved = packed_cycle(grid, right, perm, 1, pads, (pack, pack_perm), buffer)
    for p in range(grid.planes):
        update[p] = solved[p]
    planes, group = [], []
    for j in range(own + 2):
        layer = jnp.clip(dom * own + j - 1, 0, grid.nz - 1)
        group.append(layer // grid.planes)
        planes.append(update[lax.rem(layer, grid.planes)])
    for j, wide in enumerate(selector_dot(planes, lane_selector(1, LANES, 2, spread=True))):
        plane = jnp.where(group[j] == 0, wide[:, :LANES], wide[:, LANES:])
        pad = first.at[0]
        pad[pl.ds(0, nx, 2), :] = plane
        pad[pl.ds(1, nx, 2), :] = plane
        whole = first[0]
        level[2 * j] = before[2 * j] + whole
        level[2 * j + 1] = before[2 * j + 1] + whole

    def sweep(source, at, i):
        centre = source[i + 1]
        near = [coef[k, at + i] for k in range(6)]
        return stencil(centre, source[i], source[i + 2], near, KEEP * centre + const[at + i])

    def one(i):
        first[i] = sweep(level, 2, i)

    for i in range(height + 2):
        one(i)

    copies = []
    for i in range(height):
        done[i] = sweep(first, 3, i)
        copies.append(pltpu.make_async_copy(done.at[i], out.at[i], sems.at[i]))
        copies[-1].start()
    for copy in copies:
        copy.wait()


def fine_part(dom, perm, source, layers):
    height, nx, ny = perm[0].shape
    field = lambda *lead: pltpu.VMEM(lead + (nx, ny), F32)
    vmem = pl.BlockSpec(memory_space=pltpu.VMEM)
    sides = pl.pallas_call(
        side_kernel,
        out_shape=jax.ShapeDtypeStruct((5, height, nx, ny), F32),
        in_specs=[vmem],
        out_specs=vmem,
        compiler_params=pltpu.CompilerParams(vmem_limit_bytes=VMEM_LIMIT),
        name="sides",
    )(perm[0])
    smem = pl.BlockSpec(memory_space=pltpu.SMEM)
    return pl.pallas_call(
        functools.partial(fine_kernel, layers),
        out_shape=(
            jax.ShapeDtypeStruct((6, height + 6, nx, ny), F32),
            jax.ShapeDtypeStruct((height + 6, nx, ny), F32),
            jax.ShapeDtypeStruct((height + 4, nx, ny), F32),
            jax.ShapeDtypeStruct((height // 2, nx // 2, ny), F32),
        ),
        in_specs=[smem] + [vmem] * 7,
        out_specs=(vmem,) * 4,
        scratch_shapes=[
            field(3 * height),
            field(3 * height),
            field(height + 6),
            field(height // 2),
            field(height // 2),
        ],
        compiler_params=pltpu.CompilerParams(vmem_limit_bytes=VMEM_LIMIT),
        name="fine",
    )(dom, sides, *perm, *source)


def coarse_part(dom, gathered, coefs, const, values, height):
    _, nx, ny = values.shape
    field = lambda *shape: pltpu.VMEM(shape, F32)
    grid1 = Packed(gathered.shape[0] * gathered.shape[1], nx // 2, ny // 2)
    grid2 = grid1.coarser()
    pads1 = field(grid1.planes // 2, grid1.nx, LANES)
    pads2 = field(grid2.planes // 2, grid2.nx, LANES)
    vmem = pl.BlockSpec(memory_space=pltpu.VMEM)
    smem = pl.BlockSpec(memory_space=pltpu.SMEM)
    return pl.pallas_call(
        coarse_kernel,
        out_shape=jax.ShapeDtypeStruct((height, nx, ny), F32),
        in_specs=[smem] + [vmem] * 4,
        out_specs=pl.BlockSpec(memory_space=pl.ANY),
        scratch_shapes=[
            field(*values.shape),
            field(height + 2, nx, ny),
            pads1, pads1, pads2, pads2,
            field(grid1.planes, grid1.nx, LANES),
            field(1, Flat(grid2).rows, LANES),
            field(1, Flat(grid2).rows, LANES),
            field(Flat(grid2).buffer_rows, LANES),
            field(height, nx, ny),
            pltpu.SemaphoreType.DMA((height,)),
        ],
        compiler_params=pltpu.CompilerParams(vmem_limit_bytes=VMEM_LIMIT),
        name="coarse",
    )(dom, gathered, coefs, const, values)


def swaps(x, axis, step):
    return lax.ppermute(x, axis, [(i, i ^ step) for i in range(lax.axis_size(axis))])


def other_side(x):
    props, domains = lax.axis_size("prop"), lax.axis_size("dom")
    pairs = []
    for p in range(props):
        for d in range(domains):
            end = d in (0, domains - 1)
            partner = ((p ^ 1) * domains + d) if end else (p * domains + ((d + 1) ^ 1) - 1)
            pairs.append((p * domains + d, partner))
    return lax.ppermute(x, ("prop", "dom"), pairs)


def source_side(x):
    props, domains = lax.axis_size("prop"), lax.axis_size("dom")
    pairs = []
    for p in range(props):
        for d in range(domains):
            if d in (0, domains - 1):
                target = (p ^ 1) * domains + (d if p % 2 == 0 else d ^ 1)
            elif p % 2 == 0:
                target = p * domains + (d ^ 1)
            else:
                target = p * domains + ((d + 1) ^ 1) - 1
            pairs.append((p * domains + d, target))
    return lax.ppermute(x, ("prop", "dom"), pairs)


def from_accepted(mine, accepted, beside):
    props = lax.axis_size("prop")
    apart = lax.axis_index("prop") ^ accepted
    own = SHRINK * mine
    step = props // 2
    came = swaps(mine, "prop", step)
    came, own, beside = lax.optimization_barrier((came, own, beside))
    current = jnp.where(apart & step, SHRINK * came, own)
    while step > 1:
        step //= 2
        came = jnp.concatenate([swaps(x, "prop", step) for x in jnp.split(current, 2)])
        current = jnp.where(apart & step, came, current)
    return current, beside


def gather_parts(mine):
    domains = lax.axis_size("dom")
    copies = jnp.broadcast_to(mine[None], (domains,) + mine.shape)
    return lax.all_to_all(copies, "dom", 0, 0)


def body(states, accepted, noise, source):
    domains = lax.axis_size("dom")
    height = source.shape[0]
    dom = jnp.stack([lax.axis_index("dom"), lax.axis_index("prop")]).astype(jnp.int32)
    near = source_side(source)
    current, noise_part = from_accepted(states[0], accepted[0], BETA * noise[0])
    perm = jnp.exp(current + noise_part)
    _, source, near = lax.optimization_barrier((perm, source, near))
    perms = (perm, other_side(perm), swaps(perm, "dom", 1))
    sources = (OMEGA * source, near, swaps(near, "prop", 1))
    *level, coarse = fine_part(dom, perms, sources, domains * height)
    return coarse_part(dom, gather_parts(coarse), *level, height)[None]


def solution(mesh):
    in_specs = (
        P("prop", "dom", None, None),
        P(),
        P("prop", "dom", None, None),
        P("dom", None, None),
    )
    out_specs = P("prop", "dom", None, None)
    return jax.shard_map(body, mesh=mesh, in_specs=in_specs, out_specs=out_specs, check_vma=False)
```

```python
import functools
import math

import jax
import jax.numpy as jnp
from jax import lax
from jax.experimental import pallas as pl
from jax.experimental.pallas import tpu as pltpu
from jax.sharding import PartitionSpec as P

COARSE_SWEEPS = 64
POWER = 3
OMEGA = 0.7
KEEP = 1.0 - OMEGA
BETA = 0.4
SHRINK = math.sqrt(1.0 - BETA * BETA)
ZSCALE = 16.0
LANES = 128
VMEM_LIMIT = 40 * 1024 * 1024
F32 = jnp.float32
WEST, EAST, SOUTH, NORTH, BELOW, ABOVE, CONST = range(7)


def iota(shape, dim):
    return lax.broadcasted_iota(jnp.int32, shape, dim)


def roll(x, amount, axis):
    axis = axis % x.ndim
    return pltpu.roll(x, amount % x.shape[axis], axis)


def inverse_of(x):
    guess = pl.reciprocal(x, approx=True)
    return guess * (2.0 - x * guess)


def harmonic(a, b):
    return (2.0 * a) * b * inverse_of(a + b)


def selector_dot(parts, selector):
    x = jnp.concatenate(parts, axis=0) if len(parts) > 1 else parts[0]
    rows = x.shape[0]
    high = x.astype(jnp.bfloat16).astype(F32)
    rest = x - high
    middle = rest.astype(jnp.bfloat16).astype(F32)
    terms = jnp.concatenate([high, middle, rest - middle], axis=0).astype(jnp.bfloat16)
    y = jnp.dot(terms, selector, preferred_element_type=F32)
    total = y[:rows] + y[rows : 2 * rows] + y[2 * rows :]
    height = parts[0].shape[0]
    return [total[i * height : (i + 1) * height] for i in range(len(parts))]


def side_faces(perm, ny):
    shape = perm.shape
    rows = iota(shape, 0)
    columns = iota(shape, 1) & (ny - 1)
    west = jnp.where(rows == 0, 0.0, harmonic(perm, roll(perm, 1, 0)))
    east = roll(west, -1, 0)
    south = jnp.where(columns == 0, 0.0, harmonic(perm, roll(perm, 1, 1)))
    north = roll(south, -1, 1)
    ends = jnp.where(rows == 0, perm, 0.0) + jnp.where(rows == shape[0] - 1, perm, 0.0)
    ends = ends + jnp.where(columns == 0, perm, 0.0) + jnp.where(columns == ny - 1, perm, 0.0)
    return west, east, south, north, ((west + east) + (south + north)) + ends


def face_terms(perm, below, above, ny):
    *sides, total = side_faces(perm, ny)
    return (*sides, below, above), total + (below + above)


def stencil(values, lower, upper, coefs, base):
    x = coefs[0] * roll(values, 1, 0) + coefs[1] * roll(values, -1, 0)
    y = coefs[2] * roll(values, 1, 1) + coefs[3] * roll(values, -1, 1)
    z = coefs[4] * lower + coefs[5] * upper
    return (x + y) + (z + base)


def lane_selector(groups, ny, step, spread=False):
    shape = (LANES, step * LANES) if spread else (step * LANES, LANES)
    source, target = iota(shape, int(spread)), iota(shape, 1 - int(spread))
    bits = ny.bit_length() - 1
    lane = source & (LANES - 1)
    group = (lane >> bits) * step + (source >> 7)
    wanted = (group << (bits - 1)) + ((lane & (ny - 1)) >> 1)
    return jnp.where((target == wanted) & (lane < groups * ny), 1.0, 0.0).astype(jnp.bfloat16)


def side_kernel(perm, out):
    for i in range(perm.shape[0]):
        for k, x in enumerate(side_faces(perm[i], LANES)):
            out[k, i] = x


def fine_kernel(
    layers,
    dom_ref, sides,
    per, per_other, per_pair,
    src, src_near, src_next,
    coef, const, values, coarse_out,
    perm, right, diag, pair_right, pair_perm,
):
    height = per.shape[0]
    dom = dom_ref[0]
    pair_at = jnp.where(lax.rem(dom, 2) == 0, 2 * height, 0)
    other_at = 2 * height - pair_at

    near_at = jnp.where(lax.rem(dom_ref[1], 2) == 0, pair_at, other_at)
    next_at = 2 * height - near_at
    for i in range(height):
        for at, p in ((height, per), (pair_at, per_pair), (other_at, per_other)):
            perm[at + i] = p[i]
        right[height + i] = src[i]
        right[near_at + i] = OMEGA * src_near[i]
        right[next_at + i] = OMEGA * src_next[i]

    def face(i):
        z = dom * height + i - 3
        scale = jnp.where((z > 0) & (z < layers), ZSCALE, 0.0)
        at = height - 3 + i
        return scale * harmonic(perm[at - 1], perm[at])

    above = face(0)
    for i in range(height + 6):
        at = height - 3 + i
        below, above = above, face(i + 1)
        if 3 <= i < height + 3:
            faces = tuple(sides[k, i - 3] for k in range(4)) + (below, above)
            diagonal = sides[4, i - 3] + (below + above)
        else:
            faces, diagonal = face_terms(perm[at], below, above, LANES)
        inverse = inverse_of(diagonal)
        const[i] = inverse * right[at]
        if 0 < i < height + 5:
            inverse = OMEGA * inverse
            for k in range(6):
                coef[k, i] = inverse * faces[k]
        if 3 <= i < height + 3:
            diag[i] = diagonal

    def first(i):
        start = const[i + 1]
        near = [coef[k, i + 1] for k in range(6)]
        values[i] = stencil(start, const[i], const[i + 2], near, (1.0 + KEEP) * start)

    for i in range(height + 4):
        first(i)

    def residue(i):
        centre = values[i + 2]
        base = const[i + 3] - OMEGA * centre
        near = [coef[k, i + 3] for k in range(6)]
        scaled = stencil(centre, values[i + 1], values[i + 3], near, base)
        return scaled * (diag[i + 3] * (1.0 / OMEGA))

    for m in range(height // 2):
        pair_right[m] = residue(2 * m) + residue(2 * m + 1)
        pair_perm[m] = (perm[height + 2 * m] + perm[height + 2 * m + 1]) * 0.125
    half = pair_right.shape[1] // 2
    rows = []
    for m in range(height // 2):
        both = [x[m, pl.ds(0, half, 2), :] + x[m, pl.ds(1, half, 2), :] for x in (pair_right, pair_perm)]
        rows.append(jnp.concatenate(both, axis=1))
    for m, x in enumerate(selector_dot(rows, lane_selector(1, LANES, 2))):
        coarse_out[m] = x


class Packed:
    def __init__(self, nz, nx, ny):
        self.nz, self.nx, self.ny = nz, nx, ny
        self.groups = min(LANES // ny, nz)
        self.planes = nz // self.groups

    def lower(self, planes, p):
        return planes[p - 1] if p else roll(planes[self.planes - 1], self.ny, 1)

    def upper(self, planes, p):
        return planes[p + 1] if p + 1 < self.planes else roll(planes[0], -self.ny, 1)

    def system(self, perm, level):
        lane = iota((self.nx, LANES), 1)
        used = lane < self.groups * self.ny
        if self.groups * self.ny < LANES:
            perm = [jnp.where(used, x, 1.0) for x in perm]
        coefs, factors, diagonals = [], [], []
        inner = [ZSCALE * harmonic(a, b) for a, b in zip(perm[:-1], perm[1:])]
        wrapped = ZSCALE * harmonic(perm[-1], roll(perm[0], -self.ny, 1))
        last = jnp.where(lane < (self.groups - 1) * self.ny, wrapped, 0.0)
        z_faces = [roll(last, self.ny, 1)] + inner + [last]
        for p in range(self.planes):
            faces, diagonal = face_terms(perm[p], z_faces[p], z_faces[p + 1], self.ny)
            inverse = OMEGA * inverse_of(diagonal)
            coefs.append([inverse * face for face in faces])
            factors.append(inverse * (4.0**-level))
            diagonals.append(diagonal * (4.0**level / OMEGA))
        return coefs, factors, diagonals

    def apply(self, values, coefs, bases):
        return [
            stencil(values[p], self.lower(values, p), self.upper(values, p), coefs[p], bases[p])
            for p in range(self.planes)
        ]

    def sweep(self, values, coefs, const):
        return self.apply(values, coefs, [KEEP * v + c for v, c in zip(values, const)])

    def coarser(self):
        return Packed(self.nz // 2, self.nx // 2, self.ny // 2)

    def restrict(self, fields, pads):
        coarse = self.coarser()
        step = coarse.groups // self.groups
        half = coarse.nx
        parts = []
        for values, pad in zip(fields, pads):
            rows = []
            for m in range(self.planes // 2):
                pad[m] = values[2 * m] + values[2 * m + 1]
                rows.append(pad[m, pl.ds(0, half, 2), :] + pad[m, pl.ds(1, half, 2), :])
            for p in range(coarse.planes):
                blocks = rows[p :: coarse.planes]
                parts.append(jnp.concatenate(blocks, axis=1) if step > 1 else blocks[0])
        sums = selector_dot(parts, lane_selector(self.groups, self.ny, step))
        return [sums[i : i + coarse.planes] for i in range(0, len(sums), coarse.planes)]

    def prolong(self, values, pad):
        coarse = self.coarser()
        step = coarse.groups // self.groups
        half = coarse.nx
        wide = selector_dot(values, lane_selector(self.groups, self.ny, step, spread=True))
        out = []
        for m in range(self.planes // 2):
            j, p = divmod(m, coarse.planes)
            plane = wide[p][:, j * LANES : (j + 1) * LANES]
            pad[m, pl.ds(0, half, 2), :] = plane
            pad[m, pl.ds(1, half, 2), :] = plane
            out += [pad[m], pad[m]]
        return out


class Flat:
    def __init__(self, finer):
        coarse = finer.coarser()
        self.finer = finer
        self.nz, self.nx, self.ny = coarse.nz, coarse.nx, coarse.ny
        self.pairs = finer.planes // 2
        self.rows = max(8, self.nz)
        self.shape = (self.rows, LANES)
        self.buffer_rows = 2 * (self.rows + 2 * POWER)

    def selector(self, spread=False):
        wide = self.finer.groups * LANES
        shape = (wide, LANES) if spread else (LANES, wide)
        fine, flat = iota(shape, int(spread)), iota(shape, 1 - int(spread))
        bits = self.finer.ny.bit_length() - 1
        same = (fine >> bits) == (flat >> 7)
        same &= ((fine & (self.finer.ny - 1)) >> 1) == (flat & (self.ny - 1))
        return jnp.where(same, 1.0, 0.0).astype(jnp.bfloat16)

    def diagonal(self):
        shape = (self.nx, LANES)
        return iota(shape, 0) == (iota(shape, 1) >> (self.ny.bit_length() - 1))

    def restrict(self, fields, pads, pack):
        parts = []
        for values, pad in zip(fields, pads):
            for m in range(self.pairs):
                pad[m] = values[2 * m] + values[2 * m + 1]
                parts.append(pad[m, pl.ds(0, self.nx, 2), :] + pad[m, pl.ds(1, self.nx, 2), :])
        sums = selector_dot(parts, self.selector())
        mask = self.diagonal()
        pack[...] = jnp.zeros_like(pack)
        for i in range(len(fields)):
            for z in range(self.nz):
                s, m = divmod(z, self.pairs)
                block = sums[i * self.pairs + m][:, s * LANES : (s + 1) * LANES]
                row = jnp.sum(jnp.where(mask, block, 0.0), axis=0, keepdims=True)
                pack[i, z : z + 1, :] = row
        return [pack[i] for i in range(len(fields))]

    def prolong(self, values, pad, pack):
        mask = self.diagonal()
        pack[0] = values
        parts = []
        for m in range(self.pairs):
            layers = [s * self.pairs + m for s in range(self.finer.groups)]
            spread = [jnp.broadcast_to(pack[0, z : z + 1, :], mask.shape) for z in layers]
            parts.append(jnp.concatenate([jnp.where(mask, x, 0.0) for x in spread], axis=1))
        out = []
        for m, wide in enumerate(selector_dot(parts, self.selector(spread=True))):
            pad[m, pl.ds(0, self.nx, 2), :] = wide
            pad[m, pl.ds(1, self.nx, 2), :] = wide
            out += [pad[m], pad[m]]
        return out

    def system(self, perm, level):
        lane, row = iota(self.shape, 1), iota(self.shape, 0)
        x, y = lane >> (self.ny.bit_length() - 1), lane & (self.ny - 1)
        real = row < self.nz
        perm = jnp.where(real, perm, 1.0)
        west = jnp.where(x == 0, 0.0, harmonic(perm, roll(perm, self.ny, 1)))
        east = roll(west, -self.ny, 1)
        south = jnp.where(y == 0, 0.0, harmonic(perm, roll(perm, 1, 1)))
        north = roll(south, -1, 1)
        below = ZSCALE * harmonic(perm, roll(perm, 1, 0))
        below = jnp.where((row > 0) & real, below, 0.0)
        above = roll(below, -1, 0)
        faces = [west, east, south, north, below, above]
        ends = (x == 0, x == self.nx - 1, y == 0, y == self.ny - 1)
        diagonal = tree_sum(faces + [jnp.where(end, perm, 0.0) for end in ends])
        inverse = jnp.where(real, OMEGA * inverse_of(diagonal), 0.0)
        keys = ((-1, 0, 0), (1, 0, 0), (0, -1, 0), (0, 1, 0), (0, 0, -1), (0, 0, 1))
        terms = {key: inverse * face for key, face in zip(keys, faces)}
        terms[0, 0, 0] = jnp.full(self.shape, KEEP, F32)
        return terms, inverse * (4.0**-level)

    def product(self, first, second):
        sums = {}
        for (dx, dy, dz), coef in first.items():
            for other, moved in second.items():
                if dz:
                    moved = roll(moved, -dz, 0)
                if dx or dy:
                    moved = roll(moved, -(dx * self.ny + dy), 1)
                total = tuple(a + b for a, b in zip((dx, dy, dz), other))
                sums.setdefault(total, []).append(coef * moved)
        return {key: tree_sum(parts) for key, parts in sums.items()}

    def apply(self, terms, values, base, buffer):
        buffer[pl.ds(2 * POWER, self.rows, 2), :] = values
        moved = {}
        for dx, dy, dz in sorted(terms, key=lambda key: abs(key[2])):
            if (0, 0, dz) not in moved:
                moved[0, 0, dz] = buffer[pl.ds(2 * (POWER + dz), self.rows, 2), :] if dz else values
            if dx or dy:
                moved[dx, dy, dz] = roll(moved[0, 0, dz], -(dx * self.ny + dy), 1)
        return tree_sum([base] + [coef * moved[key] for key, coef in terms.items()])

    def prepare(self, perm, level):
        terms, factor = self.system(perm, level)
        power = terms
        for _ in range(POWER - 1):
            power = self.product(terms, power)
        return terms, power, factor

    def solve(self, right, prepared, buffer):
        terms, power, factor = prepared
        const = factor * right
        buffer[...] = jnp.zeros_like(buffer)
        base = const
        for _ in range(POWER - 1):
            base = self.apply(terms, base, const, buffer)
        whole = COARSE_SWEEPS % POWER == 0
        values = base if whole else const
        steps = (COARSE_SWEEPS - 1) // POWER
        assert steps * POWER + (POWER if whole else 1) == COARSE_SWEEPS
        for _ in range(steps):
            values = self.apply(power, values, base, buffer)
        return values


def tree_sum(parts):
    while len(parts) > 1:
        odd = parts[len(parts) // 2 * 2 :]
        parts = [a + b for a, b in zip(parts[::2], parts[1::2])] + odd
    return parts[0]


def packed_cycle(grid, right, perm, level, pads, packs, buffer):
    pad_right, pad_perm = pads[0]
    coefs, factors, diagonals = grid.system(perm, level)
    if len(pads) > 1:
        (coarse_perm,) = grid.restrict([perm], [pad_perm])
    else:
        flat = Flat(grid)
        (coarse_perm,) = flat.restrict([perm], [pad_perm], packs[1])
        prepared = flat.prepare(coarse_perm * 0.125, level + 1)
    const = [f * r for f, r in zip(factors, right)]
    values = grid.sweep(const, coefs, const)
    scaled = grid.apply(values, coefs, [c - OMEGA * v for c, v in zip(const, values)])
    residue = [r * d for r, d in zip(scaled, diagonals)]
    if len(pads) > 1:
        (coarse_right,) = grid.restrict([residue], [pad_right])
        coarse_perm = [x * 0.125 for x in coarse_perm]
        update = packed_cycle(
            grid.coarser(), coarse_right, coarse_perm, level + 1, pads[1:], packs, buffer
        )
        update = grid.prolong(update, pad_right)
    else:
        (coarse_right,) = flat.restrict([residue], [pad_right], packs[0])
        update = flat.prolong(flat.solve(coarse_right, prepared, buffer), pad_right, packs[0])
    values = [v + e for v, e in zip(values, update)]
    for _ in range(2):
        values = grid.sweep(values, coefs, const)
    return values


def coarse_kernel(
    count, dom_ref, *refs,
):
    parts, refs = refs[:count][::-1], refs[count:]
    coef, const, before, out, gathered, *refs = refs
    coarse_steps(parts, dom_ref, gathered, coef, const, before, out, *refs)


def coarse_steps(
    parts, dom_ref, gathered, coef, const, before, out,
    level, first, pad_right1, pad_perm1, pad_right2, pad_perm2, update, pack, pack_perm, buffer,
    done, sems,
):
    height = out.shape[0]
    dom = dom_ref[0]
    domains, own, nx, _ = gathered.shape
    for step, part in enumerate(parts):
        gathered[dom ^ step] = part[...]
    ny = LANES // 2
    grid = Packed(domains * own, nx, ny)
    left = iota((nx, LANES), 1) < ny
    right, perm = [], []
    for p in range(grid.planes):
        a = gathered[p // own, p % own]
        q = grid.planes + p
        b = gathered[q // own, q % own]
        right.append(jnp.where(left, a, roll(b, ny, 1)))
        perm.append(jnp.where(left, roll(a, ny, 1), b))
    pads = [(pad_right1, pad_perm1), (pad_right2, pad_perm2)]
    solved = packed_cycle(grid, right, perm, 1, pads, (pack, pack_perm), buffer)
    for p in range(grid.planes):
        update[p] = solved[p]
    planes, group = [], []
    for j in range(own + 2):
        layer = jnp.clip(dom * own + j - 1, 0, grid.nz - 1)
        group.append(layer // grid.planes)
        planes.append(update[lax.rem(layer, grid.planes)])
    for j, wide in enumerate(selector_dot(planes, lane_selector(1, LANES, 2, spread=True))):
        plane = jnp.where(group[j] == 0, wide[:, :LANES], wide[:, LANES:])
        pad = first.at[0]
        pad[pl.ds(0, nx, 2), :] = plane
        pad[pl.ds(1, nx, 2), :] = plane
        whole = first[0]
        level[2 * j] = before[2 * j] + whole
        level[2 * j + 1] = before[2 * j + 1] + whole

    def sweep(source, at, i):
        centre = source[i + 1]
        near = [coef[k, at + i] for k in range(6)]
        return stencil(centre, source[i], source[i + 2], near, KEEP * centre + const[at + i])

    def one(i):
        first[i] = sweep(level, 2, i)

    for i in range(height + 2):
        one(i)

    copies = []
    for i in range(height):
        done[i] = sweep(first, 3, i)
        copies.append(pltpu.make_async_copy(done.at[i], out.at[i], sems.at[i]))
        copies[-1].start()
    for copy in copies:
        copy.wait()


def fine_part(dom, perm, source, layers):
    height, nx, ny = perm[0].shape
    field = lambda *lead: pltpu.VMEM(lead + (nx, ny), F32)
    vmem = pl.BlockSpec(memory_space=pltpu.VMEM)
    sides = pl.pallas_call(
        side_kernel,
        out_shape=jax.ShapeDtypeStruct((5, height, nx, ny), F32),
        in_specs=[vmem],
        out_specs=vmem,
        compiler_params=pltpu.CompilerParams(vmem_limit_bytes=VMEM_LIMIT),
        name="sides",
    )(perm[0])
    smem = pl.BlockSpec(memory_space=pltpu.SMEM)
    return pl.pallas_call(
        functools.partial(fine_kernel, layers),
        out_shape=(
            jax.ShapeDtypeStruct((6, height + 6, nx, ny), F32),
            jax.ShapeDtypeStruct((height + 6, nx, ny), F32),
            jax.ShapeDtypeStruct((height + 4, nx, ny), F32),
            jax.ShapeDtypeStruct((height // 2, nx // 2, ny), F32),
        ),
        in_specs=[smem] + [vmem] * 7,
        out_specs=(vmem,) * 4,
        scratch_shapes=[
            field(3 * height),
            field(3 * height),
            field(height + 6),
            field(height // 2),
            field(height // 2),
        ],
        compiler_params=pltpu.CompilerParams(vmem_limit_bytes=VMEM_LIMIT),
        name="fine",
    )(dom, sides, *perm, *source)


def coarse_part(dom, parts, coefs, const, values, height):
    _, nx, ny = values.shape
    field = lambda *shape: pltpu.VMEM(shape, F32)
    whole = (len(parts),) + parts[0].shape
    grid1 = Packed(whole[0] * whole[1], nx // 2, ny // 2)
    grid2 = grid1.coarser()
    pads1 = field(grid1.planes // 2, grid1.nx, LANES)
    pads2 = field(grid2.planes // 2, grid2.nx, LANES)
    vmem = pl.BlockSpec(memory_space=pltpu.VMEM)
    smem = pl.BlockSpec(memory_space=pltpu.SMEM)
    return pl.pallas_call(
        functools.partial(coarse_kernel, whole[0]),
        out_shape=jax.ShapeDtypeStruct((height, nx, ny), F32),
        in_specs=[smem] + [vmem] * (whole[0] + 3),
        out_specs=pl.BlockSpec(memory_space=pl.ANY),
        scratch_shapes=[
            field(*whole),
            field(*values.shape),
            field(height + 2, nx, ny),
            pads1, pads1, pads2, pads2,
            field(grid1.planes, grid1.nx, LANES),
            field(1, Flat(grid2).rows, LANES),
            field(1, Flat(grid2).rows, LANES),
            field(Flat(grid2).buffer_rows, LANES),
            field(height, nx, ny),
            pltpu.SemaphoreType.DMA((height,)),
        ],
        compiler_params=pltpu.CompilerParams(vmem_limit_bytes=VMEM_LIMIT),
        name="coarse",
    )(dom, *parts[::-1], coefs, const, values)


def swaps(x, axis, step):
    return lax.ppermute(x, axis, [(i, i ^ step) for i in range(lax.axis_size(axis))])


def other_side(x):
    props, domains = lax.axis_size("prop"), lax.axis_size("dom")
    pairs = []
    for p in range(props):
        for d in range(domains):
            end = d in (0, domains - 1)
            partner = ((p ^ 1) * domains + d) if end else (p * domains + ((d + 1) ^ 1) - 1)
            pairs.append((p * domains + d, partner))
    return lax.ppermute(x, ("prop", "dom"), pairs)


def source_side(x):
    props, domains = lax.axis_size("prop"), lax.axis_size("dom")
    pairs = []
    for p in range(props):
        for d in range(domains):
            if d in (0, domains - 1):
                target = (p ^ 1) * domains + (d if p % 2 == 0 else d ^ 1)
            elif p % 2 == 0:
                target = p * domains + (d ^ 1)
            else:
                target = p * domains + ((d + 1) ^ 1) - 1
            pairs.append((p * domains + d, target))
    return lax.ppermute(x, ("prop", "dom"), pairs)


def from_accepted(mine, accepted, beside):
    props = lax.axis_size("prop")
    apart = lax.axis_index("prop") ^ accepted
    own = SHRINK * mine
    step = props // 2
    came = swaps(mine, "prop", step)
    came, own, beside = lax.optimization_barrier((came, own, beside))
    current = jnp.where(apart & step, SHRINK * came, own)
    while step > 1:
        step //= 2
        came = jnp.concatenate([swaps(x, "prop", step) for x in jnp.split(current, 2)])
        current = jnp.where(apart & step, came, current)
    return current, beside


def gather_parts(mine):
    domains = lax.axis_size("dom")
    parts = {0: mine}
    for step in range(0, domains, 2):
        if step:
            parts[step] = swaps(mine, "dom", step)
        parts[step + 1] = swaps(parts[step], "dom", 1)
    return [parts[k] for k in range(domains)]


def body(states, accepted, noise, source):
    domains = lax.axis_size("dom")
    height = source.shape[0]
    dom = jnp.stack([lax.axis_index("dom"), lax.axis_index("prop")]).astype(jnp.int32)
    near = source_side(source)
    current, noise_part = from_accepted(states[0], accepted[0], BETA * noise[0])
    perm = jnp.exp(current + noise_part)
    _, source, near = lax.optimization_barrier((perm, source, near))
    perms = (perm, other_side(perm), swaps(perm, "dom", 1))
    sources = (OMEGA * source, near, swaps(near, "prop", 1))
    *level, coarse = fine_part(dom, perms, sources, domains * height)
    return coarse_part(dom, gather_parts(coarse), *level, height)[None]


def solution(mesh):
    in_specs = (
        P("prop", "dom", None, None),
        P(),
        P("prop", "dom", None, None),
        P("dom", None, None),
    )
    out_specs = P("prop", "dom", None, None)
    return jax.shard_map(body, mesh=mesh, in_specs=in_specs, out_specs=out_specs, check_vma=False)
```

```python
import functools
import math

import jax
import jax.numpy as jnp
from jax import lax
from jax.experimental import pallas as pl
from jax.experimental.pallas import tpu as pltpu
from jax.sharding import PartitionSpec as P

COARSE_SWEEPS = 64
POWER = 3
OMEGA = 0.7
KEEP = 1.0 - OMEGA
BETA = 0.4
SHRINK = math.sqrt(1.0 - BETA * BETA)
ZSCALE = 16.0
LANES = 128
VMEM_LIMIT = 40 * 1024 * 1024
F32 = jnp.float32
WEST, EAST, SOUTH, NORTH, BELOW, ABOVE, CONST = range(7)


def iota(shape, dim):
    return lax.broadcasted_iota(jnp.int32, shape, dim)


def roll(x, amount, axis):
    axis = axis % x.ndim
    return pltpu.roll(x, amount % x.shape[axis], axis)


def inverse_of(x):
    guess = pl.reciprocal(x, approx=True)
    return guess * (2.0 - x * guess)


def harmonic(a, b):
    return (2.0 * a) * b * inverse_of(a + b)


def selector_dot(parts, selector):
    x = jnp.concatenate(parts, axis=0) if len(parts) > 1 else parts[0]
    rows = x.shape[0]
    high = x.astype(jnp.bfloat16).astype(F32)
    rest = x - high
    middle = rest.astype(jnp.bfloat16).astype(F32)
    terms = jnp.concatenate([high, middle, rest - middle], axis=0).astype(jnp.bfloat16)
    y = jnp.dot(terms, selector, preferred_element_type=F32)
    total = y[:rows] + y[rows : 2 * rows] + y[2 * rows :]
    height = parts[0].shape[0]
    return [total[i * height : (i + 1) * height] for i in range(len(parts))]


def side_faces(perm, ny):
    shape = perm.shape
    rows = iota(shape, 0)
    columns = iota(shape, 1) & (ny - 1)
    west = jnp.where(rows == 0, 0.0, harmonic(perm, roll(perm, 1, 0)))
    east = roll(west, -1, 0)
    south = jnp.where(columns == 0, 0.0, harmonic(perm, roll(perm, 1, 1)))
    north = roll(south, -1, 1)
    ends = jnp.where(rows == 0, perm, 0.0) + jnp.where(rows == shape[0] - 1, perm, 0.0)
    ends = ends + jnp.where(columns == 0, perm, 0.0) + jnp.where(columns == ny - 1, perm, 0.0)
    return west, east, south, north, ((west + east) + (south + north)) + ends


def face_terms(perm, below, above, ny):
    *sides, total = side_faces(perm, ny)
    return (*sides, below, above), total + (below + above)


def stencil(values, lower, upper, coefs, base):
    x = coefs[0] * roll(values, 1, 0) + coefs[1] * roll(values, -1, 0)
    y = coefs[2] * roll(values, 1, 1) + coefs[3] * roll(values, -1, 1)
    z = coefs[4] * lower + coefs[5] * upper
    return (x + y) + (z + base)


def lane_selector(groups, ny, step, spread=False):
    shape = (LANES, step * LANES) if spread else (step * LANES, LANES)
    source, target = iota(shape, int(spread)), iota(shape, 1 - int(spread))
    bits = ny.bit_length() - 1
    lane = source & (LANES - 1)
    group = (lane >> bits) * step + (source >> 7)
    wanted = (group << (bits - 1)) + ((lane & (ny - 1)) >> 1)
    return jnp.where((target == wanted) & (lane < groups * ny), 1.0, 0.0).astype(jnp.bfloat16)


def side_kernel(perm, out):
    for i in range(perm.shape[0]):
        for k, x in enumerate(side_faces(perm[i], LANES)):
            out[k, i] = x


def fine_kernel(
    layers,
    dom_ref, sides,
    per, per_other, per_pair,
    src, src_near, src_next,
    coef, const, values, coarse_out,
    perm, right, diag, pair_right, pair_perm,
):
    height = per.shape[0]
    dom = dom_ref[0]
    pair_at = jnp.where(lax.rem(dom, 2) == 0, 2 * height, 0)
    other_at = 2 * height - pair_at

    near_at = jnp.where(lax.rem(dom_ref[1], 2) == 0, pair_at, other_at)
    next_at = 2 * height - near_at
    for i in range(height):
        for at, p in ((height, per), (pair_at, per_pair), (other_at, per_other)):
            perm[at + i] = p[i]
        right[height + i] = src[i]
        right[near_at + i] = OMEGA * src_near[i]
        right[next_at + i] = OMEGA * src_next[i]

    def face(i):
        z = dom * height + i - 3
        scale = jnp.where((z > 0) & (z < layers), ZSCALE, 0.0)
        at = height - 3 + i
        return scale * harmonic(perm[at - 1], perm[at])

    above = face(0)
    for i in range(height + 6):
        at = height - 3 + i
        below, above = above, face(i + 1)
        if 3 <= i < height + 3:
            faces = tuple(sides[k, i - 3] for k in range(4)) + (below, above)
            diagonal = sides[4, i - 3] + (below + above)
        else:
            faces, diagonal = face_terms(perm[at], below, above, LANES)
        inverse = inverse_of(diagonal)
        const[i] = inverse * right[at]
        if 0 < i < height + 5:
            inverse = OMEGA * inverse
            for k in range(6):
                coef[k, i] = inverse * faces[k]
        if 3 <= i < height + 3:
            diag[i] = diagonal

    def first(i):
        start = const[i + 1]
        near = [coef[k, i + 1] for k in range(6)]
        values[i] = stencil(start, const[i], const[i + 2], near, (1.0 + KEEP) * start)

    for i in range(height + 4):
        first(i)

    def residue(i):
        centre = values[i + 2]
        base = const[i + 3] - OMEGA * centre
        near = [coef[k, i + 3] for k in range(6)]
        scaled = stencil(centre, values[i + 1], values[i + 3], near, base)
        return scaled * (diag[i + 3] * (1.0 / OMEGA))

    for m in range(height // 2):
        pair_right[m] = residue(2 * m) + residue(2 * m + 1)
        pair_perm[m] = (perm[height + 2 * m] + perm[height + 2 * m + 1]) * 0.125
    half = pair_right.shape[1] // 2
    rows = []
    for m in range(height // 2):
        both = [x[m, pl.ds(0, half, 2), :] + x[m, pl.ds(1, half, 2), :] for x in (pair_right, pair_perm)]
        rows.append(jnp.concatenate(both, axis=1))
    for m, x in enumerate(selector_dot(rows, lane_selector(1, LANES, 2))):
        coarse_out[m] = x


class Packed:
    def __init__(self, nz, nx, ny):
        self.nz, self.nx, self.ny = nz, nx, ny
        self.groups = min(LANES // ny, nz)
        self.planes = nz // self.groups

    def lower(self, planes, p):
        return planes[p - 1] if p else roll(planes[self.planes - 1], self.ny, 1)

    def upper(self, planes, p):
        return planes[p + 1] if p + 1 < self.planes else roll(planes[0], -self.ny, 1)

    def system(self, perm, level):
        lane = iota((self.nx, LANES), 1)
        used = lane < self.groups * self.ny
        if self.groups * self.ny < LANES:
            perm = [jnp.where(used, x, 1.0) for x in perm]
        coefs, factors, diagonals = [], [], []
        inner = [ZSCALE * harmonic(a, b) for a, b in zip(perm[:-1], perm[1:])]
        wrapped = ZSCALE * harmonic(perm[-1], roll(perm[0], -self.ny, 1))
        last = jnp.where(lane < (self.groups - 1) * self.ny, wrapped, 0.0)
        z_faces = [roll(last, self.ny, 1)] + inner + [last]
        for p in range(self.planes):
            faces, diagonal = face_terms(perm[p], z_faces[p], z_faces[p + 1], self.ny)
            inverse = OMEGA * inverse_of(diagonal)
            coefs.append([inverse * face for face in faces])
            factors.append(inverse * (4.0**-level))
            diagonals.append(diagonal * (4.0**level / OMEGA))
        return coefs, factors, diagonals

    def apply(self, values, coefs, bases):
        return [
            stencil(values[p], self.lower(values, p), self.upper(values, p), coefs[p], bases[p])
            for p in range(self.planes)
        ]

    def sweep(self, values, coefs, const):
        return self.apply(values, coefs, [KEEP * v + c for v, c in zip(values, const)])

    def coarser(self):
        return Packed(self.nz // 2, self.nx // 2, self.ny // 2)

    def restrict(self, fields, pads):
        coarse = self.coarser()
        step = coarse.groups // self.groups
        half = coarse.nx
        parts = []
        for values, pad in zip(fields, pads):
            rows = []
            for m in range(self.planes // 2):
                pad[m] = values[2 * m] + values[2 * m + 1]
                rows.append(pad[m, pl.ds(0, half, 2), :] + pad[m, pl.ds(1, half, 2), :])
            for p in range(coarse.planes):
                blocks = rows[p :: coarse.planes]
                parts.append(jnp.concatenate(blocks, axis=1) if step > 1 else blocks[0])
        sums = selector_dot(parts, lane_selector(self.groups, self.ny, step))
        return [sums[i : i + coarse.planes] for i in range(0, len(sums), coarse.planes)]

    def prolong(self, values, pad):
        coarse = self.coarser()
        step = coarse.groups // self.groups
        half = coarse.nx
        wide = selector_dot(values, lane_selector(self.groups, self.ny, step, spread=True))
        out = []
        for m in range(self.planes // 2):
            j, p = divmod(m, coarse.planes)
            plane = wide[p][:, j * LANES : (j + 1) * LANES]
            pad[m, pl.ds(0, half, 2), :] = plane
            pad[m, pl.ds(1, half, 2), :] = plane
            out += [pad[m], pad[m]]
        return out


class Flat:
    def __init__(self, finer):
        coarse = finer.coarser()
        self.finer = finer
        self.nz, self.nx, self.ny = coarse.nz, coarse.nx, coarse.ny
        self.pairs = finer.planes // 2
        self.rows = max(8, self.nz)
        self.shape = (self.rows, LANES)
        self.buffer_rows = 2 * (self.rows + 2 * POWER)

    def selector(self, spread=False):
        wide = self.finer.groups * LANES
        shape = (wide, LANES) if spread else (LANES, wide)
        fine, flat = iota(shape, int(spread)), iota(shape, 1 - int(spread))
        bits = self.finer.ny.bit_length() - 1
        same = (fine >> bits) == (flat >> 7)
        same &= ((fine & (self.finer.ny - 1)) >> 1) == (flat & (self.ny - 1))
        return jnp.where(same, 1.0, 0.0).astype(jnp.bfloat16)

    def diagonal(self):
        shape = (self.nx, LANES)
        return iota(shape, 0) == (iota(shape, 1) >> (self.ny.bit_length() - 1))

    def restrict(self, fields, pads, pack):
        parts = []
        for values, pad in zip(fields, pads):
            for m in range(self.pairs):
                pad[m] = values[2 * m] + values[2 * m + 1]
                parts.append(pad[m, pl.ds(0, self.nx, 2), :] + pad[m, pl.ds(1, self.nx, 2), :])
        sums = selector_dot(parts, self.selector())
        mask = self.diagonal()
        pack[...] = jnp.zeros_like(pack)
        for i in range(len(fields)):
            for z in range(self.nz):
                s, m = divmod(z, self.pairs)
                block = sums[i * self.pairs + m][:, s * LANES : (s + 1) * LANES]
                row = jnp.sum(jnp.where(mask, block, 0.0), axis=0, keepdims=True)
                pack[i, z : z + 1, :] = row
        return [pack[i] for i in range(len(fields))]

    def prolong(self, values, pad, pack):
        mask = self.diagonal()
        pack[0] = values
        parts = []
        for m in range(self.pairs):
            layers = [s * self.pairs + m for s in range(self.finer.groups)]
            spread = [jnp.broadcast_to(pack[0, z : z + 1, :], mask.shape) for z in layers]
            parts.append(jnp.concatenate([jnp.where(mask, x, 0.0) for x in spread], axis=1))
        out = []
        for m, wide in enumerate(selector_dot(parts, self.selector(spread=True))):
            pad[m, pl.ds(0, self.nx, 2), :] = wide
            pad[m, pl.ds(1, self.nx, 2), :] = wide
            out += [pad[m], pad[m]]
        return out

    def system(self, perm, level):
        lane, row = iota(self.shape, 1), iota(self.shape, 0)
        x, y = lane >> (self.ny.bit_length() - 1), lane & (self.ny - 1)
        real = row < self.nz
        perm = jnp.where(real, perm, 1.0)
        west = jnp.where(x == 0, 0.0, harmonic(perm, roll(perm, self.ny, 1)))
        east = roll(west, -self.ny, 1)
        south = jnp.where(y == 0, 0.0, harmonic(perm, roll(perm, 1, 1)))
        north = roll(south, -1, 1)
        below = ZSCALE * harmonic(perm, roll(perm, 1, 0))
        below = jnp.where((row > 0) & real, below, 0.0)
        above = roll(below, -1, 0)
        faces = [west, east, south, north, below, above]
        ends = (x == 0, x == self.nx - 1, y == 0, y == self.ny - 1)
        diagonal = tree_sum(faces + [jnp.where(end, perm, 0.0) for end in ends])
        inverse = jnp.where(real, OMEGA * inverse_of(diagonal), 0.0)
        keys = ((-1, 0, 0), (1, 0, 0), (0, -1, 0), (0, 1, 0), (0, 0, -1), (0, 0, 1))
        terms = {key: inverse * face for key, face in zip(keys, faces)}
        terms[0, 0, 0] = jnp.full(self.shape, KEEP, F32)
        return terms, inverse * (4.0**-level)

    def product(self, first, second):
        sums = {}
        for (dx, dy, dz), coef in first.items():
            for other, moved in second.items():
                if dz:
                    moved = roll(moved, -dz, 0)
                if dx or dy:
                    moved = roll(moved, -(dx * self.ny + dy), 1)
                total = tuple(a + b for a, b in zip((dx, dy, dz), other))
                sums.setdefault(total, []).append(coef * moved)
        return {key: tree_sum(parts) for key, parts in sums.items()}

    def apply(self, terms, values, base, buffer):
        buffer[pl.ds(2 * POWER, self.rows, 2), :] = values
        moved = {}
        for dx, dy, dz in sorted(terms, key=lambda key: abs(key[2])):
            if (0, 0, dz) not in moved:
                moved[0, 0, dz] = buffer[pl.ds(2 * (POWER + dz), self.rows, 2), :] if dz else values
            if dx or dy:
                moved[dx, dy, dz] = roll(moved[0, 0, dz], -(dx * self.ny + dy), 1)
        return tree_sum([base] + [coef * moved[key] for key, coef in terms.items()])

    def prepare(self, perm, level):
        terms, factor = self.system(perm, level)
        power = terms
        for _ in range(POWER - 1):
            power = self.product(terms, power)
        return terms, power, factor

    def solve(self, right, prepared, buffer):
        terms, power, factor = prepared
        const = factor * right
        buffer[...] = jnp.zeros_like(buffer)
        base = const
        for _ in range(POWER - 1):
            base = self.apply(terms, base, const, buffer)
        whole = COARSE_SWEEPS % POWER == 0
        values = base if whole else const
        steps = (COARSE_SWEEPS - 1) // POWER
        assert steps * POWER + (POWER if whole else 1) == COARSE_SWEEPS
        for _ in range(steps):
            values = self.apply(power, values, base, buffer)
        return values


def tree_sum(parts):
    while len(parts) > 1:
        odd = parts[len(parts) // 2 * 2 :]
        parts = [a + b for a, b in zip(parts[::2], parts[1::2])] + odd
    return parts[0]


def packed_cycle(grid, right, perm, level, pads, packs, buffer):
    pad_right, pad_perm = pads[0]
    coefs, factors, diagonals = grid.system(perm, level)
    if len(pads) > 1:
        (coarse_perm,) = grid.restrict([perm], [pad_perm])
    else:
        flat = Flat(grid)
        (coarse_perm,) = flat.restrict([perm], [pad_perm], packs[1])
        prepared = flat.prepare(coarse_perm * 0.125, level + 1)
    const = [f * r for f, r in zip(factors, right)]
    values = grid.sweep(const, coefs, const)
    scaled = grid.apply(values, coefs, [c - OMEGA * v for c, v in zip(const, values)])
    residue = [r * d for r, d in zip(scaled, diagonals)]
    if len(pads) > 1:
        (coarse_right,) = grid.restrict([residue], [pad_right])
        coarse_perm = [x * 0.125 for x in coarse_perm]
        update = packed_cycle(
            grid.coarser(), coarse_right, coarse_perm, level + 1, pads[1:], packs, buffer
        )
        update = grid.prolong(update, pad_right)
    else:
        (coarse_right,) = flat.restrict([residue], [pad_right], packs[0])
        update = flat.prolong(flat.solve(coarse_right, prepared, buffer), pad_right, packs[0])
    values = [v + e for v, e in zip(values, update)]
    for _ in range(2):
        values = grid.sweep(values, coefs, const)
    return values


def swap_order(domains):
    steps = [0, 2] + list(range(domains - 2, 2, -2))
    return [step + 1 - odd for step in steps[::-1] for odd in range(2)]


def coarse_kernel(
    count, dom_ref, *refs,
):
    parts = [refs[swap_order(count).index(k)] for k in range(count)]
    refs = refs[count:]
    coef, const, before, out, gathered, *refs = refs
    coarse_steps(parts, dom_ref, gathered, coef, const, before, out, *refs)


def coarse_steps(
    parts, dom_ref, gathered, coef, const, before, out,
    level, first, pad_right1, pad_perm1, pad_right2, pad_perm2, update, pack, pack_perm, buffer,
    done, sems,
):
    height = out.shape[0]
    dom = dom_ref[0]
    domains, own, nx, _ = gathered.shape
    for step, part in enumerate(parts):
        gathered[dom ^ step] = part[...]
    ny = LANES // 2
    grid = Packed(domains * own, nx, ny)
    left = iota((nx, LANES), 1) < ny
    right, perm = [], []
    for p in range(grid.planes):
        a = gathered[p // own, p % own]
        q = grid.planes + p
        b = gathered[q // own, q % own]
        right.append(jnp.where(left, a, roll(b, ny, 1)))
        perm.append(jnp.where(left, roll(a, ny, 1), b))
    pads = [(pad_right1, pad_perm1), (pad_right2, pad_perm2)]
    solved = packed_cycle(grid, right, perm, 1, pads, (pack, pack_perm), buffer)
    for p in range(grid.planes):
        update[p] = solved[p]
    planes, group = [], []
    for j in range(own + 2):
        layer = jnp.clip(dom * own + j - 1, 0, grid.nz - 1)
        group.append(layer // grid.planes)
        planes.append(update[lax.rem(layer, grid.planes)])
    for j, wide in enumerate(selector_dot(planes, lane_selector(1, LANES, 2, spread=True))):
        plane = jnp.where(group[j] == 0, wide[:, :LANES], wide[:, LANES:])
        pad = first.at[0]
        pad[pl.ds(0, nx, 2), :] = plane
        pad[pl.ds(1, nx, 2), :] = plane
        whole = first[0]
        level[2 * j] = before[2 * j] + whole
        level[2 * j + 1] = before[2 * j + 1] + whole

    def sweep(source, at, i):
        centre = source[i + 1]
        near = [coef[k, at + i] for k in range(6)]
        return stencil(centre, source[i], source[i + 2], near, KEEP * centre + const[at + i])

    def one(i):
        first[i] = sweep(level, 2, i)

    for i in range(height + 2):
        one(i)

    copies = []
    for i in range(height):
        done[i] = sweep(first, 3, i)
        copies.append(pltpu.make_async_copy(done.at[i], out.at[i], sems.at[i]))
        copies[-1].start()
    for copy in copies:
        copy.wait()


def fine_part(dom, perm, source, layers):
    height, nx, ny = perm[0].shape
    field = lambda *lead: pltpu.VMEM(lead + (nx, ny), F32)
    vmem = pl.BlockSpec(memory_space=pltpu.VMEM)
    sides = pl.pallas_call(
        side_kernel,
        out_shape=jax.ShapeDtypeStruct((5, height, nx, ny), F32),
        in_specs=[vmem],
        out_specs=vmem,
        compiler_params=pltpu.CompilerParams(vmem_limit_bytes=VMEM_LIMIT),
        name="sides",
    )(perm[0])
    smem = pl.BlockSpec(memory_space=pltpu.SMEM)
    return pl.pallas_call(
        functools.partial(fine_kernel, layers),
        out_shape=(
            jax.ShapeDtypeStruct((6, height + 6, nx, ny), F32),
            jax.ShapeDtypeStruct((height + 6, nx, ny), F32),
            jax.ShapeDtypeStruct((height + 4, nx, ny), F32),
            jax.ShapeDtypeStruct((height // 2, nx // 2, ny), F32),
        ),
        in_specs=[smem] + [vmem] * 7,
        out_specs=(vmem,) * 4,
        scratch_shapes=[
            field(3 * height),
            field(3 * height),
            field(height + 6),
            field(height // 2),
            field(height // 2),
        ],
        compiler_params=pltpu.CompilerParams(vmem_limit_bytes=VMEM_LIMIT),
        name="fine",
    )(dom, sides, *perm, *source)


def coarse_part(dom, parts, coefs, const, values, height):
    _, nx, ny = values.shape
    field = lambda *shape: pltpu.VMEM(shape, F32)
    whole = (len(parts),) + parts[0].shape
    grid1 = Packed(whole[0] * whole[1], nx // 2, ny // 2)
    grid2 = grid1.coarser()
    pads1 = field(grid1.planes // 2, grid1.nx, LANES)
    pads2 = field(grid2.planes // 2, grid2.nx, LANES)
    vmem = pl.BlockSpec(memory_space=pltpu.VMEM)
    smem = pl.BlockSpec(memory_space=pltpu.SMEM)
    return pl.pallas_call(
        functools.partial(coarse_kernel, whole[0]),
        out_shape=jax.ShapeDtypeStruct((height, nx, ny), F32),
        in_specs=[smem] + [vmem] * (whole[0] + 3),
        out_specs=pl.BlockSpec(memory_space=pl.ANY),
        scratch_shapes=[
            field(*whole),
            field(*values.shape),
            field(height + 2, nx, ny),
            pads1, pads1, pads2, pads2,
            field(grid1.planes, grid1.nx, LANES),
            field(1, Flat(grid2).rows, LANES),
            field(1, Flat(grid2).rows, LANES),
            field(Flat(grid2).buffer_rows, LANES),
            field(height, nx, ny),
            pltpu.SemaphoreType.DMA((height,)),
        ],
        compiler_params=pltpu.CompilerParams(vmem_limit_bytes=VMEM_LIMIT),
        name="coarse",
    )(dom, *(parts[k] for k in swap_order(len(parts))), coefs, const, values)


def swaps(x, axis, step):
    return lax.ppermute(x, axis, [(i, i ^ step) for i in range(lax.axis_size(axis))])


def other_side(x):
    props, domains = lax.axis_size("prop"), lax.axis_size("dom")
    pairs = []
    for p in range(props):
        for d in range(domains):
            end = d in (0, domains - 1)
            partner = ((p ^ 1) * domains + d) if end else (p * domains + ((d + 1) ^ 1) - 1)
            pairs.append((p * domains + d, partner))
    return lax.ppermute(x, ("prop", "dom"), pairs)


def source_side(x):
    props, domains = lax.axis_size("prop"), lax.axis_size("dom")
    pairs = []
    for p in range(props):
        for d in range(domains):
            if d in (0, domains - 1):
                target = (p ^ 1) * domains + (d if p % 2 == 0 else d ^ 1)
            elif p % 2 == 0:
                target = p * domains + (d ^ 1)
            else:
                target = p * domains + ((d + 1) ^ 1) - 1
            pairs.append((p * domains + d, target))
    return lax.ppermute(x, ("prop", "dom"), pairs)


def from_accepted(mine, accepted, beside):
    props = lax.axis_size("prop")
    apart = lax.axis_index("prop") ^ accepted
    own = SHRINK * mine
    step = props // 2
    came = swaps(mine, "prop", step)
    came, own, beside = lax.optimization_barrier((came, own, beside))
    current = jnp.where(apart & step, SHRINK * came, own)
    while step > 1:
        step //= 2
        came = jnp.concatenate([swaps(x, "prop", step) for x in jnp.split(current, 2)])
        current = jnp.where(apart & step, came, current)
    return current, beside


def gather_parts(mine):
    domains = lax.axis_size("dom")
    parts = {0: mine}
    for step in range(0, domains, 2):
        if step:
            parts[step] = swaps(mine, "dom", step)
        parts[step + 1] = swaps(parts[step], "dom", 1)
    return [parts[k] for k in range(domains)]


def body(states, accepted, noise, source):
    domains = lax.axis_size("dom")
    height = source.shape[0]
    dom = jnp.stack([lax.axis_index("dom"), lax.axis_index("prop")]).astype(jnp.int32)
    near = source_side(source)
    current, noise_part = from_accepted(states[0], accepted[0], BETA * noise[0])
    perm = jnp.exp(current + noise_part)
    _, source, near = lax.optimization_barrier((perm, source, near))
    perms = (perm, other_side(perm), swaps(perm, "dom", 1))
    sources = (OMEGA * source, near, swaps(near, "prop", 1))
    *level, coarse = fine_part(dom, perms, sources, domains * height)
    return coarse_part(dom, gather_parts(coarse), *level, height)[None]


def solution(mesh):
    in_specs = (
        P("prop", "dom", None, None),
        P(),
        P("prop", "dom", None, None),
        P("dom", None, None),
    )
    out_specs = P("prop", "dom", None, None)
    return jax.shard_map(body, mesh=mesh, in_specs=in_specs, out_specs=out_specs, check_vma=False)
```

```python
import functools
import math

import jax
import jax.numpy as jnp
from jax import lax
from jax.experimental import pallas as pl
from jax.experimental.pallas import tpu as pltpu
from jax.sharding import PartitionSpec as P

COARSE_SWEEPS = 64
POWER = 3
OMEGA = 0.7
KEEP = 1.0 - OMEGA
BETA = 0.4
SHRINK = math.sqrt(1.0 - BETA * BETA)
ZSCALE = 16.0
LANES = 128
VMEM_LIMIT = 40 * 1024 * 1024
F32 = jnp.float32
WEST, EAST, SOUTH, NORTH, BELOW, ABOVE, CONST = range(7)


def iota(shape, dim):
    return lax.broadcasted_iota(jnp.int32, shape, dim)


def roll(x, amount, axis):
    axis = axis % x.ndim
    return pltpu.roll(x, amount % x.shape[axis], axis)


def inverse_of(x):
    guess = pl.reciprocal(x, approx=True)
    return guess * (2.0 - x * guess)


def harmonic(a, b):
    return (2.0 * a) * b * inverse_of(a + b)


def selector_dot(parts, selector):
    x = jnp.concatenate(parts, axis=0) if len(parts) > 1 else parts[0]
    rows = x.shape[0]
    high = x.astype(jnp.bfloat16).astype(F32)
    rest = x - high
    middle = rest.astype(jnp.bfloat16).astype(F32)
    terms = jnp.concatenate([high, middle, rest - middle], axis=0).astype(jnp.bfloat16)
    y = jnp.dot(terms, selector, preferred_element_type=F32)
    total = y[:rows] + y[rows : 2 * rows] + y[2 * rows :]
    height = parts[0].shape[0]
    return [total[i * height : (i + 1) * height] for i in range(len(parts))]


def side_faces(perm, ny):
    shape = perm.shape
    rows = iota(shape, 0)
    columns = iota(shape, 1) & (ny - 1)
    west = jnp.where(rows == 0, 0.0, harmonic(perm, roll(perm, 1, 0)))
    east = roll(west, -1, 0)
    south = jnp.where(columns == 0, 0.0, harmonic(perm, roll(perm, 1, 1)))
    north = roll(south, -1, 1)
    ends = jnp.where(rows == 0, perm, 0.0) + jnp.where(rows == shape[0] - 1, perm, 0.0)
    ends = ends + jnp.where(columns == 0, perm, 0.0) + jnp.where(columns == ny - 1, perm, 0.0)
    return west, east, south, north, ((west + east) + (south + north)) + ends


def face_terms(perm, below, above, ny):
    *sides, total = side_faces(perm, ny)
    return (*sides, below, above), total + (below + above)


def stencil(values, lower, upper, coefs, base):
    x = coefs[0] * roll(values, 1, 0) + coefs[1] * roll(values, -1, 0)
    y = coefs[2] * roll(values, 1, 1) + coefs[3] * roll(values, -1, 1)
    z = coefs[4] * lower + coefs[5] * upper
    return (x + y) + (z + base)


def lane_selector(groups, ny, step, spread=False):
    shape = (LANES, step * LANES) if spread else (step * LANES, LANES)
    source, target = iota(shape, int(spread)), iota(shape, 1 - int(spread))
    bits = ny.bit_length() - 1
    lane = source & (LANES - 1)
    group = (lane >> bits) * step + (source >> 7)
    wanted = (group << (bits - 1)) + ((lane & (ny - 1)) >> 1)
    return jnp.where((target == wanted) & (lane < groups * ny), 1.0, 0.0).astype(jnp.bfloat16)


def side_kernel(perm, out):
    for i in range(perm.shape[0]):
        for k, x in enumerate(side_faces(perm[i], LANES)):
            out[k, i] = x


def fine_kernel(
    layers,
    dom_ref, sides,
    per, per_other, per_pair,
    src, src_near, src_next,
    coef, const, values, coarse_out,
    perm, right, diag, pair_right, pair_perm,
):
    height = per.shape[0]
    dom = dom_ref[0]
    pair_at = jnp.where(lax.rem(dom, 2) == 0, 2 * height, 0)
    other_at = 2 * height - pair_at

    near_at = jnp.where(lax.rem(dom_ref[1], 2) == 0, pair_at, other_at)
    next_at = 2 * height - near_at
    for i in range(height):
        for at, p in ((height, per), (pair_at, per_pair), (other_at, per_other)):
            perm[at + i] = p[i]
        right[height + i] = src[i]
        right[near_at + i] = OMEGA * src_near[i]
        right[next_at + i] = OMEGA * src_next[i]

    def face(i):
        z = dom * height + i - 3
        scale = jnp.where((z > 0) & (z < layers), ZSCALE, 0.0)
        at = height - 3 + i
        return scale * harmonic(perm[at - 1], perm[at])

    above = face(0)
    for i in range(height + 6):
        at = height - 3 + i
        below, above = above, face(i + 1)
        if 3 <= i < height + 3:
            faces = tuple(sides[k, i - 3] for k in range(4)) + (below, above)
            diagonal = sides[4, i - 3] + (below + above)
        else:
            faces, diagonal = face_terms(perm[at], below, above, LANES)
        inverse = inverse_of(diagonal)
        const[i] = inverse * right[at]
        if 0 < i < height + 5:
            inverse = OMEGA * inverse
            for k in range(6):
                coef[k, i] = inverse * faces[k]
        if 3 <= i < height + 3:
            diag[i] = diagonal

    def first(i):
        start = const[i + 1]
        near = [coef[k, i + 1] for k in range(6)]
        values[i] = stencil(start, const[i], const[i + 2], near, (1.0 + KEEP) * start)

    for i in range(height + 4):
        first(i)

    def residue(i):
        centre = values[i + 2]
        base = const[i + 3] - OMEGA * centre
        near = [coef[k, i + 3] for k in range(6)]
        scaled = stencil(centre, values[i + 1], values[i + 3], near, base)
        return scaled * (diag[i + 3] * (1.0 / OMEGA))

    for m in range(height // 2):
        pair_right[m] = residue(2 * m) + residue(2 * m + 1)
        pair_perm[m] = (perm[height + 2 * m] + perm[height + 2 * m + 1]) * 0.125
    half = pair_right.shape[1] // 2
    rows = []
    for m in range(height // 2):
        both = [x[m, pl.ds(0, half, 2), :] + x[m, pl.ds(1, half, 2), :] for x in (pair_right, pair_perm)]
        rows.append(jnp.concatenate(both, axis=1))
    for m, x in enumerate(selector_dot(rows, lane_selector(1, LANES, 2))):
        coarse_out[m] = x


class Packed:
    def __init__(self, nz, nx, ny):
        self.nz, self.nx, self.ny = nz, nx, ny
        self.groups = min(LANES // ny, nz)
        self.planes = nz // self.groups

    def lower(self, planes, p):
        return planes[p - 1] if p else roll(planes[self.planes - 1], self.ny, 1)

    def upper(self, planes, p):
        return planes[p + 1] if p + 1 < self.planes else roll(planes[0], -self.ny, 1)

    def system(self, perm, level):
        lane = iota((self.nx, LANES), 1)
        used = lane < self.groups * self.ny
        if self.groups * self.ny < LANES:
            perm = [jnp.where(used, x, 1.0) for x in perm]
        coefs, factors, diagonals = [], [], []
        inner = [ZSCALE * harmonic(a, b) for a, b in zip(perm[:-1], perm[1:])]
        wrapped = ZSCALE * harmonic(perm[-1], roll(perm[0], -self.ny, 1))
        last = jnp.where(lane < (self.groups - 1) * self.ny, wrapped, 0.0)
        z_faces = [roll(last, self.ny, 1)] + inner + [last]
        for p in range(self.planes):
            faces, diagonal = face_terms(perm[p], z_faces[p], z_faces[p + 1], self.ny)
            inverse = OMEGA * inverse_of(diagonal)
            coefs.append([inverse * face for face in faces])
            factors.append(inverse * (4.0**-level))
            diagonals.append(diagonal * (4.0**level / OMEGA))
        return coefs, factors, diagonals

    def apply(self, values, coefs, bases):
        return [
            stencil(values[p], self.lower(values, p), self.upper(values, p), coefs[p], bases[p])
            for p in range(self.planes)
        ]

    def sweep(self, values, coefs, const):
        return self.apply(values, coefs, [KEEP * v + c for v, c in zip(values, const)])

    def coarser(self):
        return Packed(self.nz // 2, self.nx // 2, self.ny // 2)

    def restrict(self, fields, pads):
        coarse = self.coarser()
        step = coarse.groups // self.groups
        half = coarse.nx
        parts = []
        for values, pad in zip(fields, pads):
            rows = []
            for m in range(self.planes // 2):
                pad[m] = values[2 * m] + values[2 * m + 1]
                rows.append(pad[m, pl.ds(0, half, 2), :] + pad[m, pl.ds(1, half, 2), :])
            for p in range(coarse.planes):
                blocks = rows[p :: coarse.planes]
                parts.append(jnp.concatenate(blocks, axis=1) if step > 1 else blocks[0])
        sums = selector_dot(parts, lane_selector(self.groups, self.ny, step))
        return [sums[i : i + coarse.planes] for i in range(0, len(sums), coarse.planes)]

    def prolong(self, values, pad):
        coarse = self.coarser()
        step = coarse.groups // self.groups
        half = coarse.nx
        wide = selector_dot(values, lane_selector(self.groups, self.ny, step, spread=True))
        out = []
        for m in range(self.planes // 2):
            j, p = divmod(m, coarse.planes)
            plane = wide[p][:, j * LANES : (j + 1) * LANES]
            pad[m, pl.ds(0, half, 2), :] = plane
            pad[m, pl.ds(1, half, 2), :] = plane
            out += [pad[m], pad[m]]
        return out


class Flat:
    def __init__(self, finer):
        coarse = finer.coarser()
        self.finer = finer
        self.nz, self.nx, self.ny = coarse.nz, coarse.nx, coarse.ny
        self.pairs = finer.planes // 2
        self.rows = max(8, self.nz)
        self.shape = (self.rows, LANES)
        self.buffer_rows = 2 * (self.rows + 2 * POWER)

    def selector(self, spread=False):
        wide = self.finer.groups * LANES
        shape = (wide, LANES) if spread else (LANES, wide)
        fine, flat = iota(shape, int(spread)), iota(shape, 1 - int(spread))
        bits = self.finer.ny.bit_length() - 1
        same = (fine >> bits) == (flat >> 7)
        same &= ((fine & (self.finer.ny - 1)) >> 1) == (flat & (self.ny - 1))
        return jnp.where(same, 1.0, 0.0).astype(jnp.bfloat16)

    def diagonal(self):
        shape = (self.nx, LANES)
        return iota(shape, 0) == (iota(shape, 1) >> (self.ny.bit_length() - 1))

    def restrict(self, fields, pads, pack):
        parts = []
        for values, pad in zip(fields, pads):
            for m in range(self.pairs):
                pad[m] = values[2 * m] + values[2 * m + 1]
                parts.append(pad[m, pl.ds(0, self.nx, 2), :] + pad[m, pl.ds(1, self.nx, 2), :])
        sums = selector_dot(parts, self.selector())
        mask = self.diagonal()
        pack[...] = jnp.zeros_like(pack)
        for i in range(len(fields)):
            for z in range(self.nz):
                s, m = divmod(z, self.pairs)
                block = sums[i * self.pairs + m][:, s * LANES : (s + 1) * LANES]
                row = jnp.sum(jnp.where(mask, block, 0.0), axis=0, keepdims=True)
                pack[i, z : z + 1, :] = row
        return [pack[i] for i in range(len(fields))]

    def prolong(self, values, pad, pack):
        mask = self.diagonal()
        pack[0] = values
        parts = []
        for m in range(self.pairs):
            layers = [s * self.pairs + m for s in range(self.finer.groups)]
            spread = [jnp.broadcast_to(pack[0, z : z + 1, :], mask.shape) for z in layers]
            parts.append(jnp.concatenate([jnp.where(mask, x, 0.0) for x in spread], axis=1))
        out = []
        for m, wide in enumerate(selector_dot(parts, self.selector(spread=True))):
            pad[m, pl.ds(0, self.nx, 2), :] = wide
            pad[m, pl.ds(1, self.nx, 2), :] = wide
            out += [pad[m], pad[m]]
        return out

    def system(self, perm, level):
        lane, row = iota(self.shape, 1), iota(self.shape, 0)
        x, y = lane >> (self.ny.bit_length() - 1), lane & (self.ny - 1)
        real = row < self.nz
        perm = jnp.where(real, perm, 1.0)
        west = jnp.where(x == 0, 0.0, harmonic(perm, roll(perm, self.ny, 1)))
        east = roll(west, -self.ny, 1)
        south = jnp.where(y == 0, 0.0, harmonic(perm, roll(perm, 1, 1)))
        north = roll(south, -1, 1)
        below = ZSCALE * harmonic(perm, roll(perm, 1, 0))
        below = jnp.where((row > 0) & real, below, 0.0)
        above = roll(below, -1, 0)
        faces = [west, east, south, north, below, above]
        ends = (x == 0, x == self.nx - 1, y == 0, y == self.ny - 1)
        diagonal = tree_sum(faces + [jnp.where(end, perm, 0.0) for end in ends])
        inverse = jnp.where(real, OMEGA * inverse_of(diagonal), 0.0)
        keys = ((-1, 0, 0), (1, 0, 0), (0, -1, 0), (0, 1, 0), (0, 0, -1), (0, 0, 1))
        terms = {key: inverse * face for key, face in zip(keys, faces)}
        terms[0, 0, 0] = jnp.full(self.shape, KEEP, F32)
        return terms, inverse * (4.0**-level)

    def product(self, first, second):
        sums = {}
        for (dx, dy, dz), coef in first.items():
            for other, moved in second.items():
                if dz:
                    moved = roll(moved, -dz, 0)
                if dx or dy:
                    moved = roll(moved, -(dx * self.ny + dy), 1)
                total = tuple(a + b for a, b in zip((dx, dy, dz), other))
                sums.setdefault(total, []).append(coef * moved)
        return {key: tree_sum(parts) for key, parts in sums.items()}

    def apply(self, terms, values, base, buffer):
        buffer[pl.ds(2 * POWER, self.rows, 2), :] = values
        moved = {}
        for dx, dy, dz in sorted(terms, key=lambda key: abs(key[2])):
            if (0, 0, dz) not in moved:
                moved[0, 0, dz] = buffer[pl.ds(2 * (POWER + dz), self.rows, 2), :] if dz else values
            if dx or dy:
                moved[dx, dy, dz] = roll(moved[0, 0, dz], -(dx * self.ny + dy), 1)
        return tree_sum([base] + [coef * moved[key] for key, coef in terms.items()])

    def prepare(self, perm, level):
        terms, factor = self.system(perm, level)
        power = terms
        for _ in range(POWER - 1):
            power = self.product(terms, power)
        return terms, power, factor

    def solve(self, right, prepared, buffer):
        terms, power, factor = prepared
        const = factor * right
        buffer[...] = jnp.zeros_like(buffer)
        base = const
        for _ in range(POWER - 1):
            base = self.apply(terms, base, const, buffer)
        whole = COARSE_SWEEPS % POWER == 0
        values = base if whole else const
        steps = (COARSE_SWEEPS - 1) // POWER
        assert steps * POWER + (POWER if whole else 1) == COARSE_SWEEPS
        for _ in range(steps):
            values = self.apply(power, values, base, buffer)
        return values


def tree_sum(parts):
    while len(parts) > 1:
        odd = parts[len(parts) // 2 * 2 :]
        parts = [a + b for a, b in zip(parts[::2], parts[1::2])] + odd
    return parts[0]


def packed_cycle(grid, right, perm, level, pads, packs, buffer):
    pad_right, pad_perm = pads[0]
    coefs, factors, diagonals = grid.system(perm, level)
    if len(pads) > 1:
        (coarse_perm,) = grid.restrict([perm], [pad_perm])
    else:
        flat = Flat(grid)
        (coarse_perm,) = flat.restrict([perm], [pad_perm], packs[1])
        prepared = flat.prepare(coarse_perm * 0.125, level + 1)
    const = [f * r for f, r in zip(factors, right)]
    values = grid.sweep(const, coefs, const)
    scaled = grid.apply(values, coefs, [c - OMEGA * v for c, v in zip(const, values)])
    residue = [r * d for r, d in zip(scaled, diagonals)]
    if len(pads) > 1:
        (coarse_right,) = grid.restrict([residue], [pad_right])
        coarse_perm = [x * 0.125 for x in coarse_perm]
        update = packed_cycle(
            grid.coarser(), coarse_right, coarse_perm, level + 1, pads[1:], packs, buffer
        )
        update = grid.prolong(update, pad_right)
    else:
        (coarse_right,) = flat.restrict([residue], [pad_right], packs[0])
        update = flat.prolong(flat.solve(coarse_right, prepared, buffer), pad_right, packs[0])
    values = [v + e for v, e in zip(values, update)]
    for _ in range(2):
        values = grid.sweep(values, coefs, const)
    return values


def swap_order(domains):
    steps = [0, domains - 2] + list(range(2, domains - 2, 2))
    return [step + 1 - odd for step in steps[::-1] for odd in range(2)]


def coarse_kernel(
    count, dom_ref, *refs,
):
    parts = [refs[swap_order(count).index(k)] for k in range(count)]
    refs = refs[count:]
    coef, const, before, out, gathered, *refs = refs
    coarse_steps(parts, dom_ref, gathered, coef, const, before, out, *refs)


def coarse_steps(
    parts, dom_ref, gathered, coef, const, before, out,
    level, first, pad_right1, pad_perm1, pad_right2, pad_perm2, update, pack, pack_perm, buffer,
    done, sems,
):
    height = out.shape[0]
    dom = dom_ref[0]
    domains, own, nx, _ = gathered.shape
    for step, part in enumerate(parts):
        gathered[dom ^ step] = part[...]
    ny = LANES // 2
    grid = Packed(domains * own, nx, ny)
    left = iota((nx, LANES), 1) < ny
    right, perm = [], []
    for p in range(grid.planes):
        a = gathered[p // own, p % own]
        q = grid.planes + p
        b = gathered[q // own, q % own]
        right.append(jnp.where(left, a, roll(b, ny, 1)))
        perm.append(jnp.where(left, roll(a, ny, 1), b))
    pads = [(pad_right1, pad_perm1), (pad_right2, pad_perm2)]
    solved = packed_cycle(grid, right, perm, 1, pads, (pack, pack_perm), buffer)
    for p in range(grid.planes):
        update[p] = solved[p]
    planes, group = [], []
    for j in range(own + 2):
        layer = jnp.clip(dom * own + j - 1, 0, grid.nz - 1)
        group.append(layer // grid.planes)
        planes.append(update[lax.rem(layer, grid.planes)])
    for j, wide in enumerate(selector_dot(planes, lane_selector(1, LANES, 2, spread=True))):
        plane = jnp.where(group[j] == 0, wide[:, :LANES], wide[:, LANES:])
        pad = first.at[0]
        pad[pl.ds(0, nx, 2), :] = plane
        pad[pl.ds(1, nx, 2), :] = plane
        whole = first[0]
        level[2 * j] = before[2 * j] + whole
        level[2 * j + 1] = before[2 * j + 1] + whole

    def sweep(source, at, i):
        centre = source[i + 1]
        near = [coef[k, at + i] for k in range(6)]
        return stencil(centre, source[i], source[i + 2], near, KEEP * centre + const[at + i])

    def one(i):
        first[i] = sweep(level, 2, i)

    for i in range(height + 2):
        one(i)

    copies = []
    for i in range(height):
        done[i] = sweep(first, 3, i)
        copies.append(pltpu.make_async_copy(done.at[i], out.at[i], sems.at[i]))
        copies[-1].start()
    for copy in copies:
        copy.wait()


def fine_part(dom, perm, source, layers):
    height, nx, ny = perm[0].shape
    field = lambda *lead: pltpu.VMEM(lead + (nx, ny), F32)
    vmem = pl.BlockSpec(memory_space=pltpu.VMEM)
    sides = pl.pallas_call(
        side_kernel,
        out_shape=jax.ShapeDtypeStruct((5, height, nx, ny), F32),
        in_specs=[vmem],
        out_specs=vmem,
        compiler_params=pltpu.CompilerParams(vmem_limit_bytes=VMEM_LIMIT),
        name="sides",
    )(perm[0])
    smem = pl.BlockSpec(memory_space=pltpu.SMEM)
    return pl.pallas_call(
        functools.partial(fine_kernel, layers),
        out_shape=(
            jax.ShapeDtypeStruct((6, height + 6, nx, ny), F32),
            jax.ShapeDtypeStruct((height + 6, nx, ny), F32),
            jax.ShapeDtypeStruct((height + 4, nx, ny), F32),
            jax.ShapeDtypeStruct((height // 2, nx // 2, ny), F32),
        ),
        in_specs=[smem] + [vmem] * 7,
        out_specs=(vmem,) * 4,
        scratch_shapes=[
            field(3 * height),
            field(3 * height),
            field(height + 6),
            field(height // 2),
            field(height // 2),
        ],
        compiler_params=pltpu.CompilerParams(vmem_limit_bytes=VMEM_LIMIT),
        name="fine",
    )(dom, sides, *perm, *source)


def coarse_part(dom, parts, coefs, const, values, height):
    _, nx, ny = values.shape
    field = lambda *shape: pltpu.VMEM(shape, F32)
    whole = (len(parts),) + parts[0].shape
    grid1 = Packed(whole[0] * whole[1], nx // 2, ny // 2)
    grid2 = grid1.coarser()
    pads1 = field(grid1.planes // 2, grid1.nx, LANES)
    pads2 = field(grid2.planes // 2, grid2.nx, LANES)
    vmem = pl.BlockSpec(memory_space=pltpu.VMEM)
    smem = pl.BlockSpec(memory_space=pltpu.SMEM)
    return pl.pallas_call(
        functools.partial(coarse_kernel, whole[0]),
        out_shape=jax.ShapeDtypeStruct((height, nx, ny), F32),
        in_specs=[smem] + [vmem] * (whole[0] + 3),
        out_specs=pl.BlockSpec(memory_space=pl.ANY),
        scratch_shapes=[
            field(*whole),
            field(*values.shape),
            field(height + 2, nx, ny),
            pads1, pads1, pads2, pads2,
            field(grid1.planes, grid1.nx, LANES),
            field(1, Flat(grid2).rows, LANES),
            field(1, Flat(grid2).rows, LANES),
            field(Flat(grid2).buffer_rows, LANES),
            field(height, nx, ny),
            pltpu.SemaphoreType.DMA((height,)),
        ],
        compiler_params=pltpu.CompilerParams(vmem_limit_bytes=VMEM_LIMIT),
        name="coarse",
    )(dom, *(parts[k] for k in swap_order(len(parts))), coefs, const, values)


def swaps(x, axis, step):
    return lax.ppermute(x, axis, [(i, i ^ step) for i in range(lax.axis_size(axis))])


def other_side(x):
    props, domains = lax.axis_size("prop"), lax.axis_size("dom")
    pairs = []
    for p in range(props):
        for d in range(domains):
            end = d in (0, domains - 1)
            partner = ((p ^ 1) * domains + d) if end else (p * domains + ((d + 1) ^ 1) - 1)
            pairs.append((p * domains + d, partner))
    return lax.ppermute(x, ("prop", "dom"), pairs)


def source_side(x):
    props, domains = lax.axis_size("prop"), lax.axis_size("dom")
    pairs = []
    for p in range(props):
        for d in range(domains):
            if d in (0, domains - 1):
                target = (p ^ 1) * domains + (d if p % 2 == 0 else d ^ 1)
            elif p % 2 == 0:
                target = p * domains + (d ^ 1)
            else:
                target = p * domains + ((d + 1) ^ 1) - 1
            pairs.append((p * domains + d, target))
    return lax.ppermute(x, ("prop", "dom"), pairs)


def from_accepted(mine, accepted, beside):
    props = lax.axis_size("prop")
    apart = lax.axis_index("prop") ^ accepted
    own = SHRINK * mine
    step = props // 2
    came = swaps(mine, "prop", step)
    came, own, beside = lax.optimization_barrier((came, own, beside))
    current = jnp.where(apart & step, SHRINK * came, own)
    while step > 1:
        step //= 2
        came = jnp.concatenate([swaps(x, "prop", step) for x in jnp.split(current, 2)])
        current = jnp.where(apart & step, came, current)
    return current, beside


def gather_parts(mine):
    domains = lax.axis_size("dom")
    parts = {0: mine}
    for step in range(0, domains, 2):
        if step:
            parts[step] = swaps(mine, "dom", step)
        parts[step + 1] = swaps(parts[step], "dom", 1)
    return [parts[k] for k in range(domains)]


def body(states, accepted, noise, source):
    domains = lax.axis_size("dom")
    height = source.shape[0]
    dom = jnp.stack([lax.axis_index("dom"), lax.axis_index("prop")]).astype(jnp.int32)
    near = source_side(source)
    current, noise_part = from_accepted(states[0], accepted[0], BETA * noise[0])
    perm = jnp.exp(current + noise_part)
    _, source, near = lax.optimization_barrier((perm, source, near))
    perms = (perm, other_side(perm), swaps(perm, "dom", 1))
    sources = (OMEGA * source, near, swaps(near, "prop", 1))
    *level, coarse = fine_part(dom, perms, sources, domains * height)
    return coarse_part(dom, gather_parts(coarse), *level, height)[None]


def solution(mesh):
    in_specs = (
        P("prop", "dom", None, None),
        P(),
        P("prop", "dom", None, None),
        P("dom", None, None),
    )
    out_specs = P("prop", "dom", None, None)
    return jax.shard_map(body, mesh=mesh, in_specs=in_specs, out_specs=out_specs, check_vma=False)
```

```python
import functools
import math

import jax
import jax.numpy as jnp
from jax import lax
from jax.experimental import pallas as pl
from jax.experimental.pallas import tpu as pltpu
from jax.sharding import PartitionSpec as P

COARSE_SWEEPS = 64
POWER = 3
OMEGA = 0.7
KEEP = 1.0 - OMEGA
BETA = 0.4
SHRINK = math.sqrt(1.0 - BETA * BETA)
ZSCALE = 16.0
LANES = 128
VMEM_LIMIT = 40 * 1024 * 1024
F32 = jnp.float32
WEST, EAST, SOUTH, NORTH, BELOW, ABOVE, CONST = range(7)


def iota(shape, dim):
    return lax.broadcasted_iota(jnp.int32, shape, dim)


def roll(x, amount, axis):
    axis = axis % x.ndim
    return pltpu.roll(x, amount % x.shape[axis], axis)


def inverse_of(x):
    guess = pl.reciprocal(x, approx=True)
    return guess * (2.0 - x * guess)


def harmonic(a, b):
    return (2.0 * a) * b * inverse_of(a + b)


def selector_dot(parts, selector):
    x = jnp.concatenate(parts, axis=0) if len(parts) > 1 else parts[0]
    rows = x.shape[0]
    high = x.astype(jnp.bfloat16).astype(F32)
    rest = x - high
    middle = rest.astype(jnp.bfloat16).astype(F32)
    terms = jnp.concatenate([high, middle, rest - middle], axis=0).astype(jnp.bfloat16)
    y = jnp.dot(terms, selector, preferred_element_type=F32)
    total = y[:rows] + y[rows : 2 * rows] + y[2 * rows :]
    height = parts[0].shape[0]
    return [total[i * height : (i + 1) * height] for i in range(len(parts))]


def side_faces(perm, ny):
    shape = perm.shape
    rows = iota(shape, 0)
    columns = iota(shape, 1) & (ny - 1)
    west = jnp.where(rows == 0, 0.0, harmonic(perm, roll(perm, 1, 0)))
    east = roll(west, -1, 0)
    south = jnp.where(columns == 0, 0.0, harmonic(perm, roll(perm, 1, 1)))
    north = roll(south, -1, 1)
    ends = jnp.where(rows == 0, perm, 0.0) + jnp.where(rows == shape[0] - 1, perm, 0.0)
    ends = ends + jnp.where(columns == 0, perm, 0.0) + jnp.where(columns == ny - 1, perm, 0.0)
    return west, east, south, north, ((west + east) + (south + north)) + ends


def face_terms(perm, below, above, ny):
    *sides, total = side_faces(perm, ny)
    return (*sides, below, above), total + (below + above)


def stencil(values, lower, upper, coefs, base):
    x = coefs[0] * roll(values, 1, 0) + coefs[1] * roll(values, -1, 0)
    y = coefs[2] * roll(values, 1, 1) + coefs[3] * roll(values, -1, 1)
    z = coefs[4] * lower + coefs[5] * upper
    return (x + y) + (z + base)


def lane_selector(groups, ny, step, spread=False):
    shape = (LANES, step * LANES) if spread else (step * LANES, LANES)
    source, target = iota(shape, int(spread)), iota(shape, 1 - int(spread))
    bits = ny.bit_length() - 1
    lane = source & (LANES - 1)
    group = (lane >> bits) * step + (source >> 7)
    wanted = (group << (bits - 1)) + ((lane & (ny - 1)) >> 1)
    return jnp.where((target == wanted) & (lane < groups * ny), 1.0, 0.0).astype(jnp.bfloat16)


def side_kernel(perm, out):
    for i in range(perm.shape[0]):
        for k, x in enumerate(side_faces(perm[i], LANES)):
            out[k, i] = x


def fine_kernel(
    layers,
    dom_ref, sides,
    per, per_other, per_pair,
    src, src_near, src_next,
    coef, const, values, coarse_out,
    perm, right, diag, pair_right, pair_perm,
):
    height = per.shape[0]
    dom = dom_ref[0]
    pair_at = jnp.where(lax.rem(dom, 2) == 0, 2 * height, 0)
    other_at = 2 * height - pair_at

    near_at = jnp.where(lax.rem(dom_ref[1], 2) == 0, pair_at, other_at)
    next_at = 2 * height - near_at
    for i in range(height):
        for at, p in ((height, per), (pair_at, per_pair), (other_at, per_other)):
            perm[at + i] = p[i]
        right[height + i] = src[i]
        right[near_at + i] = OMEGA * src_near[i]
        right[next_at + i] = OMEGA * src_next[i]

    def face(i):
        z = dom * height + i - 3
        scale = jnp.where((z > 0) & (z < layers), ZSCALE, 0.0)
        at = height - 3 + i
        return scale * harmonic(perm[at - 1], perm[at])

    above = face(0)
    for i in range(height + 6):
        at = height - 3 + i
        below, above = above, face(i + 1)
        if 3 <= i < height + 3:
            faces = tuple(sides[k, i - 3] for k in range(4)) + (below, above)
            diagonal = sides[4, i - 3] + (below + above)
        else:
            faces, diagonal = face_terms(perm[at], below, above, LANES)
        inverse = inverse_of(diagonal)
        const[i] = inverse * right[at]
        if 0 < i < height + 5:
            inverse = OMEGA * inverse
            for k in range(6):
                coef[k, i] = inverse * faces[k]
        if 3 <= i < height + 3:
            diag[i] = diagonal

    def first(i):
        start = const[i + 1]
        near = [coef[k, i + 1] for k in range(6)]
        values[i] = stencil(start, const[i], const[i + 2], near, (1.0 + KEEP) * start)

    for i in range(height + 4):
        first(i)

    def residue(i):
        centre = values[i + 2]
        base = const[i + 3] - OMEGA * centre
        near = [coef[k, i + 3] for k in range(6)]
        scaled = stencil(centre, values[i + 1], values[i + 3], near, base)
        return scaled * (diag[i + 3] * (1.0 / OMEGA))

    for m in range(height // 2):
        pair_right[m] = residue(2 * m) + residue(2 * m + 1)
        pair_perm[m] = (perm[height + 2 * m] + perm[height + 2 * m + 1]) * 0.125
    half = pair_right.shape[1] // 2
    rows = []
    for m in range(height // 2):
        both = [x[m, pl.ds(0, half, 2), :] + x[m, pl.ds(1, half, 2), :] for x in (pair_right, pair_perm)]
        rows.append(jnp.concatenate(both, axis=1))
    for m, x in enumerate(selector_dot(rows, lane_selector(1, LANES, 2))):
        coarse_out[m] = x


class Packed:
    def __init__(self, nz, nx, ny):
        self.nz, self.nx, self.ny = nz, nx, ny
        self.groups = min(LANES // ny, nz)
        self.planes = nz // self.groups

    def lower(self, planes, p):
        return planes[p - 1] if p else roll(planes[self.planes - 1], self.ny, 1)

    def upper(self, planes, p):
        return planes[p + 1] if p + 1 < self.planes else roll(planes[0], -self.ny, 1)

    def system(self, perm, level):
        lane = iota((self.nx, LANES), 1)
        used = lane < self.groups * self.ny
        if self.groups * self.ny < LANES:
            perm = [jnp.where(used, x, 1.0) for x in perm]
        coefs, factors, diagonals = [], [], []
        inner = [ZSCALE * harmonic(a, b) for a, b in zip(perm[:-1], perm[1:])]
        wrapped = ZSCALE * harmonic(perm[-1], roll(perm[0], -self.ny, 1))
        last = jnp.where(lane < (self.groups - 1) * self.ny, wrapped, 0.0)
        z_faces = [roll(last, self.ny, 1)] + inner + [last]
        for p in range(self.planes):
            faces, diagonal = face_terms(perm[p], z_faces[p], z_faces[p + 1], self.ny)
            inverse = OMEGA * inverse_of(diagonal)
            coefs.append([inverse * face for face in faces])
            factors.append(inverse * (4.0**-level))
            diagonals.append(diagonal * (4.0**level / OMEGA))
        return coefs, factors, diagonals

    def apply(self, values, coefs, bases):
        return [
            stencil(values[p], self.lower(values, p), self.upper(values, p), coefs[p], bases[p])
            for p in range(self.planes)
        ]

    def sweep(self, values, coefs, const):
        return self.apply(values, coefs, [KEEP * v + c for v, c in zip(values, const)])

    def coarser(self):
        return Packed(self.nz // 2, self.nx // 2, self.ny // 2)

    def restrict(self, fields, pads):
        coarse = self.coarser()
        step = coarse.groups // self.groups
        half = coarse.nx
        parts = []
        for values, pad in zip(fields, pads):
            rows = []
            for m in range(self.planes // 2):
                pad[m] = values[2 * m] + values[2 * m + 1]
                rows.append(pad[m, pl.ds(0, half, 2), :] + pad[m, pl.ds(1, half, 2), :])
            for p in range(coarse.planes):
                blocks = rows[p :: coarse.planes]
                parts.append(jnp.concatenate(blocks, axis=1) if step > 1 else blocks[0])
        sums = selector_dot(parts, lane_selector(self.groups, self.ny, step))
        return [sums[i : i + coarse.planes] for i in range(0, len(sums), coarse.planes)]

    def prolong(self, values, pad):
        coarse = self.coarser()
        step = coarse.groups // self.groups
        half = coarse.nx
        wide = selector_dot(values, lane_selector(self.groups, self.ny, step, spread=True))
        out = []
        for m in range(self.planes // 2):
            j, p = divmod(m, coarse.planes)
            plane = wide[p][:, j * LANES : (j + 1) * LANES]
            pad[m, pl.ds(0, half, 2), :] = plane
            pad[m, pl.ds(1, half, 2), :] = plane
            out += [pad[m], pad[m]]
        return out


class Flat:
    def __init__(self, finer):
        coarse = finer.coarser()
        self.finer = finer
        self.nz, self.nx, self.ny = coarse.nz, coarse.nx, coarse.ny
        self.pairs = finer.planes // 2
        self.rows = max(8, self.nz)
        self.shape = (self.rows, LANES)
        self.buffer_rows = 2 * (self.rows + 2 * POWER)

    def selector(self, spread=False):
        wide = self.finer.groups * LANES
        shape = (wide, LANES) if spread else (LANES, wide)
        fine, flat = iota(shape, int(spread)), iota(shape, 1 - int(spread))
        bits = self.finer.ny.bit_length() - 1
        same = (fine >> bits) == (flat >> 7)
        same &= ((fine & (self.finer.ny - 1)) >> 1) == (flat & (self.ny - 1))
        return jnp.where(same, 1.0, 0.0).astype(jnp.bfloat16)

    def diagonal(self):
        shape = (self.nx, LANES)
        return iota(shape, 0) == (iota(shape, 1) >> (self.ny.bit_length() - 1))

    def restrict(self, fields, pads, pack):
        parts = []
        for values, pad in zip(fields, pads):
            for m in range(self.pairs):
                pad[m] = values[2 * m] + values[2 * m + 1]
                parts.append(pad[m, pl.ds(0, self.nx, 2), :] + pad[m, pl.ds(1, self.nx, 2), :])
        sums = selector_dot(parts, self.selector())
        mask = self.diagonal()
        pack[...] = jnp.zeros_like(pack)
        for i in range(len(fields)):
            for z in range(self.nz):
                s, m = divmod(z, self.pairs)
                block = sums[i * self.pairs + m][:, s * LANES : (s + 1) * LANES]
                row = jnp.sum(jnp.where(mask, block, 0.0), axis=0, keepdims=True)
                pack[i, z : z + 1, :] = row
        return [pack[i] for i in range(len(fields))]

    def prolong(self, values, pad, pack):
        mask = self.diagonal()
        pack[0] = values
        parts = []
        for m in range(self.pairs):
            layers = [s * self.pairs + m for s in range(self.finer.groups)]
            spread = [jnp.broadcast_to(pack[0, z : z + 1, :], mask.shape) for z in layers]
            parts.append(jnp.concatenate([jnp.where(mask, x, 0.0) for x in spread], axis=1))
        out = []
        for m, wide in enumerate(selector_dot(parts, self.selector(spread=True))):
            pad[m, pl.ds(0, self.nx, 2), :] = wide
            pad[m, pl.ds(1, self.nx, 2), :] = wide
            out += [pad[m], pad[m]]
        return out

    def system(self, perm, level):
        lane, row = iota(self.shape, 1), iota(self.shape, 0)
        x, y = lane >> (self.ny.bit_length() - 1), lane & (self.ny - 1)
        real = row < self.nz
        perm = jnp.where(real, perm, 1.0)
        west = jnp.where(x == 0, 0.0, harmonic(perm, roll(perm, self.ny, 1)))
        east = roll(west, -self.ny, 1)
        south = jnp.where(y == 0, 0.0, harmonic(perm, roll(perm, 1, 1)))
        north = roll(south, -1, 1)
        below = ZSCALE * harmonic(perm, roll(perm, 1, 0))
        below = jnp.where((row > 0) & real, below, 0.0)
        above = roll(below, -1, 0)
        faces = [west, east, south, north, below, above]
        ends = (x == 0, x == self.nx - 1, y == 0, y == self.ny - 1)
        diagonal = tree_sum(faces + [jnp.where(end, perm, 0.0) for end in ends])
        inverse = jnp.where(real, OMEGA * inverse_of(diagonal), 0.0)
        keys = ((-1, 0, 0), (1, 0, 0), (0, -1, 0), (0, 1, 0), (0, 0, -1), (0, 0, 1))
        terms = {key: inverse * face for key, face in zip(keys, faces)}
        terms[0, 0, 0] = jnp.full(self.shape, KEEP, F32)
        return terms, inverse * (4.0**-level)

    def product(self, first, second):
        sums = {}
        for (dx, dy, dz), coef in first.items():
            for other, moved in second.items():
                if dz:
                    moved = roll(moved, -dz, 0)
                if dx or dy:
                    moved = roll(moved, -(dx * self.ny + dy), 1)
                total = tuple(a + b for a, b in zip((dx, dy, dz), other))
                sums.setdefault(total, []).append(coef * moved)
        return {key: tree_sum(parts) for key, parts in sums.items()}

    def apply(self, terms, values, base, buffer):
        buffer[pl.ds(2 * POWER, self.rows, 2), :] = values
        moved = {}
        for dx, dy, dz in sorted(terms, key=lambda key: abs(key[2])):
            if (0, 0, dz) not in moved:
                moved[0, 0, dz] = buffer[pl.ds(2 * (POWER + dz), self.rows, 2), :] if dz else values
            if dx or dy:
                moved[dx, dy, dz] = roll(moved[0, 0, dz], -(dx * self.ny + dy), 1)
        return tree_sum([base] + [coef * moved[key] for key, coef in terms.items()])

    def prepare(self, perm, level):
        terms, factor = self.system(perm, level)
        power = terms
        for _ in range(POWER - 1):
            power = self.product(terms, power)
        return terms, power, factor

    def solve(self, right, prepared, buffer):
        terms, power, factor = prepared
        const = factor * right
        buffer[...] = jnp.zeros_like(buffer)
        base = const
        for _ in range(POWER - 1):
            base = self.apply(terms, base, const, buffer)
        whole = COARSE_SWEEPS % POWER == 0
        values = base if whole else const
        steps = (COARSE_SWEEPS - 1) // POWER
        assert steps * POWER + (POWER if whole else 1) == COARSE_SWEEPS
        for _ in range(steps):
            values = self.apply(power, values, base, buffer)
        return values


def tree_sum(parts):
    while len(parts) > 1:
        odd = parts[len(parts) // 2 * 2 :]
        parts = [a + b for a, b in zip(parts[::2], parts[1::2])] + odd
    return parts[0]


def packed_cycle(grid, right, perm, level, pads, packs, buffer):
    pad_right, pad_perm = pads[0]
    coefs, factors, diagonals = grid.system(perm, level)
    if len(pads) > 1:
        (coarse_perm,) = grid.restrict([perm], [pad_perm])
    else:
        flat = Flat(grid)
        (coarse_perm,) = flat.restrict([perm], [pad_perm], packs[1])
        prepared = flat.prepare(coarse_perm * 0.125, level + 1)
    const = [f * r for f, r in zip(factors, right)]
    values = grid.sweep(const, coefs, const)
    scaled = grid.apply(values, coefs, [c - OMEGA * v for c, v in zip(const, values)])
    residue = [r * d for r, d in zip(scaled, diagonals)]
    if len(pads) > 1:
        (coarse_right,) = grid.restrict([residue], [pad_right])
        coarse_perm = [x * 0.125 for x in coarse_perm]
        update = packed_cycle(
            grid.coarser(), coarse_right, coarse_perm, level + 1, pads[1:], packs, buffer
        )
        update = grid.prolong(update, pad_right)
    else:
        (coarse_right,) = flat.restrict([residue], [pad_right], packs[0])
        update = flat.prolong(flat.solve(coarse_right, prepared, buffer), pad_right, packs[0])
    values = [v + e for v, e in zip(values, update)]
    for _ in range(2):
        values = grid.sweep(values, coefs, const)
    return values


def swap_order(domains):
    steps = [0] + list(range(domains - 2, 0, -2))
    return [step + 1 - odd for step in steps[::-1] for odd in range(2)]


def coarse_kernel(
    count, dom_ref, *refs,
):
    parts = [refs[swap_order(count).index(k)] for k in range(count)]
    refs = refs[count:]
    coef, const, before, out, gathered, *refs = refs
    coarse_steps(parts, dom_ref, gathered, coef, const, before, out, *refs)


def coarse_steps(
    parts, dom_ref, gathered, coef, const, before, out,
    level, first, pad_right1, pad_perm1, pad_right2, pad_perm2, update, pack, pack_perm, buffer,
    done, sems,
):
    height = out.shape[0]
    dom = dom_ref[0]
    domains, own, nx, _ = gathered.shape
    for step, part in enumerate(parts):
        gathered[dom ^ step] = part[...]
    ny = LANES // 2
    grid = Packed(domains * own, nx, ny)
    left = iota((nx, LANES), 1) < ny
    right, perm = [], []
    for p in range(grid.planes):
        a = gathered[p // own, p % own]
        q = grid.planes + p
        b = gathered[q // own, q % own]
        right.append(jnp.where(left, a, roll(b, ny, 1)))
        perm.append(jnp.where(left, roll(a, ny, 1), b))
    pads = [(pad_right1, pad_perm1), (pad_right2, pad_perm2)]
    solved = packed_cycle(grid, right, perm, 1, pads, (pack, pack_perm), buffer)
    for p in range(grid.planes):
        update[p] = solved[p]
    planes, group = [], []
    for j in range(own + 2):
        layer = jnp.clip(dom * own + j - 1, 0, grid.nz - 1)
        group.append(layer // grid.planes)
        planes.append(update[lax.rem(layer, grid.planes)])
    for j, wide in enumerate(selector_dot(planes, lane_selector(1, LANES, 2, spread=True))):
        plane = jnp.where(group[j] == 0, wide[:, :LANES], wide[:, LANES:])
        pad = first.at[0]
        pad[pl.ds(0, nx, 2), :] = plane
        pad[pl.ds(1, nx, 2), :] = plane
        whole = first[0]
        level[2 * j] = before[2 * j] + whole
        level[2 * j + 1] = before[2 * j + 1] + whole

    def sweep(source, at, i):
        centre = source[i + 1]
        near = [coef[k, at + i] for k in range(6)]
        return stencil(centre, source[i], source[i + 2], near, KEEP * centre + const[at + i])

    def one(i):
        first[i] = sweep(level, 2, i)

    for i in range(height + 2):
        one(i)

    copies = []
    for i in range(height):
        done[i] = sweep(first, 3, i)
        copies.append(pltpu.make_async_copy(done.at[i], out.at[i], sems.at[i]))
        copies[-1].start()
    for copy in copies:
        copy.wait()


def fine_part(dom, perm, source, layers):
    height, nx, ny = perm[0].shape
    field = lambda *lead: pltpu.VMEM(lead + (nx, ny), F32)
    vmem = pl.BlockSpec(memory_space=pltpu.VMEM)
    sides = pl.pallas_call(
        side_kernel,
        out_shape=jax.ShapeDtypeStruct((5, height, nx, ny), F32),
        in_specs=[vmem],
        out_specs=vmem,
        compiler_params=pltpu.CompilerParams(vmem_limit_bytes=VMEM_LIMIT),
        name="sides",
    )(perm[0])
    smem = pl.BlockSpec(memory_space=pltpu.SMEM)
    return pl.pallas_call(
        functools.partial(fine_kernel, layers),
        out_shape=(
            jax.ShapeDtypeStruct((6, height + 6, nx, ny), F32),
            jax.ShapeDtypeStruct((height + 6, nx, ny), F32),
            jax.ShapeDtypeStruct((height + 4, nx, ny), F32),
            jax.ShapeDtypeStruct((height // 2, nx // 2, ny), F32),
        ),
        in_specs=[smem] + [vmem] * 7,
        out_specs=(vmem,) * 4,
        scratch_shapes=[
            field(3 * height),
            field(3 * height),
            field(height + 6),
            field(height // 2),
            field(height // 2),
        ],
        compiler_params=pltpu.CompilerParams(vmem_limit_bytes=VMEM_LIMIT),
        name="fine",
    )(dom, sides, *perm, *source)


def coarse_part(dom, parts, coefs, const, values, height):
    _, nx, ny = values.shape
    field = lambda *shape: pltpu.VMEM(shape, F32)
    whole = (len(parts),) + parts[0].shape
    grid1 = Packed(whole[0] * whole[1], nx // 2, ny // 2)
    grid2 = grid1.coarser()
    pads1 = field(grid1.planes // 2, grid1.nx, LANES)
    pads2 = field(grid2.planes // 2, grid2.nx, LANES)
    vmem = pl.BlockSpec(memory_space=pltpu.VMEM)
    smem = pl.BlockSpec(memory_space=pltpu.SMEM)
    return pl.pallas_call(
        functools.partial(coarse_kernel, whole[0]),
        out_shape=jax.ShapeDtypeStruct((height, nx, ny), F32),
        in_specs=[smem] + [vmem] * (whole[0] + 3),
        out_specs=pl.BlockSpec(memory_space=pl.ANY),
        scratch_shapes=[
            field(*whole),
            field(*values.shape),
            field(height + 2, nx, ny),
            pads1, pads1, pads2, pads2,
            field(grid1.planes, grid1.nx, LANES),
            field(1, Flat(grid2).rows, LANES),
            field(1, Flat(grid2).rows, LANES),
            field(Flat(grid2).buffer_rows, LANES),
            field(height, nx, ny),
            pltpu.SemaphoreType.DMA((height,)),
        ],
        compiler_params=pltpu.CompilerParams(vmem_limit_bytes=VMEM_LIMIT),
        name="coarse",
    )(dom, *(parts[k] for k in swap_order(len(parts))), coefs, const, values)


def swaps(x, axis, step):
    return lax.ppermute(x, axis, [(i, i ^ step) for i in range(lax.axis_size(axis))])


def other_side(x):
    props, domains = lax.axis_size("prop"), lax.axis_size("dom")
    pairs = []
    for p in range(props):
        for d in range(domains):
            end = d in (0, domains - 1)
            partner = ((p ^ 1) * domains + d) if end else (p * domains + ((d + 1) ^ 1) - 1)
            pairs.append((p * domains + d, partner))
    return lax.ppermute(x, ("prop", "dom"), pairs)


def source_side(x):
    props, domains = lax.axis_size("prop"), lax.axis_size("dom")
    pairs = []
    for p in range(props):
        for d in range(domains):
            if d in (0, domains - 1):
                target = (p ^ 1) * domains + (d if p % 2 == 0 else d ^ 1)
            elif p % 2 == 0:
                target = p * domains + (d ^ 1)
            else:
                target = p * domains + ((d + 1) ^ 1) - 1
            pairs.append((p * domains + d, target))
    return lax.ppermute(x, ("prop", "dom"), pairs)


def from_accepted(mine, accepted, beside):
    props = lax.axis_size("prop")
    apart = lax.axis_index("prop") ^ accepted
    own = SHRINK * mine
    step = props // 2
    came = swaps(mine, "prop", step)
    came, own, beside = lax.optimization_barrier((came, own, beside))
    current = jnp.where(apart & step, SHRINK * came, own)
    while step > 1:
        step //= 2
        came = jnp.concatenate([swaps(x, "prop", step) for x in jnp.split(current, 2)])
        current = jnp.where(apart & step, came, current)
    return current, beside


def gather_parts(mine):
    domains = lax.axis_size("dom")
    parts = {0: mine}
    for step in range(0, domains, 2):
        if step:
            parts[step] = swaps(mine, "dom", step)
        parts[step + 1] = swaps(parts[step], "dom", 1)
    return [parts[k] for k in range(domains)]


def body(states, accepted, noise, source):
    domains = lax.axis_size("dom")
    height = source.shape[0]
    dom = jnp.stack([lax.axis_index("dom"), lax.axis_index("prop")]).astype(jnp.int32)
    near = source_side(source)
    current, noise_part = from_accepted(states[0], accepted[0], BETA * noise[0])
    perm = jnp.exp(current + noise_part)
    _, source, near = lax.optimization_barrier((perm, source, near))
    perms = (perm, other_side(perm), swaps(perm, "dom", 1))
    sources = (OMEGA * source, near, swaps(near, "prop", 1))
    *level, coarse = fine_part(dom, perms, sources, domains * height)
    return coarse_part(dom, gather_parts(coarse), *level, height)[None]


def solution(mesh):
    in_specs = (
        P("prop", "dom", None, None),
        P(),
        P("prop", "dom", None, None),
        P("dom", None, None),
    )
    out_specs = P("prop", "dom", None, None)
    return jax.shard_map(body, mesh=mesh, in_specs=in_specs, out_specs=out_specs, check_vma=False)
```

```python
import functools
import math

import jax
import jax.numpy as jnp
from jax import lax
from jax.experimental import pallas as pl
from jax.experimental.pallas import tpu as pltpu
from jax.sharding import PartitionSpec as P

COARSE_SWEEPS = 64
POWER = 3
OMEGA = 0.7
KEEP = 1.0 - OMEGA
BETA = 0.4
SHRINK = math.sqrt(1.0 - BETA * BETA)
ZSCALE = 16.0
LANES = 128
VMEM_LIMIT = 40 * 1024 * 1024
F32 = jnp.float32
WEST, EAST, SOUTH, NORTH, BELOW, ABOVE, CONST = range(7)


def iota(shape, dim):
    return lax.broadcasted_iota(jnp.int32, shape, dim)


def roll(x, amount, axis):
    axis = axis % x.ndim
    return pltpu.roll(x, amount % x.shape[axis], axis)


def inverse_of(x):
    guess = pl.reciprocal(x, approx=True)
    return guess * (2.0 - x * guess)


def harmonic(a, b):
    return (2.0 * a) * b * inverse_of(a + b)


def selector_dot(parts, selector):
    x = jnp.concatenate(parts, axis=0) if len(parts) > 1 else parts[0]
    rows = x.shape[0]
    high = x.astype(jnp.bfloat16).astype(F32)
    rest = x - high
    middle = rest.astype(jnp.bfloat16).astype(F32)
    terms = jnp.concatenate([high, middle], axis=0).astype(jnp.bfloat16)
    y = jnp.dot(terms, selector, preferred_element_type=F32)
    total = y[:rows] + y[rows:]
    height = parts[0].shape[0]
    return [total[i * height : (i + 1) * height] for i in range(len(parts))]


def side_faces(perm, ny):
    shape = perm.shape
    rows = iota(shape, 0)
    columns = iota(shape, 1) & (ny - 1)
    west = jnp.where(rows == 0, 0.0, harmonic(perm, roll(perm, 1, 0)))
    east = roll(west, -1, 0)
    south = jnp.where(columns == 0, 0.0, harmonic(perm, roll(perm, 1, 1)))
    north = roll(south, -1, 1)
    ends = jnp.where(rows == 0, perm, 0.0) + jnp.where(rows == shape[0] - 1, perm, 0.0)
    ends = ends + jnp.where(columns == 0, perm, 0.0) + jnp.where(columns == ny - 1, perm, 0.0)
    return west, east, south, north, ((west + east) + (south + north)) + ends


def face_terms(perm, below, above, ny):
    *sides, total = side_faces(perm, ny)
    return (*sides, below, above), total + (below + above)


def stencil(values, lower, upper, coefs, base):
    x = coefs[0] * roll(values, 1, 0) + coefs[1] * roll(values, -1, 0)
    y = coefs[2] * roll(values, 1, 1) + coefs[3] * roll(values, -1, 1)
    z = coefs[4] * lower + coefs[5] * upper
    return (x + y) + (z + base)


def lane_selector(groups, ny, step, spread=False):
    shape = (LANES, step * LANES) if spread else (step * LANES, LANES)
    source, target = iota(shape, int(spread)), iota(shape, 1 - int(spread))
    bits = ny.bit_length() - 1
    lane = source & (LANES - 1)
    group = (lane >> bits) * step + (source >> 7)
    wanted = (group << (bits - 1)) + ((lane & (ny - 1)) >> 1)
    return jnp.where((target == wanted) & (lane < groups * ny), 1.0, 0.0).astype(jnp.bfloat16)


def side_kernel(perm, out):
    for i in range(perm.shape[0]):
        for k, x in enumerate(side_faces(perm[i], LANES)):
            out[k, i] = x


def fine_kernel(
    layers,
    dom_ref, sides,
    per, per_other, per_pair,
    src, src_near, src_next,
    coef, const, values, coarse_out,
    perm, right, diag, pair_right, pair_perm,
):
    height = per.shape[0]
    dom = dom_ref[0]
    pair_at = jnp.where(lax.rem(dom, 2) == 0, 2 * height, 0)
    other_at = 2 * height - pair_at

    near_at = jnp.where(lax.rem(dom_ref[1], 2) == 0, pair_at, other_at)
    next_at = 2 * height - near_at
    for i in range(height):
        for at, p in ((height, per), (pair_at, per_pair), (other_at, per_other)):
            perm[at + i] = p[i]
        right[height + i] = src[i]
        right[near_at + i] = OMEGA * src_near[i]
        right[next_at + i] = OMEGA * src_next[i]

    def face(i):
        z = dom * height + i - 3
        scale = jnp.where((z > 0) & (z < layers), ZSCALE, 0.0)
        at = height - 3 + i
        return scale * harmonic(perm[at - 1], perm[at])

    above = face(0)
    for i in range(height + 6):
        at = height - 3 + i
        below, above = above, face(i + 1)
        if 3 <= i < height + 3:
            faces = tuple(sides[k, i - 3] for k in range(4)) + (below, above)
            diagonal = sides[4, i - 3] + (below + above)
        else:
            faces, diagonal = face_terms(perm[at], below, above, LANES)
        inverse = inverse_of(diagonal)
        const[i] = inverse * right[at]
        if 0 < i < height + 5:
            inverse = OMEGA * inverse
            for k in range(6):
                coef[k, i] = inverse * faces[k]
        if 3 <= i < height + 3:
            diag[i] = diagonal

    def first(i):
        start = const[i + 1]
        near = [coef[k, i + 1] for k in range(6)]
        values[i] = stencil(start, const[i], const[i + 2], near, (1.0 + KEEP) * start)

    for i in range(height + 4):
        first(i)

    def residue(i):
        centre = values[i + 2]
        base = const[i + 3] - OMEGA * centre
        near = [coef[k, i + 3] for k in range(6)]
        scaled = stencil(centre, values[i + 1], values[i + 3], near, base)
        return scaled * (diag[i + 3] * (1.0 / OMEGA))

    for m in range(height // 2):
        pair_right[m] = residue(2 * m) + residue(2 * m + 1)
        pair_perm[m] = (perm[height + 2 * m] + perm[height + 2 * m + 1]) * 0.125
    half = pair_right.shape[1] // 2
    rows = []
    for m in range(height // 2):
        both = [x[m, pl.ds(0, half, 2), :] + x[m, pl.ds(1, half, 2), :] for x in (pair_right, pair_perm)]
        rows.append(jnp.concatenate(both, axis=1))
    for m, x in enumerate(selector_dot(rows, lane_selector(1, LANES, 2))):
        coarse_out[m] = x


class Packed:
    def __init__(self, nz, nx, ny):
        self.nz, self.nx, self.ny = nz, nx, ny
        self.groups = min(LANES // ny, nz)
        self.planes = nz // self.groups

    def lower(self, planes, p):
        return planes[p - 1] if p else roll(planes[self.planes - 1], self.ny, 1)

    def upper(self, planes, p):
        return planes[p + 1] if p + 1 < self.planes else roll(planes[0], -self.ny, 1)

    def system(self, perm, level):
        lane = iota((self.nx, LANES), 1)
        used = lane < self.groups * self.ny
        if self.groups * self.ny < LANES:
            perm = [jnp.where(used, x, 1.0) for x in perm]
        coefs, factors, diagonals = [], [], []
        inner = [ZSCALE * harmonic(a, b) for a, b in zip(perm[:-1], perm[1:])]
        wrapped = ZSCALE * harmonic(perm[-1], roll(perm[0], -self.ny, 1))
        last = jnp.where(lane < (self.groups - 1) * self.ny, wrapped, 0.0)
        z_faces = [roll(last, self.ny, 1)] + inner + [last]
        for p in range(self.planes):
            faces, diagonal = face_terms(perm[p], z_faces[p], z_faces[p + 1], self.ny)
            inverse = OMEGA * inverse_of(diagonal)
            coefs.append([inverse * face for face in faces])
            factors.append(inverse * (4.0**-level))
            diagonals.append(diagonal * (4.0**level / OMEGA))
        return coefs, factors, diagonals

    def apply(self, values, coefs, bases):
        return [
            stencil(values[p], self.lower(values, p), self.upper(values, p), coefs[p], bases[p])
            for p in range(self.planes)
        ]

    def sweep(self, values, coefs, const):
        return self.apply(values, coefs, [KEEP * v + c for v, c in zip(values, const)])

    def coarser(self):
        return Packed(self.nz // 2, self.nx // 2, self.ny // 2)

    def restrict(self, fields, pads):
        coarse = self.coarser()
        step = coarse.groups // self.groups
        half = coarse.nx
        parts = []
        for values, pad in zip(fields, pads):
            rows = []
            for m in range(self.planes // 2):
                pad[m] = values[2 * m] + values[2 * m + 1]
                rows.append(pad[m, pl.ds(0, half, 2), :] + pad[m, pl.ds(1, half, 2), :])
            for p in range(coarse.planes):
                blocks = rows[p :: coarse.planes]
                parts.append(jnp.concatenate(blocks, axis=1) if step > 1 else blocks[0])
        sums = selector_dot(parts, lane_selector(self.groups, self.ny, step))
        return [sums[i : i + coarse.planes] for i in range(0, len(sums), coarse.planes)]

    def prolong(self, values, pad):
        coarse = self.coarser()
        step = coarse.groups // self.groups
        half = coarse.nx
        wide = selector_dot(values, lane_selector(self.groups, self.ny, step, spread=True))
        out = []
        for m in range(self.planes // 2):
            j, p = divmod(m, coarse.planes)
            plane = wide[p][:, j * LANES : (j + 1) * LANES]
            pad[m, pl.ds(0, half, 2), :] = plane
            pad[m, pl.ds(1, half, 2), :] = plane
            out += [pad[m], pad[m]]
        return out


class Flat:
    def __init__(self, finer):
        coarse = finer.coarser()
        self.finer = finer
        self.nz, self.nx, self.ny = coarse.nz, coarse.nx, coarse.ny
        self.pairs = finer.planes // 2
        self.rows = max(8, self.nz)
        self.shape = (self.rows, LANES)
        self.buffer_rows = 2 * (self.rows + 2 * POWER)

    def selector(self, spread=False):
        wide = self.finer.groups * LANES
        shape = (wide, LANES) if spread else (LANES, wide)
        fine, flat = iota(shape, int(spread)), iota(shape, 1 - int(spread))
        bits = self.finer.ny.bit_length() - 1
        same = (fine >> bits) == (flat >> 7)
        same &= ((fine & (self.finer.ny - 1)) >> 1) == (flat & (self.ny - 1))
        return jnp.where(same, 1.0, 0.0).astype(jnp.bfloat16)

    def diagonal(self):
        shape = (self.nx, LANES)
        return iota(shape, 0) == (iota(shape, 1) >> (self.ny.bit_length() - 1))

    def restrict(self, fields, pads, pack):
        parts = []
        for values, pad in zip(fields, pads):
            for m in range(self.pairs):
                pad[m] = values[2 * m] + values[2 * m + 1]
                parts.append(pad[m, pl.ds(0, self.nx, 2), :] + pad[m, pl.ds(1, self.nx, 2), :])
        sums = selector_dot(parts, self.selector())
        mask = self.diagonal()
        pack[...] = jnp.zeros_like(pack)
        for i in range(len(fields)):
            for z in range(self.nz):
                s, m = divmod(z, self.pairs)
                block = sums[i * self.pairs + m][:, s * LANES : (s + 1) * LANES]
                row = jnp.sum(jnp.where(mask, block, 0.0), axis=0, keepdims=True)
                pack[i, z : z + 1, :] = row
        return [pack[i] for i in range(len(fields))]

    def prolong(self, values, pad, pack):
        mask = self.diagonal()
        pack[0] = values
        parts = []
        for m in range(self.pairs):
            layers = [s * self.pairs + m for s in range(self.finer.groups)]
            spread = [jnp.broadcast_to(pack[0, z : z + 1, :], mask.shape) for z in layers]
            parts.append(jnp.concatenate([jnp.where(mask, x, 0.0) for x in spread], axis=1))
        out = []
        for m, wide in enumerate(selector_dot(parts, self.selector(spread=True))):
            pad[m, pl.ds(0, self.nx, 2), :] = wide
            pad[m, pl.ds(1, self.nx, 2), :] = wide
            out += [pad[m], pad[m]]
        return out

    def system(self, perm, level):
        lane, row = iota(self.shape, 1), iota(self.shape, 0)
        x, y = lane >> (self.ny.bit_length() - 1), lane & (self.ny - 1)
        real = row < self.nz
        perm = jnp.where(real, perm, 1.0)
        west = jnp.where(x == 0, 0.0, harmonic(perm, roll(perm, self.ny, 1)))
        east = roll(west, -self.ny, 1)
        south = jnp.where(y == 0, 0.0, harmonic(perm, roll(perm, 1, 1)))
        north = roll(south, -1, 1)
        below = ZSCALE * harmonic(perm, roll(perm, 1, 0))
        below = jnp.where((row > 0) & real, below, 0.0)
        above = roll(below, -1, 0)
        faces = [west, east, south, north, below, above]
        ends = (x == 0, x == self.nx - 1, y == 0, y == self.ny - 1)
        diagonal = tree_sum(faces + [jnp.where(end, perm, 0.0) for end in ends])
        inverse = jnp.where(real, OMEGA * inverse_of(diagonal), 0.0)
        keys = ((-1, 0, 0), (1, 0, 0), (0, -1, 0), (0, 1, 0), (0, 0, -1), (0, 0, 1))
        terms = {key: inverse * face for key, face in zip(keys, faces)}
        terms[0, 0, 0] = jnp.full(self.shape, KEEP, F32)
        return terms, inverse * (4.0**-level)

    def product(self, first, second):
        sums = {}
        for (dx, dy, dz), coef in first.items():
            for other, moved in second.items():
                if dz:
                    moved = roll(moved, -dz, 0)
                if dx or dy:
                    moved = roll(moved, -(dx * self.ny + dy), 1)
                total = tuple(a + b for a, b in zip((dx, dy, dz), other))
                sums.setdefault(total, []).append(coef * moved)
        return {key: tree_sum(parts) for key, parts in sums.items()}

    def apply(self, terms, values, base, buffer):
        buffer[pl.ds(2 * POWER, self.rows, 2), :] = values
        moved = {}
        for dx, dy, dz in sorted(terms, key=lambda key: abs(key[2])):
            if (0, 0, dz) not in moved:
                moved[0, 0, dz] = buffer[pl.ds(2 * (POWER + dz), self.rows, 2), :] if dz else values
            if dx or dy:
                moved[dx, dy, dz] = roll(moved[0, 0, dz], -(dx * self.ny + dy), 1)
        return tree_sum([base] + [coef * moved[key] for key, coef in terms.items()])

    def prepare(self, perm, level):
        terms, factor = self.system(perm, level)
        power = terms
        for _ in range(POWER - 1):
            power = self.product(terms, power)
        return terms, power, factor

    def solve(self, right, prepared, buffer):
        terms, power, factor = prepared
        const = factor * right
        buffer[...] = jnp.zeros_like(buffer)
        base = const
        for _ in range(POWER - 1):
            base = self.apply(terms, base, const, buffer)
        whole = COARSE_SWEEPS % POWER == 0
        values = base if whole else const
        steps = (COARSE_SWEEPS - 1) // POWER
        assert steps * POWER + (POWER if whole else 1) == COARSE_SWEEPS
        for _ in range(steps):
            values = self.apply(power, values, base, buffer)
        return values


def tree_sum(parts):
    while len(parts) > 1:
        odd = parts[len(parts) // 2 * 2 :]
        parts = [a + b for a, b in zip(parts[::2], parts[1::2])] + odd
    return parts[0]


def packed_cycle(grid, right, perm, level, pads, packs, buffer):
    pad_right, pad_perm = pads[0]
    coefs, factors, diagonals = grid.system(perm, level)
    if len(pads) > 1:
        (coarse_perm,) = grid.restrict([perm], [pad_perm])
    else:
        flat = Flat(grid)
        (coarse_perm,) = flat.restrict([perm], [pad_perm], packs[1])
        prepared = flat.prepare(coarse_perm * 0.125, level + 1)
    const = [f * r for f, r in zip(factors, right)]
    values = grid.sweep(const, coefs, const)
    scaled = grid.apply(values, coefs, [c - OMEGA * v for c, v in zip(const, values)])
    residue = [r * d for r, d in zip(scaled, diagonals)]
    if len(pads) > 1:
        (coarse_right,) = grid.restrict([residue], [pad_right])
        coarse_perm = [x * 0.125 for x in coarse_perm]
        update = packed_cycle(
            grid.coarser(), coarse_right, coarse_perm, level + 1, pads[1:], packs, buffer
        )
        update = grid.prolong(update, pad_right)
    else:
        (coarse_right,) = flat.restrict([residue], [pad_right], packs[0])
        update = flat.prolong(flat.solve(coarse_right, prepared, buffer), pad_right, packs[0])
    values = [v + e for v, e in zip(values, update)]
    for _ in range(2):
        values = grid.sweep(values, coefs, const)
    return values


def swap_order(domains):
    steps = [0, domains - 2] + list(range(2, domains - 2, 2))
    return [step + 1 - odd for step in steps[::-1] for odd in range(2)]


def coarse_kernel(
    count, dom_ref, *refs,
):
    parts = [refs[swap_order(count).index(k)] for k in range(count)]
    refs = refs[count:]
    coef, const, before, out, gathered, *refs = refs
    coarse_steps(parts, dom_ref, gathered, coef, const, before, out, *refs)


def coarse_steps(
    parts, dom_ref, gathered, coef, const, before, out,
    level, first, pad_right1, pad_perm1, pad_right2, pad_perm2, update, pack, pack_perm, buffer,
    done, sems,
):
    height = out.shape[0]
    dom = dom_ref[0]
    domains, own, nx, _ = gathered.shape
    for step, part in enumerate(parts):
        gathered[dom ^ step] = part[...]
    ny = LANES // 2
    grid = Packed(domains * own, nx, ny)
    left = iota((nx, LANES), 1) < ny
    right, perm = [], []
    for p in range(grid.planes):
        a = gathered[p // own, p % own]
        q = grid.planes + p
        b = gathered[q // own, q % own]
        right.append(jnp.where(left, a, roll(b, ny, 1)))
        perm.append(jnp.where(left, roll(a, ny, 1), b))
    pads = [(pad_right1, pad_perm1), (pad_right2, pad_perm2)]
    solved = packed_cycle(grid, right, perm, 1, pads, (pack, pack_perm), buffer)
    for p in range(grid.planes):
        update[p] = solved[p]
    planes, group = [], []
    for j in range(own + 2):
        layer = jnp.clip(dom * own + j - 1, 0, grid.nz - 1)
        group.append(layer // grid.planes)
        planes.append(update[lax.rem(layer, grid.planes)])
    for j, wide in enumerate(selector_dot(planes, lane_selector(1, LANES, 2, spread=True))):
        plane = jnp.where(group[j] == 0, wide[:, :LANES], wide[:, LANES:])
        pad = first.at[0]
        pad[pl.ds(0, nx, 2), :] = plane
        pad[pl.ds(1, nx, 2), :] = plane
        whole = first[0]
        level[2 * j] = before[2 * j] + whole
        level[2 * j + 1] = before[2 * j + 1] + whole

    def sweep(source, at, i):
        centre = source[i + 1]
        near = [coef[k, at + i] for k in range(6)]
        return stencil(centre, source[i], source[i + 2], near, KEEP * centre + const[at + i])

    def one(i):
        first[i] = sweep(level, 2, i)

    for i in range(height + 2):
        one(i)

    copies = []
    for i in range(height):
        done[i] = sweep(first, 3, i)
        copies.append(pltpu.make_async_copy(done.at[i], out.at[i], sems.at[i]))
        copies[-1].start()
    for copy in copies:
        copy.wait()


def fine_part(dom, perm, source, layers):
    height, nx, ny = perm[0].shape
    field = lambda *lead: pltpu.VMEM(lead + (nx, ny), F32)
    vmem = pl.BlockSpec(memory_space=pltpu.VMEM)
    sides = pl.pallas_call(
        side_kernel,
        out_shape=jax.ShapeDtypeStruct((5, height, nx, ny), F32),
        in_specs=[vmem],
        out_specs=vmem,
        compiler_params=pltpu.CompilerParams(vmem_limit_bytes=VMEM_LIMIT),
        name="sides",
    )(perm[0])
    smem = pl.BlockSpec(memory_space=pltpu.SMEM)
    return pl.pallas_call(
        functools.partial(fine_kernel, layers),
        out_shape=(
            jax.ShapeDtypeStruct((6, height + 6, nx, ny), F32),
            jax.ShapeDtypeStruct((height + 6, nx, ny), F32),
            jax.ShapeDtypeStruct((height + 4, nx, ny), F32),
            jax.ShapeDtypeStruct((height // 2, nx // 2, ny), F32),
        ),
        in_specs=[smem] + [vmem] * 7,
        out_specs=(vmem,) * 4,
        scratch_shapes=[
            field(3 * height),
            field(3 * height),
            field(height + 6),
            field(height // 2),
            field(height // 2),
        ],
        compiler_params=pltpu.CompilerParams(vmem_limit_bytes=VMEM_LIMIT),
        name="fine",
    )(dom, sides, *perm, *source)


def coarse_part(dom, parts, coefs, const, values, height):
    _, nx, ny = values.shape
    field = lambda *shape: pltpu.VMEM(shape, F32)
    whole = (len(parts),) + parts[0].shape
    grid1 = Packed(whole[0] * whole[1], nx // 2, ny // 2)
    grid2 = grid1.coarser()
    pads1 = field(grid1.planes // 2, grid1.nx, LANES)
    pads2 = field(grid2.planes // 2, grid2.nx, LANES)
    vmem = pl.BlockSpec(memory_space=pltpu.VMEM)
    smem = pl.BlockSpec(memory_space=pltpu.SMEM)
    return pl.pallas_call(
        functools.partial(coarse_kernel, whole[0]),
        out_shape=jax.ShapeDtypeStruct((height, nx, ny), F32),
        in_specs=[smem] + [vmem] * (whole[0] + 3),
        out_specs=pl.BlockSpec(memory_space=pl.ANY),
        scratch_shapes=[
            field(*whole),
            field(*values.shape),
            field(height + 2, nx, ny),
            pads1, pads1, pads2, pads2,
            field(grid1.planes, grid1.nx, LANES),
            field(1, Flat(grid2).rows, LANES),
            field(1, Flat(grid2).rows, LANES),
            field(Flat(grid2).buffer_rows, LANES),
            field(height, nx, ny),
            pltpu.SemaphoreType.DMA((height,)),
        ],
        compiler_params=pltpu.CompilerParams(vmem_limit_bytes=VMEM_LIMIT),
        name="coarse",
    )(dom, *(parts[k] for k in swap_order(len(parts))), coefs, const, values)


def swaps(x, axis, step):
    return lax.ppermute(x, axis, [(i, i ^ step) for i in range(lax.axis_size(axis))])


def other_side(x):
    props, domains = lax.axis_size("prop"), lax.axis_size("dom")
    pairs = []
    for p in range(props):
        for d in range(domains):
            end = d in (0, domains - 1)
            partner = ((p ^ 1) * domains + d) if end else (p * domains + ((d + 1) ^ 1) - 1)
            pairs.append((p * domains + d, partner))
    return lax.ppermute(x, ("prop", "dom"), pairs)


def source_side(x):
    props, domains = lax.axis_size("prop"), lax.axis_size("dom")
    pairs = []
    for p in range(props):
        for d in range(domains):
            if d in (0, domains - 1):
                target = (p ^ 1) * domains + (d if p % 2 == 0 else d ^ 1)
            elif p % 2 == 0:
                target = p * domains + (d ^ 1)
            else:
                target = p * domains + ((d + 1) ^ 1) - 1
            pairs.append((p * domains + d, target))
    return lax.ppermute(x, ("prop", "dom"), pairs)


def from_accepted(mine, accepted, beside):
    props = lax.axis_size("prop")
    apart = lax.axis_index("prop") ^ accepted
    own = SHRINK * mine
    step = props // 2
    came = swaps(mine, "prop", step)
    came, own, beside = lax.optimization_barrier((came, own, beside))
    current = jnp.where(apart & step, SHRINK * came, own)
    while step > 1:
        step //= 2
        came = jnp.concatenate([swaps(x, "prop", step) for x in jnp.split(current, 2)])
        current = jnp.where(apart & step, came, current)
    return current, beside


def gather_parts(mine):
    domains = lax.axis_size("dom")
    parts = {0: mine}
    for step in range(0, domains, 2):
        if step:
            parts[step] = swaps(mine, "dom", step)
        parts[step + 1] = swaps(parts[step], "dom", 1)
    return [parts[k] for k in range(domains)]


def body(states, accepted, noise, source):
    domains = lax.axis_size("dom")
    height = source.shape[0]
    dom = jnp.stack([lax.axis_index("dom"), lax.axis_index("prop")]).astype(jnp.int32)
    near = source_side(source)
    current, noise_part = from_accepted(states[0], accepted[0], BETA * noise[0])
    perm = jnp.exp(current + noise_part)
    _, source, near = lax.optimization_barrier((perm, source, near))
    perms = (perm, other_side(perm), swaps(perm, "dom", 1))
    sources = (OMEGA * source, near, swaps(near, "prop", 1))
    *level, coarse = fine_part(dom, perms, sources, domains * height)
    return coarse_part(dom, gather_parts(coarse), *level, height)[None]


def solution(mesh):
    in_specs = (
        P("prop", "dom", None, None),
        P(),
        P("prop", "dom", None, None),
        P("dom", None, None),
    )
    out_specs = P("prop", "dom", None, None)
    return jax.shard_map(body, mesh=mesh, in_specs=in_specs, out_specs=out_specs, check_vma=False)
```

```python
import functools
import math

import jax
import jax.numpy as jnp
from jax import lax
from jax.experimental import pallas as pl
from jax.experimental.pallas import tpu as pltpu
from jax.sharding import PartitionSpec as P

COARSE_SWEEPS = 64
POWER = 2
OMEGA = 0.7
KEEP = 1.0 - OMEGA
BETA = 0.4
SHRINK = math.sqrt(1.0 - BETA * BETA)
ZSCALE = 16.0
LANES = 128
VMEM_LIMIT = 40 * 1024 * 1024
F32 = jnp.float32
WEST, EAST, SOUTH, NORTH, BELOW, ABOVE, CONST = range(7)


def iota(shape, dim):
    return lax.broadcasted_iota(jnp.int32, shape, dim)


def roll(x, amount, axis):
    axis = axis % x.ndim
    return pltpu.roll(x, amount % x.shape[axis], axis)


def inverse_of(x):
    guess = pl.reciprocal(x, approx=True)
    return guess * (2.0 - x * guess)


def harmonic(a, b):
    return (2.0 * a) * b * inverse_of(a + b)


def selector_dot(parts, selector):
    x = jnp.concatenate(parts, axis=0) if len(parts) > 1 else parts[0]
    rows = x.shape[0]
    high = x.astype(jnp.bfloat16).astype(F32)
    rest = x - high
    middle = rest.astype(jnp.bfloat16).astype(F32)
    terms = jnp.concatenate([high, middle], axis=0).astype(jnp.bfloat16)
    y = jnp.dot(terms, selector, preferred_element_type=F32)
    total = y[:rows] + y[rows:]
    height = parts[0].shape[0]
    return [total[i * height : (i + 1) * height] for i in range(len(parts))]


def side_faces(perm, ny):
    shape = perm.shape
    rows = iota(shape, 0)
    columns = iota(shape, 1) & (ny - 1)
    west = jnp.where(rows == 0, 0.0, harmonic(perm, roll(perm, 1, 0)))
    east = roll(west, -1, 0)
    south = jnp.where(columns == 0, 0.0, harmonic(perm, roll(perm, 1, 1)))
    north = roll(south, -1, 1)
    ends = jnp.where(rows == 0, perm, 0.0) + jnp.where(rows == shape[0] - 1, perm, 0.0)
    ends = ends + jnp.where(columns == 0, perm, 0.0) + jnp.where(columns == ny - 1, perm, 0.0)
    return west, east, south, north, ((west + east) + (south + north)) + ends


def face_terms(perm, below, above, ny):
    *sides, total = side_faces(perm, ny)
    return (*sides, below, above), total + (below + above)


def stencil(values, lower, upper, coefs, base):
    x = coefs[0] * roll(values, 1, 0) + coefs[1] * roll(values, -1, 0)
    y = coefs[2] * roll(values, 1, 1) + coefs[3] * roll(values, -1, 1)
    z = coefs[4] * lower + coefs[5] * upper
    return (x + y) + (z + base)


def lane_selector(groups, ny, step, spread=False):
    shape = (LANES, step * LANES) if spread else (step * LANES, LANES)
    source, target = iota(shape, int(spread)), iota(shape, 1 - int(spread))
    bits = ny.bit_length() - 1
    lane = source & (LANES - 1)
    group = (lane >> bits) * step + (source >> 7)
    wanted = (group << (bits - 1)) + ((lane & (ny - 1)) >> 1)
    return jnp.where((target == wanted) & (lane < groups * ny), 1.0, 0.0).astype(jnp.bfloat16)


def side_kernel(perm, out):
    for i in range(perm.shape[0]):
        for k, x in enumerate(side_faces(perm[i], LANES)):
            out[k, i] = x


def fine_kernel(
    layers,
    dom_ref, sides,
    per, per_other, per_pair,
    src, src_near, src_next,
    coef, const, values, coarse_out,
    perm, right, diag, pair_right, pair_perm,
):
    height = per.shape[0]
    dom = dom_ref[0]
    pair_at = jnp.where(lax.rem(dom, 2) == 0, 2 * height, 0)
    other_at = 2 * height - pair_at

    near_at = jnp.where(lax.rem(dom_ref[1], 2) == 0, pair_at, other_at)
    next_at = 2 * height - near_at
    for i in range(height):
        for at, p in ((height, per), (pair_at, per_pair), (other_at, per_other)):
            perm[at + i] = p[i]
        right[height + i] = src[i]
        right[near_at + i] = OMEGA * src_near[i]
        right[next_at + i] = OMEGA * src_next[i]

    def face(i):
        z = dom * height + i - 3
        scale = jnp.where((z > 0) & (z < layers), ZSCALE, 0.0)
        at = height - 3 + i
        return scale * harmonic(perm[at - 1], perm[at])

    above = face(0)
    for i in range(height + 6):
        at = height - 3 + i
        below, above = above, face(i + 1)
        if 3 <= i < height + 3:
            faces = tuple(sides[k, i - 3] for k in range(4)) + (below, above)
            diagonal = sides[4, i - 3] + (below + above)
        else:
            faces, diagonal = face_terms(perm[at], below, above, LANES)
        inverse = inverse_of(diagonal)
        const[i] = inverse * right[at]
        if 0 < i < height + 5:
            inverse = OMEGA * inverse
            for k in range(6):
                coef[k, i] = inverse * faces[k]
        if 3 <= i < height + 3:
            diag[i] = diagonal

    def first(i):
        start = const[i + 1]
        near = [coef[k, i + 1] for k in range(6)]
        values[i] = stencil(start, const[i], const[i + 2], near, (1.0 + KEEP) * start)

    for i in range(height + 4):
        first(i)

    def residue(i):
        centre = values[i + 2]
        base = const[i + 3] - OMEGA * centre
        near = [coef[k, i + 3] for k in range(6)]
        scaled = stencil(centre, values[i + 1], values[i + 3], near, base)
        return scaled * (diag[i + 3] * (1.0 / OMEGA))

    for m in range(height // 2):
        pair_right[m] = residue(2 * m) + residue(2 * m + 1)
        pair_perm[m] = (perm[height + 2 * m] + perm[height + 2 * m + 1]) * 0.125
    half = pair_right.shape[1] // 2
    rows = []
    for m in range(height // 2):
        both = [x[m, pl.ds(0, half, 2), :] + x[m, pl.ds(1, half, 2), :] for x in (pair_right, pair_perm)]
        rows.append(jnp.concatenate(both, axis=1))
    for m, x in enumerate(selector_dot(rows, lane_selector(1, LANES, 2))):
        coarse_out[m] = x


class Packed:
    def __init__(self, nz, nx, ny):
        self.nz, self.nx, self.ny = nz, nx, ny
        self.groups = min(LANES // ny, nz)
        self.planes = nz // self.groups

    def lower(self, planes, p):
        return planes[p - 1] if p else roll(planes[self.planes - 1], self.ny, 1)

    def upper(self, planes, p):
        return planes[p + 1] if p + 1 < self.planes else roll(planes[0], -self.ny, 1)

    def system(self, perm, level):
        lane = iota((self.nx, LANES), 1)
        used = lane < self.groups * self.ny
        if self.groups * self.ny < LANES:
            perm = [jnp.where(used, x, 1.0) for x in perm]
        coefs, factors, diagonals = [], [], []
        inner = [ZSCALE * harmonic(a, b) for a, b in zip(perm[:-1], perm[1:])]
        wrapped = ZSCALE * harmonic(perm[-1], roll(perm[0], -self.ny, 1))
        last = jnp.where(lane < (self.groups - 1) * self.ny, wrapped, 0.0)
        z_faces = [roll(last, self.ny, 1)] + inner + [last]
        for p in range(self.planes):
            faces, diagonal = face_terms(perm[p], z_faces[p], z_faces[p + 1], self.ny)
            inverse = OMEGA * inverse_of(diagonal)
            coefs.append([inverse * face for face in faces])
            factors.append(inverse * (4.0**-level))
            diagonals.append(diagonal * (4.0**level / OMEGA))
        return coefs, factors, diagonals

    def apply(self, values, coefs, bases):
        return [
            stencil(values[p], self.lower(values, p), self.upper(values, p), coefs[p], bases[p])
            for p in range(self.planes)
        ]

    def sweep(self, values, coefs, const):
        return self.apply(values, coefs, [KEEP * v + c for v, c in zip(values, const)])

    def coarser(self):
        return Packed(self.nz // 2, self.nx // 2, self.ny // 2)

    def restrict(self, fields, pads):
        coarse = self.coarser()
        step = coarse.groups // self.groups
        half = coarse.nx
        parts = []
        for values, pad in zip(fields, pads):
            rows = []
            for m in range(self.planes // 2):
                pad[m] = values[2 * m] + values[2 * m + 1]
                rows.append(pad[m, pl.ds(0, half, 2), :] + pad[m, pl.ds(1, half, 2), :])
            for p in range(coarse.planes):
                blocks = rows[p :: coarse.planes]
                parts.append(jnp.concatenate(blocks, axis=1) if step > 1 else blocks[0])
        sums = selector_dot(parts, lane_selector(self.groups, self.ny, step))
        return [sums[i : i + coarse.planes] for i in range(0, len(sums), coarse.planes)]

    def prolong(self, values, pad):
        coarse = self.coarser()
        step = coarse.groups // self.groups
        half = coarse.nx
        wide = selector_dot(values, lane_selector(self.groups, self.ny, step, spread=True))
        out = []
        for m in range(self.planes // 2):
            j, p = divmod(m, coarse.planes)
            plane = wide[p][:, j * LANES : (j + 1) * LANES]
            pad[m, pl.ds(0, half, 2), :] = plane
            pad[m, pl.ds(1, half, 2), :] = plane
            out += [pad[m], pad[m]]
        return out


class Flat:
    def __init__(self, finer):
        coarse = finer.coarser()
        self.finer = finer
        self.nz, self.nx, self.ny = coarse.nz, coarse.nx, coarse.ny
        self.pairs = finer.planes // 2
        self.rows = max(8, self.nz)
        self.shape = (self.rows, LANES)
        self.buffer_rows = 2 * (self.rows + 2 * POWER)

    def selector(self, spread=False):
        wide = self.finer.groups * LANES
        shape = (wide, LANES) if spread else (LANES, wide)
        fine, flat = iota(shape, int(spread)), iota(shape, 1 - int(spread))
        bits = self.finer.ny.bit_length() - 1
        same = (fine >> bits) == (flat >> 7)
        same &= ((fine & (self.finer.ny - 1)) >> 1) == (flat & (self.ny - 1))
        return jnp.where(same, 1.0, 0.0).astype(jnp.bfloat16)

    def diagonal(self):
        shape = (self.nx, LANES)
        return iota(shape, 0) == (iota(shape, 1) >> (self.ny.bit_length() - 1))

    def restrict(self, fields, pads, pack):
        parts = []
        for values, pad in zip(fields, pads):
            for m in range(self.pairs):
                pad[m] = values[2 * m] + values[2 * m + 1]
                parts.append(pad[m, pl.ds(0, self.nx, 2), :] + pad[m, pl.ds(1, self.nx, 2), :])
        sums = selector_dot(parts, self.selector())
        mask = self.diagonal()
        pack[...] = jnp.zeros_like(pack)
        for i in range(len(fields)):
            for z in range(self.nz):
                s, m = divmod(z, self.pairs)
                block = sums[i * self.pairs + m][:, s * LANES : (s + 1) * LANES]
                row = jnp.sum(jnp.where(mask, block, 0.0), axis=0, keepdims=True)
                pack[i, z : z + 1, :] = row
        return [pack[i] for i in range(len(fields))]

    def prolong(self, values, pad, pack):
        mask = self.diagonal()
        pack[0] = values
        parts = []
        for m in range(self.pairs):
            layers = [s * self.pairs + m for s in range(self.finer.groups)]
            spread = [jnp.broadcast_to(pack[0, z : z + 1, :], mask.shape) for z in layers]
            parts.append(jnp.concatenate([jnp.where(mask, x, 0.0) for x in spread], axis=1))
        out = []
        for m, wide in enumerate(selector_dot(parts, self.selector(spread=True))):
            pad[m, pl.ds(0, self.nx, 2), :] = wide
            pad[m, pl.ds(1, self.nx, 2), :] = wide
            out += [pad[m], pad[m]]
        return out

    def system(self, perm, level):
        lane, row = iota(self.shape, 1), iota(self.shape, 0)
        x, y = lane >> (self.ny.bit_length() - 1), lane & (self.ny - 1)
        real = row < self.nz
        perm = jnp.where(real, perm, 1.0)
        west = jnp.where(x == 0, 0.0, harmonic(perm, roll(perm, self.ny, 1)))
        east = roll(west, -self.ny, 1)
        south = jnp.where(y == 0, 0.0, harmonic(perm, roll(perm, 1, 1)))
        north = roll(south, -1, 1)
        below = ZSCALE * harmonic(perm, roll(perm, 1, 0))
        below = jnp.where((row > 0) & real, below, 0.0)
        above = roll(below, -1, 0)
        faces = [west, east, south, north, below, above]
        ends = (x == 0, x == self.nx - 1, y == 0, y == self.ny - 1)
        diagonal = tree_sum(faces + [jnp.where(end, perm, 0.0) for end in ends])
        inverse = jnp.where(real, OMEGA * inverse_of(diagonal), 0.0)
        keys = ((-1, 0, 0), (1, 0, 0), (0, -1, 0), (0, 1, 0), (0, 0, -1), (0, 0, 1))
        terms = {key: inverse * face for key, face in zip(keys, faces)}
        terms[0, 0, 0] = jnp.full(self.shape, KEEP, F32)
        return terms, inverse * (4.0**-level)

    def product(self, first, second):
        sums = {}
        for (dx, dy, dz), coef in first.items():
            for other, moved in second.items():
                if dz:
                    moved = roll(moved, -dz, 0)
                if dx or dy:
                    moved = roll(moved, -(dx * self.ny + dy), 1)
                total = tuple(a + b for a, b in zip((dx, dy, dz), other))
                sums.setdefault(total, []).append(coef * moved)
        return {key: tree_sum(parts) for key, parts in sums.items()}

    def apply(self, terms, values, base, buffer):
        buffer[pl.ds(2 * POWER, self.rows, 2), :] = values
        moved = {}
        for dx, dy, dz in sorted(terms, key=lambda key: abs(key[2])):
            if (0, 0, dz) not in moved:
                moved[0, 0, dz] = buffer[pl.ds(2 * (POWER + dz), self.rows, 2), :] if dz else values
            if dx or dy:
                moved[dx, dy, dz] = roll(moved[0, 0, dz], -(dx * self.ny + dy), 1)
        return tree_sum([base] + [coef * moved[key] for key, coef in terms.items()])

    def prepare(self, perm, level):
        terms, factor = self.system(perm, level)
        power = terms
        for _ in range(POWER - 1):
            power = self.product(terms, power)
        return terms, power, factor

    def solve(self, right, prepared, buffer):
        terms, power, factor = prepared
        const = factor * right
        buffer[...] = jnp.zeros_like(buffer)
        base = const
        for _ in range(POWER - 1):
            base = self.apply(terms, base, const, buffer)
        whole = COARSE_SWEEPS % POWER == 0
        values = base if whole else const
        steps = (COARSE_SWEEPS - 1) // POWER
        assert steps * POWER + (POWER if whole else 1) == COARSE_SWEEPS
        for _ in range(steps):
            values = self.apply(power, values, base, buffer)
        return values


def tree_sum(parts):
    while len(parts) > 1:
        odd = parts[len(parts) // 2 * 2 :]
        parts = [a + b for a, b in zip(parts[::2], parts[1::2])] + odd
    return parts[0]


def packed_cycle(grid, right, perm, level, pads, packs, buffer):
    pad_right, pad_perm = pads[0]
    coefs, factors, diagonals = grid.system(perm, level)
    if len(pads) > 1:
        (coarse_perm,) = grid.restrict([perm], [pad_perm])
    else:
        flat = Flat(grid)
        (coarse_perm,) = flat.restrict([perm], [pad_perm], packs[1])
        prepared = flat.prepare(coarse_perm * 0.125, level + 1)
    const = [f * r for f, r in zip(factors, right)]
    values = grid.sweep(const, coefs, const)
    scaled = grid.apply(values, coefs, [c - OMEGA * v for c, v in zip(const, values)])
    residue = [r * d for r, d in zip(scaled, diagonals)]
    if len(pads) > 1:
        (coarse_right,) = grid.restrict([residue], [pad_right])
        coarse_perm = [x * 0.125 for x in coarse_perm]
        update = packed_cycle(
            grid.coarser(), coarse_right, coarse_perm, level + 1, pads[1:], packs, buffer
        )
        update = grid.prolong(update, pad_right)
    else:
        (coarse_right,) = flat.restrict([residue], [pad_right], packs[0])
        update = flat.prolong(flat.solve(coarse_right, prepared, buffer), pad_right, packs[0])
    values = [v + e for v, e in zip(values, update)]
    for _ in range(2):
        values = grid.sweep(values, coefs, const)
    return values


def swap_order(domains):
    steps = [0, domains - 2] + list(range(2, domains - 2, 2))
    return [step + 1 - odd for step in steps[::-1] for odd in range(2)]


def coarse_kernel(
    count, dom_ref, *refs,
):
    parts = [refs[swap_order(count).index(k)] for k in range(count)]
    refs = refs[count:]
    coef, const, before, out, gathered, *refs = refs
    coarse_steps(parts, dom_ref, gathered, coef, const, before, out, *refs)


def coarse_steps(
    parts, dom_ref, gathered, coef, const, before, out,
    level, first, pad_right1, pad_perm1, pad_right2, pad_perm2, update, pack, pack_perm, buffer,
    done, sems,
):
    height = out.shape[0]
    dom = dom_ref[0]
    domains, own, nx, _ = gathered.shape
    for step, part in enumerate(parts):
        gathered[dom ^ step] = part[...]
    ny = LANES // 2
    grid = Packed(domains * own, nx, ny)
    left = iota((nx, LANES), 1) < ny
    right, perm = [], []
    for p in range(grid.planes):
        a = gathered[p // own, p % own]
        q = grid.planes + p
        b = gathered[q // own, q % own]
        right.append(jnp.where(left, a, roll(b, ny, 1)))
        perm.append(jnp.where(left, roll(a, ny, 1), b))
    pads = [(pad_right1, pad_perm1), (pad_right2, pad_perm2)]
    solved = packed_cycle(grid, right, perm, 1, pads, (pack, pack_perm), buffer)
    for p in range(grid.planes):
        update[p] = solved[p]
    planes, group = [], []
    for j in range(own + 2):
        layer = jnp.clip(dom * own + j - 1, 0, grid.nz - 1)
        group.append(layer // grid.planes)
        planes.append(update[lax.rem(layer, grid.planes)])
    for j, wide in enumerate(selector_dot(planes, lane_selector(1, LANES, 2, spread=True))):
        plane = jnp.where(group[j] == 0, wide[:, :LANES], wide[:, LANES:])
        pad = first.at[0]
        pad[pl.ds(0, nx, 2), :] = plane
        pad[pl.ds(1, nx, 2), :] = plane
        whole = first[0]
        level[2 * j] = before[2 * j] + whole
        level[2 * j + 1] = before[2 * j + 1] + whole

    def sweep(source, at, i):
        centre = source[i + 1]
        near = [coef[k, at + i] for k in range(6)]
        return stencil(centre, source[i], source[i + 2], near, KEEP * centre + const[at + i])

    def one(i):
        first[i] = sweep(level, 2, i)

    for i in range(height + 2):
        one(i)

    copies = []
    for i in range(height):
        done[i] = sweep(first, 3, i)
        copies.append(pltpu.make_async_copy(done.at[i], out.at[i], sems.at[i]))
        copies[-1].start()
    for copy in copies:
        copy.wait()


def fine_part(dom, perm, source, layers):
    height, nx, ny = perm[0].shape
    field = lambda *lead: pltpu.VMEM(lead + (nx, ny), F32)
    vmem = pl.BlockSpec(memory_space=pltpu.VMEM)
    sides = pl.pallas_call(
        side_kernel,
        out_shape=jax.ShapeDtypeStruct((5, height, nx, ny), F32),
        in_specs=[vmem],
        out_specs=vmem,
        compiler_params=pltpu.CompilerParams(vmem_limit_bytes=VMEM_LIMIT),
        name="sides",
    )(perm[0])
    smem = pl.BlockSpec(memory_space=pltpu.SMEM)
    return pl.pallas_call(
        functools.partial(fine_kernel, layers),
        out_shape=(
            jax.ShapeDtypeStruct((6, height + 6, nx, ny), F32),
            jax.ShapeDtypeStruct((height + 6, nx, ny), F32),
            jax.ShapeDtypeStruct((height + 4, nx, ny), F32),
            jax.ShapeDtypeStruct((height // 2, nx // 2, ny), F32),
        ),
        in_specs=[smem] + [vmem] * 7,
        out_specs=(vmem,) * 4,
        scratch_shapes=[
            field(3 * height),
            field(3 * height),
            field(height + 6),
            field(height // 2),
            field(height // 2),
        ],
        compiler_params=pltpu.CompilerParams(vmem_limit_bytes=VMEM_LIMIT),
        name="fine",
    )(dom, sides, *perm, *source)


def coarse_part(dom, parts, coefs, const, values, height):
    _, nx, ny = values.shape
    field = lambda *shape: pltpu.VMEM(shape, F32)
    whole = (len(parts),) + parts[0].shape
    grid1 = Packed(whole[0] * whole[1], nx // 2, ny // 2)
    grid2 = grid1.coarser()
    pads1 = field(grid1.planes // 2, grid1.nx, LANES)
    pads2 = field(grid2.planes // 2, grid2.nx, LANES)
    vmem = pl.BlockSpec(memory_space=pltpu.VMEM)
    smem = pl.BlockSpec(memory_space=pltpu.SMEM)
    return pl.pallas_call(
        functools.partial(coarse_kernel, whole[0]),
        out_shape=jax.ShapeDtypeStruct((height, nx, ny), F32),
        in_specs=[smem] + [vmem] * (whole[0] + 3),
        out_specs=pl.BlockSpec(memory_space=pl.ANY),
        scratch_shapes=[
            field(*whole),
            field(*values.shape),
            field(height + 2, nx, ny),
            pads1, pads1, pads2, pads2,
            field(grid1.planes, grid1.nx, LANES),
            field(1, Flat(grid2).rows, LANES),
            field(1, Flat(grid2).rows, LANES),
            field(Flat(grid2).buffer_rows, LANES),
            field(height, nx, ny),
            pltpu.SemaphoreType.DMA((height,)),
        ],
        compiler_params=pltpu.CompilerParams(vmem_limit_bytes=VMEM_LIMIT),
        name="coarse",
    )(dom, *(parts[k] for k in swap_order(len(parts))), coefs, const, values)


def swaps(x, axis, step):
    return lax.ppermute(x, axis, [(i, i ^ step) for i in range(lax.axis_size(axis))])


def other_side(x):
    props, domains = lax.axis_size("prop"), lax.axis_size("dom")
    pairs = []
    for p in range(props):
        for d in range(domains):
            end = d in (0, domains - 1)
            partner = ((p ^ 1) * domains + d) if end else (p * domains + ((d + 1) ^ 1) - 1)
            pairs.append((p * domains + d, partner))
    return lax.ppermute(x, ("prop", "dom"), pairs)


def source_side(x):
    props, domains = lax.axis_size("prop"), lax.axis_size("dom")
    pairs = []
    for p in range(props):
        for d in range(domains):
            if d in (0, domains - 1):
                target = (p ^ 1) * domains + (d if p % 2 == 0 else d ^ 1)
            elif p % 2 == 0:
                target = p * domains + (d ^ 1)
            else:
                target = p * domains + ((d + 1) ^ 1) - 1
            pairs.append((p * domains + d, target))
    return lax.ppermute(x, ("prop", "dom"), pairs)


def from_accepted(mine, accepted, beside):
    props = lax.axis_size("prop")
    apart = lax.axis_index("prop") ^ accepted
    own = SHRINK * mine
    step = props // 2
    came = swaps(mine, "prop", step)
    came, own, beside = lax.optimization_barrier((came, own, beside))
    current = jnp.where(apart & step, SHRINK * came, own)
    while step > 1:
        step //= 2
        came = jnp.concatenate([swaps(x, "prop", step) for x in jnp.split(current, 2)])
        current = jnp.where(apart & step, came, current)
    return current, beside


def gather_parts(mine):
    domains = lax.axis_size("dom")
    parts = {0: mine}
    for step in range(0, domains, 2):
        if step:
            parts[step] = swaps(mine, "dom", step)
        parts[step + 1] = swaps(parts[step], "dom", 1)
    return [parts[k] for k in range(domains)]


def body(states, accepted, noise, source):
    domains = lax.axis_size("dom")
    height = source.shape[0]
    dom = jnp.stack([lax.axis_index("dom"), lax.axis_index("prop")]).astype(jnp.int32)
    near = source_side(source)
    current, noise_part = from_accepted(states[0], accepted[0], BETA * noise[0])
    perm = jnp.exp(current + noise_part)
    _, source, near = lax.optimization_barrier((perm, source, near))
    perms = (perm, other_side(perm), swaps(perm, "dom", 1))
    sources = (OMEGA * source, near, swaps(near, "prop", 1))
    *level, coarse = fine_part(dom, perms, sources, domains * height)
    return coarse_part(dom, gather_parts(coarse), *level, height)[None]


def solution(mesh):
    in_specs = (
        P("prop", "dom", None, None),
        P(),
        P("prop", "dom", None, None),
        P("dom", None, None),
    )
    out_specs = P("prop", "dom", None, None)
    return jax.shard_map(body, mesh=mesh, in_specs=in_specs, out_specs=out_specs, check_vma=False)
```
